32 devices in a mesh: grp: 4 (over x, core), row: 2 (over y), col: 4 (over z).
Axes of the slice: x: 2, y: 2, z: 4, core: 2. Of those that a mesh axis runs over, the one named last changes fastest.
Arguments:
- tokens: bfloat16 [9216, 2048], P(('grp', 'col'), 'row'), may hold values from -6 to 6
- gain: bfloat16 [2048], P(('row', 'grp')), may hold values from 0.5 to 1.5
- in_proj: bfloat16 [2048, 2, 4096], P('row', None, ('col', 'grp')), may hold values from -0.125 to 0.125
- conv_weight: bfloat16 [4, 4096], P(None, ('col', 'row', 'grp')), may hold values from -3 to 3
- conv_bias: bfloat16 [4096], P(('col', 'row', 'grp')), may hold values from -1.5 to 1.5
- x_proj: bfloat16 [4096, 160], P(('col', 'row', 'grp')), may hold values from -0.09375 to 0.09375
- dt_proj: bfloat16 [128, 4096], P(None, ('col', 'row', 'grp')), may hold values from -0.5 to 0.5
- dt_bias: bfloat16 [4096], P(('col', 'row', 'grp')), may hold values from -6 to -2.5
- a_log: bfloat16 [16, 4096], P(None, ('col', 'row', 'grp')), may hold values from 0 to 2.6875
- d_skip: bfloat16 [4096], P(('col', 'row', 'grp')), may hold values from 0.25 to 1.75
- out_proj: bfloat16 [4096, 2048], P('col', ('row', 'grp')), may hold values from -0.1875 to 0.1875
- table: int32 [8], P('grp'), may hold values from 0 to 1
- cotangent: bfloat16 [9216, 2048], P(('grp', 'col'), 'row'), may hold values from -6 to 6
Outputs:
- output: bfloat16 [9216, 2048], P(('grp', 'col'), 'row')
- input_grad: bfloat16 [9216, 2048], P(('grp', 'col'), 'row')
- gain_grad: float32 [2048], P(('row', 'grp'))
- in_proj_grad: float32 [2048, 2, 4096], P('row', None, ('col', 'grp'))
- conv_weight_grad: float32 [4, 4096], P(None, ('col', 'row', 'grp'))
- conv_bias_grad: float32 [4096], P(('col', 'row', 'grp'))
- x_proj_grad: float32 [4096, 160], P(('col', 'row', 'grp'))
- dt_proj_grad: float32 [128, 4096], P(None, ('col', 'row', 'grp'))
- dt_bias_grad: float32 [4096], P(('col', 'row', 'grp'))
- a_log_grad: float32 [16, 4096], P(None, ('col', 'row', 'grp'))
- d_skip_grad: float32 [4096], P(('col', 'row', 'grp'))
- out_proj_grad: float32 [4096, 2048], P('col', ('row', 'grp'))
The draws below stay inside these ranges and needn't reach their ends.
Inputs may be any that keep to these rules, and one draw needn't show every extreme that they name: `table`: entry k * 2 + j names which of group k's prompts its j-th continuation resumes.
All inputs are finite; a program needn't handle non-finite values.
Results may differ from the reference program's by a relative error of at most 0.011.
Values may be sent and summed in bfloat16 or wider, within the bound.
A program may use at most 320 MiB of HBM per device.

```python
import jax
import jax.numpy as jnp
from jax import lax

D = 2048
E = 4096
NSTATE = 16
KCONV = 4
RANK = 128
NPROMPT = 2
LP = 1024
LC = 128
NCONT = 2
XWIDTH = 160
T_GRP = 2304
TOKENS = 9216
CONTS = 8
N_GRP = 4


def set_ends(drawn, own_key, smallest, largest):
    longest = drawn.shape.index(max(drawn.shape))
    spots = []
    for shift in (0, 1):
        where = [jax.random.randint(jax.random.fold_in(own_key, axis), (), 0, length) for axis, length in enumerate(drawn.shape)]
        where[longest] = (where[longest] + shift) % drawn.shape[longest]
        spots.append(tuple(where))
    return drawn.at[spots[0]].set(smallest).at[spots[1]].set(largest)


def levels(key, extent, split, smallest, largest):
    level = 1.0
    for dim, blocks in split:
        heights = jax.random.uniform(jax.random.fold_in(jax.random.fold_in(key, 6), dim), (blocks,), jnp.float32, smallest / len(split), largest / len(split))
        level = level * jnp.repeat(jnp.exp(heights), extent[dim] // blocks).reshape((-1,) + (1,) * (len(extent) - 1 - dim))
    return level


def bell_draw(stream_key, dims, width, limit, cuts=(), held_as=jnp.bfloat16):
    entries = jax.random.normal(stream_key, dims, jnp.float32) * width
    if len(cuts) > 0:
        entries = levels(stream_key, dims, cuts, -0.22, 0.18) * entries
    return jnp.clip(entries, min=-limit, max=limit).astype(held_as)


def setup_inputs(seed: int = 0) -> dict:
    seeds = jax.random.split(jax.random.key(seed), 14)
    return {
        "tokens": bell_draw(seeds[0], (TOKENS, D), 1.0, 6.0, ((0, 16), (1, 2))),
        "gain": jnp.clip(1.0 + 0.1 * jax.random.normal(seeds[1], (D,), jnp.float32), 0.5, 1.5).astype(jnp.bfloat16),
        "in_proj": bell_draw(seeds[2], (D, 2, E), D ** -0.5, 0.125, ((0, 2), (2, 16))),
        "conv_weight": bell_draw(seeds[3], (KCONV, E), KCONV ** -0.5, 3.0, ((1, 32),)),
        "conv_bias": bell_draw(seeds[4], (E,), 0.3, 1.5, ((0, 32),)),
        "x_proj": bell_draw(seeds[5], (E, XWIDTH), E ** -0.5, 0.09375, ((0, 32),)),
        "dt_proj": bell_draw(seeds[6], (RANK, E), RANK ** -0.5, 0.5, ((1, 32),)),
        "dt_bias": jnp.clip(-6.0 + 3.5 * jax.random.uniform(seeds[7], (E,), jnp.float32) ** levels(seeds[7], (E,), ((0, 32),), -0.2, 0.2), -6.0, -2.5).astype(jnp.bfloat16),
        "a_log": jnp.clip(2.6875 * jax.random.uniform(seeds[8], (NSTATE, E), jnp.float32) ** levels(seeds[8], (NSTATE, E), ((1, 32),), -0.2, 0.2), 0.0, 2.6875).astype(jnp.bfloat16),
        "d_skip": jnp.clip(1.0 + 0.15 * jax.random.normal(seeds[9], (E,), jnp.float32), 0.25, 1.75).astype(jnp.bfloat16),
        "out_proj": bell_draw(seeds[10], (E, D), (E // 4) ** -0.5, 0.1875, ((0, 4), (1, 8))),
        "table": set_ends(jax.random.randint(seeds[11], (CONTS,), 0, NPROMPT), jax.random.fold_in(seeds[11], 1), 0, NPROMPT - 1).astype(jnp.int32),
        "cotangent": bell_draw(seeds[12], (TOKENS, D), 1.0, 6.0, ((0, 16), (1, 2))),
    }


@jax.custom_vjp
def low(v):
    return lax.optimization_barrier(v.astype(jnp.bfloat16)).astype(jnp.float32)

@jax.custom_vjp
def low_back(v):
    return v

def low_keep(v):
    return (low(v), None)

def low_pass(kept, grad):
    return (grad,)

def back_keep(v):
    return (v, None)

def back_low(kept, grad):
    return (low(grad),)
low.defvjp(low_keep, low_pass)
low_back.defvjp(back_keep, back_low)
eps = 1e-05
highest = lax.Precision.HIGHEST

def run_scan(start, step_size, values, input_map, read_map, decay_rate):
    length = step_size.shape[1]
    block_len = min(64, length)

    def time_first(source):
        swapped = jnp.swapaxes(source, 0, 1)
        return swapped.reshape((length // block_len, block_len) + swapped.shape[1:])

    def advance(hidden, step_in):
        step_t, value_t, input_t, read_t = step_in
        factor = jnp.exp(step_t[:, None, :] * decay_rate[None])
        hidden = factor * hidden + (step_t * value_t)[:, None, :] * input_t[:, :, None]
        return (hidden, lax.optimization_barrier(jnp.sum(hidden * read_t[:, :, None], axis=1)))

    @jax.checkpoint
    def run_block(hidden, block_in):
        return lax.scan(advance, hidden, block_in)
    final, results = lax.scan(run_block, start, (time_first(step_size), time_first(values), time_first(input_map), time_first(read_map)))
    results = results.reshape((length,) + results.shape[2:])
    return (final, jnp.swapaxes(results, 0, 1))

def convolve(padded, kernel, shift_bias, length):
    summed = shift_bias
    for offset in range(kernel.shape[0]):
        summed = summed + kernel[offset] * padded[:, offset:offset + length]
    return summed

def group_forward(tokens, table, weights):
    gain, in_w, conv_w, conv_b, xproj_w, dtproj_w, dtb, alog, dskip, out_w = weights
    inv_rms = lax.rsqrt(lax.optimization_barrier(jnp.mean(tokens * tokens, axis=-1, keepdims=True)) + eps)
    normed = low(tokens * gain)
    projected = low_back(jnp.einsum('td,dke->tke', normed, in_w, precision=highest))
    mixed = inv_rms[:, :, None] * projected
    inner_part = mixed[:, 0]
    gate_part = mixed[:, 1]
    prompts = inner_part[:NPROMPT * LP].reshape(NPROMPT, LP, E)
    conts = inner_part[NPROMPT * LP:].reshape(NCONT, LC, E)
    choose = (table[:, None] == jnp.arange(NPROMPT)[None, :]).astype(jnp.float32)
    tails = jnp.einsum('cp,pke->cke', choose, prompts[:, LP - KCONV + 1:], precision=highest)
    prompt_pad = jnp.concatenate([jnp.zeros((NPROMPT, KCONV - 1, E), jnp.float32), prompts], axis=1)
    cont_pad = jnp.concatenate([tails, conts], axis=1)
    conv_out = jnp.concatenate([convolve(prompt_pad, conv_w, conv_b, LP).reshape(-1, E), convolve(cont_pad, conv_w, conv_b, LC).reshape(-1, E)], axis=0)
    xconv = low(jax.nn.silu(conv_out))
    xdbl = low_back(jnp.dot(xconv, xproj_w, precision=highest))
    dtlow = low(xdbl[:, :RANK])
    input_map = xdbl[:, RANK:RANK + NSTATE]
    read_map = xdbl[:, RANK + NSTATE:]
    step_size = jax.nn.softplus(low_back(jnp.dot(dtlow, dtproj_w, precision=highest)) + dtb)
    decay_rate = -jnp.exp(alog)
    split_at = NPROMPT * LP

    def prompt_rows(source):
        return source[:split_at].reshape((NPROMPT, LP) + source.shape[1:])

    def cont_rows(source):
        return source[split_at:].reshape((NCONT, LC) + source.shape[1:])
    finals, prompt_out = run_scan(jnp.zeros((NPROMPT, NSTATE, E), jnp.float32), prompt_rows(step_size), prompt_rows(xconv), prompt_rows(input_map), prompt_rows(read_map), decay_rate)
    anchor = jnp.einsum('cp,pne->cne', choose, finals, precision=highest)
    ignored, cont_out = run_scan(anchor, cont_rows(step_size), cont_rows(xconv), cont_rows(input_map), cont_rows(read_map), decay_rate)
    yscan = jnp.concatenate([prompt_out.reshape(-1, E), cont_out.reshape(-1, E)], axis=0)
    yfull = yscan + dskip * xconv
    gated = low(yfull * jax.nn.silu(gate_part))
    return tokens + jnp.dot(gated, out_w, precision=highest)

def reference(tokens, gain, in_proj, conv_weight, conv_bias, x_proj, dt_proj, dt_bias, a_log, d_skip, out_proj, table, cotangent):
    weights = tuple((source.astype(jnp.float32) for source in (gain, in_proj, conv_weight, conv_bias, x_proj, dt_proj, dt_bias, a_log, d_skip, out_proj)))
    grouped = tokens.astype(jnp.float32).reshape(N_GRP, T_GRP, D)
    tables = table.reshape(N_GRP, NCONT)

    def whole(grouped_in, weights_in):

        def per_group(group_pair):
            return group_forward(group_pair[0], group_pair[1], weights_in)
        return lax.map(jax.checkpoint(per_group), (grouped_in, tables))
    output, pullback = jax.vjp(whole, grouped, weights)
    d_tokens, d_weights = pullback(cotangent.astype(jnp.float32).reshape(N_GRP, T_GRP, D))
    return (output.reshape(TOKENS, D).astype(jnp.bfloat16), d_tokens.reshape(TOKENS, D).astype(jnp.bfloat16), d_weights[0], d_weights[1], d_weights[2], d_weights[3], d_weights[4], d_weights[5], d_weights[6], d_weights[7], d_weights[8], d_weights[9])
```

```python
import functools

import jax
import jax.numpy as jnp
from jax import lax
from jax.experimental import pallas as pl
from jax.experimental.pallas import tpu as pltpu
from jax.sharding import PartitionSpec as P

D = 2048
NSTATE = 16
KCONV = 4
RANK = 128
NPROMPT = 2
LP = 1024
LC = 128
NCONT = 2

eps = 1e-05
CH = 128
SUB = 16
PC = LP // CH
SEQ = LP + LC
NCH = SEQ // CH
XW = RANK + 2 * NSTATE
SPAN = SUB * NSTATE
LOG2E = 1.4426950408889634
VMEM_LIMIT = 56 * 1024 * 1024

f32 = jnp.float32
bf16 = jnp.bfloat16


def dot_nn(a, b):
    return lax.dot_general(a, b, (((1,), (0,)), ((), ())), preferred_element_type=f32)


def dot_nt(a, b):
    return lax.dot_general(a, b, (((1,), (1,)), ((), ())), preferred_element_type=f32)


def dot_tn(a, b):
    return lax.dot_general(a, b, (((0,), (0,)), ((), ())), preferred_element_type=f32)


def expand_tile():
    lane = lax.broadcasted_iota(jnp.int32, (NSTATE, SPAN), 1)
    row = lax.broadcasted_iota(jnp.int32, (NSTATE, SPAN), 0)
    return jnp.where(lane % NSTATE == row, 1.0, 0.0)


def own_token(rows):
    lane = lax.broadcasted_iota(jnp.int32, (rows, SPAN), 1)
    row = lax.broadcasted_iota(jnp.int32, (rows, SPAN), 0)
    return lane // NSTATE == row % SUB


def conv_forward(inner_ref, inv_ref, tail_ref, conv_ref, xproj_ref, xconv_ref, xdbl_ref, buf):
    i = pl.program_id(0)

    @pl.when(i == 0)
    def _():
        buf[0:8] = jnp.zeros_like(buf[0:8])

    @pl.when(i == PC)
    def _():
        buf[0:8] = tail_ref[...]

    @pl.when((i > 0) & (i < PC))
    def _():
        buf[0:8] = buf[CH : CH + 8]

    buf[8 : CH + 8] = inv_ref[...] * inner_ref[...]
    out = conv_ref[4:5]
    for k in range(KCONV):
        out = out + conv_ref[k : k + 1] * buf[5 + k : 5 + k + CH]
    xconv = (out * jax.nn.sigmoid(out)).astype(bf16)
    xconv_ref[...] = xconv
    xdbl_ref[...] = dot_nt(xproj_ref[...], xconv)


def softplus(v):
    return jnp.maximum(v, 0.0) + jnp.log1p(jnp.exp(-jnp.abs(v)))


def by_sub(v):
    return v.reshape(CH // SUB, SUB, v.shape[-1])


def scan_forward(kept, xdbl_ref, xconv_ref, gate_ref, inv_ref, dtp_ref, vec_ref, rate_ref, start_ref, *refs):
    gated_ref, yfull_ref, starts_ref, final_ref, dt_s, u_s, cb_s, h_s, y_s = refs[kept:]
    i = pl.program_id(0)

    @pl.when(i == 0)
    def _():
        final_ref[...] = start_ref[...]

    starts_ref[0] = final_ref[...]
    xconv = xconv_ref[...].astype(f32)
    step = softplus(dot_tn(xdbl_ref[:RANK].astype(bf16), dtp_ref[...]) + vec_ref[0:1])
    dt_s[...] = by_sub(step)
    u_s[...] = by_sub(step * xconv)
    reads = dot_tn(xdbl_ref[RANK + NSTATE :].astype(bf16), expand_tile().astype(bf16))
    cb_s[...] = jnp.where(own_token(CH), reads, 0.0).astype(bf16)
    rate = rate_ref[...] * LOG2E

    def block(j, carried):
        h, maps = carried
        for t in range(SUB):
            a = jnp.exp2(dt_s[j, t : t + 1, :] * rate)
            h = a * h + u_s[j, t : t + 1, :] * maps[:, t : t + 1]
            h_s[t * NSTATE : (t + 1) * NSTATE, :] = h.astype(bf16)
        rows = pl.ds(pl.multiple_of(j * SUB, SUB), SUB)
        y_s[rows, :] = dot_nn(cb_s[rows, :], h_s[...])
        return (h, pltpu.roll(maps, CH - SUB, 1))

    h, _ = lax.fori_loop(0, CH // SUB, block, (final_ref[...], xdbl_ref[RANK : RANK + NSTATE]))
    final_ref[...] = h
    yfull = y_s[...] + vec_ref[1:2] * xconv
    gate = inv_ref[...] * gate_ref[...]
    gated_ref[...] = (yfull * (gate * jax.nn.sigmoid(gate))).astype(bf16)
    yfull_ref[...] = yfull.astype(bf16)


def scan_backward(kept, xdbl_ref, xconv_ref, dy_ref, dtp_ref, vec_ref, rate_ref, starts_ref, carry_ref, alog0_ref, sums0_ref, dtpg0_ref, *refs):
    dxdbl_ref, dxc_ref, alog_ref, sums_ref, dtpg_ref, first_ref = refs[kept : kept + 6]
    dt_s, u_s, x_s, dy_s, a_s, h_s, g_s, w_s, b_s, m1_s, m2_s, ds_s, dx_s, sig_s = refs[kept + 6 :]
    i = pl.program_id(0)

    @pl.when(i == 0)
    def _():
        alog_ref[...] = alog0_ref[...]
        sums_ref[...] = sums0_ref[...]
        dtpg_ref[...] = dtpg0_ref[...]
        first_ref[...] = carry_ref[...]

    low = xdbl_ref[:RANK].astype(bf16)
    step_inner = dot_tn(low, dtp_ref[...]) + vec_ref[0:1]
    step = softplus(step_inner)
    sig_s[...] = jax.nn.sigmoid(step_inner)
    xconv = xconv_ref[...].astype(f32)
    dy = dy_ref[...]
    dt_s[...] = by_sub(step)
    u_s[...] = by_sub(step * xconv)
    x_s[...] = by_sub(xconv)
    dy_s[...] = by_sub(dy)
    tile = expand_tile().astype(bf16)
    b_s[...] = jnp.where(own_token(CH), dot_tn(xdbl_ref[RANK : RANK + NSTATE].astype(bf16), tile), 0.0).astype(bf16)
    rate = rate_ref[...]
    rate2 = rate * LOG2E
    h_s[0:NSTATE] = starts_ref[0]

    def ahead(j, carried):
        h, maps = carried
        for t in range(SUB):
            a = jnp.exp2(dt_s[j, t : t + 1, :] * rate2)
            h = a * h + u_s[j, t : t + 1, :] * maps[:, t : t + 1]
            a_s[j, t * NSTATE : (t + 1) * NSTATE, :] = a
            at = pl.multiple_of(j * SPAN + (t + 1) * NSTATE, NSTATE)
            h_s[pl.ds(at, NSTATE), :] = h
        return (h, pltpu.roll(maps, CH - SUB, 1))

    lax.fori_loop(0, CH // SUB, ahead, (starts_ref[0], xdbl_ref[RANK : RANK + NSTATE]))
    ones = jnp.where(own_token(SUB), 1.0, 0.0).astype(bf16)
    mine_sub = own_token(SUB)

    def back(jj, carried):
        g, alog, maps = carried
        j = CH // SUB - 1 - jj
        maps = pltpu.roll(maps, SUB, 1)
        for t in reversed(range(SUB)):
            dt = dt_s[j, t : t + 1, :]
            gs = maps[:, t : t + 1] * dy_s[j, t : t + 1, :] + g
            g = a_s[j, t * NSTATE : (t + 1) * NSTATE, :] * gs
            prior = h_s[pl.ds(pl.multiple_of(j * SPAN + t * NSTATE, NSTATE), NSTATE), :]
            w = g * prior
            alog = alog + w * dt
            g_s[t * NSTATE : (t + 1) * NSTATE, :] = gs.astype(bf16)
            w_s[t * NSTATE : (t + 1) * NSTATE, :] = (w * rate).astype(bf16)
        rows = pl.ds(pl.multiple_of(j * SUB, SUB), SUB)
        gs_all = g_s[...]
        through = dot_nn(b_s[rows, :], gs_all)
        ds_s[rows, :] = dot_nn(ones, w_s[...]) + x_s[j] * through
        dx_s[rows, :] = dt_s[j] * through + vec_ref[1:2] * dy_s[j]
        hs = h_s[pl.ds(pl.multiple_of(j * SPAN + NSTATE, NSTATE), SPAN), :].astype(bf16)
        m1_s[rows, :] = jnp.where(mine_sub, dot_nt(u_s[j].astype(bf16), gs_all), 0.0).astype(bf16)
        m2_s[rows, :] = jnp.where(mine_sub, dot_nt(dy_s[j].astype(bf16), hs), 0.0).astype(bf16)
        return (g, alog, maps)

    g, alog, _ = lax.fori_loop(0, CH // SUB, back, (first_ref[...], alog_ref[...], xdbl_ref[RANK + NSTATE :]))
    first_ref[...] = g
    alog_ref[...] = alog
    d_inner = ds_s[...] * sig_s[...]
    d_low = d_inner.astype(bf16)
    sums_ref[0:1] = sums_ref[0:1] + jnp.sum(d_inner, axis=0, keepdims=True)
    sums_ref[1:2] = sums_ref[1:2] + jnp.sum(dy * xconv, axis=0, keepdims=True)
    dtpg_ref[...] = dtpg_ref[...] + dot_nn(low, d_low)
    dxdbl_ref[:RANK] = dot_nt(dtp_ref[...], d_low)
    dxdbl_ref[RANK : RANK + NSTATE] = dot_nt(tile, m1_s[...])
    dxdbl_ref[RANK + NSTATE :] = dot_nt(tile, m2_s[...])
    dxc_ref[...] = dx_s[...]


def conv_backward(kept, chunks, first, inner_ref, halo_ref, inv_ref, halo_inv_ref, tail_ref, conv_ref, xproj_ref, dxc_ref, dxdbl_ref, follow_ref, sums0_ref, xprojg0_ref, *refs):
    dproj_ref, dscale_ref, sums_ref, xprojg_ref, head_ref, buf, dbuf = refs[kept:]
    i = pl.program_id(0)
    chunk = first + chunks - 1 - i

    @pl.when(i == 0)
    def _():
        sums_ref[...] = sums0_ref[...]
        xprojg_ref[...] = xprojg0_ref[...]
        head_ref[...] = follow_ref[...]

    projected = inner_ref[...]
    inv = inv_ref[...]
    before = halo_inv_ref[...] * halo_ref[...]
    before = jnp.where(chunk == 0, 0.0, jnp.where(chunk == PC, tail_ref[...], before))
    buf[0:8] = before
    buf[8 : CH + 8] = inv * projected
    out = conv_ref[4:5]
    for k in range(KCONV):
        out = out + conv_ref[k : k + 1] * buf[5 + k : 5 + k + CH]
    sig = jax.nn.sigmoid(out)
    xconv = (out * sig).astype(bf16)
    dxdbl = dxdbl_ref[...].astype(bf16)
    xprojg_ref[...] = xprojg_ref[...] + dot_nn(dxdbl, xconv)
    d_x = dxc_ref[...] + dot_tn(dxdbl, xproj_ref[...])
    d_conv = d_x * (sig * (1.0 + out * (1.0 - sig)))
    dbuf[CH : CH + 8] = head_ref[...]
    dbuf[0:CH] = d_conv
    d_inner = conv_ref[3:4] * d_conv
    for k in range(KCONV - 1):
        d_inner = d_inner + conv_ref[k : k + 1] * dbuf[3 - k : 3 - k + CH]
    for k in range(KCONV):
        sums_ref[k : k + 1] = sums_ref[k : k + 1] + jnp.sum(buf[5 + k : 5 + k + CH] * d_conv, axis=0, keepdims=True)
    sums_ref[4:5] = sums_ref[4:5] + jnp.sum(d_conv, axis=0, keepdims=True)
    dproj_ref[...] = (inv * d_inner).astype(bf16)
    dscale_ref[...] = jnp.sum(d_inner * projected, axis=1, keepdims=True)
    head_ref[...] = d_conv[0:8]


def call(body, chunks, args, in_specs, outs, out_specs, scratch, micros, aliases=None):
    return pl.pallas_call(
        body,
        grid=(chunks,),
        in_specs=in_specs,
        out_specs=out_specs,
        scratch_shapes=scratch,
        out_shape=outs,
        input_output_aliases=aliases or {},
        compiler_params=pltpu.CompilerParams(dimension_semantics=("arbitrary",), vmem_limit_bytes=VMEM_LIMIT),
        cost_estimate=pl.CostEstimate(flops=micros * 1000000000, bytes_accessed=1000000, transcendentals=0),
    )(*args)


def shaped(*shape, dtype=f32):
    return jax.ShapeDtypeStruct(shape, dtype)


def rows_of(width, place):
    return pl.BlockSpec((CH, width), lambda i: (place(i), 0))


def lanes_of(height, place):
    return pl.BlockSpec((height, CH), lambda i: (0, place(i)))


def whole(*shape):
    return pl.BlockSpec(shape, lambda i: (0,) * len(shape))


ANY = pl.BlockSpec(memory_space=pl.ANY)


def run_conv_forward(inner, inv, tail, conv, xproj):
    w = inner.shape[1]
    at = lambda i: i
    return call(
        conv_forward,
        NCH,
        (inner, inv, tail, conv, xproj),
        [rows_of(w, at), rows_of(1, at), whole(8, w), whole(8, w), whole(XW, w)],
        (shaped(SEQ, w, dtype=bf16), shaped(XW, SEQ)),
        (rows_of(w, at), lanes_of(XW, at)),
        [pltpu.VMEM((CH + 8, w), f32)],
        12,
    )


def run_scan_forward(first, chunks, xdbl, xconv, gate, inv, dtp, vec, rate, start, kept=()):
    w = xconv.shape[1]
    at = lambda i: first + i
    return call(
        functools.partial(scan_forward, len(kept)),
        chunks,
        (xdbl, xconv, gate, inv, dtp, vec, rate, start, *kept),
        [lanes_of(XW, at), rows_of(w, at), rows_of(w, at), rows_of(1, at), whole(RANK, w), whole(8, w), whole(NSTATE, w), whole(NSTATE, w)] + [ANY] * len(kept),
        (shaped(SEQ, w, dtype=bf16), shaped(SEQ, w, dtype=bf16), shaped(NCH, NSTATE, w), shaped(NSTATE, w)),
        (rows_of(w, at), rows_of(w, at), pl.BlockSpec((1, NSTATE, w), lambda i: (first + i, 0, 0)), whole(NSTATE, w)),
        [
            pltpu.VMEM((CH // SUB, SUB, w), f32),
            pltpu.VMEM((CH // SUB, SUB, w), f32),
            pltpu.VMEM((CH, SPAN), bf16),
            pltpu.VMEM((SPAN, w), bf16),
            pltpu.VMEM((CH, w), f32),
        ],
        5 * chunks,
        {8 + k: k for k in range(len(kept))},
    )


def run_scan_backward(first, chunks, xdbl, xconv, dy, dtp, vec, rate, starts, carry, sums, kept=()):
    w = xconv.shape[1]
    at = lambda i: first + chunks - 1 - i
    local = lambda i: chunks - 1 - i
    sub = pltpu.VMEM((CH // SUB, SUB, w), f32)
    return call(
        functools.partial(scan_backward, len(kept)),
        chunks,
        (xdbl, xconv, dy, dtp, vec, rate, starts, carry, *sums, *kept),
        [
            lanes_of(XW, at),
            rows_of(w, at),
            rows_of(w, at),
            whole(RANK, w),
            whole(8, w),
            whole(NSTATE, w),
            pl.BlockSpec((1, NSTATE, w), lambda i: (at(i), 0, 0)),
            whole(NSTATE, w),
            whole(NSTATE, w),
            whole(8, w),
            whole(RANK, w),
        ]
        + [ANY] * len(kept),
        (shaped(XW, chunks * CH), shaped(SEQ, w), shaped(NSTATE, w), shaped(8, w), shaped(RANK, w), shaped(NSTATE, w)),
        (lanes_of(XW, local), rows_of(w, at), whole(NSTATE, w), whole(8, w), whole(RANK, w), whole(NSTATE, w)),
        [
            sub,
            sub,
            sub,
            sub,
            pltpu.VMEM((CH // SUB, SPAN, w), f32),
            pltpu.VMEM(((CH + 1) * NSTATE, w), f32),
            pltpu.VMEM((SPAN, w), bf16),
            pltpu.VMEM((SPAN, w), bf16),
            pltpu.VMEM((CH, SPAN), bf16),
            pltpu.VMEM((CH, SPAN), bf16),
            pltpu.VMEM((CH, SPAN), bf16),
            pltpu.VMEM((CH, w), f32),
            pltpu.VMEM((CH, w), f32),
            pltpu.VMEM((CH, w), f32),
        ],
        11 * chunks,
        {11 + k: 1 + k for k in range(len(kept))},
    )


def run_conv_backward(first, chunks, inner, inv, tail, conv, xproj, dxc, dxdbl, follow, sums, kept=()):
    w = inner.shape[1]
    at = lambda i: first + chunks - 1 - i
    local = lambda i: chunks - 1 - i
    before = lambda i: (jnp.maximum(at(i) * (CH // 8) - 1, 0), 0)
    return call(
        functools.partial(conv_backward, len(kept), chunks, first),
        chunks,
        (inner, inner, inv, inv, tail, conv, xproj, dxc, dxdbl, follow, *sums, *kept),
        [
            rows_of(w, at),
            pl.BlockSpec((8, w), before),
            rows_of(1, at),
            pl.BlockSpec((8, 1), before),
            whole(8, w),
            whole(8, w),
            whole(XW, w),
            rows_of(w, at),
            lanes_of(XW, local),
            whole(8, w),
            whole(8, w),
            whole(XW, w),
        ]
        + [ANY] * len(kept),
        (shaped(SEQ, w, dtype=bf16), shaped(SEQ, 1), shaped(8, w), shaped(XW, w), shaped(8, w)),
        (rows_of(w, at), rows_of(1, at), whole(8, w), whole(XW, w), whole(8, w)),
        [pltpu.VMEM((CH + 8, w), f32), pltpu.VMEM((CH + 8, w), f32)],
        2 * chunks,
        {12 + k: k for k in range(len(kept))},
    )


MESH = pl.DeviceIdType.MESH
SLOTS = 4


def remote(src, dst, send, recv, device):
    return pltpu.make_async_remote_copy(src_ref=src, dst_ref=dst, send_sem=send, recv_sem=recv, device_id=device, device_id_type=MESH)


def xor_bit(a, b):
    return a + b - 2 * a * b


def token_pieces(c, local):
    cut = local - LC
    low = cut - LC
    if c == 0:
        return [(0, local, 0, 0)]
    if c == 1:
        return [(0, cut, 0, local), (cut, local, 1, 0)]
    if c == 2:
        return [(0, local, 1, LC)]
    return [(0, low, 1, LC + local), (low, cut, 0, LP), (cut, local, 1, LP)]


def gather_start(tokens, in_i, in_g, out_w, small, raw, wi, wg, wo, small_all, w_send, w_recv, t_send, t_recv, here):
    g, r, c = lax.axis_index("grp"), lax.axis_index("row"), lax.axis_index("col")
    x, core = g // 2, g % 2
    local = tokens.shape[0]
    odd = c % 2
    same_half = xor_bit(r, odd)
    same_col = 2 * same_half + c // 2
    other_col = 2 * (1 - same_half) + c // 2
    alone = same_col == c
    gx = (1 - x) * 2 + core
    gc = x * 2 + 1 - core
    gxc = (1 - x) * 2 + 1 - core

    barrier = pltpu.get_barrier_semaphore()
    for dr in range(2):
        for dc in range(4):
            if dr or dc:
                pl.semaphore_signal(barrier, inc=1, device_id=(g, (r + dr) % 2, (c + dc) % 4), device_id_type=MESH)
    pl.semaphore_signal(barrier, inc=1, device_id=(gx, r, c), device_id_type=MESH)
    pl.semaphore_signal(barrier, inc=1, device_id=(gc, r, c), device_id_type=MESH)
    pl.semaphore_wait(barrier, 9)

    natural = lambda k, d: 2 * (g, gx, gc, gxc)[k] + d
    relative = lambda k, d: 2 * k + d
    origin = (r, 1 - r)
    by_row = lambda k, d: origin[d] * 4 + (g, gx, gc, gxc)[k]
    weights = [(small, small_all, by_row), (in_i, wi, natural), (in_g, wg, natural), (out_w, wo, relative)]

    def first_hop(n, d):
        src, dst, slot = weights[n]
        if slot is by_row:
            at = r * 4 + g
        else:
            at = slot(0, d)
        device = (g, r, same_col) if d == 0 else (g, 1 - r, other_col)
        return remote(src, dst.at[at], w_send.at[n, d], w_recv.at[n, d], device)

    def hop(n, d, k, device, came):
        src, dst, slot = weights[n]
        at = slot(k, d)
        to = relative(came, d) if slot is relative else at
        i = (0, 2, 4, 6)[came] + d
        return remote(dst.at[at], dst.at[to], w_send.at[n, i], w_recv.at[n, i], device)

    def begin(n):
        src, dst, slot = weights[n]

        @pl.when(alone)
        def _():
            pltpu.make_async_copy(src, dst.at[by_row(0, 0) if slot is by_row else slot(0, 0)], here.at[n]).start()

        @pl.when(jnp.logical_not(alone))
        def _():
            first_hop(n, 0).start()

        first_hop(n, 1).start()

    def arrived_first(n, d):
        src, dst, slot = weights[n]
        if d == 0:

            @pl.when(alone)
            def _():
                pltpu.make_async_copy(src, dst.at[by_row(0, 0) if slot is by_row else slot(0, 0)], here.at[n]).wait()

            @pl.when(jnp.logical_not(alone))
            def _():
                first_hop(n, 0).wait_recv()
        else:
            first_hop(n, 1).wait_recv()

    x_dev, core_dev = (gx, r, c), (gc, r, c)

    def forward(n):
        for d in range(2):
            arrived_first(n, d)
            hop(n, d, 0, x_dev, 1).start()
            hop(n, d, 0, core_dev, 2).start()

    def forward_again(n):
        for d in range(2):
            hop(n, d, 0, x_dev, 1).wait_recv()
            hop(n, d, 1, core_dev, 3).start()

    def token_copies(k):
        copies, mine = [], []
        for a, b, s, at in token_pieces(k, local):
            for dr in range(2):
                for dc in range(2):
                    target = 2 * s + dc
                    dst = raw.at[dr, pl.ds(at, b - a)]
                    src = tokens.at[pl.ds(a, b - a)]
                    if dr == 0 and target == k:
                        mine.append(pltpu.make_async_copy(src, dst, here.at[4 + len(mine)]))
                    else:
                        device = (g, r if dr == 0 else 1 - r, target)
                        copies.append(remote(src, dst, t_send.at[len(copies)], t_recv.at[dr], device))
        return copies, mine

    begin(0)
    begin(1)
    for k in range(4):

        @pl.when(c == k)
        def _(k=k):
            copies, mine = token_copies(k)
            for copy in mine + copies:
                copy.start()

    begin(2)
    begin(3)
    for n in range(4):
        forward(n)
    for n in range(4):
        forward_again(n)
    for k in range(4):

        @pl.when(c == k)
        def _(k=k):
            copies, mine = token_copies(k)
            held = sum(b - a for a, b, s, at in token_pieces(k, local) if s == k // 2)
            rest = raw.at[0, pl.ds(0, SEQ - held)]
            pltpu.make_async_copy(rest, rest, t_recv.at[0]).wait()
            pltpu.make_async_copy(raw.at[1], raw.at[1], t_recv.at[1]).wait()
            for copy in mine:
                copy.wait()
            for copy in copies:
                copy.wait_send()

    for n in range(4):
        for d in range(2):
            hop(n, d, 0, core_dev, 2).wait_recv()
            hop(n, d, 1, core_dev, 3).wait_recv()
            hop(n, d, 0, x_dev, 1).wait_send()
            hop(n, d, 0, core_dev, 2).wait_send()
            hop(n, d, 1, core_dev, 3).wait_send()

        @pl.when(jnp.logical_not(alone))
        def _(n=n):
            first_hop(n, 0).wait_send()

        first_hop(n, 1).wait_send()


def run_gather_start(tokens, in_i, in_g, out_w, small):
    rows, width = tokens.shape
    return pl.pallas_call(
        gather_start,
        in_specs=[ANY] * 5,
        out_specs=[ANY] * 5,
        out_shape=(
            shaped(2, SEQ, width, dtype=bf16),
            shaped(8, *in_i.shape, dtype=bf16),
            shaped(8, *in_g.shape, dtype=bf16),
            shaped(8, *out_w.shape, dtype=bf16),
            shaped(8, *small.shape, dtype=bf16),
        ),
        scratch_shapes=[
            pltpu.SemaphoreType.DMA((4, 8)),
            pltpu.SemaphoreType.DMA((4, 8)),
            pltpu.SemaphoreType.DMA((12,)),
            pltpu.SemaphoreType.DMA((2,)),
            pltpu.SemaphoreType.DMA((6,)),
        ],
        compiler_params=pltpu.CompilerParams(collective_id=0, has_side_effects=True, vmem_limit_bytes=VMEM_LIMIT),
    )(tokens, in_i, in_g, out_w, small)


def project_first(raw_ref, gain_ref, w_ref, normed_ref, inv_ref, out_ref):
    low = raw_ref[0].astype(f32)
    high = raw_ref[1].astype(f32)
    squares = jnp.sum(low * low + high * high, axis=1, keepdims=True)
    inv_ref[...] = lax.rsqrt(squares / D + eps)
    low = (low * gain_ref[0:1]).astype(bf16)
    high = (high * gain_ref[1:2]).astype(bf16)
    normed_ref[0] = low
    normed_ref[1] = high
    n = w_ref.shape[2]
    for k in range(SLOTS):
        out_ref[:, k * n : (k + 1) * n] = dot_nn(low, w_ref[2 * k]) + dot_nn(high, w_ref[2 * k + 1])


def project_second(normed_ref, w_ref, out_ref):
    n = w_ref.shape[2]
    for k in range(SLOTS):
        out_ref[:, k * n : (k + 1) * n] = dot_nn(normed_ref[0], w_ref[2 * k]) + dot_nn(normed_ref[1], w_ref[2 * k + 1])


def split_rows(width, at):
    return pl.BlockSpec((2, CH, width), lambda i: (0, at(i), 0))


def run_project_first(raw, gain, w):
    width = raw.shape[2]
    at = lambda i: i
    n = SLOTS * w.shape[2]
    return call(
        project_first,
        NCH,
        (raw, gain, w),
        [split_rows(width, at), whole(2, width), whole(*w.shape)],
        (shaped(2, SEQ, width, dtype=bf16), shaped(SEQ, 1), shaped(SEQ, n)),
        (split_rows(width, at), rows_of(1, at), rows_of(n, at)),
        [],
        9,
    )


def run_project_second(normed, w):
    width = normed.shape[2]
    at = lambda i: i
    n = SLOTS * w.shape[2]
    return call(
        project_second,
        NCH,
        (normed, w),
        [split_rows(width, at), whole(*w.shape)],
        shaped(SEQ, n),
        rows_of(n, at),
        [],
        7,
    )


def gate_backward(cot_ref, wo_ref, gate_ref, yfull_ref, inv_ref, dy_ref, dproj_ref, dscale_ref):
    n = wo_ref.shape[2]
    d_gated = jnp.zeros(dy_ref.shape, f32)
    for k in range(SLOTS):
        for d in range(2):
            d_gated = d_gated + dot_nt(cot_ref[d, :, k * n : (k + 1) * n], wo_ref[2 * k + d])
    gate_in = gate_ref[...]
    inv = inv_ref[...]
    gate = inv * gate_in
    sig = jax.nn.sigmoid(gate)
    dy_ref[...] = d_gated * (gate * sig)
    d_gate = d_gated * yfull_ref[...].astype(f32) * (sig * (1.0 + gate * (1.0 - sig)))
    dproj_ref[...] = (inv * d_gate).astype(bf16)
    dscale_ref[...] = jnp.sum(d_gate * gate_in, axis=1, keepdims=True)


def run_gate_backward(cot, wo, gate_in, yfull, inv):
    width = cot.shape[2]
    w = gate_in.shape[1]
    at = lambda i: i
    return call(
        gate_backward,
        NCH,
        (cot, wo, gate_in, yfull, inv),
        [split_rows(width, at), whole(*wo.shape), rows_of(w, at), rows_of(w, at), rows_of(1, at)],
        (shaped(SEQ, w), shaped(SEQ, w, dtype=bf16), shaped(SEQ, 1)),
        (rows_of(w, at), rows_of(w, at), rows_of(1, at)),
        [],
        9,
    )


def branch_forward(gated_ref, wo_ref, own_ref, oth_ref):
    n = wo_ref.shape[2]
    for k in range(SLOTS):
        own_ref[:, k * n : (k + 1) * n] = dot_nn(gated_ref[...], wo_ref[2 * k])
        oth_ref[:, k * n : (k + 1) * n] = dot_nn(gated_ref[...], wo_ref[2 * k + 1]).astype(bf16)


def run_branch(gated, wo):
    w = gated.shape[1]
    at = lambda i: i
    n = SLOTS * wo.shape[2]
    return call(
        branch_forward,
        NCH,
        (gated, wo),
        [rows_of(w, at), whole(*wo.shape)],
        (shaped(SEQ, n), shaped(SEQ, n, dtype=bf16)),
        (rows_of(n, at), rows_of(n, at)),
        [],
        7,
    )


def normed_backward(inner_ref, gate_ref, wi_ref, wg_ref, own_ref, oth_ref):
    n = wi_ref.shape[2]
    for d, out_ref in ((1, oth_ref), (0, own_ref)):
        total = jnp.zeros(out_ref.shape, f32)
        for k in range(SLOTS):
            total = total + dot_nt(inner_ref[:, k * n : (k + 1) * n], wi_ref[2 * k + d])
            total = total + dot_nt(gate_ref[:, k * n : (k + 1) * n], wg_ref[2 * k + d])
        out_ref[...] = total.astype(out_ref.dtype)


def run_normed_backward(d_inner, d_gate, wi, wg):
    w = d_inner.shape[1]
    width = wi.shape[1]
    at = lambda i: i
    return call(
        normed_backward,
        NCH,
        (d_inner, d_gate, wi, wg),
        [rows_of(w, at), rows_of(w, at), whole(*wi.shape), whole(*wg.shape)],
        (shaped(SEQ, width), shaped(SEQ, width, dtype=bf16)),
        (rows_of(width, at), rows_of(width, at)),
        [],
        12,
    )


def per_device(
    tokens,
    gain,
    in_proj,
    conv_weight,
    conv_bias,
    x_proj,
    dt_proj,
    dt_bias,
    a_log,
    d_skip,
    out_proj,
    table,
    cotangent,
):
    row = lax.axis_index("row")
    col = lax.axis_index("col")
    grp = lax.axis_index("grp")
    low_row = row == 0
    low_pair = col % 2 == 0
    half = col // 2
    places = [(r, c) for r in range(2) for c in range(4)]
    quick = lax.axis_size("grp") == 4

    def spot(r, c):
        return r * 4 + c

    def send(v, pairs):
        return lax.ppermute(v, ("row", "col"), [(spot(*a), spot(*b)) for a, b in pairs])

    def swap(v):
        return send(v, [((r, c), (1 - r, c)) for r, c in places])

    def pair(v):
        return send(v, [((r, c), (r, c ^ 1)) for r, c in places])

    def across(v):
        return send(v, [((r, c), (1 - r, c ^ 2)) for r, c in places])

    def quarter_spot(q, s):
        return ((q & 1) ^ s, 2 * s + (q >> 1))

    same = [((r, q), quarter_spot(q, r ^ (q & 1))) for r, q in places]
    other = [((r, q), quarter_spot(q, 1 ^ r ^ (q & 1))) for r, q in places]
    spread = [((r, q), quarter_spot(q, r)) for r, q in places]

    def back(pairs):
        return [(b, a) for a, b in pairs]

    def flip(v, bit):
        return lax.ppermute(v, "grp", [(g, g ^ bit) for g in range(4)])

    def scatter_grp(v, axis):
        return lax.psum_scatter(v, "grp", scatter_dimension=axis, tiled=True)

    def exchange_blocks(p):
        p = [jnp.where(grp < 2, p[k], p[k ^ 2]) for k in range(4)]
        return [jnp.where(grp % 2 == 0, p[k], p[k ^ 1]) for k in range(4)]

    def to_relative(v, axis):
        if not quick:
            return v
        p = exchange_blocks(jnp.split(v, 4, axis=axis))
        return jnp.concatenate([p[0], p[2], p[1], p[3]], axis=axis)

    def from_relative(v, axis):
        if not quick:
            return v
        p = jnp.split(v, 4, axis=axis)
        return jnp.concatenate(exchange_blocks([p[0], p[2], p[1], p[3]]), axis=axis)

    def by_pair(own, paired):
        return jnp.where(low_pair, own, paired), jnp.where(low_pair, paired, own)

    local = tokens.shape[0]
    cut = local - LC
    tail_at = cut - LC

    def to_sequences(v):
        got = send(jnp.where(col == 3, v[tail_at:cut], v[cut:]), [((r, a), (r, b)) for r in range(2) for a, b in ((1, 2), (2, 3), (3, 1))])
        low = jnp.concatenate([v[:cut], jnp.where(col == 0, v[cut:], got)], axis=0)
        two = jnp.concatenate([got, v[:cut]], axis=0)
        three = jnp.concatenate([got, v[:tail_at], v[cut:]], axis=0)
        return jnp.where(col < 2, low, jnp.where(col == 2, two, three))

    def from_sequences(v):
        got = send(jnp.where(col == 1, v[cut:], v[:LC]), [((r, b), (r, a)) for r in range(2) for a, b in ((1, 2), (2, 3), (3, 1))])
        low = jnp.concatenate([v[:cut], jnp.where(col == 0, v[cut:], got)], axis=0)
        two = jnp.concatenate([v[LC:], got], axis=0)
        three = jnp.concatenate([v[LC:cut], got, v[cut:]], axis=0)
        return jnp.where(col < 2, low, jnp.where(col == 2, two, three))

    def gather_quad(v):
        swapped = swap(v)
        paired = pair(v)
        mid = v.shape[0] // 2
        diagonal = jnp.concatenate([pair(swapped[:mid]), swap(paired[mid:])], axis=0)
        first_own, second_own = by_pair(v, paired)
        first_oth, second_oth = by_pair(swapped, diagonal)
        return jnp.stack([jnp.concatenate([first_own, second_own], axis=0), jnp.concatenate([first_oth, second_oth], axis=0)])

    def scatter_quad(own, oth):
        v = own + swap(oth.astype(bf16)).astype(f32)
        first, second = v[:local], v[local:]
        kept, sent = jnp.where(low_pair, first, second), jnp.where(low_pair, second, first)
        return kept + pair(sent.astype(bf16)).astype(f32)

    own_table = jnp.where(half == 0, table[0], table[1])
    oth_table = jnp.where(half == 0, table[1], table[0])
    resumes_own = own_table == half
    resumed_by_other = oth_table == half

    small = jnp.concatenate([conv_weight, conv_bias[None], dt_bias[None], d_skip[None], a_log, dt_proj, x_proj.T], axis=0)
    lanes = small.shape[1]
    used = small.shape[0]
    gain_rows = gain.size // lanes
    width = tokens.shape[1]
    if quick:
        small = jnp.concatenate([small, gain.reshape(gain_rows, lanes)], axis=0)
        small = jnp.pad(small, ((0, -small.shape[0] % 16), (0, 0)))
        raw, wi, wg, wo, small = run_gather_start(tokens, in_proj[:, 0], in_proj[:, 1], out_proj, small)
        gain_all = small[:, used : used + gain_rows].reshape(2, width).astype(f32)
        small = jnp.swapaxes(small, 0, 1).reshape(small.shape[1], 8 * lanes)
    else:
        raw = gather_quad(to_sequences(tokens))

        def weight(shard):
            v = lax.all_gather(jnp.stack([send(shard, same), send(shard, other)]), "grp", axis=2, tiled=True)
            v = v.reshape(2, v.shape[1], SLOTS, v.shape[2] // SLOTS)
            return jnp.transpose(v, (2, 0, 1, 3)).reshape(2 * SLOTS, v.shape[1], v.shape[3])

        wi, wg, wo = weight(in_proj[:, 0]), weight(in_proj[:, 1]), weight(out_proj)
        small = send(lax.all_gather(small, ("row", "grp"), axis=1, tiled=True), spread)
        gain_all = lax.all_gather(gain, ("row", "grp"), axis=0, tiled=True).astype(f32).reshape(2, width)
    w = small.shape[1]
    zero_row = jnp.zeros((1, w), f32)
    conv = jnp.concatenate([small[0:5].astype(f32)] + [zero_row] * 3, axis=0)
    vec = jnp.concatenate([small[5:7].astype(f32)] + [zero_row] * 6, axis=0)
    rate = -jnp.exp(small[7 : 7 + NSTATE].astype(f32))
    dtp = small[7 + NSTATE : 7 + NSTATE + RANK]
    xproj = small[7 + NSTATE + RANK : 7 + NSTATE + RANK + XW]
    gain_own = jnp.where(low_row, gain_all[0], gain_all[1])
    gain_two = jnp.stack([gain_own, jnp.where(low_row, gain_all[1], gain_all[0])])

    normed, inv, inner = run_project_first(raw, gain_two, wi)
    tail_own = (inv * inner)[LP - 8 : LP]
    tail = jnp.where(resumes_own, tail_own, across(tail_own))
    gate_in = run_project_second(normed, wg)
    xconv, xdbl_part = run_conv_forward(inner, inv, tail, conv, xproj)

    low_part, map_part = xdbl_part[:RANK], xdbl_part[RANK:]
    for move in (swap, pair):
        low_part = low_part + move(low_part.astype(bf16)).astype(f32)
        map_part = map_part + move(map_part)
    xdbl = jnp.concatenate([low_part, map_part], axis=0)

    zero_state = jnp.zeros((NSTATE, w), f32)
    *kept, final = run_scan_forward(0, PC, xdbl, xconv, gate_in, inv, dtp, vec, rate, zero_state)
    resumed = jnp.where(resumes_own, final, across(final))
    gated, yfull, starts, _ = run_scan_forward(PC, NCH - PC, xdbl, xconv, gate_in, inv, dtp, vec, rate, resumed, kept)

    cot = gather_quad(to_sequences(to_relative(cotangent, 1)))
    d_yfull, d_gate_proj, gate_scale = run_gate_backward(cot, wo, gate_in, yfull, inv)

    branch = scatter_quad(*run_branch(gated, wo))
    output = (tokens.astype(f32) + from_sequences(from_relative(branch, 1).astype(bf16)).astype(f32)).astype(bf16)

    def collect(v):
        return send(v[0].astype(bf16), back(same)).astype(f32) + send(v[1].astype(bf16), back(other)).astype(f32)

    def rows_product(a, b, out_dtype):
        return lax.dot_general(a, b, (((1,), (0,)), ((), ())), preferred_element_type=f32).astype(out_dtype)

    if quick:
        n = width // 4
        part = [[dot_tn(gated, cot[d, :, k * 2 * n : (k + 1) * 2 * n]) for k in range(2)] for d in range(2)]
        part = [part[d][0] + flip(part[d][1].astype(bf16), 1).astype(f32) for d in range(2)]
        part = [part[d][:, :n] + flip(part[d][:, n:].astype(bf16), 2).astype(f32) for d in range(2)]
    else:
        part = [scatter_grp(dot_tn(gated, cot[d]), 1) for d in range(2)]
    out_grad = collect(part)

    mid = PC // 2
    sums = (zero_state, jnp.zeros((8, w), f32), jnp.zeros((RANK, w), f32))
    scan = functools.partial(run_scan_backward, xdbl=xdbl, xconv=xconv, dy=d_yfull, dtp=dtp, vec=vec, rate=rate, starts=starts)
    dx_c, dxc, *sums, g_first = scan(PC, NCH - PC, carry=zero_state, sums=sums)
    g_into = jnp.where(resumes_own, g_first, 0.0) + jnp.where(resumed_by_other, across(g_first), 0.0)
    dx_hi, dxc, *sums, g_first = scan(mid, PC - mid, carry=g_into, sums=sums, kept=(dxc,))

    def sum_quad(v):
        for move in (swap, pair):
            v = v + move(v.astype(bf16)).astype(f32)
        return v

    late = sum_quad(jnp.concatenate([dx_hi, dx_c], axis=1))
    dx_lo, dxc, *sums, _ = scan(0, mid, carry=g_first, sums=sums, kept=(dxc,))
    alog_grad, scan_sums, dtp_grad = sums
    early = sum_quad(dx_lo)

    conv_back = functools.partial(run_conv_backward, inner=inner, inv=inv, tail=tail, conv=conv, xproj=xproj, dxc=dxc)
    sums = (jnp.zeros((8, w), f32), jnp.zeros((XW, w), f32))
    zero_head = jnp.zeros((8, w), f32)
    hi_width = (PC - mid) * CH
    dp, ds, *sums, head = conv_back(PC, NCH - PC, dxdbl=late[:, hi_width:], follow=zero_head, sums=sums)
    follow = jnp.where(resumes_own, head, 0.0) + jnp.where(resumed_by_other, across(head), 0.0)
    dp, ds, *sums, head = conv_back(mid, PC - mid, dxdbl=late[:, :hi_width], follow=follow, sums=sums, kept=(dp, ds))
    d_inner_proj, inner_scale, conv_sums, xproj_grad, _ = conv_back(0, mid, dxdbl=early, follow=head, sums=sums, kept=(dp, ds))

    d_normed = scatter_quad(*run_normed_backward(d_inner_proj, d_gate_proj, wi, wg))
    scale = gate_scale + inner_scale
    scale = scale + swap(scale)
    first, second = scale[:local], scale[local:]
    scale_own = jnp.where(low_pair, first, second) + pair(jnp.where(low_pair, second, first))
    inv_own = jnp.where(low_pair, inv[:local], inv[local:])
    fixed_wide = jnp.where(low_pair, raw[0, :local], raw[0, local:]).astype(f32)
    gain_part = jnp.sum(d_normed * fixed_wide, axis=0)
    pulled = d_normed * gain_own - (scale_own * inv_own * inv_own * inv_own / D) * fixed_wide
    input_grad = (cotangent.astype(f32) + from_sequences(pulled.astype(bf16)).astype(f32)).astype(bf16)

    def in_grad(d_proj):
        if not quick:
            return collect([scatter_grp(dot_tn(normed[d], d_proj), 1) for d in range(2)])
        n = w // 4
        blocks = [d_proj[:, k * n : (k + 1) * n] for k in range(4)]
        low_core = grp % 2 == 0
        kept = jnp.concatenate([jnp.where(low_core, blocks[0], blocks[1]), jnp.where(low_core, blocks[2], blocks[3])], axis=1)
        sent = jnp.concatenate([jnp.where(low_core, blocks[1], blocks[0]), jnp.where(low_core, blocks[3], blocks[2])], axis=1)
        part = rows_product(normed, kept, f32) + flip(rows_product(normed, sent, bf16), 1).astype(f32)
        low, high = part[:, :, :n], part[:, :, n:]
        part = jnp.where(grp < 2, low, high) + flip(jnp.where(grp < 2, high, low).astype(bf16), 2).astype(f32)
        return collect(part)

    in_grads = jnp.stack([in_grad(d_inner_proj), in_grad(d_gate_proj)], axis=1)
    gain_grad = lax.psum_scatter(lax.psum(gain_part, "col"), "grp", scatter_dimension=0, tiled=True)
    small_grad = jnp.concatenate([conv_sums[0:5], scan_sums[0:2], alog_grad * rate, dtp_grad, xproj_grad], axis=0)
    small_grad = jnp.pad(small_grad, ((0, -small_grad.shape[0] % 8), (0, 0)))
    small_grad = send(small_grad, back(spread))
    small_grad = lax.psum_scatter(small_grad, ("row", "grp"), scatter_dimension=1, tiled=True)
    return (
        output,
        input_grad,
        gain_grad,
        in_grads,
        small_grad[0:4],
        small_grad[4],
        small_grad[7 + NSTATE + RANK : 7 + NSTATE + RANK + XW].T,
        small_grad[7 + NSTATE : 7 + NSTATE + RANK],
        small_grad[5],
        small_grad[7 : 7 + NSTATE],
        small_grad[6],
        out_grad,
    )


def solution(mesh):
    placed = (
        P(("grp", "col"), "row"),
        P(("row", "grp")),
        P("row", None, ("col", "grp")),
        P(None, ("col", "row", "grp")),
        P(("col", "row", "grp")),
        P(("col", "row", "grp"), None),
        P(None, ("col", "row", "grp")),
        P(("col", "row", "grp")),
        P(None, ("col", "row", "grp")),
        P(("col", "row", "grp")),
        P("col", ("row", "grp")),
        P("grp"),
        P(("grp", "col"), "row"),
    )
    return jax.shard_map(
        per_device,
        mesh=mesh,
        in_specs=placed,
        out_specs=(
            P(("grp", "col"), "row"),
            P(("grp", "col"), "row"),
            P(("row", "grp")),
            P("row", None, ("col", "grp")),
            P(None, ("col", "row", "grp")),
            P(("col", "row", "grp")),
            P(("col", "row", "grp"), None),
            P(None, ("col", "row", "grp")),
            P(("col", "row", "grp")),
            P(None, ("col", "row", "grp")),
            P(("col", "row", "grp")),
            P("col", ("row", "grp")),
        ),
        check_vma=False,
    )
```

```python
import functools

import jax
import jax.numpy as jnp
from jax import lax
from jax.experimental import pallas as pl
from jax.experimental.pallas import tpu as pltpu
from jax.sharding import PartitionSpec as P

D = 2048
NSTATE = 16
KCONV = 4
RANK = 128
NPROMPT = 2
LP = 1024
LC = 128
NCONT = 2

eps = 1e-05
CH = 128
SUB = 16
PC = LP // CH
SEQ = LP + LC
NCH = SEQ // CH
XW = RANK + 2 * NSTATE
SPAN = SUB * NSTATE
LOG2E = 1.4426950408889634
VMEM_LIMIT = 58 * 1024 * 1024

f32 = jnp.float32
bf16 = jnp.bfloat16


def dot_nn(a, b):
    return lax.dot_general(a, b, (((1,), (0,)), ((), ())), preferred_element_type=f32)


def dot_nt(a, b):
    return lax.dot_general(a, b, (((1,), (1,)), ((), ())), preferred_element_type=f32)


def dot_tn(a, b):
    return lax.dot_general(a, b, (((0,), (0,)), ((), ())), preferred_element_type=f32)


def expand_tile():
    lane = lax.broadcasted_iota(jnp.int32, (NSTATE, SPAN), 1)
    row = lax.broadcasted_iota(jnp.int32, (NSTATE, SPAN), 0)
    return jnp.where(lane % NSTATE == row, 1.0, 0.0)


def own_token(rows):
    lane = lax.broadcasted_iota(jnp.int32, (rows, SPAN), 1)
    row = lax.broadcasted_iota(jnp.int32, (rows, SPAN), 0)
    return lane // NSTATE == row % SUB


def conv_forward(inner_ref, inv_ref, tail_ref, conv_ref, xproj_ref, xconv_ref, xdbl_ref, buf):
    i = pl.program_id(0)

    @pl.when(i == 0)
    def _():
        buf[0:8] = jnp.zeros_like(buf[0:8])

    @pl.when(i == PC)
    def _():
        buf[0:8] = tail_ref[...]

    @pl.when((i > 0) & (i < PC))
    def _():
        buf[0:8] = buf[CH : CH + 8]

    buf[8 : CH + 8] = inv_ref[...] * inner_ref[...]
    out = conv_ref[4:5]
    for k in range(KCONV):
        out = out + conv_ref[k : k + 1] * buf[5 + k : 5 + k + CH]
    xconv = (out * jax.nn.sigmoid(out)).astype(bf16)
    xconv_ref[...] = xconv
    xdbl_ref[...] = dot_nt(xproj_ref[...], xconv)


def softplus(v):
    return jnp.maximum(v, 0.0) + jnp.log1p(jnp.exp(-jnp.abs(v)))


def by_sub(v):
    return v.reshape(CH // SUB, SUB, v.shape[-1])


def scan_chunk(xdbl_ref, xconv, dtp_ref, vec_ref, rate_ref, state, dt_s, u_s, cb_s, h_s, y_s):
    step = softplus(dot_tn(xdbl_ref[:RANK].astype(bf16), dtp_ref[...]) + vec_ref[0:1])
    dt_s[...] = by_sub(step)
    u_s[...] = by_sub(step * xconv)
    reads = dot_tn(xdbl_ref[RANK + NSTATE :].astype(bf16), expand_tile().astype(bf16))
    cb_s[...] = jnp.where(own_token(CH), reads, 0.0).astype(bf16)
    rate = rate_ref[...] * LOG2E

    def block(j, carried):
        h, maps = carried
        for t in range(SUB):
            a = jnp.exp2(dt_s[j, t : t + 1, :] * rate)
            h = a * h + u_s[j, t : t + 1, :] * maps[:, t : t + 1]
            h_s[t * NSTATE : (t + 1) * NSTATE, :] = h.astype(bf16)
        rows = pl.ds(pl.multiple_of(j * SUB, SUB), SUB)
        y_s[rows, :] = dot_nn(cb_s[rows, :], h_s[...])
        return (h, pltpu.roll(maps, CH - SUB, 1))

    h, _ = lax.fori_loop(0, CH // SUB, block, (state, xdbl_ref[RANK : RANK + NSTATE]))
    return h, y_s[...] + vec_ref[1:2] * xconv


def scan_scratch(w):
    return [
        pltpu.VMEM((CH // SUB, SUB, w), f32),
        pltpu.VMEM((CH // SUB, SUB, w), f32),
        pltpu.VMEM((CH, SPAN), bf16),
        pltpu.VMEM((SPAN, w), bf16),
        pltpu.VMEM((CH, w), f32),
    ]


def scan_forward(kept, xdbl_ref, xconv_ref, dtp_ref, vec_ref, rate_ref, start_ref, *refs):
    yfull_ref, starts_ref, final_ref, *scratch = refs[kept:]

    @pl.when(pl.program_id(0) == 0)
    def _():
        final_ref[...] = start_ref[...]

    starts_ref[0] = final_ref[...]
    h, yfull = scan_chunk(xdbl_ref, xconv_ref[...].astype(f32), dtp_ref, vec_ref, rate_ref, final_ref[...], *scratch)
    final_ref[...] = h
    yfull_ref[...] = yfull.astype(bf16)


def chunk_backward(xdbl_ref, xconv_ref, dy_ref, dtp_ref, vec_ref, rate_ref, starts_ref, dxdbl_ref, dxc_ref, alog_ref, sums_ref, dtpg_ref, first_ref,
                   dt_s, u_s, x_s, dy_s, a_s, h_s, g_s, w_s, b_s, m1_s, m2_s, ds_s, dx_s, sig_s):
    low = xdbl_ref[:RANK].astype(bf16)
    step_inner = dot_tn(low, dtp_ref[...]) + vec_ref[0:1]
    step = softplus(step_inner)
    sig_s[...] = jax.nn.sigmoid(step_inner)
    xconv = xconv_ref[...].astype(f32)
    dy = dy_ref[...]
    dt_s[...] = by_sub(step)
    u_s[...] = by_sub(step * xconv)
    x_s[...] = by_sub(xconv)
    dy_s[...] = by_sub(dy)
    tile = expand_tile().astype(bf16)
    b_s[...] = jnp.where(own_token(CH), dot_tn(xdbl_ref[RANK : RANK + NSTATE].astype(bf16), tile), 0.0).astype(bf16)
    rate = rate_ref[...]
    rate2 = rate * LOG2E
    h_s[0:NSTATE] = starts_ref[0]

    def ahead(j, carried):
        h, maps = carried
        for t in range(SUB):
            a = jnp.exp2(dt_s[j, t : t + 1, :] * rate2)
            h = a * h + u_s[j, t : t + 1, :] * maps[:, t : t + 1]
            a_s[j, t * NSTATE : (t + 1) * NSTATE, :] = a
            at = pl.multiple_of(j * SPAN + (t + 1) * NSTATE, NSTATE)
            h_s[pl.ds(at, NSTATE), :] = h
        return (h, pltpu.roll(maps, CH - SUB, 1))

    lax.fori_loop(0, CH // SUB, ahead, (starts_ref[0], xdbl_ref[RANK : RANK + NSTATE]))
    ones = jnp.where(own_token(SUB), 1.0, 0.0).astype(bf16)
    mine_sub = own_token(SUB)

    def back(jj, carried):
        g, alog, maps = carried
        j = CH // SUB - 1 - jj
        maps = pltpu.roll(maps, SUB, 1)
        for t in reversed(range(SUB)):
            dt = dt_s[j, t : t + 1, :]
            gs = maps[:, t : t + 1] * dy_s[j, t : t + 1, :] + g
            g = a_s[j, t * NSTATE : (t + 1) * NSTATE, :] * gs
            prior = h_s[pl.ds(pl.multiple_of(j * SPAN + t * NSTATE, NSTATE), NSTATE), :]
            w = g * prior
            alog = alog + w * dt
            g_s[t * NSTATE : (t + 1) * NSTATE, :] = gs.astype(bf16)
            w_s[t * NSTATE : (t + 1) * NSTATE, :] = (w * rate).astype(bf16)
        rows = pl.ds(pl.multiple_of(j * SUB, SUB), SUB)
        gs_all = g_s[...]
        through = dot_nn(b_s[rows, :], gs_all)
        ds_s[rows, :] = dot_nn(ones, w_s[...]) + x_s[j] * through
        dx_s[rows, :] = dt_s[j] * through + vec_ref[1:2] * dy_s[j]
        hs = h_s[pl.ds(pl.multiple_of(j * SPAN + NSTATE, NSTATE), SPAN), :].astype(bf16)
        m1_s[rows, :] = jnp.where(mine_sub, dot_nt(u_s[j].astype(bf16), gs_all), 0.0).astype(bf16)
        m2_s[rows, :] = jnp.where(mine_sub, dot_nt(dy_s[j].astype(bf16), hs), 0.0).astype(bf16)
        return (g, alog, maps)

    g, alog, _ = lax.fori_loop(0, CH // SUB, back, (first_ref[...], alog_ref[...], xdbl_ref[RANK + NSTATE :]))
    first_ref[...] = g
    alog_ref[...] = alog
    d_inner = ds_s[...] * sig_s[...]
    d_low = d_inner.astype(bf16)
    sums_ref[0:1] = sums_ref[0:1] + jnp.sum(d_inner, axis=0, keepdims=True)
    sums_ref[1:2] = sums_ref[1:2] + jnp.sum(dy * xconv, axis=0, keepdims=True)
    dtpg_ref[...] = dtpg_ref[...] + dot_nn(low, d_low)
    dxdbl_ref[:RANK] = dot_nt(dtp_ref[...], d_low)
    dxdbl_ref[RANK : RANK + NSTATE] = dot_nt(tile, m1_s[...])
    dxdbl_ref[RANK + NSTATE :] = dot_nt(tile, m2_s[...])
    dxc_ref[...] = dx_s[...]


def scan_backward(kept, *refs):
    given, sums0, out = refs[:7], refs[7:11], refs[11 + kept :]
    dxdbl_ref, dxc_ref, alog_ref, sums_ref, dtpg_ref, first_ref = out[:6]

    @pl.when(pl.program_id(0) == 0)
    def _():
        first_ref[...] = sums0[0][...]
        alog_ref[...] = sums0[1][...]
        sums_ref[...] = sums0[2][...]
        dtpg_ref[...] = sums0[3][...]

    chunk_backward(*given, dxdbl_ref, dxc_ref, alog_ref, sums_ref, dtpg_ref, first_ref, *out[6:])


def backward_scratch(w):
    sub = pltpu.VMEM((CH // SUB, SUB, w), f32)
    return [
        sub,
        sub,
        sub,
        sub,
        pltpu.VMEM((CH // SUB, SPAN, w), f32),
        pltpu.VMEM(((CH + 1) * NSTATE, w), f32),
        pltpu.VMEM((SPAN, w), bf16),
        pltpu.VMEM((SPAN, w), bf16),
        pltpu.VMEM((CH, SPAN), bf16),
        pltpu.VMEM((CH, SPAN), bf16),
        pltpu.VMEM((CH, SPAN), bf16),
        pltpu.VMEM((CH, w), f32),
        pltpu.VMEM((CH, w), f32),
        pltpu.VMEM((CH, w), f32),
    ]


def conv_backward(kept, chunks, first, inner_ref, halo_ref, inv_ref, halo_inv_ref, tail_ref, conv_ref, xproj_ref, dxc_ref, dxdbl_ref, follow_ref, sums0_ref, xprojg0_ref, *refs):
    dproj_ref, dscale_ref, sums_ref, xprojg_ref, head_ref, buf, dbuf = refs[kept:]
    i = pl.program_id(0)
    chunk = first + chunks - 1 - i

    @pl.when(i == 0)
    def _():
        sums_ref[...] = sums0_ref[...]
        xprojg_ref[...] = xprojg0_ref[...]
        head_ref[...] = follow_ref[...]

    projected = inner_ref[...]
    inv = inv_ref[...]
    before = halo_inv_ref[...] * halo_ref[...]
    before = jnp.where(chunk == 0, 0.0, jnp.where(chunk == PC, tail_ref[...], before))
    buf[0:8] = before
    buf[8 : CH + 8] = inv * projected
    out = conv_ref[4:5]
    for k in range(KCONV):
        out = out + conv_ref[k : k + 1] * buf[5 + k : 5 + k + CH]
    sig = jax.nn.sigmoid(out)
    xconv = (out * sig).astype(bf16)
    dxdbl = dxdbl_ref[...].astype(bf16)
    xprojg_ref[...] = xprojg_ref[...] + dot_nn(dxdbl, xconv)
    d_x = dxc_ref[...] + dot_tn(dxdbl, xproj_ref[...])
    d_conv = d_x * (sig * (1.0 + out * (1.0 - sig)))
    dbuf[CH : CH + 8] = head_ref[...]
    dbuf[0:CH] = d_conv
    d_inner = conv_ref[3:4] * d_conv
    for k in range(KCONV - 1):
        d_inner = d_inner + conv_ref[k : k + 1] * dbuf[3 - k : 3 - k + CH]
    for k in range(KCONV):
        sums_ref[k : k + 1] = sums_ref[k : k + 1] + jnp.sum(buf[5 + k : 5 + k + CH] * d_conv, axis=0, keepdims=True)
    sums_ref[4:5] = sums_ref[4:5] + jnp.sum(d_conv, axis=0, keepdims=True)
    dproj_ref[...] = (inv * d_inner).astype(bf16)
    dscale_ref[...] = jnp.sum(d_inner * projected, axis=1, keepdims=True)
    head_ref[...] = d_conv[0:8]


def call(body, chunks, args, in_specs, outs, out_specs, scratch, micros, aliases=None):
    return pl.pallas_call(
        body,
        grid=(chunks,),
        in_specs=in_specs,
        out_specs=out_specs,
        scratch_shapes=scratch,
        out_shape=outs,
        input_output_aliases=aliases or {},
        compiler_params=pltpu.CompilerParams(dimension_semantics=("arbitrary",), vmem_limit_bytes=VMEM_LIMIT),
        cost_estimate=pl.CostEstimate(flops=micros * 1000000000, bytes_accessed=1000000, transcendentals=0),
    )(*args)


def shaped(*shape, dtype=f32):
    return jax.ShapeDtypeStruct(shape, dtype)


def rows_of(width, place, tall=CH):
    return pl.BlockSpec((tall, width), lambda i: (place(i), 0))


def lanes_of(height, place):
    return pl.BlockSpec((height, CH), lambda i: (0, place(i)))


def whole(*shape):
    return pl.BlockSpec(shape, lambda i: (0,) * len(shape))


ANY = pl.BlockSpec(memory_space=pl.ANY)


def run_conv_forward(inner, inv, tail, conv, xproj):
    w = inner.shape[1]
    at = lambda i: i
    return call(
        conv_forward,
        NCH,
        (inner, inv, tail, conv, xproj),
        [rows_of(w, at), rows_of(1, at), whole(8, w), whole(8, w), whole(XW, w)],
        (shaped(SEQ, w, dtype=bf16), shaped(XW, SEQ)),
        (rows_of(w, at), lanes_of(XW, at)),
        [pltpu.VMEM((CH + 8, w), f32)],
        12,
    )


def chunk_of(height, place):
    return pl.BlockSpec((None, height, CH), lambda i: (place(i), 0, 0))


def run_scan_forward(first, chunks, xdbl, xconv, dtp, vec, rate, start, kept=()):
    w = xconv.shape[1]
    at = lambda i: first + i
    return call(
        functools.partial(scan_forward, len(kept)),
        chunks,
        (xdbl, xconv, dtp, vec, rate, start, *kept),
        [chunk_of(XW, at), rows_of(w, at), whole(RANK, w), whole(8, w), whole(NSTATE, w), whole(NSTATE, w)] + [ANY] * len(kept),
        (shaped(SEQ, w, dtype=bf16), shaped(NCH, NSTATE, w), shaped(NSTATE, w)),
        (rows_of(w, at), pl.BlockSpec((1, NSTATE, w), lambda i: (first + i, 0, 0)), whole(NSTATE, w)),
        scan_scratch(w),
        5 * chunks,
        {6 + k: k for k in range(len(kept))},
    )


def run_scan_backward(first, chunks, xdbl, xconv, dy, dtp, vec, rate, starts, carry, sums, kept=()):
    w = xconv.shape[1]
    at = lambda i: first + chunks - 1 - i
    local = lambda i: chunks - 1 - i
    return call(
        functools.partial(scan_backward, len(kept)),
        chunks,
        (xdbl, xconv, dy, dtp, vec, rate, starts, carry, *sums, *kept),
        [
            chunk_of(XW, at),
            rows_of(w, at),
            rows_of(w, at),
            whole(RANK, w),
            whole(8, w),
            whole(NSTATE, w),
            pl.BlockSpec((1, NSTATE, w), lambda i: (at(i), 0, 0)),
            whole(NSTATE, w),
            whole(NSTATE, w),
            whole(8, w),
            whole(RANK, w),
        ]
        + [ANY] * len(kept),
        (shaped(XW, chunks * CH), shaped(SEQ, w), shaped(NSTATE, w), shaped(8, w), shaped(RANK, w), shaped(NSTATE, w)),
        (lanes_of(XW, local), rows_of(w, at), whole(NSTATE, w), whole(8, w), whole(RANK, w), whole(NSTATE, w)),
        backward_scratch(w),
        11 * chunks,
        {11 + k: 1 + k for k in range(len(kept))},
    )


def run_conv_backward(first, chunks, inner, inv, tail, conv, xproj, dxc, dxdbl, follow, sums, kept=()):
    w = inner.shape[1]
    at = lambda i: first + chunks - 1 - i
    before = lambda i: (jnp.maximum(at(i) * (CH // 8) - 1, 0), 0)
    return call(
        functools.partial(conv_backward, len(kept), chunks, first),
        chunks,
        (inner, inner, inv, inv, tail, conv, xproj, dxc, dxdbl, follow, *sums, *kept),
        [
            rows_of(w, at),
            pl.BlockSpec((8, w), before),
            rows_of(1, at),
            pl.BlockSpec((8, 1), before),
            whole(8, w),
            whole(8, w),
            whole(XW, w),
            rows_of(w, at),
            chunk_of(XW, at),
            whole(8, w),
            whole(8, w),
            whole(XW, w),
        ]
        + [ANY] * len(kept),
        (shaped(SEQ, w, dtype=bf16), shaped(SEQ, 1), shaped(8, w), shaped(XW, w), shaped(8, w)),
        (rows_of(w, at), rows_of(1, at), whole(8, w), whole(XW, w), whole(8, w)),
        [pltpu.VMEM((CH + 8, w), f32), pltpu.VMEM((CH + 8, w), f32)],
        2 * chunks,
        {12 + k: k for k in range(len(kept))},
    )


MESH = pl.DeviceIdType.MESH
BIG = 384
BIG_STEPS = SEQ // BIG
SLOTS = 4


def remote(src, dst, send, recv, device):
    return pltpu.make_async_remote_copy(src_ref=src, dst_ref=dst, send_sem=send, recv_sem=recv, device_id=device, device_id_type=MESH)


def xor_bit(a, b):
    return a + b - 2 * a * b


def token_pieces(c, local):
    cut = local - LC
    low = cut - LC
    if c == 0:
        return [(0, local, 0, 0)]
    if c == 1:
        return [(0, cut, 0, local), (cut, local, 1, 0)]
    if c == 2:
        return [(0, local, 1, LC)]
    return [(0, low, 1, LC + local), (low, cut, 0, LP), (cut, local, 1, LP)]


class Gather:
    def __init__(self, weights, tokens, raw, w_send, w_recv, t_send, t_recv, here):
        g, r, c = lax.axis_index("grp"), lax.axis_index("row"), lax.axis_index("col")
        x, core = g // 2, g % 2
        self.g, self.r, self.c = g, r, c
        half = xor_bit(r, c % 2)
        self.firsts = ((g, r, 2 * half + c // 2), (g, 1 - r, 2 * (1 - half) + c // 2))
        self.alone = 2 * half + c // 2 == c
        self.ranks = (g, (1 - x) * 2 + core, x * 2 + 1 - core)
        self.x_dev, self.core_dev = (self.ranks[1], r, c), (self.ranks[2], r, c)
        self.weights, self.tokens, self.raw = weights, tokens, raw
        self.w_send, self.w_recv, self.t_send, self.t_recv, self.here = w_send, w_recv, t_send, t_recv, here

    def greet(self):
        barrier = pltpu.get_barrier_semaphore()
        for dr in range(2):
            for dc in range(4):
                if dr or dc:
                    device = (self.g, (self.r + dr) % 2, (self.c + dc) % 4)
                    pl.semaphore_signal(barrier, inc=1, device_id=device, device_id_type=MESH)
        for device in (self.x_dev, self.core_dev):
            pl.semaphore_signal(barrier, inc=1, device_id=device, device_id_type=MESH)
        pl.semaphore_wait(barrier, 9)

    def slot(self, n, k, d):
        if self.weights[n][2]:
            return (self.r if d == 0 else 1 - self.r) * 4 + self.ranks[k]
        return 2 * self.ranks[k] + d

    def first_hop(self, n, d):
        src, dst, by_row = self.weights[n]
        at = self.slot(n, 0, 0) if by_row else self.slot(n, 0, d)
        return remote(src, dst.at[at], self.w_send.at[n, d], self.w_recv.at[n, d], self.firsts[d])

    def at_home(self, n):
        src, dst, _ = self.weights[n]
        return pltpu.make_async_copy(src, dst.at[self.slot(n, 0, 0)], self.here.at[n])

    def hop(self, n, d, k, came):
        dst = self.weights[n][1]
        at = self.slot(n, k, d)
        i = (0, 2, 4, 6)[came] + d
        device = self.x_dev if came == 1 else self.core_dev
        return remote(dst.at[at], dst.at[at], self.w_send.at[n, i], self.w_recv.at[n, i], device)

    def begin(self, n):
        @pl.when(self.alone)
        def _():
            self.at_home(n).start()

        @pl.when(jnp.logical_not(self.alone))
        def _():
            self.first_hop(n, 0).start()

        self.first_hop(n, 1).start()

    def forward(self, n):
        for d in range(2):
            if d == 0:

                @pl.when(self.alone)
                def _():
                    self.at_home(n).wait()

                @pl.when(jnp.logical_not(self.alone))
                def _():
                    self.first_hop(n, 0).wait_recv()
            else:
                self.first_hop(n, 1).wait_recv()
            self.hop(n, d, 0, 1).start()
            self.hop(n, d, 0, 2).start()

    def forward_again(self, n):
        for d in range(2):
            self.hop(n, d, 0, 1).wait_recv()
            self.hop(n, d, 1, 3).start()

    def end(self, n):
        for d in range(2):
            self.hop(n, d, 0, 2).wait_recv()
            self.hop(n, d, 1, 3).wait_recv()
            self.hop(n, d, 0, 1).wait_send()
            self.hop(n, d, 0, 2).wait_send()
            self.hop(n, d, 1, 3).wait_send()

        @pl.when(jnp.logical_not(self.alone))
        def _():
            self.first_hop(n, 0).wait_send()

        self.first_hop(n, 1).wait_send()

    def token_copies(self, k):
        copies, mine = [], []
        for a, b, s, at in token_pieces(k, self.tokens.shape[0]):
            for dr in range(2):
                for dc in range(2):
                    target = 2 * s + dc
                    dst = self.raw.at[dr, pl.ds(at, b - a)]
                    src = self.tokens.at[pl.ds(a, b - a)]
                    if dr == 0 and target == k:
                        mine.append(pltpu.make_async_copy(src, dst, self.here.at[2 + len(mine)]))
                    else:
                        device = (self.g, self.r if dr == 0 else 1 - self.r, target)
                        copies.append(remote(src, dst, self.t_send.at[len(copies)], self.t_recv.at[dr], device))
        return copies, mine

    def begin_tokens(self):
        for k in range(4):

            @pl.when(self.c == k)
            def _(k=k):
                copies, mine = self.token_copies(k)
                for copy in mine + copies:
                    copy.start()

    def end_tokens(self):
        for k in range(4):

            @pl.when(self.c == k)
            def _(k=k):
                copies, mine = self.token_copies(k)
                held = sum(b - a for a, b, s, at in token_pieces(k, self.tokens.shape[0]) if s == k // 2)
                rest = self.raw.at[0, pl.ds(0, SEQ - held)]
                pltpu.make_async_copy(rest, rest, self.t_recv.at[0]).wait()
                pltpu.make_async_copy(self.raw.at[1], self.raw.at[1], self.t_recv.at[1]).wait()
                for copy in mine:
                    copy.wait()
                for copy in copies:
                    copy.wait_send()


def gather_semaphores():
    return [pltpu.SemaphoreType.DMA(shape) for shape in ((2, 8), (2, 8), (12,), (2,), (4,))]


def gather_start(tokens, in_i, small, raw, wi, small_all, *sems):
    gather = Gather([(small, small_all, True), (in_i, wi, False)], tokens, raw, *sems)
    gather.greet()
    gather.begin(0)
    gather.begin(1)
    gather.begin_tokens()
    for n in range(2):
        gather.forward(n)
    for n in range(2):
        gather.forward_again(n)
    gather.end_tokens()
    for n in range(2):
        gather.end(n)


def run_gather_start(tokens, in_i, small):
    width = tokens.shape[1]
    return pl.pallas_call(
        gather_start,
        in_specs=[ANY] * 3,
        out_specs=[ANY] * 3,
        out_shape=(
            shaped(2, SEQ, width, dtype=bf16),
            shaped(8, *in_i.shape, dtype=bf16),
            shaped(8, *small.shape, dtype=bf16),
        ),
        scratch_shapes=gather_semaphores(),
        compiler_params=pltpu.CompilerParams(collective_id=0, has_side_effects=True, vmem_limit_bytes=VMEM_LIMIT),
    )(tokens, in_i, small)


LAG = 2


def forward(inner_ref, inv_ref, tail_ref, inv_tail_ref, mix_ref, conv_ref, xproj_ref, dtp_ref, vec_ref, rate_ref, in_g, out_w, cot_in,
            xconv_ref, yfull_ref, starts_ref, xdbl_ref, joined_ref, wg, wo, cot,
            buf, xc_s, part, yr, zs, zr, tail_s, tail_r, state, last, last_r,
            dt_s, u_s, cb_s, h_s, y_s, y_send, y_recv, z_send, z_recv, e_send, e_recv, *sems):
    i = pl.program_id(0)
    gather = Gather([(in_g, wg, False), (out_w, wo, False)], cot_in, cot, *sems)
    g, r, c = gather.g, gather.r, gather.c
    y_dev, z_dev = (g, 1 - r, c), (g, r, c + 1 - 2 * (c % 2))
    far_dev = (g, 1 - r, (c + 2) % 4)
    to_tail = remote(tail_s, tail_r, e_send.at[0], e_recv.at[0], far_dev)
    to_last = remote(last, last_r, e_send.at[1], e_recv.at[1], far_dev)

    def to_y(k):
        return remote(part.at[k], yr.at[k], y_send.at[k], y_recv.at[k], y_dev)

    def to_z(k):
        return remote(zs.at[k], zr.at[k], z_send.at[k], z_recv.at[k], z_dev)

    @pl.when(i == 0)
    def _():
        gather.greet()
        tail_s[...] = inv_tail_ref[...] * tail_ref[...]
        to_tail.start()
        gather.begin(0)
        gather.begin(1)
        buf[0:8] = jnp.zeros_like(buf[0:8])
        state[...] = jnp.zeros_like(state)

    mix = mix_ref[...]

    @pl.when(i == PC)
    def _():
        to_tail.wait()
        joined = mix * tail_s[...] + (1.0 - mix) * tail_r[...]
        buf[0:8] = joined
        joined_ref[...] = joined

    @pl.when((i > 0) & (i < PC))
    def _():
        buf[0:8] = buf[CH : CH + 8]

    @pl.when(i < NCH)
    def _():
        buf[8 : CH + 8] = inv_ref[...] * inner_ref[...]
        out = conv_ref[4:5]
        for k in range(KCONV):
            out = out + conv_ref[k : k + 1] * buf[5 + k : 5 + k + CH]
        xconv = (out * jax.nn.sigmoid(out)).astype(bf16)
        xconv_ref[...] = xconv
        xc_s[i] = xconv
        part[i] = dot_nt(xproj_ref[...], xconv)
        to_y(i).start()

    @pl.when((i >= LAG) & (i < NCH + LAG))
    def _():
        k = i - LAG
        to_y(k).wait_recv()
        zs[k] = part[k] + yr[k]
        to_z(k).start()

    @pl.when((i >= 2 * LAG) & (i < NCH + 2 * LAG))
    def _():
        k = i - 2 * LAG
        to_z(k).wait_recv()
        xdbl_ref[k] = zs[k] + zr[k]

    @pl.when(i == NCH)
    def _():
        gather.begin_tokens()

    @pl.when(i == NCH + 2)
    def _():
        gather.forward(0)

    @pl.when(i == NCH + 4)
    def _():
        gather.forward(1)

    @pl.when(i == NCH + 6)
    def _():
        gather.forward_again(0)

    @pl.when(i == 2 * NCH - 1)
    def _():
        to_last.wait()
        state[...] = mix_ref[0:1] * last[...] + (1.0 - mix_ref[0:1]) * last_r[...]

    @pl.when(i >= NCH)
    def _():
        k = i - NCH
        starts_ref[0] = state[...]
        h, yfull = scan_chunk(xdbl_ref.at[k], xc_s[k].astype(f32), dtp_ref, vec_ref, rate_ref, state[...], dt_s, u_s, cb_s, h_s, y_s)
        state[...] = h
        yfull_ref[...] = yfull.astype(bf16)

    @pl.when(i == 2 * NCH - 2)
    def _():
        last[...] = state[...]
        to_last.start()

    @pl.when(i == 2 * NCH - 1)
    def _():
        gather.forward_again(1)
        gather.end_tokens()
        gather.end(0)
        gather.end(1)

        def sent(k, _):
            to_y(k).wait_send()
            to_z(k).wait_send()
            return 0

        lax.fori_loop(0, NCH, sent, 0)


def run_forward(inner, inv, mix, conv, xproj, dtp, vec, rate, in_g, out_w, cot):
    w = inner.shape[1]
    first = lambda i: jnp.minimum(i, NCH - 1)
    second = lambda i: jnp.maximum(i - NCH, 0)
    tail = lambda i: (LP // 8 - 1, 0)
    dma = pltpu.SemaphoreType.DMA
    sums = pltpu.VMEM((NCH, XW, CH), f32)
    return pl.pallas_call(
        forward,
        grid=(2 * NCH,),
        in_specs=[
            rows_of(w, first),
            rows_of(1, first),
            pl.BlockSpec((8, w), tail),
            pl.BlockSpec((8, 1), tail),
            whole(8, w),
            whole(8, w),
            whole(XW, w),
            whole(RANK, w),
            whole(8, w),
            whole(NSTATE, w),
            ANY,
            ANY,
            ANY,
        ],
        out_specs=(
            rows_of(w, first),
            rows_of(w, second),
            pl.BlockSpec((1, NSTATE, w), lambda i: (second(i), 0, 0)),
            whole(NCH, XW, CH),
            whole(8, w),
            ANY,
            ANY,
            ANY,
        ),
        out_shape=(
            shaped(SEQ, w, dtype=bf16),
            shaped(SEQ, w, dtype=bf16),
            shaped(NCH, NSTATE, w),
            shaped(NCH, XW, CH),
            shaped(8, w),
            shaped(8, *in_g.shape, dtype=bf16),
            shaped(8, *out_w.shape, dtype=bf16),
            shaped(2, SEQ, cot.shape[1], dtype=bf16),
        ),
        scratch_shapes=[
            pltpu.VMEM((CH + 8, w), f32),
            pltpu.VMEM((NCH, CH, w), bf16),
            sums,
            sums,
            sums,
            sums,
            pltpu.VMEM((8, w), f32),
            pltpu.VMEM((8, w), f32),
            pltpu.VMEM((NSTATE, w), f32),
            pltpu.VMEM((NSTATE, w), f32),
            pltpu.VMEM((NSTATE, w), f32),
            *scan_scratch(w),
            dma((NCH,)),
            dma((NCH,)),
            dma((NCH,)),
            dma((NCH,)),
            dma((2,)),
            dma((2,)),
            *gather_semaphores(),
        ],
        compiler_params=pltpu.CompilerParams(
            dimension_semantics=("arbitrary",), collective_id=2, has_side_effects=True, vmem_limit_bytes=VMEM_LIMIT
        ),
        cost_estimate=pl.CostEstimate(flops=60 * 1000000000, bytes_accessed=1000000, transcendentals=0),
    )(inner, inv, inner, inv, mix, conv, xproj, dtp, vec, rate, in_g, out_w, cot)


def project_first(raw_ref, gain_ref, w_ref, normed_ref, inv_ref, out_ref):
    low = raw_ref[0].astype(f32)
    high = raw_ref[1].astype(f32)
    squares = jnp.sum(low * low + high * high, axis=1, keepdims=True)
    inv_ref[...] = lax.rsqrt(squares / D + eps)
    low = (low * gain_ref[0:1]).astype(bf16)
    high = (high * gain_ref[1:2]).astype(bf16)
    normed_ref[0] = low
    normed_ref[1] = high
    n = w_ref.shape[2]
    for k in range(SLOTS):
        out_ref[:, k * n : (k + 1) * n] = dot_nn(low, w_ref[2 * k]) + dot_nn(high, w_ref[2 * k + 1])


def split_rows(width, at, tall=CH):
    return pl.BlockSpec((2, tall, width), lambda i: (0, at(i), 0))


def run_project_first(raw, gain, w):
    width = raw.shape[2]
    at = lambda i: i
    n = SLOTS * w.shape[2]
    return call(
        project_first,
        BIG_STEPS,
        (raw, gain, w),
        [split_rows(width, at, BIG), whole(2, width), whole(*w.shape)],
        (shaped(2, SEQ, width, dtype=bf16), shaped(SEQ, 1), shaped(SEQ, n)),
        (split_rows(width, at, BIG), rows_of(1, at, BIG), rows_of(n, at, BIG)),
        [],
        9,
    )


def gate_backward(normed_ref, wg_ref, cot_ref, wo_ref, yfull_ref, inv_ref, gated_ref, dy_ref, dproj_ref, dscale_ref, own_ref, oth_ref, gate_s):
    n = wo_ref.shape[2]
    for k in range(SLOTS):
        gate_s[:, k * n : (k + 1) * n] = dot_nn(normed_ref[0], wg_ref[2 * k]) + dot_nn(normed_ref[1], wg_ref[2 * k + 1])
    d_gated = jnp.zeros(dy_ref.shape, f32)
    for k in range(SLOTS):
        for d in range(2):
            d_gated = d_gated + dot_nt(cot_ref[d, :, k * n : (k + 1) * n], wo_ref[2 * k + d])
    gate_in = gate_s[...]
    inv = inv_ref[...]
    yfull = yfull_ref[...].astype(f32)
    gate = inv * gate_in
    sig = jax.nn.sigmoid(gate)
    passed = gate * sig
    gated = (yfull * passed).astype(bf16)
    gated_ref[...] = gated
    for k in range(SLOTS):
        own_ref[:, k * n : (k + 1) * n] = dot_nn(gated, wo_ref[2 * k])
        oth_ref[:, k * n : (k + 1) * n] = dot_nn(gated, wo_ref[2 * k + 1]).astype(bf16)
    dy_ref[...] = d_gated * passed
    d_gate = d_gated * yfull * (sig * (1.0 + gate * (1.0 - sig)))
    dproj_ref[...] = (inv * d_gate).astype(bf16)
    dscale_ref[...] = jnp.sum(d_gate * gate_in, axis=1, keepdims=True)


def run_gate_backward(normed, wg, cot, wo, yfull, inv):
    width = cot.shape[2]
    w = yfull.shape[1]
    at = lambda i: i
    return call(
        gate_backward,
        BIG_STEPS,
        (normed, wg, cot, wo, yfull, inv),
        [split_rows(width, at, BIG), whole(*wg.shape), split_rows(width, at, BIG), whole(*wo.shape), rows_of(w, at, BIG), rows_of(1, at, BIG)],
        (shaped(SEQ, w, dtype=bf16), shaped(SEQ, w), shaped(SEQ, w, dtype=bf16), shaped(SEQ, 1), shaped(SEQ, width), shaped(SEQ, width, dtype=bf16)),
        (rows_of(w, at, BIG), rows_of(w, at, BIG), rows_of(w, at, BIG), rows_of(1, at, BIG), rows_of(width, at, BIG), rows_of(width, at, BIG)),
        [pltpu.VMEM((BIG, w), f32)],
        22,
    )


def normed_backward(inner_ref, gate_ref, wi_ref, wg_ref, own_ref, oth_ref):
    n = wi_ref.shape[2]
    for d, out_ref in ((1, oth_ref), (0, own_ref)):
        total = jnp.zeros(out_ref.shape, f32)
        for k in range(SLOTS):
            total = total + dot_nt(inner_ref[:, k * n : (k + 1) * n], wi_ref[2 * k + d])
            total = total + dot_nt(gate_ref[:, k * n : (k + 1) * n], wg_ref[2 * k + d])
        out_ref[...] = total.astype(out_ref.dtype)


def run_normed_backward(d_inner, d_gate, wi, wg):
    w = d_inner.shape[1]
    width = wi.shape[1]
    at = lambda i: i
    return call(
        normed_backward,
        BIG_STEPS,
        (d_inner, d_gate, wi, wg),
        [rows_of(w, at, BIG), rows_of(w, at, BIG), whole(*wi.shape), whole(*wg.shape)],
        (shaped(SEQ, width), shaped(SEQ, width, dtype=bf16)),
        (rows_of(width, at, BIG), rows_of(width, at, BIG)),
        [],
        12,
    )


def finish(inner_hbm, gate_hbm, normed_hbm, raw_hbm, wi_hbm, wg_hbm, dn_ref, grad_ref, gain_ref,
           inner, gate, normed, raw, wi, wg, cs, cr, kept, xs, xr, fs, fr, ys, yr, zs, zr, own, gs, gr,
           loc, c_send, c_recv, x_send, x_recv, f_send, f_recv, y_send, y_recv, z_send, z_recv, b_send, b_recv, g_send, g_recv):
    g, r, c = lax.axis_index("grp"), lax.axis_index("row"), lax.axis_index("col")
    x, core, s, p = g // 2, g % 2, c // 2, c % 2
    tall, width = raw.shape
    part = tall // 2
    n = wi.shape[2]
    q = 2 * p + xor_bit(r, s)
    y_dev, z_dev = (g, 1 - r, c), (g, r, 2 * s + 1 - p)
    x_dev, core_dev = ((1 - x) * 2 + core, r, c), (2 * x + 1 - core, r, c)
    alone = q == c

    loads = [
        pltpu.make_async_copy(normed_hbm, normed, loc.at[0]),
        pltpu.make_async_copy(inner_hbm, inner, loc.at[1]),
        pltpu.make_async_copy(gate_hbm, gate, loc.at[2]),
        pltpu.make_async_copy(wi_hbm, wi, loc.at[3]),
        pltpu.make_async_copy(wg_hbm, wg, loc.at[4]),
        pltpu.make_async_copy(raw_hbm.at[0, pl.ds(pl.multiple_of(p * tall, 64), tall)], raw, loc.at[5]),
    ]
    for copy in loads:
        copy.start()

    barrier = pltpu.get_barrier_semaphore()
    for dg in range(4):
        for dc in range(4):
            if dg or dc:
                pl.semaphore_signal(barrier, inc=1, device_id=((g + dg) % 4, r, (c + dc) % 4), device_id_type=MESH)
    for dc in range(4):
        pl.semaphore_signal(barrier, inc=1, device_id=(g, 1 - r, (c + dc) % 4), device_id_type=MESH)
    pl.semaphore_wait(barrier, 19)

    def weight_grad(d, block, store):
        cols = pl.ds(pl.multiple_of(block * n, 128), n)

        def tile(t, _):
            rows = pl.ds(pl.multiple_of(t * n, 128), n)
            store(rows, dot_tn(normed[d, :, rows], inner[:, cols]))
            return 0

        lax.fori_loop(0, width // n, tile, 0)

    def to_core(i, d):
        return remote(cs.at[i, d], cr.at[i, d], c_send.at[2 * i + d], c_recv.at[2 * i + d], core_dev)

    def to_x(d):
        return remote(xs.at[d], xr.at[d], x_send.at[d], x_recv.at[d], x_dev)

    def to_owner(d):
        return remote(fs.at[d], fr.at[d], f_send.at[d], f_recv.at[d], (g, r if d == 0 else 1 - r, q))

    def grad_to_core(i):
        block = 2 * (1 - x if i == 0 else x) + 1 - core
        for d in range(2):

            def store(rows, v, d=d):
                cs[i, d, rows, :] = v.astype(bf16)

            weight_grad(d, block, store)
            to_core(i, d).start()

    def start_of(mine, h):
        return pl.multiple_of((p if mine else 1 - p) * tall + h * part, 32)

    def normed_part(mine, h, d, store):
        rows = pl.ds(start_of(mine, h), part)

        def tile(t, _):
            cols = pl.ds(pl.multiple_of(t * n, 128), n)
            total = dot_nt(inner[rows, 0:n], wi[d, cols, :])
            for j in range(1, SLOTS):
                total = total + dot_nt(inner[rows, j * n : (j + 1) * n], wi[2 * j + d, cols, :])
            for j in range(SLOTS):
                total = total + dot_nt(gate[rows, j * n : (j + 1) * n], wg[2 * j + d, cols, :])
            store(cols, total)
            return 0

        lax.fori_loop(0, width // n, tile, 0)

    def to_y(i):
        return remote(ys.at[i], yr.at[i], y_send.at[i], y_recv.at[i], y_dev)

    def to_z(i):
        return remote(zs.at[i], zr.at[i], z_send.at[i], z_recv.at[i], z_dev)

    def into(ref, i, added=None):
        def store(cols, v):
            if added is not None:
                v = v + added[0, :, cols].astype(f32)
            ref[i, :, cols] = v.astype(bf16)

        return store

    loads[0].wait()
    loads[1].wait()
    grad_to_core(0)
    for copy in loads[2:5]:
        copy.wait()
    normed_part(False, 0, 1, into(ys, 0))
    to_y(0).start()
    normed_part(False, 1, 1, into(zs, 0))
    to_z(0).start()
    grad_to_core(1)

    for d in range(2):

        def hold(rows, v, d=d):
            kept[d, rows, :] = v

        weight_grad(d, 2 * (1 - x) + core, hold)
    for d in range(2):
        to_core(0, d).wait_recv()
        xs[d] = (kept[d] + cr[0, d].astype(f32)).astype(bf16)
        to_x(d).start()

    normed_part(False, 1, 0, into(zs, 2))
    to_z(2).start()
    normed_part(True, 0, 1, into(ys, 1))
    to_y(1).start()
    to_y(0).wait_recv()
    normed_part(False, 0, 0, into(zs, 1, yr))
    to_z(1).start()
    to_z(0).wait_recv()
    normed_part(True, 1, 1, into(ys, 2, zr))
    to_y(2).start()

    for d in range(2):

        def hold(rows, v, d=d):
            kept[d, rows, :] = v

        weight_grad(d, 2 * x + core, hold)
    for d in range(2):
        to_core(1, d).wait_recv()
        to_x(d).wait_recv()
        fs[d] = (kept[d] + cr[1, d].astype(f32) + xr[d].astype(f32)).astype(bf16)
        if d == 0:

            @pl.when(alone)
            def _():
                fr[0] = fs[0]

            @pl.when(jnp.logical_not(alone))
            def _():
                to_owner(0).start()
        else:
            to_owner(1).start()

    for h in range(2):

        def store(cols, v, h=h):
            own[h * part : (h + 1) * part, cols] = v

        normed_part(True, h, 0, store)

    loads[5].wait()
    for h in range(2):
        to_y(1 + h).wait_recv()
        to_z(1 + h).wait_recv()
        total = own[h * part : (h + 1) * part, :] + yr[1 + h].astype(f32) + zr[1 + h].astype(f32)
        own[h * part : (h + 1) * part, :] = total
        product = total * raw[h * part : (h + 1) * part, :].astype(f32)
        folded = jnp.sum(product.reshape(part // 8, 8, width), axis=0)
        for b in range(SLOTS):
            if h == 0:
                gs[b] = folded[:, b * n : (b + 1) * n]
            else:
                gs[b] = gs[b] + folded[:, b * n : (b + 1) * n]

    cut = tall - LC
    low = cut - LC
    moves = {
        0: ([(0, tall, 0)], None),
        1: ([(0, cut, 0)], (cut, 3, low)),
        2: ([(LC, tall, 0)], (0, 1, cut)),
        3: ([(LC, cut, 0), (cut, tall, cut)], (0, 2, cut)),
    }

    def border(k):
        stays, leaves = moves[k]
        mine = [pltpu.make_async_copy(own.at[a:b], dn_ref.at[at : at + b - a], loc.at[i]) for i, (a, b, at) in enumerate(stays)]
        if leaves is None:
            return mine, None
        a, to, at = leaves
        return mine, remote(own.at[a : a + LC], dn_ref.at[at : at + LC], b_send.at[0], b_recv.at[0], (g, r, to))

    for k in range(4):

        @pl.when(c == k)
        def _(k=k):
            mine, gone = border(k)
            if gone is not None:
                gone.start()
            for copy in mine:
                copy.start()

    def gain_copy(dg, dc):
        to = ((g + dg) % 4, r, (c + dc) % 4)
        i = 4 * dg + dc - 1
        return remote(gs.at[(g + dg) % 4], gr.at[i], g_send.at[i], g_recv.at[0], to)

    pairs = [(dg, dc) for dg in range(4) for dc in range(4) if dg or dc]
    for dg, dc in pairs:
        gain_copy(dg, dc).start()

    @pl.when(jnp.logical_not(alone))
    def _():
        to_owner(0).wait_recv()

    to_owner(1).wait_recv()
    grad_ref[...] = fr[0].astype(f32) + fr[1].astype(f32)

    pltpu.make_async_copy(gr, gr, g_recv.at[0]).wait()
    gain_ref[...] = jnp.sum(gr[...], axis=0) + gs[g]

    for k in range(4):

        @pl.when(c == k)
        def _(k=k):
            mine, gone = border(k)
            for copy in mine:
                copy.wait()
            if gone is not None:
                gone.wait()

    for dg, dc in pairs:
        gain_copy(dg, dc).wait_send()
    for i in range(3):
        to_y(i).wait_send()
        to_z(i).wait_send()
    for d in range(2):
        for i in range(2):
            to_core(i, d).wait_send()
        to_x(d).wait_send()

    @pl.when(jnp.logical_not(alone))
    def _():
        to_owner(0).wait_send()

    to_owner(1).wait_send()


def run_finish(d_inner, d_gate, normed, raw, wi, wg):
    w = d_inner.shape[1]
    width, n = wi.shape[1], wi.shape[2]
    tall = SEQ // 2
    part = tall // 2
    dma = pltpu.SemaphoreType.DMA
    low = lambda *shape: pltpu.VMEM(shape, bf16)
    vmem = pl.BlockSpec(memory_space=pltpu.VMEM)
    return pl.pallas_call(
        finish,
        in_specs=[ANY] * 6,
        out_specs=[ANY, vmem, vmem],
        out_shape=(shaped(tall, width), shaped(width, n), shaped(8, n)),
        scratch_shapes=[
            low(SEQ, w),
            low(SEQ, w),
            low(2, SEQ, width),
            low(tall, width),
            low(2 * SLOTS, width, n),
            low(2 * SLOTS, width, n),
            low(2, 2, width, n),
            low(2, 2, width, n),
            pltpu.VMEM((2, width, n), f32),
            low(2, width, n),
            low(2, width, n),
            low(2, width, n),
            low(2, width, n),
            low(3, part, width),
            low(3, part, width),
            low(3, part, width),
            low(3, part, width),
            pltpu.VMEM((tall, width), f32),
            pltpu.VMEM((SLOTS, 8, n), f32),
            pltpu.VMEM((15, 8, n), f32),
            dma((6,)),
            dma((4,)),
            dma((4,)),
            dma((2,)),
            dma((2,)),
            dma((2,)),
            dma((2,)),
            dma((3,)),
            dma((3,)),
            dma((3,)),
            dma((3,)),
            dma((1,)),
            dma((1,)),
            dma((15,)),
            dma((1,)),
        ],
        compiler_params=pltpu.CompilerParams(collective_id=1, has_side_effects=True, vmem_limit_bytes=VMEM_LIMIT),
        cost_estimate=pl.CostEstimate(flops=60 * 1000000000, bytes_accessed=1000000, transcendentals=0),
    )(d_inner, d_gate, normed, raw, wi, wg)


def late_parts(order_ref, normed_ref, gate_ref, gated_ref, cot_ref, gate_sent, out_sent, gate_kept, out_kept):
    t = pl.program_id(0)
    for d in range(2):
        low = dot_tn(normed_ref[d], gate_ref[...])
        high = dot_tn(gated_ref[...], cot_ref[d])

        @pl.when(t < 2)
        def _(d=d, low=low, high=high):
            gate_sent[0, d] = low.astype(bf16)
            out_sent[0, d] = high.astype(bf16)

        @pl.when(t >= 2)
        def _(d=d, low=low, high=high):
            gate_kept[0, d] = low
            out_kept[0, d] = high


def run_late_parts(order, normed, d_gate, gated, cot):
    width = normed.shape[2]
    w = gated.shape[1]
    n = w // SLOTS
    sent = pl.BlockSpec((1, 2, width, n), lambda t, o: (jnp.minimum(t, 1), 0, 0, 0))
    kept = pl.BlockSpec((1, 2, width, n), lambda t, o: (jnp.maximum(t - 2, 0), 0, 0, 0))
    return pl.pallas_call(
        late_parts,
        grid_spec=pltpu.PrefetchScalarGridSpec(
            num_scalar_prefetch=1,
            grid=(SLOTS,),
            in_specs=[
                pl.BlockSpec((2, SEQ, width), lambda t, o: (0, 0, 0)),
                pl.BlockSpec((SEQ, n), lambda t, o: (0, o[t])),
                pl.BlockSpec((SEQ, w), lambda t, o: (0, 0)),
                pl.BlockSpec((2, SEQ, n), lambda t, o: (0, 0, o[t])),
            ],
            out_specs=(sent, sent, kept, kept),
        ),
        out_shape=(shaped(2, 2, width, n, dtype=bf16), shaped(2, 2, width, n, dtype=bf16), shaped(2, 2, width, n), shaped(2, 2, width, n)),
        compiler_params=pltpu.CompilerParams(dimension_semantics=("arbitrary",), vmem_limit_bytes=VMEM_LIMIT),
        cost_estimate=pl.CostEstimate(flops=14 * 1000000000, bytes_accessed=1000000, transcendentals=0),
    )(order, normed, d_gate, gated, cot)


PIECES = 8
PIECE = SEQ // PIECES
PIECE_STEP = (0, 0, 1, 1, 2, 3, 4, 5)


def border_moves(tall):
    cut = tall - LC
    low = cut - LC
    return {
        0: ([(0, tall, 0)], None),
        1: ([(0, cut, 0)], (cut, 3, low)),
        2: ([(LC, tall, 0)], (0, 1, cut)),
        3: ([(LC, cut, 0), (cut, tall, cut)], (0, 2, cut)),
    }


def backward(xdbl_ref, xconv_ref, dy_ref, dtp_ref, vec_ref, rate_ref, starts_ref, mix_ref, into_ref, sent_hbm, kept_hbm, own_hbm, oth_hbm,
             dxdbl_ref, dxc_ref, alog_ref, sums_ref, dtpg_ref, grad_ref, branch_ref,
             first, first_s, first_r, part, yr, zs, zr, cr, kp, xs, xr, fs, fr, out, own, by, bz_s, bz, fin,
             y_send, y_recv, z_send, z_recv, e_send, e_recv, c_send, c_recv, x_send, x_recv, f_send, f_recv,
             p_send, p_recv, q_send, q_recv, b_send, b_recv, load_k, load_o, stay, put, *scratch):
    i = pl.program_id(0)
    g, r, c = lax.axis_index("grp"), lax.axis_index("row"), lax.axis_index("col")
    x, core, s, p = g // 2, g % 2, c // 2, c % 2
    q = 2 * p + xor_bit(r, s)
    tall = SEQ // 2
    alone = q == c
    y_dev, z_dev, far_dev = (g, 1 - r, c), (g, r, 2 * s + 1 - p), (g, 1 - r, (c + 2) % 4)
    x_dev, core_dev = ((1 - x) * 2 + core, r, c), (2 * x + 1 - core, r, c)
    to_first = remote(first_s, first_r, e_send.at[0], e_recv.at[0], far_dev)

    def to_y(k):
        return remote(part.at[k], yr.at[k], y_send.at[k], y_recv.at[k], y_dev)

    def to_z(k):
        return remote(zs.at[k], zr.at[k], z_send.at[k], z_recv.at[k], z_dev)

    def to_core(n, j):
        return remote(sent_hbm[n].at[j], cr.at[n, j], c_send.at[n, j], c_recv.at[n, j], core_dev)

    def load(n, j):
        return pltpu.make_async_copy(kept_hbm[n].at[j], kp.at[n], load_k.at[n])

    def to_x(n):
        return remote(xs.at[n], xr.at[n], x_send.at[n], x_recv.at[n], x_dev)

    def to_owner(n, d):
        return remote(fs.at[n, d], fr.at[n, d], f_send.at[n, d], f_recv.at[n, d], (g, r if d == 0 else 1 - r, q))

    def rows_at(m):
        base = (1 - p) if m < PIECES // 2 else p
        return pl.ds(pl.multiple_of(base * tall + (m % (PIECES // 2)) * PIECE, 16), PIECE)

    def branch_y(m):
        return remote(oth_hbm.at[rows_at(m)], by.at[m], p_send.at[m], p_recv.at[m], y_dev)

    def branch_z(m):
        return remote(bz_s.at[m], bz.at[m], q_send.at[m], q_recv.at[m], z_dev)

    def border(k):
        stays, leaves = border_moves(tall)[k]
        mine = [pltpu.make_async_copy(fin.at[a:b], branch_ref.at[at : at + b - a], stay.at[n]) for n, (a, b, at) in enumerate(stays)]
        if leaves is None:
            return mine, None
        a, to, at = leaves
        return mine, remote(fin.at[a : a + LC], branch_ref.at[at : at + LC], b_send.at[0], b_recv.at[0], (g, r, to))

    def at_border(act):
        for k in range(4):

            @pl.when(c == k)
            def _(k=k):
                act(*border(k))

    @pl.when(i == 0)
    def _():
        barrier = pltpu.get_barrier_semaphore()
        for dr in range(2):
            for dc in range(4):
                if dr or dc:
                    pl.semaphore_signal(barrier, inc=1, device_id=(g, (r + dr) % 2, (c + dc) % 4), device_id_type=MESH)
        for device in (x_dev, core_dev):
            pl.semaphore_signal(barrier, inc=1, device_id=device, device_id_type=MESH)
        pl.semaphore_wait(barrier, 9)
        for n in range(2):
            for j in range(2):
                to_core(n, j).start()
            load(n, 0).start()
        pltpu.make_async_copy(own_hbm, own, load_o.at[0]).start()
        first[...] = jnp.zeros_like(first)
        alog_ref[...] = jnp.zeros_like(alog_ref)
        sums_ref[...] = jnp.zeros_like(sums_ref)
        dtpg_ref[...] = jnp.zeros_like(dtpg_ref)

    @pl.when(i == 1)
    def _():
        to_first.wait()
        first[...] = mix_ref[0:1] * first_s[...] + into_ref[0:1] * first_r[...]

    chunk_backward(xdbl_ref, xconv_ref, dy_ref, dtp_ref, vec_ref, rate_ref, starts_ref, part.at[i], dxc_ref, alog_ref, sums_ref, dtpg_ref, first, *scratch)

    @pl.when(i == 0)
    def _():
        first_s[...] = first[...]
        to_first.start()

    @pl.when(i == 1)
    def _():
        pltpu.make_async_copy(own_hbm, own, load_o.at[0]).wait()
        for n in range(2):
            to_core(n, 0).wait_recv()
            load(n, 0).wait()
            xs[n] = (kp[n] + cr[n, 0].astype(f32)).astype(bf16)
            to_x(n).start()
            load(n, 1).start()

    for n in range(2):

        @pl.when(i == 3 + n)
        def _(n=n):
            load(n, 1).wait()
            to_core(n, 1).wait_recv()
            to_x(n).wait_recv()
            fs[n] = (kp[n] + cr[n, 1].astype(f32) + xr[n].astype(f32)).astype(bf16)

            @pl.when(alone)
            def _():
                fr[n, 0] = fs[n, 0]

            @pl.when(jnp.logical_not(alone))
            def _():
                to_owner(n, 0).start()

            to_owner(n, 1).start()

        @pl.when(i == 6 + n)
        def _(n=n):
            @pl.when(jnp.logical_not(alone))
            def _():
                to_owner(n, 0).wait_recv()

            to_owner(n, 1).wait_recv()
            out[n] = fr[n, 0].astype(f32) + fr[n, 1].astype(f32)
            pltpu.make_async_copy(out.at[n], grad_ref.at[n], put.at[n]).start()

    for m in range(PIECES):

        @pl.when(i == PIECE_STEP[m] + 1)
        def _(m=m):
            branch_y(m).wait_recv()
            total = own[rows_at(m), :] + by[m].astype(f32)
            if m < PIECES // 2:
                bz_s[m] = total.astype(bf16)
                branch_z(m).start()
            else:
                j = m - PIECES // 2
                branch_z(j).wait_recv()
                fin[j * PIECE : (j + 1) * PIECE, :] = (total + bz[j].astype(f32)).astype(bf16)

    @pl.when(i == 7)
    def _():
        def begin(mine, gone):
            if gone is not None:
                gone.start()
            for copy in mine:
                copy.start()

        at_border(begin)

    @pl.when((i >= 1) & (i <= NCH - 1))
    def _():
        k = i - 1
        to_y(k).wait_recv()
        zs[k] = part[k] + yr[k]
        to_z(k).start()

    @pl.when(i >= 3)
    def _():
        k = i - 3
        to_z(k).wait_recv()
        dxdbl_ref[NCH - 1 - k] = zs[k] + zr[k]

    to_y(i).start()
    for m in range(PIECES):

        @pl.when(i == PIECE_STEP[m])
        def _(m=m):
            branch_y(m).start()

    @pl.when(i == NCH - 1)
    def _():
        to_y(NCH - 1).wait_recv()
        zs[NCH - 1] = part[NCH - 1] + yr[NCH - 1]
        to_z(NCH - 1).start()
        for k in (NCH - 3, NCH - 2, NCH - 1):
            to_z(k).wait_recv()
            dxdbl_ref[NCH - 1 - k] = zs[k] + zr[k]

        def finish_border(mine, gone):
            for copy in mine:
                copy.wait()
            if gone is not None:
                gone.wait()

        at_border(finish_border)

        def sent(k, _):
            to_y(k).wait_send()
            to_z(k).wait_send()
            return 0

        lax.fori_loop(0, NCH, sent, 0)
        for n in range(2):
            for j in range(2):
                to_core(n, j).wait_send()
            to_x(n).wait_send()

            @pl.when(jnp.logical_not(alone))
            def _(n=n):
                to_owner(n, 0).wait_send()

            to_owner(n, 1).wait_send()
            pltpu.make_async_copy(out.at[n], grad_ref.at[n], put.at[n]).wait()
        for m in range(PIECES):
            branch_y(m).wait_send()
            if m < PIECES // 2:
                branch_z(m).wait_send()


def backward_kernel(*refs):
    backward(*refs[:9], refs[9:11], refs[11:13], *refs[13:])


def run_backward(xdbl, xconv, dy, dtp, vec, rate, starts, mix, into, sent, kept, own, oth):
    w = xconv.shape[1]
    width = own.shape[1]
    _, _, tall, n = sent[0].shape
    at = lambda i: NCH - 1 - i
    dma = pltpu.SemaphoreType.DMA
    low = lambda *shape: pltpu.VMEM(shape, bf16)
    sums = pltpu.VMEM((NCH, XW, CH), f32)
    state = pltpu.VMEM((NSTATE, w), f32)
    return pl.pallas_call(
        backward_kernel,
        grid=(NCH,),
        in_specs=[
            chunk_of(XW, at),
            rows_of(w, at),
            rows_of(w, at),
            whole(RANK, w),
            whole(8, w),
            whole(NSTATE, w),
            pl.BlockSpec((1, NSTATE, w), lambda i: (at(i), 0, 0)),
            whole(8, w),
            whole(8, w),
        ]
        + [ANY] * 6,
        out_specs=(whole(NCH, XW, CH), rows_of(w, at), whole(NSTATE, w), whole(8, w), whole(RANK, w), ANY, ANY),
        out_shape=(
            shaped(NCH, XW, CH),
            shaped(SEQ, w),
            shaped(NSTATE, w),
            shaped(8, w),
            shaped(RANK, w),
            shaped(2, tall, n),
            shaped(SEQ // 2, width, dtype=bf16),
        ),
        scratch_shapes=[
            state,
            state,
            state,
            sums,
            sums,
            sums,
            sums,
            low(2, 2, 2, tall, n),
            pltpu.VMEM((2, 2, tall, n), f32),
            low(2, 2, tall, n),
            low(2, 2, tall, n),
            low(2, 2, tall, n),
            low(2, 2, tall, n),
            pltpu.VMEM((2, tall, n), f32),
            pltpu.VMEM((SEQ, width), f32),
            low(PIECES, PIECE, width),
            low(PIECES // 2, PIECE, width),
            low(PIECES // 2, PIECE, width),
            low(SEQ // 2, width),
            dma((NCH,)),
            dma((NCH,)),
            dma((NCH,)),
            dma((NCH,)),
            dma((1,)),
            dma((1,)),
            dma((2, 2)),
            dma((2, 2)),
            dma((2,)),
            dma((2,)),
            dma((2, 2)),
            dma((2, 2)),
            dma((PIECES,)),
            dma((PIECES,)),
            dma((PIECES // 2,)),
            dma((PIECES // 2,)),
            dma((1,)),
            dma((1,)),
            dma((2,)),
            dma((1,)),
            dma((2,)),
            dma((2,)),
            *backward_scratch(w),
        ],
        compiler_params=pltpu.CompilerParams(
            dimension_semantics=("arbitrary",), collective_id=3, has_side_effects=True, vmem_limit_bytes=61 * 1024 * 1024
        ),
        cost_estimate=pl.CostEstimate(flops=120 * 1000000000, bytes_accessed=1000000, transcendentals=0),
    )(xdbl, xconv, dy, dtp, vec, rate, starts, mix, into, *sent, *kept, own, oth)


def per_device(
    tokens,
    gain,
    in_proj,
    conv_weight,
    conv_bias,
    x_proj,
    dt_proj,
    dt_bias,
    a_log,
    d_skip,
    out_proj,
    table,
    cotangent,
):
    row = lax.axis_index("row")
    col = lax.axis_index("col")
    grp = lax.axis_index("grp")
    low_row = row == 0
    low_pair = col % 2 == 0
    half = col // 2
    places = [(r, c) for r in range(2) for c in range(4)]
    quick = lax.axis_size("grp") == 4

    def spot(r, c):
        return r * 4 + c

    def send(v, pairs):
        return lax.ppermute(v, ("row", "col"), [(spot(*a), spot(*b)) for a, b in pairs])

    def swap(v):
        return send(v, [((r, c), (1 - r, c)) for r, c in places])

    def pair(v):
        return send(v, [((r, c), (r, c ^ 1)) for r, c in places])

    def across(v):
        return send(v, [((r, c), (1 - r, c ^ 2)) for r, c in places])

    def quarter_spot(q, s):
        return ((q & 1) ^ s, 2 * s + (q >> 1))

    same = [((r, q), quarter_spot(q, r ^ (q & 1))) for r, q in places]
    other = [((r, q), quarter_spot(q, 1 ^ r ^ (q & 1))) for r, q in places]
    spread = [((r, q), quarter_spot(q, r)) for r, q in places]

    def back(pairs):
        return [(b, a) for a, b in pairs]

    def flip(v, bit):
        return lax.ppermute(v, "grp", [(g, g ^ bit) for g in range(4)])

    def scatter_grp(v, axis):
        return lax.psum_scatter(v, "grp", scatter_dimension=axis, tiled=True)

    def by_pair(own, paired):
        return jnp.where(low_pair, own, paired), jnp.where(low_pair, paired, own)

    local = tokens.shape[0]
    cut = local - LC
    tail_at = cut - LC

    def to_sequences(v):
        got = send(jnp.where(col == 3, v[tail_at:cut], v[cut:]), [((r, a), (r, b)) for r in range(2) for a, b in ((1, 2), (2, 3), (3, 1))])
        low = jnp.concatenate([v[:cut], jnp.where(col == 0, v[cut:], got)], axis=0)
        two = jnp.concatenate([got, v[:cut]], axis=0)
        three = jnp.concatenate([got, v[:tail_at], v[cut:]], axis=0)
        return jnp.where(col < 2, low, jnp.where(col == 2, two, three))

    def from_sequences(v):
        got = send(jnp.where(col == 1, v[cut:], v[:LC]), [((r, b), (r, a)) for r in range(2) for a, b in ((1, 2), (2, 3), (3, 1))])
        low = jnp.concatenate([v[:cut], jnp.where(col == 0, v[cut:], got)], axis=0)
        two = jnp.concatenate([v[LC:], got], axis=0)
        three = jnp.concatenate([v[LC:cut], got, v[cut:]], axis=0)
        return jnp.where(col < 2, low, jnp.where(col == 2, two, three))

    def gather_quad(v):
        swapped = swap(v)
        paired = pair(v)
        mid = v.shape[0] // 2
        diagonal = jnp.concatenate([pair(swapped[:mid]), swap(paired[mid:])], axis=0)
        first_own, second_own = by_pair(v, paired)
        first_oth, second_oth = by_pair(swapped, diagonal)
        return jnp.stack([jnp.concatenate([first_own, second_own], axis=0), jnp.concatenate([first_oth, second_oth], axis=0)])

    def scatter_quad(own, oth):
        v = own + swap(oth.astype(bf16)).astype(f32)
        first, second = v[:local], v[local:]
        kept, sent = jnp.where(low_pair, first, second), jnp.where(low_pair, second, first)
        return kept + pair(sent.astype(bf16)).astype(f32)

    own_table = jnp.where(half == 0, table[0], table[1])
    oth_table = jnp.where(half == 0, table[1], table[0])
    resumes_own = own_table == half
    resumed_by_other = oth_table == half

    small = jnp.concatenate([conv_weight, conv_bias[None], dt_bias[None], d_skip[None], a_log, dt_proj, x_proj.T], axis=0)
    lanes = small.shape[1]
    used = small.shape[0]
    gain_rows = gain.size // lanes
    width = tokens.shape[1]
    if quick:
        small = jnp.concatenate([small, gain.reshape(gain_rows, lanes)], axis=0)
        small = jnp.pad(small, ((0, -small.shape[0] % 16), (0, 0)))
        raw, wi, small = run_gather_start(tokens, in_proj[:, 0], small)
        gain_all = small[:, used : used + gain_rows].reshape(2, width).astype(f32)
        small = jnp.swapaxes(small, 0, 1).reshape(small.shape[1], 8 * lanes)
    else:
        raw = gather_quad(to_sequences(tokens))

        def weight(shard):
            v = lax.all_gather(jnp.stack([send(shard, same), send(shard, other)]), "grp", axis=2, tiled=True)
            v = v.reshape(2, v.shape[1], SLOTS, v.shape[2] // SLOTS)
            return jnp.transpose(v, (2, 0, 1, 3)).reshape(2 * SLOTS, v.shape[1], v.shape[3])

        wi = weight(in_proj[:, 0])
        small = send(lax.all_gather(small, ("row", "grp"), axis=1, tiled=True), spread)
        gain_all = lax.all_gather(gain, ("row", "grp"), axis=0, tiled=True).astype(f32).reshape(2, width)
    w = small.shape[1]
    zero_row = jnp.zeros((1, w), f32)
    conv = jnp.concatenate([small[0:5].astype(f32)] + [zero_row] * 3, axis=0)
    vec = jnp.concatenate([small[5:7].astype(f32)] + [zero_row] * 6, axis=0)
    rate = -jnp.exp(small[7 : 7 + NSTATE].astype(f32))
    dtp = small[7 + NSTATE : 7 + NSTATE + RANK]
    xproj = small[7 + NSTATE + RANK : 7 + NSTATE + RANK + XW]
    gain_own = jnp.where(low_row, gain_all[0], gain_all[1])
    gain_two = jnp.stack([gain_own, jnp.where(low_row, gain_all[1], gain_all[0])])

    normed, inv, inner = run_project_first(raw, gain_two, wi)
    zero_state = jnp.zeros((NSTATE, w), f32)
    if quick:
        mix = jnp.broadcast_to(resumes_own.astype(f32), (8, w))
        xconv, yfull, starts, xdbl, tail, wg, wo, cot = run_forward(inner, inv, mix, conv, xproj, dtp, vec, rate, in_proj[:, 1], out_proj, cotangent)
    else:
        tail_own = (inv * inner)[LP - 8 : LP]
        tail = jnp.where(resumes_own, tail_own, across(tail_own))
        xconv, xdbl = run_conv_forward(inner, inv, tail, conv, xproj)
        for move in (swap, pair):
            xdbl = xdbl + move(xdbl)
        xdbl = jnp.swapaxes(xdbl.reshape(XW, NCH, CH), 0, 1)
        *kept, final = run_scan_forward(0, PC, xdbl, xconv, dtp, vec, rate, zero_state)
        resumed = jnp.where(resumes_own, final, across(final))
        yfull, starts, _ = run_scan_forward(PC, NCH - PC, xdbl, xconv, dtp, vec, rate, resumed, kept)
        wg, wo = weight(in_proj[:, 1]), weight(out_proj)
        cot = gather_quad(to_sequences(cotangent))
    gated, d_yfull, d_gate_proj, gate_scale, branch_own, branch_oth = run_gate_backward(normed, wg, cot, wo, yfull, inv)

    def collect(v):
        return send(v[0].astype(bf16), back(same)).astype(f32) + send(v[1].astype(bf16), back(other)).astype(f32)

    def rows_product(a, b, out_dtype):
        return lax.dot_general(a, b, (((1,), (0,)), ((), ())), preferred_element_type=f32).astype(out_dtype)

    zero_head = jnp.zeros((8, w), f32)
    conv_back = functools.partial(run_conv_backward, inner=inner, inv=inv, tail=tail, conv=conv, xproj=xproj)
    if quick:
        x, core = grp // 2, grp % 2
        order = jnp.stack([2 * (1 - x) + 1 - core, 2 * x + 1 - core, 2 * (1 - x) + core, 2 * x + core]).astype(jnp.int32)
        gate_sent, out_sent, gate_kept, out_kept = run_late_parts(order, normed, d_gate_proj, gated, cot)
        sent, kept = (gate_sent, out_sent), (gate_kept, out_kept)
        into = jnp.broadcast_to(resumed_by_other.astype(f32), (8, w))
        dxdbl, dxc, alog_grad, scan_sums, dtp_grad, late_grads, branch = run_backward(
            xdbl, xconv, d_yfull, dtp, vec, rate, starts, mix, into, sent, kept, branch_own, branch_oth
        )
        gate_grad, out_grad = late_grads[0], late_grads[1]
    else:
        branch = from_sequences(scatter_quad(branch_own, branch_oth).astype(bf16))
        out_grad = collect([scatter_grp(dot_tn(gated, cot[d]), 1) for d in range(2)])
        gate_grad = collect([scatter_grp(dot_tn(normed[d], d_gate_proj), 1) for d in range(2)])
        sums = (zero_state, jnp.zeros((8, w), f32), jnp.zeros((RANK, w), f32))
        scan = functools.partial(run_scan_backward, xdbl=xdbl, xconv=xconv, dy=d_yfull, dtp=dtp, vec=vec, rate=rate, starts=starts)
        dx_c, dxc, *sums, g_first = scan(PC, NCH - PC, carry=zero_state, sums=sums)
        g_into = jnp.where(resumes_own, g_first, 0.0) + jnp.where(resumed_by_other, across(g_first), 0.0)
        dx_p, dxc, *sums, _ = scan(0, PC, carry=g_into, sums=sums, kept=(dxc,))
        alog_grad, scan_sums, dtp_grad = sums
        dxdbl = jnp.concatenate([dx_p, dx_c], axis=1)
        for move in (swap, pair):
            dxdbl = dxdbl + move(dxdbl)
        dxdbl = jnp.swapaxes(dxdbl.reshape(XW, NCH, CH), 0, 1)

    output = (tokens.astype(f32) + branch.astype(f32)).astype(bf16)
    sums = (jnp.zeros((8, w), f32), jnp.zeros((XW, w), f32))
    dp, ds, *sums, head = conv_back(PC, NCH - PC, dxc=dxc, dxdbl=dxdbl, follow=zero_head, sums=sums)
    follow = jnp.where(resumes_own, head, 0.0) + jnp.where(resumed_by_other, across(head), 0.0)
    d_inner_proj, inner_scale, conv_sums, xproj_grad, _ = conv_back(0, PC, dxc=dxc, dxdbl=dxdbl, follow=follow, sums=sums, kept=(dp, ds))

    scale = gate_scale + inner_scale
    scale = scale + swap(scale)
    first, second = scale[:local], scale[local:]
    scale_own = jnp.where(low_pair, first, second) + pair(jnp.where(low_pair, second, first))
    inv_own = jnp.where(low_pair, inv[:local], inv[local:])
    pull = from_sequences(scale_own * inv_own * inv_own * inv_own / D)
    if quick:
        d_normed, inner_grad, gain_sum = run_finish(d_inner_proj, d_gate_proj, normed, raw, wi, wg)
        gain_grad = jnp.sum(gain_sum, axis=0)
    else:
        inner_grad = collect([scatter_grp(dot_tn(normed[d], d_inner_proj), 1) for d in range(2)])
        d_normed = from_sequences(scatter_quad(*run_normed_backward(d_inner_proj, d_gate_proj, wi, wg)))
        gain_grad = jnp.sum(d_normed * tokens.astype(f32), axis=0)
        gain_grad = lax.psum_scatter(lax.psum(gain_grad, "col"), "grp", scatter_dimension=0, tiled=True)
    input_grad = (cotangent.astype(f32) + d_normed * gain_own - pull * tokens.astype(f32)).astype(bf16)
    in_grads = jnp.stack([inner_grad, gate_grad], axis=1)
    small_grad = jnp.concatenate([conv_sums[0:5], scan_sums[0:2], alog_grad * rate, dtp_grad, xproj_grad], axis=0)
    small_grad = jnp.pad(small_grad, ((0, -small_grad.shape[0] % 8), (0, 0)))
    small_grad = send(small_grad, back(spread))
    small_grad = lax.psum_scatter(small_grad, ("row", "grp"), scatter_dimension=1, tiled=True)
    return (
        output,
        input_grad,
        gain_grad,
        in_grads,
        small_grad[0:4],
        small_grad[4],
        small_grad[7 + NSTATE + RANK : 7 + NSTATE + RANK + XW].T,
        small_grad[7 + NSTATE : 7 + NSTATE + RANK],
        small_grad[5],
        small_grad[7 : 7 + NSTATE],
        small_grad[6],
        out_grad,
    )


def solution(mesh):
    placed = (
        P(("grp", "col"), "row"),
        P(("row", "grp")),
        P("row", None, ("col", "grp")),
        P(None, ("col", "row", "grp")),
        P(("col", "row", "grp")),
        P(("col", "row", "grp"), None),
        P(None, ("col", "row", "grp")),
        P(("col", "row", "grp")),
        P(None, ("col", "row", "grp")),
        P(("col", "row", "grp")),
        P("col", ("row", "grp")),
        P("grp"),
        P(("grp", "col"), "row"),
    )
    return jax.shard_map(
        per_device,
        mesh=mesh,
        in_specs=placed,
        out_specs=(
            P(("grp", "col"), "row"),
            P(("grp", "col"), "row"),
            P(("row", "grp")),
            P("row", None, ("col", "grp")),
            P(None, ("col", "row", "grp")),
            P(("col", "row", "grp")),
            P(("col", "row", "grp"), None),
            P(None, ("col", "row", "grp")),
            P(("col", "row", "grp")),
            P(None, ("col", "row", "grp")),
            P(("col", "row", "grp")),
            P("col", ("row", "grp")),
        ),
        check_vma=False,
    )
```

```python
import functools

import jax
import jax.numpy as jnp
from jax import lax
from jax.experimental import pallas as pl
from jax.experimental.pallas import tpu as pltpu
from jax.sharding import PartitionSpec as P

D = 2048
NSTATE = 16
KCONV = 4
RANK = 128
NPROMPT = 2
LP = 1024
LC = 128
NCONT = 2

eps = 1e-05
CH = 128
SUB = 16
PC = LP // CH
SEQ = LP + LC
NCH = SEQ // CH
XW = RANK + 2 * NSTATE
SPAN = SUB * NSTATE
LOG2E = 1.4426950408889634
VMEM_LIMIT = 58 * 1024 * 1024

f32 = jnp.float32
bf16 = jnp.bfloat16


def dot_nn(a, b):
    return lax.dot_general(a, b, (((1,), (0,)), ((), ())), preferred_element_type=f32)


def dot_nt(a, b):
    return lax.dot_general(a, b, (((1,), (1,)), ((), ())), preferred_element_type=f32)


def dot_tn(a, b):
    return lax.dot_general(a, b, (((0,), (0,)), ((), ())), preferred_element_type=f32)


def expand_tile():
    lane = lax.broadcasted_iota(jnp.int32, (NSTATE, SPAN), 1)
    row = lax.broadcasted_iota(jnp.int32, (NSTATE, SPAN), 0)
    return jnp.where(lane % NSTATE == row, 1.0, 0.0)


def own_token(rows):
    lane = lax.broadcasted_iota(jnp.int32, (rows, SPAN), 1)
    row = lax.broadcasted_iota(jnp.int32, (rows, SPAN), 0)
    return lane // NSTATE == row % SUB


def conv_forward(inner_ref, inv_ref, tail_ref, conv_ref, xproj_ref, xconv_ref, xdbl_ref, buf):
    i = pl.program_id(0)

    @pl.when(i == 0)
    def _():
        buf[0:8] = jnp.zeros_like(buf[0:8])

    @pl.when(i == PC)
    def _():
        buf[0:8] = tail_ref[...]

    @pl.when((i > 0) & (i < PC))
    def _():
        buf[0:8] = buf[CH : CH + 8]

    buf[8 : CH + 8] = inv_ref[...] * inner_ref[...]
    out = conv_ref[4:5]
    for k in range(KCONV):
        out = out + conv_ref[k : k + 1] * buf[5 + k : 5 + k + CH]
    xconv = (out * jax.nn.sigmoid(out)).astype(bf16)
    xconv_ref[...] = xconv
    xdbl_ref[...] = dot_nt(xproj_ref[...], xconv)


def softplus(v):
    return jnp.maximum(v, 0.0) + jnp.log1p(jnp.exp(-jnp.abs(v)))


def by_sub(v):
    return v.reshape(CH // SUB, SUB, v.shape[-1])


def scan_chunk(xdbl_ref, xconv, dtp_ref, vec_ref, rate_ref, state, dt_s, u_s, cb_s, h_s, y_s):
    step = softplus(dot_tn(xdbl_ref[:RANK].astype(bf16), dtp_ref[...]) + vec_ref[0:1])
    dt_s[...] = by_sub(step)
    u_s[...] = by_sub(step * xconv)
    reads = dot_tn(xdbl_ref[RANK + NSTATE :].astype(bf16), expand_tile().astype(bf16))
    cb_s[...] = jnp.where(own_token(CH), reads, 0.0).astype(bf16)
    rate = rate_ref[...] * LOG2E

    def block(j, carried):
        h, maps = carried
        for t in range(SUB):
            a = jnp.exp2(dt_s[j, t : t + 1, :] * rate)
            h = a * h + u_s[j, t : t + 1, :] * maps[:, t : t + 1]
            h_s[t * NSTATE : (t + 1) * NSTATE, :] = h.astype(bf16)
        rows = pl.ds(pl.multiple_of(j * SUB, SUB), SUB)
        y_s[rows, :] = dot_nn(cb_s[rows, :], h_s[...])
        return (h, pltpu.roll(maps, CH - SUB, 1))

    h, _ = lax.fori_loop(0, CH // SUB, block, (state, xdbl_ref[RANK : RANK + NSTATE]))
    return h, y_s[...] + vec_ref[1:2] * xconv


def scan_scratch(w):
    return [
        pltpu.VMEM((CH // SUB, SUB, w), f32),
        pltpu.VMEM((CH // SUB, SUB, w), f32),
        pltpu.VMEM((CH, SPAN), bf16),
        pltpu.VMEM((SPAN, w), bf16),
        pltpu.VMEM((CH, w), f32),
    ]


def scan_forward(kept, xdbl_ref, xconv_ref, dtp_ref, vec_ref, rate_ref, start_ref, *refs):
    yfull_ref, starts_ref, final_ref, *scratch = refs[kept:]

    @pl.when(pl.program_id(0) == 0)
    def _():
        final_ref[...] = start_ref[...]

    starts_ref[0] = final_ref[...]
    h, yfull = scan_chunk(xdbl_ref, xconv_ref[...].astype(f32), dtp_ref, vec_ref, rate_ref, final_ref[...], *scratch)
    final_ref[...] = h
    yfull_ref[...] = yfull.astype(bf16)


def chunk_backward(xdbl_ref, xconv_ref, dy_ref, dtp_ref, vec_ref, rate_ref, starts_ref, dxdbl_ref, dxc_ref, alog_ref, sums_ref, dtpg_ref, first_ref,
                   dt_s, u_s, x_s, dy_s, a_s, h_s, g_s, w_s, b_s, m1_s, m2_s, ds_s, dx_s, sig_s):
    low = xdbl_ref[:RANK].astype(bf16)
    step_inner = dot_tn(low, dtp_ref[...]) + vec_ref[0:1]
    step = softplus(step_inner)
    sig_s[...] = jax.nn.sigmoid(step_inner)
    xconv = xconv_ref[...].astype(f32)
    dy = dy_ref[...]
    dt_s[...] = by_sub(step)
    u_s[...] = by_sub(step * xconv)
    x_s[...] = by_sub(xconv)
    dy_s[...] = by_sub(dy)
    tile = expand_tile().astype(bf16)
    b_s[...] = jnp.where(own_token(CH), dot_tn(xdbl_ref[RANK : RANK + NSTATE].astype(bf16), tile), 0.0).astype(bf16)
    rate = rate_ref[...]
    rate2 = rate * LOG2E
    h_s[0:NSTATE] = starts_ref[0]

    def ahead(j, carried):
        h, maps = carried
        for t in range(SUB):
            a = jnp.exp2(dt_s[j, t : t + 1, :] * rate2)
            h = a * h + u_s[j, t : t + 1, :] * maps[:, t : t + 1]
            a_s[j, t * NSTATE : (t + 1) * NSTATE, :] = a
            at = pl.multiple_of(j * SPAN + (t + 1) * NSTATE, NSTATE)
            h_s[pl.ds(at, NSTATE), :] = h
        return (h, pltpu.roll(maps, CH - SUB, 1))

    lax.fori_loop(0, CH // SUB, ahead, (starts_ref[0], xdbl_ref[RANK : RANK + NSTATE]))
    ones = jnp.where(own_token(SUB), 1.0, 0.0).astype(bf16)
    mine_sub = own_token(SUB)

    def back(jj, carried):
        g, alog, maps = carried
        j = CH // SUB - 1 - jj
        maps = pltpu.roll(maps, SUB, 1)
        for t in reversed(range(SUB)):
            dt = dt_s[j, t : t + 1, :]
            gs = maps[:, t : t + 1] * dy_s[j, t : t + 1, :] + g
            g = a_s[j, t * NSTATE : (t + 1) * NSTATE, :] * gs
            prior = h_s[pl.ds(pl.multiple_of(j * SPAN + t * NSTATE, NSTATE), NSTATE), :]
            w = g * prior
            alog = alog + w * dt
            g_s[t * NSTATE : (t + 1) * NSTATE, :] = gs.astype(bf16)
            w_s[t * NSTATE : (t + 1) * NSTATE, :] = (w * rate).astype(bf16)
        rows = pl.ds(pl.multiple_of(j * SUB, SUB), SUB)
        gs_all = g_s[...]
        through = dot_nn(b_s[rows, :], gs_all)
        ds_s[rows, :] = dot_nn(ones, w_s[...]) + x_s[j] * through
        dx_s[rows, :] = dt_s[j] * through + vec_ref[1:2] * dy_s[j]
        hs = h_s[pl.ds(pl.multiple_of(j * SPAN + NSTATE, NSTATE), SPAN), :].astype(bf16)
        m1_s[rows, :] = jnp.where(mine_sub, dot_nt(u_s[j].astype(bf16), gs_all), 0.0).astype(bf16)
        m2_s[rows, :] = jnp.where(mine_sub, dot_nt(dy_s[j].astype(bf16), hs), 0.0).astype(bf16)
        return (g, alog, maps)

    g, alog, _ = lax.fori_loop(0, CH // SUB, back, (first_ref[...], alog_ref[...], xdbl_ref[RANK + NSTATE :]))
    first_ref[...] = g
    alog_ref[...] = alog
    d_inner = ds_s[...] * sig_s[...]
    d_low = d_inner.astype(bf16)
    sums_ref[0:1] = sums_ref[0:1] + jnp.sum(d_inner, axis=0, keepdims=True)
    sums_ref[1:2] = sums_ref[1:2] + jnp.sum(dy * xconv, axis=0, keepdims=True)
    dtpg_ref[...] = dtpg_ref[...] + dot_nn(low, d_low)
    dxdbl_ref[:RANK] = dot_nt(dtp_ref[...], d_low)
    dxdbl_ref[RANK : RANK + NSTATE] = dot_nt(tile, m1_s[...])
    dxdbl_ref[RANK + NSTATE :] = dot_nt(tile, m2_s[...])
    dxc_ref[...] = dx_s[...]


def scan_backward(kept, *refs):
    given, sums0, out = refs[:7], refs[7:11], refs[11 + kept :]
    dxdbl_ref, dxc_ref, alog_ref, sums_ref, dtpg_ref, first_ref = out[:6]

    @pl.when(pl.program_id(0) == 0)
    def _():
        first_ref[...] = sums0[0][...]
        alog_ref[...] = sums0[1][...]
        sums_ref[...] = sums0[2][...]
        dtpg_ref[...] = sums0[3][...]

    chunk_backward(*given, dxdbl_ref, dxc_ref, alog_ref, sums_ref, dtpg_ref, first_ref, *out[6:])


def backward_scratch(w):
    sub = pltpu.VMEM((CH // SUB, SUB, w), f32)
    return [
        sub,
        sub,
        sub,
        sub,
        pltpu.VMEM((CH // SUB, SPAN, w), f32),
        pltpu.VMEM(((CH + 1) * NSTATE, w), f32),
        pltpu.VMEM((SPAN, w), bf16),
        pltpu.VMEM((SPAN, w), bf16),
        pltpu.VMEM((CH, SPAN), bf16),
        pltpu.VMEM((CH, SPAN), bf16),
        pltpu.VMEM((CH, SPAN), bf16),
        pltpu.VMEM((CH, w), f32),
        pltpu.VMEM((CH, w), f32),
        pltpu.VMEM((CH, w), f32),
    ]


def conv_backward(kept, chunks, first, inner_ref, halo_ref, inv_ref, halo_inv_ref, tail_ref, conv_ref, xproj_ref, dxc_ref, dxdbl_ref, follow_ref, sums0_ref, xprojg0_ref, *refs):
    dproj_ref, dscale_ref, sums_ref, xprojg_ref, head_ref, buf, dbuf = refs[kept:]
    i = pl.program_id(0)
    chunk = first + chunks - 1 - i

    @pl.when(i == 0)
    def _():
        sums_ref[...] = sums0_ref[...]
        xprojg_ref[...] = xprojg0_ref[...]
        head_ref[...] = follow_ref[...]

    projected = inner_ref[...]
    inv = inv_ref[...]
    before = halo_inv_ref[...] * halo_ref[...]
    before = jnp.where(chunk == 0, 0.0, jnp.where(chunk == PC, tail_ref[...], before))
    buf[0:8] = before
    buf[8 : CH + 8] = inv * projected
    out = conv_ref[4:5]
    for k in range(KCONV):
        out = out + conv_ref[k : k + 1] * buf[5 + k : 5 + k + CH]
    sig = jax.nn.sigmoid(out)
    xconv = (out * sig).astype(bf16)
    dxdbl = dxdbl_ref[...].astype(bf16)
    xprojg_ref[...] = xprojg_ref[...] + dot_nn(dxdbl, xconv)
    d_x = dxc_ref[...] + dot_tn(dxdbl, xproj_ref[...])
    d_conv = d_x * (sig * (1.0 + out * (1.0 - sig)))
    dbuf[CH : CH + 8] = head_ref[...]
    dbuf[0:CH] = d_conv
    d_inner = conv_ref[3:4] * d_conv
    for k in range(KCONV - 1):
        d_inner = d_inner + conv_ref[k : k + 1] * dbuf[3 - k : 3 - k + CH]
    for k in range(KCONV):
        sums_ref[k : k + 1] = sums_ref[k : k + 1] + jnp.sum(buf[5 + k : 5 + k + CH] * d_conv, axis=0, keepdims=True)
    sums_ref[4:5] = sums_ref[4:5] + jnp.sum(d_conv, axis=0, keepdims=True)
    dproj_ref[...] = (inv * d_inner).astype(bf16)
    dscale_ref[...] = jnp.sum(d_inner * projected, axis=1, keepdims=True)
    head_ref[...] = d_conv[0:8]


def call(body, chunks, args, in_specs, outs, out_specs, scratch, micros, aliases=None):
    return pl.pallas_call(
        body,
        grid=(chunks,),
        in_specs=in_specs,
        out_specs=out_specs,
        scratch_shapes=scratch,
        out_shape=outs,
        input_output_aliases=aliases or {},
        compiler_params=pltpu.CompilerParams(dimension_semantics=("arbitrary",), vmem_limit_bytes=VMEM_LIMIT),
        cost_estimate=pl.CostEstimate(flops=micros * 1000000000, bytes_accessed=1000000, transcendentals=0),
    )(*args)


def shaped(*shape, dtype=f32):
    return jax.ShapeDtypeStruct(shape, dtype)


def rows_of(width, place, tall=CH):
    return pl.BlockSpec((tall, width), lambda i: (place(i), 0))


def lanes_of(height, place):
    return pl.BlockSpec((height, CH), lambda i: (0, place(i)))


def whole(*shape):
    return pl.BlockSpec(shape, lambda i: (0,) * len(shape))


ANY = pl.BlockSpec(memory_space=pl.ANY)


def run_conv_forward(inner, inv, tail, conv, xproj):
    w = inner.shape[1]
    at = lambda i: i
    return call(
        conv_forward,
        NCH,
        (inner, inv, tail, conv, xproj),
        [rows_of(w, at), rows_of(1, at), whole(8, w), whole(8, w), whole(XW, w)],
        (shaped(SEQ, w, dtype=bf16), shaped(XW, SEQ)),
        (rows_of(w, at), lanes_of(XW, at)),
        [pltpu.VMEM((CH + 8, w), f32)],
        12,
    )


def chunk_of(height, place):
    return pl.BlockSpec((None, height, CH), lambda i: (place(i), 0, 0))


def run_scan_forward(first, chunks, xdbl, xconv, dtp, vec, rate, start, kept=()):
    w = xconv.shape[1]
    at = lambda i: first + i
    return call(
        functools.partial(scan_forward, len(kept)),
        chunks,
        (xdbl, xconv, dtp, vec, rate, start, *kept),
        [chunk_of(XW, at), rows_of(w, at), whole(RANK, w), whole(8, w), whole(NSTATE, w), whole(NSTATE, w)] + [ANY] * len(kept),
        (shaped(SEQ, w, dtype=bf16), shaped(NCH, NSTATE, w), shaped(NSTATE, w)),
        (rows_of(w, at), pl.BlockSpec((1, NSTATE, w), lambda i: (first + i, 0, 0)), whole(NSTATE, w)),
        scan_scratch(w),
        5 * chunks,
        {6 + k: k for k in range(len(kept))},
    )


def run_scan_backward(first, chunks, xdbl, xconv, dy, dtp, vec, rate, starts, carry, sums, kept=()):
    w = xconv.shape[1]
    at = lambda i: first + chunks - 1 - i
    local = lambda i: chunks - 1 - i
    return call(
        functools.partial(scan_backward, len(kept)),
        chunks,
        (xdbl, xconv, dy, dtp, vec, rate, starts, carry, *sums, *kept),
        [
            chunk_of(XW, at),
            rows_of(w, at),
            rows_of(w, at),
            whole(RANK, w),
            whole(8, w),
            whole(NSTATE, w),
            pl.BlockSpec((1, NSTATE, w), lambda i: (at(i), 0, 0)),
            whole(NSTATE, w),
            whole(NSTATE, w),
            whole(8, w),
            whole(RANK, w),
        ]
        + [ANY] * len(kept),
        (shaped(XW, chunks * CH), shaped(SEQ, w), shaped(NSTATE, w), shaped(8, w), shaped(RANK, w), shaped(NSTATE, w)),
        (lanes_of(XW, local), rows_of(w, at), whole(NSTATE, w), whole(8, w), whole(RANK, w), whole(NSTATE, w)),
        backward_scratch(w),
        11 * chunks,
        {11 + k: 1 + k for k in range(len(kept))},
    )


def run_conv_backward(first, chunks, inner, inv, tail, conv, xproj, dxc, dxdbl, follow, sums, kept=()):
    w = inner.shape[1]
    at = lambda i: first + chunks - 1 - i
    before = lambda i: (jnp.maximum(at(i) * (CH // 8) - 1, 0), 0)
    return call(
        functools.partial(conv_backward, len(kept), chunks, first),
        chunks,
        (inner, inner, inv, inv, tail, conv, xproj, dxc, dxdbl, follow, *sums, *kept),
        [
            rows_of(w, at),
            pl.BlockSpec((8, w), before),
            rows_of(1, at),
            pl.BlockSpec((8, 1), before),
            whole(8, w),
            whole(8, w),
            whole(XW, w),
            rows_of(w, at),
            chunk_of(XW, at),
            whole(8, w),
            whole(8, w),
            whole(XW, w),
        ]
        + [ANY] * len(kept),
        (shaped(SEQ, w, dtype=bf16), shaped(SEQ, 1), shaped(8, w), shaped(XW, w), shaped(8, w)),
        (rows_of(w, at), rows_of(1, at), whole(8, w), whole(XW, w), whole(8, w)),
        [pltpu.VMEM((CH + 8, w), f32), pltpu.VMEM((CH + 8, w), f32)],
        2 * chunks,
        {12 + k: k for k in range(len(kept))},
    )


MESH = pl.DeviceIdType.MESH
BIG = 384
BIG_STEPS = SEQ // BIG
SLOTS = 4


def remote(src, dst, send, recv, device):
    return pltpu.make_async_remote_copy(src_ref=src, dst_ref=dst, send_sem=send, recv_sem=recv, device_id=device, device_id_type=MESH)


def xor_bit(a, b):
    return a + b - 2 * a * b


def token_pieces(c, local):
    cut = local - LC
    low = cut - LC
    if c == 0:
        return [(0, local, 0, 0)]
    if c == 1:
        return [(0, cut, 0, local), (cut, local, 1, 0)]
    if c == 2:
        return [(0, local, 1, LC)]
    return [(0, low, 1, LC + local), (low, cut, 0, LP), (cut, local, 1, LP)]


class Gather:
    def __init__(self, weights, tokens, raw, w_send, w_recv, t_send, t_recv, here):
        g, r, c = lax.axis_index("grp"), lax.axis_index("row"), lax.axis_index("col")
        x, core = g // 2, g % 2
        self.g, self.r, self.c = g, r, c
        half = xor_bit(r, c % 2)
        self.firsts = ((g, r, 2 * half + c // 2), (g, 1 - r, 2 * (1 - half) + c // 2))
        self.alone = 2 * half + c // 2 == c
        self.ranks = (g, (1 - x) * 2 + core, x * 2 + 1 - core)
        self.x_dev, self.core_dev = (self.ranks[1], r, c), (self.ranks[2], r, c)
        self.y_dev, self.z_dev = (g, 1 - r, c), (g, r, c + 1 - 2 * (c % 2))
        self.weights, self.tokens, self.raw = weights, tokens, raw
        self.w_send, self.w_recv, self.t_send, self.t_recv, self.here = w_send, w_recv, t_send, t_recv, here

    def greet(self):
        barrier = pltpu.get_barrier_semaphore()
        for dr in range(2):
            for dc in range(4):
                if dr or dc:
                    device = (self.g, (self.r + dr) % 2, (self.c + dc) % 4)
                    pl.semaphore_signal(barrier, inc=1, device_id=device, device_id_type=MESH)
        for device in (self.x_dev, self.core_dev):
            pl.semaphore_signal(barrier, inc=1, device_id=device, device_id_type=MESH)
        pl.semaphore_wait(barrier, 9)

    def slot(self, n, k, d):
        if self.weights[n][2]:
            return (self.r if d == 0 else 1 - self.r) * 4 + self.ranks[k]
        return 2 * self.ranks[k] + d

    def first_hop(self, n, d):
        src, dst, by_row = self.weights[n]
        at = self.slot(n, 0, 0) if by_row else self.slot(n, 0, d)
        return remote(src, dst.at[at], self.w_send.at[n, d], self.w_recv.at[n, d], self.firsts[d])

    def at_home(self, n):
        src, dst, _ = self.weights[n]
        return pltpu.make_async_copy(src, dst.at[self.slot(n, 0, 0)], self.here.at[n])

    def hop(self, n, d, k, came):
        dst = self.weights[n][1]
        at = self.slot(n, k, d)
        i = (0, 2, 4, 6)[came] + d
        device = self.x_dev if came == 1 else self.core_dev
        return remote(dst.at[at], dst.at[at], self.w_send.at[n, i], self.w_recv.at[n, i], device)

    def begin(self, n):
        @pl.when(self.alone)
        def _():
            self.at_home(n).start()

        @pl.when(jnp.logical_not(self.alone))
        def _():
            self.first_hop(n, 0).start()

        self.first_hop(n, 1).start()

    def forward(self, n):
        for d in range(2):
            if d == 0:

                @pl.when(self.alone)
                def _():
                    self.at_home(n).wait()

                @pl.when(jnp.logical_not(self.alone))
                def _():
                    self.first_hop(n, 0).wait_recv()
            else:
                self.first_hop(n, 1).wait_recv()
            self.hop(n, d, 0, 1).start()
            self.hop(n, d, 0, 2).start()

    def forward_again(self, n):
        for d in range(2):
            self.hop(n, d, 0, 1).wait_recv()
            self.hop(n, d, 1, 3).start()

    def end(self, n):
        for d in range(2):
            self.hop(n, d, 0, 2).wait_recv()
            self.hop(n, d, 1, 3).wait_recv()
            self.hop(n, d, 0, 1).wait_send()
            self.hop(n, d, 0, 2).wait_send()
            self.hop(n, d, 1, 3).wait_send()

        @pl.when(jnp.logical_not(self.alone))
        def _():
            self.first_hop(n, 0).wait_send()

        self.first_hop(n, 1).wait_send()

    def ranges(self, k):
        local = self.tokens.shape[0]
        held = {0: (0, local), 1: (local, LP), 2: (LC, LC + local), 3: (LC + local, SEQ)}
        return held[k], held[k ^ 1], (LP, SEQ) if k < 2 else (0, LC)

    def part(self, d, rows):
        return self.raw.at[d, pl.ds(rows[0], rows[1] - rows[0])]

    def on_col(self, act):
        for k in range(4):

            @pl.when(self.c == k)
            def _(k=k):
                act(k)

    def sources(self, k, lo, hi):
        for a, b, s, at in token_pieces(k, self.tokens.shape[0]):
            first, end = max(lo, at), min(hi, at + b - a)
            if s == k // 2 and first < end:
                yield a + first - at, first, end

    def begin_half(self, h):
        def act(k):
            lo, hi = split(self.ranges(k)[0])[h]
            for src, first, end in self.sources(k, lo, hi):
                rows = self.tokens.at[pl.ds(src, end - first)]
                pltpu.make_async_copy(rows, self.part(0, (first, end)), self.here.at[2 + h]).start()
                remote(rows, self.part(1, (first, end)), self.t_send.at[h], self.t_recv.at[h], self.y_dev).start()
                remote(rows, self.part(0, (first, end)), self.t_send.at[2 + h], self.t_recv.at[2 + h], self.z_dev).start()

        self.on_col(act)

    def foreign_copies(self, k):
        copies = []
        for a, b, s, at in token_pieces(k, self.tokens.shape[0]):
            if s != k // 2:
                for dr in range(2):
                    for dc in range(2):
                        device = (self.g, self.r if dr == 0 else 1 - self.r, 2 * s + dc)
                        sems = self.t_send.at[6 + 2 * dr + dc], self.t_recv.at[6 + dr]
                        copies.append(remote(self.tokens.at[pl.ds(a, b - a)], self.part(dr, (at, at + b - a)), *sems, device))
        return copies

    def begin_foreign(self):
        def act(k):
            for copy in self.foreign_copies(k):
                copy.start()

        self.on_col(act)

    def relays(self, k):
        own, paired, _ = self.ranges(k)
        early, late = split(paired)[0], split(own)[1]
        return (
            remote(self.part(0, early), self.part(1, early), self.t_send.at[4], self.t_recv.at[4], self.y_dev),
            remote(self.part(1, late), self.part(1, late), self.t_send.at[5], self.t_recv.at[5], self.z_dev),
        )

    def settle(self, d, rows, sem):
        pltpu.make_async_copy(self.part(d, rows), self.part(d, rows), sem).wait()

    def relay(self):
        def act(k):
            own, paired, _ = self.ranges(k)
            by_y, by_z = self.relays(k)
            self.settle(0, split(paired)[0], self.t_recv.at[2])
            by_y.start()
            self.settle(1, split(own)[1], self.t_recv.at[1])
            by_z.start()

        self.on_col(act)

    def end_tokens(self):
        def act(k):
            own, paired, foreign = self.ranges(k)
            own, paired = split(own), split(paired)
            by_y, by_z = self.relays(k)
            self.settle(1, own[0], self.t_recv.at[0])
            self.settle(0, paired[1], self.t_recv.at[3])
            self.settle(1, paired[0], self.t_recv.at[4])
            self.settle(1, paired[1], self.t_recv.at[5])
            self.settle(0, foreign, self.t_recv.at[6])
            self.settle(1, foreign, self.t_recv.at[7])
            for h in range(2):
                self.settle(0, own[h], self.here.at[2 + h])
                self.settle(0, own[h], self.t_send.at[h])
                self.settle(0, own[h], self.t_send.at[2 + h])
            by_y.wait_send()
            by_z.wait_send()
            for copy in self.foreign_copies(k):
                copy.wait_send()

        self.on_col(act)


def split(rows):
    lo, hi = rows
    mid = lo + (hi - lo) // 2
    return (lo, mid), (mid, hi)


def gather_semaphores():
    return [pltpu.SemaphoreType.DMA(shape) for shape in ((2, 8), (2, 8), (10,), (8,), (4,))]


def gather_start(tokens, in_i, small, raw, wi, small_all, *sems):
    gather = Gather([(small, small_all, True), (in_i, wi, False)], tokens, raw, *sems)
    gather.greet()
    gather.begin(0)
    gather.begin(1)
    gather.begin_half(0)
    gather.begin_half(1)
    gather.begin_foreign()
    for n in range(2):
        gather.forward(n)
    gather.relay()
    for n in range(2):
        gather.forward_again(n)
    gather.end_tokens()
    for n in range(2):
        gather.end(n)


def run_gather_start(tokens, in_i, small):
    width = tokens.shape[1]
    return pl.pallas_call(
        gather_start,
        in_specs=[ANY] * 3,
        out_specs=[ANY] * 3,
        out_shape=(
            shaped(2, SEQ, width, dtype=bf16),
            shaped(8, *in_i.shape, dtype=bf16),
            shaped(8, *small.shape, dtype=bf16),
        ),
        scratch_shapes=gather_semaphores(),
        compiler_params=pltpu.CompilerParams(collective_id=0, has_side_effects=True, vmem_limit_bytes=VMEM_LIMIT),
    )(tokens, in_i, small)


LAG = 4
FIRST = BIG_STEPS
SECOND = FIRST + NCH
LAST = SECOND + NCH - 1
BEGIN = (0, SECOND)
FORWARD = (FIRST + 8, SECOND + 5)
FORWARD_AGAIN = (SECOND + 3, LAST)
HALVES = (FIRST + 6, SECOND + 1)
FOREIGN = SECOND + 2
RELAY = SECOND + 6


def pack_sum(ref, k, v):
    high = v[RANK:].astype(bf16)
    ref[k, :RANK] = v[:RANK].astype(bf16)
    ref[k, RANK:XW] = high
    ref[k, XW:] = (v[RANK:] - high.astype(f32)).astype(bf16)


def unpack_sum(ref, k):
    return jnp.concatenate([ref[k, :RANK].astype(f32), ref[k, RANK:XW].astype(f32) + ref[k, XW:].astype(f32)], axis=0)


def forward(raw_ref, gain_ref, wi_ref, mix_ref, conv_ref, xproj_ref, dtp_ref, vec_ref, rate_ref, in_g, out_w, cot_in,
            normed_ref, inv_ref, inner_ref, xconv_ref, yfull_ref, starts_ref, xdbl_ref, joined_ref, wg, wo, cot,
            inner_s, inv_s, buf, xc_s, part, ys, yr, zs, zr, tail_s, tail_r, state, last, last_r,
            dt_s, u_s, cb_s, h_s, y_s, y_send, y_recv, z_send, z_recv, e_send, e_recv, *sems):
    i = pl.program_id(0)
    gather = Gather([(in_g, wg, False), (out_w, wo, False)], cot_in, cot, *sems)
    g, r, c = gather.g, gather.r, gather.c
    y_dev, z_dev = gather.y_dev, gather.z_dev
    far_dev = (g, 1 - r, (c + 2) % 4)
    to_tail = remote(tail_s, tail_r, e_send.at[0], e_recv.at[0], far_dev)
    to_last = remote(last, last_r, e_send.at[1], e_recv.at[1], far_dev)

    def to_y(k):
        return remote(ys.at[k], yr.at[k], y_send.at[k], y_recv.at[k], y_dev)

    def to_z(k):
        return remote(zs.at[k], zr.at[k], z_send.at[k], z_recv.at[k], z_dev)

    @pl.when(i == 0)
    def _():
        gather.greet()

    @pl.when(i < FIRST)
    def _():
        rows = pl.ds(pl.multiple_of(i * BIG, BIG), BIG)
        project_first(raw_ref, gain_ref, wi_ref, normed_ref, inv_ref, inner_ref)
        inner_s[rows, :] = inner_ref[...]
        inv_s[rows, :] = inv_ref[...]

    @pl.when(i == FIRST)
    def _():
        tail_s[...] = inv_s[LP - 8 : LP] * inner_s[LP - 8 : LP]
        to_tail.start()
        buf[0:8] = jnp.zeros_like(buf[0:8])
        state[...] = jnp.zeros_like(state)

    mix = mix_ref[...]

    @pl.when(i == FIRST + PC)
    def _():
        to_tail.wait()
        joined = mix * tail_s[...] + (1.0 - mix) * tail_r[...]
        buf[0:8] = joined
        joined_ref[...] = joined

    @pl.when((i > FIRST) & (i < FIRST + PC))
    def _():
        buf[0:8] = buf[CH : CH + 8]

    @pl.when((i >= FIRST) & (i < SECOND))
    def _():
        k = i - FIRST
        rows = pl.ds(pl.multiple_of(k * CH, CH), CH)
        buf[8 : CH + 8] = inv_s[rows, :] * inner_s[rows, :]
        out = conv_ref[4:5]
        for tap in range(KCONV):
            out = out + conv_ref[tap : tap + 1] * buf[5 + tap : 5 + tap + CH]
        xconv = (out * jax.nn.sigmoid(out)).astype(bf16)
        xconv_ref[...] = xconv
        xc_s[k] = xconv
        part[k] = dot_nt(xproj_ref[...], xconv)
        pack_sum(ys, k, part[k])
        to_y(k).start()

    @pl.when((i >= FIRST + LAG) & (i < SECOND + LAG))
    def _():
        k = i - FIRST - LAG
        to_y(k).wait_recv()
        part[k] = part[k] + unpack_sum(yr, k)
        pack_sum(zs, k, part[k])
        to_z(k).start()

    @pl.when((i >= FIRST + 2 * LAG) & (i < SECOND + 2 * LAG))
    def _():
        k = i - FIRST - 2 * LAG
        to_z(k).wait_recv()
        xdbl_ref[k] = part[k] + unpack_sum(zr, k)

    for n in range(2):

        @pl.when(i == BEGIN[n])
        def _(n=n):
            gather.begin(n)

        @pl.when(i == FORWARD[n])
        def _(n=n):
            gather.forward(n)

        @pl.when(i == FORWARD_AGAIN[n])
        def _(n=n):
            gather.forward_again(n)

    for h in range(2):

        @pl.when(i == HALVES[h])
        def _(h=h):
            gather.begin_half(h)

    @pl.when(i == FOREIGN)
    def _():
        gather.begin_foreign()

    @pl.when(i == RELAY)
    def _():
        gather.relay()

    @pl.when(i == LAST)
    def _():
        to_last.wait()
        state[...] = mix_ref[0:1] * last[...] + (1.0 - mix_ref[0:1]) * last_r[...]

    @pl.when(i >= SECOND)
    def _():
        k = i - SECOND
        starts_ref[0] = state[...]
        h, yfull = scan_chunk(xdbl_ref.at[k], xc_s[k].astype(f32), dtp_ref, vec_ref, rate_ref, state[...], dt_s, u_s, cb_s, h_s, y_s)
        state[...] = h
        yfull_ref[...] = yfull.astype(bf16)

    @pl.when(i == LAST - 1)
    def _():
        last[...] = state[...]
        to_last.start()

    @pl.when(i == LAST)
    def _():
        gather.end_tokens()
        gather.end(0)
        gather.end(1)

        def sent(k, _):
            to_y(k).wait_send()
            to_z(k).wait_send()
            return 0

        lax.fori_loop(0, NCH, sent, 0)


def run_forward(raw, gain, wi, mix, conv, xproj, dtp, vec, rate, in_g, out_w, cot):
    w = SLOTS * wi.shape[2]
    width = raw.shape[2]
    zero = lambda i: jnp.minimum(i, FIRST - 1)
    first = lambda i: jnp.clip(i - FIRST, 0, NCH - 1)
    second = lambda i: jnp.maximum(i - SECOND, 0)
    dma = pltpu.SemaphoreType.DMA
    sums = pltpu.VMEM((NCH, XW + 2 * NSTATE, CH), bf16)
    return pl.pallas_call(
        forward,
        grid=(LAST + 1,),
        in_specs=[
            split_rows(width, zero, BIG),
            whole(2, width),
            whole(*wi.shape),
            whole(8, w),
            whole(8, w),
            whole(XW, w),
            whole(RANK, w),
            whole(8, w),
            whole(NSTATE, w),
            ANY,
            ANY,
            ANY,
        ],
        out_specs=(
            split_rows(width, zero, BIG),
            rows_of(1, zero, BIG),
            rows_of(w, zero, BIG),
            rows_of(w, first),
            rows_of(w, second),
            pl.BlockSpec((1, NSTATE, w), lambda i: (second(i), 0, 0)),
            whole(NCH, XW, CH),
            whole(8, w),
            ANY,
            ANY,
            ANY,
        ),
        out_shape=(
            shaped(2, SEQ, width, dtype=bf16),
            shaped(SEQ, 1),
            shaped(SEQ, w),
            shaped(SEQ, w, dtype=bf16),
            shaped(SEQ, w, dtype=bf16),
            shaped(NCH, NSTATE, w),
            shaped(NCH, XW, CH),
            shaped(8, w),
            shaped(8, *in_g.shape, dtype=bf16),
            shaped(8, *out_w.shape, dtype=bf16),
            shaped(2, SEQ, cot.shape[1], dtype=bf16),
        ),
        scratch_shapes=[
            pltpu.VMEM((SEQ, w), f32),
            pltpu.VMEM((SEQ, 1), f32),
            pltpu.VMEM((CH + 8, w), f32),
            pltpu.VMEM((NCH, CH, w), bf16),
            pltpu.VMEM((NCH, XW, CH), f32),
            sums,
            sums,
            sums,
            sums,
            pltpu.VMEM((8, w), f32),
            pltpu.VMEM((8, w), f32),
            pltpu.VMEM((NSTATE, w), f32),
            pltpu.VMEM((NSTATE, w), f32),
            pltpu.VMEM((NSTATE, w), f32),
            *scan_scratch(w),
            dma((NCH,)),
            dma((NCH,)),
            dma((NCH,)),
            dma((NCH,)),
            dma((2,)),
            dma((2,)),
            *gather_semaphores(),
        ],
        compiler_params=pltpu.CompilerParams(
            dimension_semantics=("arbitrary",), collective_id=2, has_side_effects=True, vmem_limit_bytes=VMEM_LIMIT
        ),
        cost_estimate=pl.CostEstimate(flops=60 * 1000000000, bytes_accessed=1000000, transcendentals=0),
    )(raw, gain, wi, mix, conv, xproj, dtp, vec, rate, in_g, out_w, cot)


def project_first(raw_ref, gain_ref, w_ref, normed_ref, inv_ref, out_ref):
    low = raw_ref[0].astype(f32)
    high = raw_ref[1].astype(f32)
    squares = jnp.sum(low * low + high * high, axis=1, keepdims=True)
    inv_ref[...] = lax.rsqrt(squares / D + eps)
    low = (low * gain_ref[0:1]).astype(bf16)
    high = (high * gain_ref[1:2]).astype(bf16)
    normed_ref[0] = low
    normed_ref[1] = high
    n = w_ref.shape[2]
    for k in range(SLOTS):
        out_ref[:, k * n : (k + 1) * n] = dot_nn(low, w_ref[2 * k]) + dot_nn(high, w_ref[2 * k + 1])


def split_rows(width, at, tall=CH):
    return pl.BlockSpec((2, tall, width), lambda i: (0, at(i), 0))


def run_project_first(raw, gain, w):
    width = raw.shape[2]
    at = lambda i: i
    n = SLOTS * w.shape[2]
    return call(
        project_first,
        BIG_STEPS,
        (raw, gain, w),
        [split_rows(width, at, BIG), whole(2, width), whole(*w.shape)],
        (shaped(2, SEQ, width, dtype=bf16), shaped(SEQ, 1), shaped(SEQ, n)),
        (split_rows(width, at, BIG), rows_of(1, at, BIG), rows_of(n, at, BIG)),
        [],
        9,
    )


def gate_backward(normed_ref, wg_ref, cot_ref, wo_ref, yfull_ref, inv_ref, gated_ref, dy_ref, dproj_ref, dscale_ref, own_ref, oth_ref, gate_s):
    n = wo_ref.shape[2]
    for k in range(SLOTS):
        gate_s[:, k * n : (k + 1) * n] = dot_nn(normed_ref[0], wg_ref[2 * k]) + dot_nn(normed_ref[1], wg_ref[2 * k + 1])
    d_gated = jnp.zeros(dy_ref.shape, f32)
    for k in range(SLOTS):
        for d in range(2):
            d_gated = d_gated + dot_nt(cot_ref[d, :, k * n : (k + 1) * n], wo_ref[2 * k + d])
    gate_in = gate_s[...]
    inv = inv_ref[...]
    yfull = yfull_ref[...].astype(f32)
    gate = inv * gate_in
    sig = jax.nn.sigmoid(gate)
    passed = gate * sig
    gated = (yfull * passed).astype(bf16)
    gated_ref[...] = gated
    for k in range(SLOTS):
        own_ref[:, k * n : (k + 1) * n] = dot_nn(gated, wo_ref[2 * k])
        oth_ref[:, k * n : (k + 1) * n] = dot_nn(gated, wo_ref[2 * k + 1]).astype(bf16)
    dy_ref[...] = d_gated * passed
    d_gate = d_gated * yfull * (sig * (1.0 + gate * (1.0 - sig)))
    dproj_ref[...] = (inv * d_gate).astype(bf16)
    dscale_ref[...] = jnp.sum(d_gate * gate_in, axis=1, keepdims=True)


def run_gate_backward(normed, wg, cot, wo, yfull, inv):
    width = cot.shape[2]
    w = yfull.shape[1]
    at = lambda i: i
    return call(
        gate_backward,
        BIG_STEPS,
        (normed, wg, cot, wo, yfull, inv),
        [split_rows(width, at, BIG), whole(*wg.shape), split_rows(width, at, BIG), whole(*wo.shape), rows_of(w, at, BIG), rows_of(1, at, BIG)],
        (shaped(SEQ, w, dtype=bf16), shaped(SEQ, w), shaped(SEQ, w, dtype=bf16), shaped(SEQ, 1), shaped(SEQ, width), shaped(SEQ, width, dtype=bf16)),
        (rows_of(w, at, BIG), rows_of(w, at, BIG), rows_of(w, at, BIG), rows_of(1, at, BIG), rows_of(width, at, BIG), rows_of(width, at, BIG)),
        [pltpu.VMEM((BIG, w), f32)],
        22,
    )


def normed_backward(inner_ref, gate_ref, wi_ref, wg_ref, own_ref, oth_ref):
    n = wi_ref.shape[2]
    for d, out_ref in ((1, oth_ref), (0, own_ref)):
        total = jnp.zeros(out_ref.shape, f32)
        for k in range(SLOTS):
            total = total + dot_nt(inner_ref[:, k * n : (k + 1) * n], wi_ref[2 * k + d])
            total = total + dot_nt(gate_ref[:, k * n : (k + 1) * n], wg_ref[2 * k + d])
        out_ref[...] = total.astype(out_ref.dtype)


def run_normed_backward(d_inner, d_gate, wi, wg):
    w = d_inner.shape[1]
    width = wi.shape[1]
    at = lambda i: i
    return call(
        normed_backward,
        BIG_STEPS,
        (d_inner, d_gate, wi, wg),
        [rows_of(w, at, BIG), rows_of(w, at, BIG), whole(*wi.shape), whole(*wg.shape)],
        (shaped(SEQ, width), shaped(SEQ, width, dtype=bf16)),
        (rows_of(width, at, BIG), rows_of(width, at, BIG)),
        [],
        12,
    )


def finish(inner_hbm, gate_hbm, normed_hbm, raw_hbm, wi_hbm, wg_hbm, dn_ref, grad_ref, gain_ref,
           inner, gate, normed, raw, wi, wg, cs, cr, pairs, xs, xr, fs, fr, ys, yr, zs, zr, own, fin, gs, gr,
           loc, c_send, c_recv, x_send, x_recv, f_send, f_recv, y_send, y_recv, z_send, z_recv, b_send, b_recv, g_send, g_recv):
    g, r, c = lax.axis_index("grp"), lax.axis_index("row"), lax.axis_index("col")
    x, core, s, p = g // 2, g % 2, c // 2, c % 2
    tall, width = raw.shape
    part = tall // 2
    n = wi_hbm.shape[2]
    q = 2 * p + xor_bit(r, s)
    y_dev, z_dev = (g, 1 - r, c), (g, r, 2 * s + 1 - p)
    x_dev, core_dev = ((1 - x) * 2 + core, r, c), (2 * x + 1 - core, r, c)
    alone = q == c

    loads = [
        pltpu.make_async_copy(normed_hbm, normed, loc.at[0]),
        pltpu.make_async_copy(inner_hbm, inner, loc.at[1]),
        pltpu.make_async_copy(gate_hbm, gate, loc.at[2]),
        pltpu.make_async_copy(raw_hbm.at[0, pl.ds(pl.multiple_of(p * tall, 64), tall)], raw, loc.at[5]),
    ]
    for copy in loads[:3]:
        copy.start()
    for k in range(SLOTS):
        for d in range(2):
            cols = pl.ds(k * n, n)
            pltpu.make_async_copy(wi_hbm.at[2 * k + d], wi.at[d, :, cols], loc.at[3]).start()
            pltpu.make_async_copy(wg_hbm.at[2 * k + d], wg.at[d, :, cols], loc.at[4]).start()
    loads[3].start()

    barrier = pltpu.get_barrier_semaphore()
    for dg in range(4):
        for dc in range(4):
            if dg or dc:
                pl.semaphore_signal(barrier, inc=1, device_id=((g + dg) % 4, r, (c + dc) % 4), device_id_type=MESH)
    for dc in range(4):
        pl.semaphore_signal(barrier, inc=1, device_id=(g, 1 - r, (c + dc) % 4), device_id_type=MESH)
    pl.semaphore_wait(barrier, 19)

    def weight_grad(at_x, d):
        cols = pl.ds(pl.multiple_of(at_x * 2 * n, 128), 2 * n)

        def tile(t, _):
            rows = pl.ds(pl.multiple_of(t * n, 128), n)
            pairs[d, rows, :] = dot_tn(normed[d, :, rows], inner[:, cols])
            return 0

        lax.fori_loop(0, width // n, tile, 0)

    def of_core(at_core):
        return pl.ds(pl.multiple_of(at_core * n, 128), n)

    def to_core(i, d):
        return remote(cs.at[i, d], cr.at[i, d], c_send.at[2 * i + d], c_recv.at[2 * i + d], core_dev)

    def to_x(d):
        return remote(xs.at[d], xr.at[d], x_send.at[d], x_recv.at[d], x_dev)

    def to_owner(d):
        return remote(fs.at[d], fr.at[d], f_send.at[d], f_recv.at[d], (g, r if d == 0 else 1 - r, q))

    def grad_to_core(i):
        for d in range(2):
            weight_grad(1 - x if i == 0 else x, d)
            cs[i, d] = pairs[d, :, of_core(1 - core)].astype(bf16)
            to_core(i, d).start()

    def start_of(mine, h):
        return pl.multiple_of((p if mine else 1 - p) * tall + h * part, 32)

    def normed_part(mine, h, d, store):
        rows = pl.ds(start_of(mine, h), part)

        def tile(t, _):
            cols = pl.ds(pl.multiple_of(t * n, 128), n)
            total = dot_nt(inner[rows, :], wi[d, cols, :]) + dot_nt(gate[rows, :], wg[d, cols, :])
            store(cols, total)
            return 0

        lax.fori_loop(0, width // n, tile, 0)

    def to_y(i):
        return remote(ys.at[i], yr.at[i], y_send.at[i], y_recv.at[i], y_dev)

    def to_z(i):
        return remote(zs.at[i], zr.at[i], z_send.at[i], z_recv.at[i], z_dev)

    def into(ref, i, added=None):
        def store(cols, v):
            if added is not None:
                v = v + added[0, :, cols].astype(f32)
            ref[i, :, cols] = v.astype(bf16)

        return store

    loads[0].wait()
    loads[1].wait()
    grad_to_core(0)
    loads[2].wait()
    pltpu.make_async_copy(wi, wi, loc.at[3]).wait()
    pltpu.make_async_copy(wg, wg, loc.at[4]).wait()
    for d in range(2):
        to_core(0, d).wait_recv()
        xs[d] = (pairs[d, :, of_core(core)] + cr[0, d].astype(f32)).astype(bf16)
        to_x(d).start()

    normed_part(False, 0, 1, into(ys, 0))
    to_y(0).start()
    normed_part(False, 1, 1, into(zs, 0))
    to_z(0).start()
    normed_part(False, 1, 0, into(zs, 2))
    to_z(2).start()
    normed_part(True, 0, 1, into(ys, 1))
    to_y(1).start()
    grad_to_core(1)
    to_y(0).wait_recv()
    normed_part(False, 0, 0, into(zs, 1, yr))
    to_z(1).start()
    to_z(0).wait_recv()
    normed_part(True, 1, 1, into(ys, 2, zr))
    to_y(2).start()

    for d in range(2):
        to_core(1, d).wait_recv()
        to_x(d).wait_recv()
        fs[d] = (pairs[d, :, of_core(core)] + cr[1, d].astype(f32) + xr[d].astype(f32)).astype(bf16)
        if d == 0:

            @pl.when(alone)
            def _():
                fr[0] = fs[0]

            @pl.when(jnp.logical_not(alone))
            def _():
                to_owner(0).start()
        else:
            to_owner(1).start()

    for h in range(2):

        def store(cols, v, h=h):
            own[h * part : (h + 1) * part, cols] = v

        normed_part(True, h, 0, store)

    loads[3].wait()
    for h in range(2):
        to_y(1 + h).wait_recv()
        to_z(1 + h).wait_recv()
        total = own[h * part : (h + 1) * part, :] + yr[1 + h].astype(f32) + zr[1 + h].astype(f32)
        fin[h * part : (h + 1) * part, :] = total.astype(bf16)
        product = total * raw[h * part : (h + 1) * part, :].astype(f32)
        folded = jnp.sum(product.reshape(part // 8, 8, width), axis=0)
        for b in range(SLOTS):
            if h == 0:
                gs[b] = folded[:, b * n : (b + 1) * n]
            else:
                gs[b] = gs[b] + folded[:, b * n : (b + 1) * n]

    cut = tall - LC
    low = cut - LC
    moves = {
        0: ([(0, tall, 0)], None),
        1: ([(0, cut, 0)], (cut, 3, low)),
        2: ([(LC, tall, 0)], (0, 1, cut)),
        3: ([(LC, cut, 0), (cut, tall, cut)], (0, 2, cut)),
    }

    def border(k):
        stays, leaves = moves[k]
        mine = [pltpu.make_async_copy(fin.at[a:b], dn_ref.at[at : at + b - a], loc.at[i]) for i, (a, b, at) in enumerate(stays)]
        if leaves is None:
            return mine, None
        a, to, at = leaves
        return mine, remote(fin.at[a : a + LC], dn_ref.at[at : at + LC], b_send.at[0], b_recv.at[0], (g, r, to))

    for k in range(4):

        @pl.when(c == k)
        def _(k=k):
            mine, gone = border(k)
            if gone is not None:
                gone.start()
            for copy in mine:
                copy.start()

    def gain_copy(dg, dc):
        to = ((g + dg) % 4, r, (c + dc) % 4)
        i = 4 * dg + dc - 1
        return remote(gs.at[(g + dg) % 4], gr.at[i], g_send.at[i], g_recv.at[0], to)

    pairs = [(dg, dc) for dg in range(4) for dc in range(4) if dg or dc]
    for dg, dc in pairs:
        gain_copy(dg, dc).start()

    @pl.when(jnp.logical_not(alone))
    def _():
        to_owner(0).wait_recv()

    to_owner(1).wait_recv()
    grad_ref[...] = fr[0].astype(f32) + fr[1].astype(f32)

    pltpu.make_async_copy(gr, gr, g_recv.at[0]).wait()
    gain_ref[...] = jnp.sum(gr[...], axis=0) + gs[g]

    for k in range(4):

        @pl.when(c == k)
        def _(k=k):
            mine, gone = border(k)
            for copy in mine:
                copy.wait()
            if gone is not None:
                gone.wait()

    for dg, dc in pairs:
        gain_copy(dg, dc).wait_send()
    for i in range(3):
        to_y(i).wait_send()
        to_z(i).wait_send()
    for d in range(2):
        for i in range(2):
            to_core(i, d).wait_send()
        to_x(d).wait_send()

    @pl.when(jnp.logical_not(alone))
    def _():
        to_owner(0).wait_send()

    to_owner(1).wait_send()


def run_finish(d_inner, d_gate, normed, raw, wi, wg):
    w = d_inner.shape[1]
    width, n = wi.shape[1], wi.shape[2]
    tall = SEQ // 2
    part = tall // 2
    dma = pltpu.SemaphoreType.DMA
    low = lambda *shape: pltpu.VMEM(shape, bf16)
    vmem = pl.BlockSpec(memory_space=pltpu.VMEM)
    return pl.pallas_call(
        finish,
        in_specs=[ANY] * 6,
        out_specs=[ANY, vmem, vmem],
        out_shape=(shaped(tall, width, dtype=bf16), shaped(width, n), shaped(8, n)),
        scratch_shapes=[
            low(SEQ, w),
            low(SEQ, w),
            low(2, SEQ, width),
            low(tall, width),
            low(2, width, w),
            low(2, width, w),
            low(2, 2, width, n),
            low(2, 2, width, n),
            pltpu.VMEM((2, width, 2 * n), f32),
            low(2, width, n),
            low(2, width, n),
            low(2, width, n),
            low(2, width, n),
            low(3, part, width),
            low(3, part, width),
            low(3, part, width),
            low(3, part, width),
            pltpu.VMEM((tall, width), f32),
            low(tall, width),
            pltpu.VMEM((SLOTS, 8, n), f32),
            pltpu.VMEM((15, 8, n), f32),
            dma((6,)),
            dma((4,)),
            dma((4,)),
            dma((2,)),
            dma((2,)),
            dma((2,)),
            dma((2,)),
            dma((3,)),
            dma((3,)),
            dma((3,)),
            dma((3,)),
            dma((1,)),
            dma((1,)),
            dma((15,)),
            dma((1,)),
        ],
        compiler_params=pltpu.CompilerParams(collective_id=1, has_side_effects=True, vmem_limit_bytes=VMEM_LIMIT),
        cost_estimate=pl.CostEstimate(flops=60 * 1000000000, bytes_accessed=1000000, transcendentals=0),
    )(d_inner, d_gate, normed, raw, wi, wg)


def late_parts(order_ref, normed_ref, gate_ref, gated_ref, cot_ref, gate_sent, out_sent, gate_kept, out_kept):
    t = pl.program_id(0)
    for d in range(2):
        low = dot_tn(normed_ref[d], gate_ref[...])
        high = dot_tn(gated_ref[...], cot_ref[d])

        @pl.when(t < 2)
        def _(d=d, low=low, high=high):
            gate_sent[0, d] = low.astype(bf16)
            out_sent[0, d] = high.astype(bf16)

        @pl.when(t >= 2)
        def _(d=d, low=low, high=high):
            gate_kept[0, d] = low
            out_kept[0, d] = high


def run_late_parts(order, normed, d_gate, gated, cot):
    width = normed.shape[2]
    w = gated.shape[1]
    n = w // SLOTS
    sent = pl.BlockSpec((1, 2, width, n), lambda t, o: (jnp.minimum(t, 1), 0, 0, 0))
    kept = pl.BlockSpec((1, 2, width, n), lambda t, o: (jnp.maximum(t - 2, 0), 0, 0, 0))
    return pl.pallas_call(
        late_parts,
        grid_spec=pltpu.PrefetchScalarGridSpec(
            num_scalar_prefetch=1,
            grid=(SLOTS,),
            in_specs=[
                pl.BlockSpec((2, SEQ, width), lambda t, o: (0, 0, 0)),
                pl.BlockSpec((SEQ, n), lambda t, o: (0, o[t])),
                pl.BlockSpec((SEQ, w), lambda t, o: (0, 0)),
                pl.BlockSpec((2, SEQ, n), lambda t, o: (0, 0, o[t])),
            ],
            out_specs=(sent, sent, kept, kept),
        ),
        out_shape=(shaped(2, 2, width, n, dtype=bf16), shaped(2, 2, width, n, dtype=bf16), shaped(2, 2, width, n), shaped(2, 2, width, n)),
        compiler_params=pltpu.CompilerParams(dimension_semantics=("arbitrary",), vmem_limit_bytes=VMEM_LIMIT),
        cost_estimate=pl.CostEstimate(flops=14 * 1000000000, bytes_accessed=1000000, transcendentals=0),
    )(order, normed, d_gate, gated, cot)


QUARTERS = 4
SUM_LAG = 3
PIECE = SEQ // 2 // QUARTERS
OTHER_STEP = (1, 2, 3, 4)
PAIR_STEP = (3, 4, 1, 2)
FINAL_STEP = (7, 7, 7, 7)
X_STEP = (0, 1)
OWNER_STEP = (2, 4)
DONE_STEP = (8, 8)
QUARTER_STEP = ((2, 3, 4, 5), (4, 5, 6, 7))


def border_moves(tall):
    cut = tall - LC
    low = cut - LC
    return {
        0: ([(0, tall, 0)], None),
        1: ([(0, cut, 0)], (cut, 3, low)),
        2: ([(LC, tall, 0)], (0, 1, cut)),
        3: ([(LC, cut, 0), (cut, tall, cut)], (0, 2, cut)),
    }


def backward(xdbl_ref, xconv_ref, dy_ref, dtp_ref, vec_ref, rate_ref, starts_ref, mix_ref, into_ref, sent_hbm, kept_hbm, own_hbm, oth_hbm,
             dxdbl_ref, dxc_ref, alog_ref, sums_ref, dtpg_ref, grad_ref, branch_ref,
             first, first_s, first_r, part, ys, yr, zs, zr, cr, kp, xs, xr, fs, fr, out, own, oth, by_s, by, bz_s, bz, fin,
             y_send, y_recv, z_send, z_recv, e_send, e_recv, c_send, c_recv, x_send, x_recv, f_send, f_recv,
             p_send, p_recv, q_send, q_recv, b_send, b_recv, load_k, load_o, stay, put, *scratch):
    i = pl.program_id(0)
    g, r, c = lax.axis_index("grp"), lax.axis_index("row"), lax.axis_index("col")
    x, core, s, p = g // 2, g % 2, c // 2, c % 2
    q = 2 * p + xor_bit(r, s)
    tall = SEQ // 2
    alone = q == c
    y_dev, z_dev, far_dev = (g, 1 - r, c), (g, r, 2 * s + 1 - p), (g, 1 - r, (c + 2) % 4)
    x_dev, core_dev = ((1 - x) * 2 + core, r, c), (2 * x + 1 - core, r, c)
    to_first = remote(first_s, first_r, e_send.at[0], e_recv.at[0], far_dev)

    def to_y(k):
        return remote(ys.at[k], yr.at[k], y_send.at[k], y_recv.at[k], y_dev)

    def to_z(k):
        return remote(zs.at[k], zr.at[k], z_send.at[k], z_recv.at[k], z_dev)

    def to_core(n, j):
        return remote(sent_hbm[n].at[j], cr.at[n, j], c_send.at[n, j], c_recv.at[n, j], core_dev)

    def load(n, j):
        return pltpu.make_async_copy(kept_hbm[n].at[j], kp.at[n], load_k.at[n])

    def to_x(n):
        return remote(xs.at[n], xr.at[n], x_send.at[n], x_recv.at[n], x_dev)

    def to_owner(n, d, at=None):
        device = (g, r if d == 0 else 1 - r, q)
        if at is None:
            return remote(fs.at[n, d], fr.at[n, d], f_send.at[n, d], f_recv.at[n, d], device)
        tall = fs.shape[2] // QUARTERS
        rows = pl.ds(at * tall, tall)
        return remote(fs.at[n, d, rows], fr.at[n, d, rows], f_send.at[n, d], f_recv.at[n, d], device)

    def rows_at(mine, j):
        return pl.ds(pl.multiple_of((p if mine else 1 - p) * tall + j * PIECE, 16), PIECE)

    def branch_y(m):
        if m >= QUARTERS:
            src = oth_hbm.at[rows_at(False, m - QUARTERS)]
        elif m < 2:
            src = oth_hbm.at[rows_at(True, m)]
        else:
            src = by_s.at[m - 2]
        return remote(src, by.at[m], p_send.at[m], p_recv.at[m], y_dev)

    def branch_z(m):
        src = bz_s.at[m] if m < QUARTERS else oth_hbm.at[rows_at(False, m - 2)]
        return remote(src, bz.at[m], q_send.at[m], q_recv.at[m], z_dev)

    load_own = pltpu.make_async_copy(own_hbm, own, load_o.at[0])
    load_oth = pltpu.make_async_copy(oth_hbm.at[pl.ds(pl.multiple_of(p * tall + 2 * PIECE, 16), 2 * PIECE)], oth, load_o.at[1])

    def border(k):
        stays, leaves = border_moves(tall)[k]
        mine = [pltpu.make_async_copy(fin.at[a:b], branch_ref.at[at : at + b - a], stay.at[n]) for n, (a, b, at) in enumerate(stays)]
        if leaves is None:
            return mine, None
        a, to, at = leaves
        return mine, remote(fin.at[a : a + LC], branch_ref.at[at : at + LC], b_send.at[0], b_recv.at[0], (g, r, to))

    def at_border(act):
        for k in range(4):

            @pl.when(c == k)
            def _(k=k):
                act(*border(k))

    def pass_on(k):
        to_y(k).wait_recv()
        part[k] = part[k] + yr[k].astype(f32)
        zs[k] = part[k].astype(bf16)
        to_z(k).start()

    def settle(k):
        to_z(k).wait_recv()
        dxdbl_ref[NCH - 1 - k] = part[k] + zr[k].astype(f32)

    @pl.when(i == 0)
    def _():
        barrier = pltpu.get_barrier_semaphore()
        for dr in range(2):
            for dc in range(4):
                if dr or dc:
                    pl.semaphore_signal(barrier, inc=1, device_id=(g, (r + dr) % 2, (c + dc) % 4), device_id_type=MESH)
        for device in (x_dev, core_dev):
            pl.semaphore_signal(barrier, inc=1, device_id=device, device_id_type=MESH)
        pl.semaphore_wait(barrier, 9)
        for j in range(2):
            for n in range(2):
                to_core(n, j).start()
        for n in range(2):
            load(n, 0).start()
        load_own.start()
        load_oth.start()
        for m in (QUARTERS, QUARTERS + 1):
            branch_y(m).start()
            branch_z(m).start()
        first[...] = jnp.zeros_like(first)
        alog_ref[...] = jnp.zeros_like(alog_ref)
        sums_ref[...] = jnp.zeros_like(sums_ref)
        dtpg_ref[...] = jnp.zeros_like(dtpg_ref)

    @pl.when(i == 1)
    def _():
        to_first.wait()
        first[...] = mix_ref[0:1] * first_s[...] + into_ref[0:1] * first_r[...]

    chunk_backward(xdbl_ref, xconv_ref, dy_ref, dtp_ref, vec_ref, rate_ref, starts_ref, part.at[i], dxc_ref, alog_ref, sums_ref, dtpg_ref, first, *scratch)

    @pl.when(i == 0)
    def _():
        first_s[...] = first[...]
        to_first.start()

    @pl.when(i == 1)
    def _():
        load_own.wait()
        load_oth.wait()

    for n in range(2):

        @pl.when(i == X_STEP[n])
        def _(n=n):
            to_core(n, 0).wait_recv()
            load(n, 0).wait()
            xs[n] = (kp[n] + cr[n, 0].astype(f32)).astype(bf16)
            to_x(n).start()
            load(n, 1).start()

        @pl.when(i == OWNER_STEP[n])
        def _(n=n):
            load(n, 1).wait()
            to_core(n, 1).wait_recv()
            to_x(n).wait_recv()
            fs[n] = (kp[n] + cr[n, 1].astype(f32) + xr[n].astype(f32)).astype(bf16)

            @pl.when(alone)
            def _():
                fr[n, 0] = fs[n, 0]

        for k in range(QUARTERS):

            @pl.when(i == QUARTER_STEP[n][k])
            def _(n=n, k=k):
                @pl.when(jnp.logical_not(alone))
                def _():
                    to_owner(n, 0, k).start()

                to_owner(n, 1, k).start()

        @pl.when(i == DONE_STEP[n])
        def _(n=n):
            @pl.when(jnp.logical_not(alone))
            def _():
                to_owner(n, 0).wait_recv()

            to_owner(n, 1).wait_recv()
            out[n] = fr[n, 0].astype(f32) + fr[n, 1].astype(f32)
            pltpu.make_async_copy(out.at[n], grad_ref.at[n], put.at[n]).start()

    for j in range(QUARTERS):

        @pl.when(i == OTHER_STEP[j])
        def _(j=j):
            if j >= 2:
                branch_z(QUARTERS + j - 2).wait_recv()
                mine = oth[(j - 2) * PIECE : (j - 1) * PIECE, :].astype(f32)
                by_s[j - 2] = (mine + bz[QUARTERS + j - 2].astype(f32)).astype(bf16)
            branch_y(j).start()

        @pl.when(i == PAIR_STEP[j])
        def _(j=j):
            total = own[rows_at(False, j), :]
            if j < 2:
                branch_y(QUARTERS + j).wait_recv()
                total = total + by[QUARTERS + j].astype(f32)
            bz_s[j] = total.astype(bf16)
            branch_z(j).start()

        @pl.when(i == FINAL_STEP[j])
        def _(j=j):
            branch_y(j).wait_recv()
            branch_z(j).wait_recv()
            fin[j * PIECE : (j + 1) * PIECE, :] = (own[rows_at(True, j), :] + by[j].astype(f32) + bz[j].astype(f32)).astype(bf16)

    @pl.when(i == 7)
    def _():
        def begin(mine, gone):
            if gone is not None:
                gone.start()
            for copy in mine:
                copy.start()

        at_border(begin)

    @pl.when(i >= SUM_LAG)
    def _():
        pass_on(i - SUM_LAG)

    ys[i] = part[i].astype(bf16)
    to_y(i).start()
    @pl.when(i == NCH - 1)
    def _():
        for k in range(NCH - SUM_LAG, NCH):
            pass_on(k)
        for k in range(NCH):
            settle(k)

        def finish_border(mine, gone):
            for copy in mine:
                copy.wait()
            if gone is not None:
                gone.wait()

        at_border(finish_border)

        def sent(k, _):
            to_y(k).wait_send()
            to_z(k).wait_send()
            return 0

        lax.fori_loop(0, NCH, sent, 0)
        for n in range(2):
            for j in range(2):
                to_core(n, j).wait_send()
            to_x(n).wait_send()

            @pl.when(jnp.logical_not(alone))
            def _(n=n):
                to_owner(n, 0).wait_send()

            to_owner(n, 1).wait_send()
            pltpu.make_async_copy(out.at[n], grad_ref.at[n], put.at[n]).wait()
        for m in range(QUARTERS + 2):
            branch_y(m).wait_send()
            branch_z(m).wait_send()


def backward_kernel(*refs):
    backward(*refs[:9], refs[9:11], refs[11:13], *refs[13:])


def run_backward(xdbl, xconv, dy, dtp, vec, rate, starts, mix, into, sent, kept, own, oth):
    w = xconv.shape[1]
    width = own.shape[1]
    _, _, tall, n = sent[0].shape
    at = lambda i: NCH - 1 - i
    dma = pltpu.SemaphoreType.DMA
    low = lambda *shape: pltpu.VMEM(shape, bf16)
    sums = low(NCH, XW, CH)
    state = pltpu.VMEM((NSTATE, w), f32)
    return pl.pallas_call(
        backward_kernel,
        grid=(NCH,),
        in_specs=[
            chunk_of(XW, at),
            rows_of(w, at),
            rows_of(w, at),
            whole(RANK, w),
            whole(8, w),
            whole(NSTATE, w),
            pl.BlockSpec((1, NSTATE, w), lambda i: (at(i), 0, 0)),
            whole(8, w),
            whole(8, w),
        ]
        + [ANY] * 6,
        out_specs=(whole(NCH, XW, CH), rows_of(w, at), whole(NSTATE, w), whole(8, w), whole(RANK, w), ANY, ANY),
        out_shape=(
            shaped(NCH, XW, CH),
            shaped(SEQ, w),
            shaped(NSTATE, w),
            shaped(8, w),
            shaped(RANK, w),
            shaped(2, tall, n),
            shaped(SEQ // 2, width, dtype=bf16),
        ),
        scratch_shapes=[
            state,
            state,
            state,
            pltpu.VMEM((NCH, XW, CH), f32),
            sums,
            sums,
            sums,
            sums,
            low(2, 2, 2, tall, n),
            pltpu.VMEM((2, 2, tall, n), f32),
            low(2, 2, tall, n),
            low(2, 2, tall, n),
            low(2, 2, tall, n),
            low(2, 2, tall, n),
            pltpu.VMEM((2, tall, n), f32),
            pltpu.VMEM((SEQ, width), f32),
            low(2 * PIECE, width),
            low(2, PIECE, width),
            low(QUARTERS + 2, PIECE, width),
            low(QUARTERS, PIECE, width),
            low(QUARTERS + 2, PIECE, width),
            low(SEQ // 2, width),
            dma((NCH,)),
            dma((NCH,)),
            dma((NCH,)),
            dma((NCH,)),
            dma((1,)),
            dma((1,)),
            dma((2, 2)),
            dma((2, 2)),
            dma((2,)),
            dma((2,)),
            dma((2, 2)),
            dma((2, 2)),
            dma((QUARTERS + 2,)),
            dma((QUARTERS + 2,)),
            dma((QUARTERS + 2,)),
            dma((QUARTERS + 2,)),
            dma((1,)),
            dma((1,)),
            dma((2,)),
            dma((2,)),
            dma((2,)),
            dma((2,)),
            *backward_scratch(w),
        ],
        compiler_params=pltpu.CompilerParams(
            dimension_semantics=("arbitrary",), collective_id=3, has_side_effects=True, vmem_limit_bytes=61 * 1024 * 1024
        ),
        cost_estimate=pl.CostEstimate(flops=120 * 1000000000, bytes_accessed=1000000, transcendentals=0),
    )(xdbl, xconv, dy, dtp, vec, rate, starts, mix, into, *sent, *kept, own, oth)


def per_device(
    tokens,
    gain,
    in_proj,
    conv_weight,
    conv_bias,
    x_proj,
    dt_proj,
    dt_bias,
    a_log,
    d_skip,
    out_proj,
    table,
    cotangent,
):
    row = lax.axis_index("row")
    col = lax.axis_index("col")
    grp = lax.axis_index("grp")
    low_row = row == 0
    low_pair = col % 2 == 0
    half = col // 2
    places = [(r, c) for r in range(2) for c in range(4)]
    quick = lax.axis_size("grp") == 4

    def spot(r, c):
        return r * 4 + c

    def send(v, pairs):
        return lax.ppermute(v, ("row", "col"), [(spot(*a), spot(*b)) for a, b in pairs])

    def swap(v):
        return send(v, [((r, c), (1 - r, c)) for r, c in places])

    def pair(v):
        return send(v, [((r, c), (r, c ^ 1)) for r, c in places])

    def across(v):
        return send(v, [((r, c), (1 - r, c ^ 2)) for r, c in places])

    def quarter_spot(q, s):
        return ((q & 1) ^ s, 2 * s + (q >> 1))

    same = [((r, q), quarter_spot(q, r ^ (q & 1))) for r, q in places]
    other = [((r, q), quarter_spot(q, 1 ^ r ^ (q & 1))) for r, q in places]
    spread = [((r, q), quarter_spot(q, r)) for r, q in places]

    def back(pairs):
        return [(b, a) for a, b in pairs]

    def flip(v, bit):
        return lax.ppermute(v, "grp", [(g, g ^ bit) for g in range(4)])

    def scatter_grp(v, axis):
        return lax.psum_scatter(v, "grp", scatter_dimension=axis, tiled=True)

    def by_pair(own, paired):
        return jnp.where(low_pair, own, paired), jnp.where(low_pair, paired, own)

    local = tokens.shape[0]
    cut = local - LC
    tail_at = cut - LC

    def to_sequences(v):
        got = send(jnp.where(col == 3, v[tail_at:cut], v[cut:]), [((r, a), (r, b)) for r in range(2) for a, b in ((1, 2), (2, 3), (3, 1))])
        low = jnp.concatenate([v[:cut], jnp.where(col == 0, v[cut:], got)], axis=0)
        two = jnp.concatenate([got, v[:cut]], axis=0)
        three = jnp.concatenate([got, v[:tail_at], v[cut:]], axis=0)
        return jnp.where(col < 2, low, jnp.where(col == 2, two, three))

    def from_sequences(v):
        got = send(jnp.where(col == 1, v[cut:], v[:LC]), [((r, b), (r, a)) for r in range(2) for a, b in ((1, 2), (2, 3), (3, 1))])
        low = jnp.concatenate([v[:cut], jnp.where(col == 0, v[cut:], got)], axis=0)
        two = jnp.concatenate([v[LC:], got], axis=0)
        three = jnp.concatenate([v[LC:cut], got, v[cut:]], axis=0)
        return jnp.where(col < 2, low, jnp.where(col == 2, two, three))

    def gather_quad(v):
        swapped = swap(v)
        paired = pair(v)
        mid = v.shape[0] // 2
        diagonal = jnp.concatenate([pair(swapped[:mid]), swap(paired[mid:])], axis=0)
        first_own, second_own = by_pair(v, paired)
        first_oth, second_oth = by_pair(swapped, diagonal)
        return jnp.stack([jnp.concatenate([first_own, second_own], axis=0), jnp.concatenate([first_oth, second_oth], axis=0)])

    def scatter_quad(own, oth):
        v = own + swap(oth.astype(bf16)).astype(f32)
        first, second = v[:local], v[local:]
        kept, sent = jnp.where(low_pair, first, second), jnp.where(low_pair, second, first)
        return kept + pair(sent.astype(bf16)).astype(f32)

    own_table = jnp.where(half == 0, table[0], table[1])
    oth_table = jnp.where(half == 0, table[1], table[0])
    resumes_own = own_table == half
    resumed_by_other = oth_table == half

    small = jnp.concatenate([conv_weight, conv_bias[None], dt_bias[None], d_skip[None], a_log, dt_proj, x_proj.T], axis=0)
    lanes = small.shape[1]
    used = small.shape[0]
    gain_rows = gain.size // lanes
    width = tokens.shape[1]
    if quick:
        small = jnp.concatenate([small, gain.reshape(gain_rows, lanes)], axis=0)
        small = jnp.pad(small, ((0, -small.shape[0] % 16), (0, 0)))
        raw, wi, small = run_gather_start(tokens, in_proj[:, 0], small)
        gain_all = small[:, used : used + gain_rows].reshape(2, width).astype(f32)
        small = jnp.swapaxes(small, 0, 1).reshape(small.shape[1], 8 * lanes)
    else:
        raw = gather_quad(to_sequences(tokens))

        def weight(shard):
            v = lax.all_gather(jnp.stack([send(shard, same), send(shard, other)]), "grp", axis=2, tiled=True)
            v = v.reshape(2, v.shape[1], SLOTS, v.shape[2] // SLOTS)
            return jnp.transpose(v, (2, 0, 1, 3)).reshape(2 * SLOTS, v.shape[1], v.shape[3])

        wi = weight(in_proj[:, 0])
        small = send(lax.all_gather(small, ("row", "grp"), axis=1, tiled=True), spread)
        gain_all = lax.all_gather(gain, ("row", "grp"), axis=0, tiled=True).astype(f32).reshape(2, width)
    w = small.shape[1]
    zero_row = jnp.zeros((1, w), f32)
    conv = jnp.concatenate([small[0:5].astype(f32)] + [zero_row] * 3, axis=0)
    vec = jnp.concatenate([small[5:7].astype(f32)] + [zero_row] * 6, axis=0)
    rate = -jnp.exp(small[7 : 7 + NSTATE].astype(f32))
    dtp = small[7 + NSTATE : 7 + NSTATE + RANK]
    xproj = small[7 + NSTATE + RANK : 7 + NSTATE + RANK + XW]
    gain_own = jnp.where(low_row, gain_all[0], gain_all[1])
    gain_two = jnp.stack([gain_own, jnp.where(low_row, gain_all[1], gain_all[0])])

    zero_state = jnp.zeros((NSTATE, w), f32)
    if quick:
        mix = jnp.broadcast_to(resumes_own.astype(f32), (8, w))
        normed, inv, inner, xconv, yfull, starts, xdbl, tail, wg, wo, cot = run_forward(raw, gain_two, wi, mix, conv, xproj, dtp, vec, rate, in_proj[:, 1], out_proj, cotangent)
    else:
        normed, inv, inner = run_project_first(raw, gain_two, wi)
        tail_own = (inv * inner)[LP - 8 : LP]
        tail = jnp.where(resumes_own, tail_own, across(tail_own))
        xconv, xdbl = run_conv_forward(inner, inv, tail, conv, xproj)
        for move in (swap, pair):
            xdbl = xdbl + move(xdbl)
        xdbl = jnp.swapaxes(xdbl.reshape(XW, NCH, CH), 0, 1)
        *kept, final = run_scan_forward(0, PC, xdbl, xconv, dtp, vec, rate, zero_state)
        resumed = jnp.where(resumes_own, final, across(final))
        yfull, starts, _ = run_scan_forward(PC, NCH - PC, xdbl, xconv, dtp, vec, rate, resumed, kept)
        wg, wo = weight(in_proj[:, 1]), weight(out_proj)
        cot = gather_quad(to_sequences(cotangent))
    gated, d_yfull, d_gate_proj, gate_scale, branch_own, branch_oth = run_gate_backward(normed, wg, cot, wo, yfull, inv)

    def collect(v):
        return send(v[0].astype(bf16), back(same)).astype(f32) + send(v[1].astype(bf16), back(other)).astype(f32)

    def rows_product(a, b, out_dtype):
        return lax.dot_general(a, b, (((1,), (0,)), ((), ())), preferred_element_type=f32).astype(out_dtype)

    zero_head = jnp.zeros((8, w), f32)
    conv_back = functools.partial(run_conv_backward, inner=inner, inv=inv, tail=tail, conv=conv, xproj=xproj)
    if quick:
        x, core = grp // 2, grp % 2
        order = jnp.stack([2 * (1 - x) + 1 - core, 2 * x + 1 - core, 2 * (1 - x) + core, 2 * x + core]).astype(jnp.int32)
        gate_sent, out_sent, gate_kept, out_kept = run_late_parts(order, normed, d_gate_proj, gated, cot)
        sent, kept = (gate_sent, out_sent), (gate_kept, out_kept)
        into = jnp.broadcast_to(resumed_by_other.astype(f32), (8, w))
        dxdbl, dxc, alog_grad, scan_sums, dtp_grad, late_grads, branch = run_backward(
            xdbl, xconv, d_yfull, dtp, vec, rate, starts, mix, into, sent, kept, branch_own, branch_oth
        )
        gate_grad, out_grad = late_grads[0], late_grads[1]
    else:
        branch = from_sequences(scatter_quad(branch_own, branch_oth).astype(bf16))
        out_grad = collect([scatter_grp(dot_tn(gated, cot[d]), 1) for d in range(2)])
        gate_grad = collect([scatter_grp(dot_tn(normed[d], d_gate_proj), 1) for d in range(2)])
        sums = (zero_state, jnp.zeros((8, w), f32), jnp.zeros((RANK, w), f32))
        scan = functools.partial(run_scan_backward, xdbl=xdbl, xconv=xconv, dy=d_yfull, dtp=dtp, vec=vec, rate=rate, starts=starts)
        dx_c, dxc, *sums, g_first = scan(PC, NCH - PC, carry=zero_state, sums=sums)
        g_into = jnp.where(resumes_own, g_first, 0.0) + jnp.where(resumed_by_other, across(g_first), 0.0)
        dx_p, dxc, *sums, _ = scan(0, PC, carry=g_into, sums=sums, kept=(dxc,))
        alog_grad, scan_sums, dtp_grad = sums
        dxdbl = jnp.concatenate([dx_p, dx_c], axis=1)
        for move in (swap, pair):
            dxdbl = dxdbl + move(dxdbl)
        dxdbl = jnp.swapaxes(dxdbl.reshape(XW, NCH, CH), 0, 1)

    output = (tokens.astype(f32) + branch.astype(f32)).astype(bf16)
    sums = (jnp.zeros((8, w), f32), jnp.zeros((XW, w), f32))
    dp, ds, *sums, head = conv_back(PC, NCH - PC, dxc=dxc, dxdbl=dxdbl, follow=zero_head, sums=sums)
    follow = jnp.where(resumes_own, head, 0.0) + jnp.where(resumed_by_other, across(head), 0.0)
    d_inner_proj, inner_scale, conv_sums, xproj_grad, _ = conv_back(0, PC, dxc=dxc, dxdbl=dxdbl, follow=follow, sums=sums, kept=(dp, ds))

    scale = gate_scale + inner_scale
    scale = scale + swap(scale)
    first, second = scale[:local], scale[local:]
    scale_own = jnp.where(low_pair, first, second) + pair(jnp.where(low_pair, second, first))
    inv_own = jnp.where(low_pair, inv[:local], inv[local:])
    pull = from_sequences(scale_own * inv_own * inv_own * inv_own / D)
    if quick:
        d_normed, inner_grad, gain_sum = run_finish(d_inner_proj, d_gate_proj, normed, raw, wi, wg)
        gain_grad = jnp.sum(gain_sum, axis=0)
    else:
        inner_grad = collect([scatter_grp(dot_tn(normed[d], d_inner_proj), 1) for d in range(2)])
        d_normed = from_sequences(scatter_quad(*run_normed_backward(d_inner_proj, d_gate_proj, wi, wg)))
        gain_grad = jnp.sum(d_normed * tokens.astype(f32), axis=0)
        gain_grad = lax.psum_scatter(lax.psum(gain_grad, "col"), "grp", scatter_dimension=0, tiled=True)
    input_grad = (cotangent.astype(f32) + d_normed.astype(f32) * gain_own - pull * tokens.astype(f32)).astype(bf16)
    in_grads = jnp.stack([inner_grad, gate_grad], axis=1)
    small_grad = jnp.concatenate([conv_sums[0:5], scan_sums[0:2], alog_grad * rate, dtp_grad, xproj_grad], axis=0)
    small_grad = jnp.pad(small_grad, ((0, -small_grad.shape[0] % 8), (0, 0)))
    small_grad = send(small_grad, back(spread))
    small_grad = lax.psum_scatter(small_grad, ("row", "grp"), scatter_dimension=1, tiled=True)
    return (
        output,
        input_grad,
        gain_grad,
        in_grads,
        small_grad[0:4],
        small_grad[4],
        small_grad[7 + NSTATE + RANK : 7 + NSTATE + RANK + XW].T,
        small_grad[7 + NSTATE : 7 + NSTATE + RANK],
        small_grad[5],
        small_grad[7 : 7 + NSTATE],
        small_grad[6],
        out_grad,
    )


def solution(mesh):
    placed = (
        P(("grp", "col"), "row"),
        P(("row", "grp")),
        P("row", None, ("col", "grp")),
        P(None, ("col", "row", "grp")),
        P(("col", "row", "grp")),
        P(("col", "row", "grp"), None),
        P(None, ("col", "row", "grp")),
        P(("col", "row", "grp")),
        P(None, ("col", "row", "grp")),
        P(("col", "row", "grp")),
        P("col", ("row", "grp")),
        P("grp"),
        P(("grp", "col"), "row"),
    )
    return jax.shard_map(
        per_device,
        mesh=mesh,
        in_specs=placed,
        out_specs=(
            P(("grp", "col"), "row"),
            P(("grp", "col"), "row"),
            P(("row", "grp")),
            P("row", None, ("col", "grp")),
            P(None, ("col", "row", "grp")),
            P(("col", "row", "grp")),
            P(("col", "row", "grp"), None),
            P(None, ("col", "row", "grp")),
            P(("col", "row", "grp")),
            P(None, ("col", "row", "grp")),
            P(("col", "row", "grp")),
            P("col", ("row", "grp")),
        ),
        check_vma=False,
    )
```

```python
import functools

import jax
import jax.numpy as jnp
from jax import lax
from jax.experimental import pallas as pl
from jax.experimental.pallas import tpu as pltpu
from jax.sharding import PartitionSpec as P

D = 2048
NSTATE = 16
KCONV = 4
RANK = 128
NPROMPT = 2
LP = 1024
LC = 128
NCONT = 2

eps = 1e-05
CH = 128
SUB = 16
PC = LP // CH
SEQ = LP + LC
NCH = SEQ // CH
XW = RANK + 2 * NSTATE
SPAN = SUB * NSTATE
LOG2E = 1.4426950408889634
VMEM_LIMIT = 58 * 1024 * 1024

f32 = jnp.float32
bf16 = jnp.bfloat16


def dot_nn(a, b):
    return lax.dot_general(a, b, (((1,), (0,)), ((), ())), preferred_element_type=f32)


def dot_nt(a, b):
    return lax.dot_general(a, b, (((1,), (1,)), ((), ())), preferred_element_type=f32)


def dot_tn(a, b):
    return lax.dot_general(a, b, (((0,), (0,)), ((), ())), preferred_element_type=f32)


def expand_tile():
    lane = lax.broadcasted_iota(jnp.int32, (NSTATE, SPAN), 1)
    row = lax.broadcasted_iota(jnp.int32, (NSTATE, SPAN), 0)
    return jnp.where(lane % NSTATE == row, 1.0, 0.0)


def own_token(rows):
    lane = lax.broadcasted_iota(jnp.int32, (rows, SPAN), 1)
    row = lax.broadcasted_iota(jnp.int32, (rows, SPAN), 0)
    return lane // NSTATE == row % SUB


def conv_forward(inner_ref, inv_ref, tail_ref, conv_ref, xproj_ref, xconv_ref, xdbl_ref, buf):
    i = pl.program_id(0)

    @pl.when(i == 0)
    def _():
        buf[0:8] = jnp.zeros_like(buf[0:8])

    @pl.when(i == PC)
    def _():
        buf[0:8] = tail_ref[...]

    @pl.when((i > 0) & (i < PC))
    def _():
        buf[0:8] = buf[CH : CH + 8]

    buf[8 : CH + 8] = inv_ref[...] * inner_ref[...]
    out = conv_ref[4:5]
    for k in range(KCONV):
        out = out + conv_ref[k : k + 1] * buf[5 + k : 5 + k + CH]
    xconv = (out * jax.nn.sigmoid(out)).astype(bf16)
    xconv_ref[...] = xconv
    xdbl_ref[...] = dot_nt(xproj_ref[...], xconv)


def softplus(v):
    return jnp.maximum(v, 0.0) + jnp.log1p(jnp.exp(-jnp.abs(v)))


def by_sub(v):
    return v.reshape(CH // SUB, SUB, v.shape[-1])


def scan_chunk(xdbl_ref, xconv, dtp_ref, vec_ref, rate_ref, state, dt_s, u_s, cb_s, h_s, y_s):
    step = softplus(dot_tn(xdbl_ref[:RANK].astype(bf16), dtp_ref[...]) + vec_ref[0:1])
    dt_s[...] = by_sub(step)
    u_s[...] = by_sub(step * xconv)
    reads = dot_tn(xdbl_ref[RANK + NSTATE :].astype(bf16), expand_tile().astype(bf16))
    cb_s[...] = jnp.where(own_token(CH), reads, 0.0).astype(bf16)
    rate = rate_ref[...] * LOG2E

    def block(j, carried):
        h, maps = carried
        for t in range(SUB):
            a = jnp.exp2(dt_s[j, t : t + 1, :] * rate)
            h = a * h + u_s[j, t : t + 1, :] * maps[:, t : t + 1]
            h_s[t * NSTATE : (t + 1) * NSTATE, :] = h.astype(bf16)
        rows = pl.ds(pl.multiple_of(j * SUB, SUB), SUB)
        y_s[rows, :] = dot_nn(cb_s[rows, :], h_s[...])
        return (h, pltpu.roll(maps, CH - SUB, 1))

    h, _ = lax.fori_loop(0, CH // SUB, block, (state, xdbl_ref[RANK : RANK + NSTATE]))
    return h, y_s[...] + vec_ref[1:2] * xconv


def scan_scratch(w):
    return [
        pltpu.VMEM((CH // SUB, SUB, w), f32),
        pltpu.VMEM((CH // SUB, SUB, w), f32),
        pltpu.VMEM((CH, SPAN), bf16),
        pltpu.VMEM((SPAN, w), bf16),
        pltpu.VMEM((CH, w), f32),
    ]


def scan_forward(kept, xdbl_ref, xconv_ref, dtp_ref, vec_ref, rate_ref, start_ref, *refs):
    yfull_ref, starts_ref, final_ref, *scratch = refs[kept:]

    @pl.when(pl.program_id(0) == 0)
    def _():
        final_ref[...] = start_ref[...]

    starts_ref[0] = final_ref[...]
    h, yfull = scan_chunk(xdbl_ref, xconv_ref[...].astype(f32), dtp_ref, vec_ref, rate_ref, final_ref[...], *scratch)
    final_ref[...] = h
    yfull_ref[...] = yfull.astype(bf16)


def chunk_backward(xdbl_ref, xconv_ref, dy_ref, dtp_ref, vec_ref, rate_ref, starts_ref, dxdbl_ref, dxc_ref, alog_ref, sums_ref, dtpg_ref, first_ref,
                   dt_s, u_s, x_s, dy_s, a_s, h_s, g_s, w_s, b_s, m1_s, m2_s, ds_s, dx_s, sig_s):
    low = xdbl_ref[:RANK].astype(bf16)
    step_inner = dot_tn(low, dtp_ref[...]) + vec_ref[0:1]
    step = softplus(step_inner)
    sig_s[...] = jax.nn.sigmoid(step_inner)
    xconv = xconv_ref[...].astype(f32)
    dy = dy_ref[...]
    dt_s[...] = by_sub(step)
    u_s[...] = by_sub(step * xconv)
    x_s[...] = by_sub(xconv)
    dy_s[...] = by_sub(dy)
    tile = expand_tile().astype(bf16)
    b_s[...] = jnp.where(own_token(CH), dot_tn(xdbl_ref[RANK : RANK + NSTATE].astype(bf16), tile), 0.0).astype(bf16)
    rate = rate_ref[...]
    rate2 = rate * LOG2E
    h_s[0:NSTATE] = starts_ref[0]

    def ahead(j, carried):
        h, maps = carried
        for t in range(SUB):
            a = jnp.exp2(dt_s[j, t : t + 1, :] * rate2)
            h = a * h + u_s[j, t : t + 1, :] * maps[:, t : t + 1]
            a_s[j, t * NSTATE : (t + 1) * NSTATE, :] = a
            at = pl.multiple_of(j * SPAN + (t + 1) * NSTATE, NSTATE)
            h_s[pl.ds(at, NSTATE), :] = h
        return (h, pltpu.roll(maps, CH - SUB, 1))

    lax.fori_loop(0, CH // SUB, ahead, (starts_ref[0], xdbl_ref[RANK : RANK + NSTATE]))
    ones = jnp.where(own_token(SUB), 1.0, 0.0).astype(bf16)
    mine_sub = own_token(SUB)

    def back(jj, carried):
        g, alog, maps = carried
        j = CH // SUB - 1 - jj
        maps = pltpu.roll(maps, SUB, 1)
        for t in reversed(range(SUB)):
            dt = dt_s[j, t : t + 1, :]
            gs = maps[:, t : t + 1] * dy_s[j, t : t + 1, :] + g
            g = a_s[j, t * NSTATE : (t + 1) * NSTATE, :] * gs
            prior = h_s[pl.ds(pl.multiple_of(j * SPAN + t * NSTATE, NSTATE), NSTATE), :]
            w = g * prior
            alog = alog + w * dt
            g_s[t * NSTATE : (t + 1) * NSTATE, :] = gs.astype(bf16)
            w_s[t * NSTATE : (t + 1) * NSTATE, :] = (w * rate).astype(bf16)
        rows = pl.ds(pl.multiple_of(j * SUB, SUB), SUB)
        gs_all = g_s[...]
        through = dot_nn(b_s[rows, :], gs_all)
        ds_s[rows, :] = dot_nn(ones, w_s[...]) + x_s[j] * through
        dx_s[rows, :] = dt_s[j] * through + vec_ref[1:2] * dy_s[j]
        hs = h_s[pl.ds(pl.multiple_of(j * SPAN + NSTATE, NSTATE), SPAN), :].astype(bf16)
        m1_s[rows, :] = jnp.where(mine_sub, dot_nt(u_s[j].astype(bf16), gs_all), 0.0).astype(bf16)
        m2_s[rows, :] = jnp.where(mine_sub, dot_nt(dy_s[j].astype(bf16), hs), 0.0).astype(bf16)
        return (g, alog, maps)

    g, alog, _ = lax.fori_loop(0, CH // SUB, back, (first_ref[...], alog_ref[...], xdbl_ref[RANK + NSTATE :]))
    first_ref[...] = g
    alog_ref[...] = alog
    d_inner = ds_s[...] * sig_s[...]
    d_low = d_inner.astype(bf16)
    sums_ref[0:1] = sums_ref[0:1] + jnp.sum(d_inner, axis=0, keepdims=True)
    sums_ref[1:2] = sums_ref[1:2] + jnp.sum(dy * xconv, axis=0, keepdims=True)
    dtpg_ref[...] = dtpg_ref[...] + dot_nn(low, d_low)
    dxdbl_ref[:RANK] = dot_nt(dtp_ref[...], d_low)
    dxdbl_ref[RANK : RANK + NSTATE] = dot_nt(tile, m1_s[...])
    dxdbl_ref[RANK + NSTATE :] = dot_nt(tile, m2_s[...])
    dxc_ref[...] = dx_s[...]


def scan_backward(kept, *refs):
    given, sums0, out = refs[:7], refs[7:11], refs[11 + kept :]
    dxdbl_ref, dxc_ref, alog_ref, sums_ref, dtpg_ref, first_ref = out[:6]

    @pl.when(pl.program_id(0) == 0)
    def _():
        first_ref[...] = sums0[0][...]
        alog_ref[...] = sums0[1][...]
        sums_ref[...] = sums0[2][...]
        dtpg_ref[...] = sums0[3][...]

    chunk_backward(*given, dxdbl_ref, dxc_ref, alog_ref, sums_ref, dtpg_ref, first_ref, *out[6:])


def backward_scratch(w):
    sub = pltpu.VMEM((CH // SUB, SUB, w), f32)
    return [
        sub,
        sub,
        sub,
        sub,
        pltpu.VMEM((CH // SUB, SPAN, w), f32),
        pltpu.VMEM(((CH + 1) * NSTATE, w), f32),
        pltpu.VMEM((SPAN, w), bf16),
        pltpu.VMEM((SPAN, w), bf16),
        pltpu.VMEM((CH, SPAN), bf16),
        pltpu.VMEM((CH, SPAN), bf16),
        pltpu.VMEM((CH, SPAN), bf16),
        pltpu.VMEM((CH, w), f32),
        pltpu.VMEM((CH, w), f32),
        pltpu.VMEM((CH, w), f32),
    ]


def conv_chunk(chunk, inner_ref, halo_ref, inv_ref, halo_inv_ref, tail_ref, conv_ref, xproj_ref, dxc_ref, dxdbl_ref, dproj_ref, dscale_ref, sums_ref, xprojg_ref, head_ref, buf, dbuf):
    projected = inner_ref[...]
    inv = inv_ref[...]
    before = halo_inv_ref[...] * halo_ref[...]
    before = jnp.where(chunk == 0, 0.0, jnp.where(chunk == PC, tail_ref[...], before))
    buf[0:8] = before
    buf[8 : CH + 8] = inv * projected
    out = conv_ref[4:5]
    for k in range(KCONV):
        out = out + conv_ref[k : k + 1] * buf[5 + k : 5 + k + CH]
    sig = jax.nn.sigmoid(out)
    xconv = (out * sig).astype(bf16)
    dxdbl = dxdbl_ref[...].astype(bf16)
    xprojg_ref[...] = xprojg_ref[...] + dot_nn(dxdbl, xconv)
    d_x = dxc_ref[...] + dot_tn(dxdbl, xproj_ref[...])
    d_conv = d_x * (sig * (1.0 + out * (1.0 - sig)))
    dbuf[CH : CH + 8] = head_ref[...]
    dbuf[0:CH] = d_conv
    d_inner = conv_ref[3:4] * d_conv
    for k in range(KCONV - 1):
        d_inner = d_inner + conv_ref[k : k + 1] * dbuf[3 - k : 3 - k + CH]
    for k in range(KCONV):
        sums_ref[k : k + 1] = sums_ref[k : k + 1] + jnp.sum(buf[5 + k : 5 + k + CH] * d_conv, axis=0, keepdims=True)
    sums_ref[4:5] = sums_ref[4:5] + jnp.sum(d_conv, axis=0, keepdims=True)
    dproj_ref[...] = (inv * d_inner).astype(bf16)
    dscale_ref[...] = jnp.sum(d_inner * projected, axis=1, keepdims=True)
    head_ref[...] = d_conv[0:8]


def conv_backward(kept, chunks, first, *refs):
    given, init, out = refs[:9], refs[9:12], refs[12 + kept :]
    dproj_ref, dscale_ref, sums_ref, xprojg_ref, head_ref, buf, dbuf = out
    i = pl.program_id(0)

    @pl.when(i == 0)
    def _():
        head_ref[...] = init[0][...]
        sums_ref[...] = init[1][...]
        xprojg_ref[...] = init[2][...]

    conv_chunk(first + chunks - 1 - i, *given, *out)


def call(body, chunks, args, in_specs, outs, out_specs, scratch, micros, aliases=None):
    return pl.pallas_call(
        body,
        grid=(chunks,),
        in_specs=in_specs,
        out_specs=out_specs,
        scratch_shapes=scratch,
        out_shape=outs,
        input_output_aliases=aliases or {},
        compiler_params=pltpu.CompilerParams(dimension_semantics=("arbitrary",), vmem_limit_bytes=VMEM_LIMIT),
        cost_estimate=pl.CostEstimate(flops=micros * 1000000000, bytes_accessed=1000000, transcendentals=0),
    )(*args)


def shaped(*shape, dtype=f32):
    return jax.ShapeDtypeStruct(shape, dtype)


def rows_of(width, place, tall=CH):
    return pl.BlockSpec((tall, width), lambda i: (place(i), 0))


def lanes_of(height, place):
    return pl.BlockSpec((height, CH), lambda i: (0, place(i)))


def whole(*shape):
    return pl.BlockSpec(shape, lambda i: (0,) * len(shape))


ANY = pl.BlockSpec(memory_space=pl.ANY)


def run_conv_forward(inner, inv, tail, conv, xproj):
    w = inner.shape[1]
    at = lambda i: i
    return call(
        conv_forward,
        NCH,
        (inner, inv, tail, conv, xproj),
        [rows_of(w, at), rows_of(1, at), whole(8, w), whole(8, w), whole(XW, w)],
        (shaped(SEQ, w, dtype=bf16), shaped(XW, SEQ)),
        (rows_of(w, at), lanes_of(XW, at)),
        [pltpu.VMEM((CH + 8, w), f32)],
        12,
    )


def chunk_of(height, place):
    return pl.BlockSpec((None, height, CH), lambda i: (place(i), 0, 0))


def run_scan_forward(first, chunks, xdbl, xconv, dtp, vec, rate, start, kept=()):
    w = xconv.shape[1]
    at = lambda i: first + i
    return call(
        functools.partial(scan_forward, len(kept)),
        chunks,
        (xdbl, xconv, dtp, vec, rate, start, *kept),
        [chunk_of(XW, at), rows_of(w, at), whole(RANK, w), whole(8, w), whole(NSTATE, w), whole(NSTATE, w)] + [ANY] * len(kept),
        (shaped(SEQ, w, dtype=bf16), shaped(NCH, NSTATE, w), shaped(NSTATE, w)),
        (rows_of(w, at), pl.BlockSpec((1, NSTATE, w), lambda i: (first + i, 0, 0)), whole(NSTATE, w)),
        scan_scratch(w),
        5 * chunks,
        {6 + k: k for k in range(len(kept))},
    )


def run_scan_backward(first, chunks, xdbl, xconv, dy, dtp, vec, rate, starts, carry, sums, kept=()):
    w = xconv.shape[1]
    at = lambda i: first + chunks - 1 - i
    local = lambda i: chunks - 1 - i
    return call(
        functools.partial(scan_backward, len(kept)),
        chunks,
        (xdbl, xconv, dy, dtp, vec, rate, starts, carry, *sums, *kept),
        [
            chunk_of(XW, at),
            rows_of(w, at),
            rows_of(w, at),
            whole(RANK, w),
            whole(8, w),
            whole(NSTATE, w),
            pl.BlockSpec((1, NSTATE, w), lambda i: (at(i), 0, 0)),
            whole(NSTATE, w),
            whole(NSTATE, w),
            whole(8, w),
            whole(RANK, w),
        ]
        + [ANY] * len(kept),
        (shaped(XW, chunks * CH), shaped(SEQ, w), shaped(NSTATE, w), shaped(8, w), shaped(RANK, w), shaped(NSTATE, w)),
        (lanes_of(XW, local), rows_of(w, at), whole(NSTATE, w), whole(8, w), whole(RANK, w), whole(NSTATE, w)),
        backward_scratch(w),
        11 * chunks,
        {11 + k: 1 + k for k in range(len(kept))},
    )


def run_conv_backward(first, chunks, inner, inv, tail, conv, xproj, dxc, dxdbl, follow, sums, kept=()):
    w = inner.shape[1]
    at = lambda i: first + chunks - 1 - i
    before = lambda i: (jnp.maximum(at(i) * (CH // 8) - 1, 0), 0)
    return call(
        functools.partial(conv_backward, len(kept), chunks, first),
        chunks,
        (inner, inner, inv, inv, tail, conv, xproj, dxc, dxdbl, follow, *sums, *kept),
        [
            rows_of(w, at),
            pl.BlockSpec((8, w), before),
            rows_of(1, at),
            pl.BlockSpec((8, 1), before),
            whole(8, w),
            whole(8, w),
            whole(XW, w),
            rows_of(w, at),
            chunk_of(XW, at),
            whole(8, w),
            whole(8, w),
            whole(XW, w),
        ]
        + [ANY] * len(kept),
        (shaped(SEQ, w, dtype=bf16), shaped(SEQ, 1), shaped(8, w), shaped(XW, w), shaped(8, w)),
        (rows_of(w, at), rows_of(1, at), whole(8, w), whole(XW, w), whole(8, w)),
        [pltpu.VMEM((CH + 8, w), f32), pltpu.VMEM((CH + 8, w), f32)],
        2 * chunks,
        {12 + k: k for k in range(len(kept))},
    )


MESH = pl.DeviceIdType.MESH
BIG = 384
BIG_STEPS = SEQ // BIG
SLOTS = 4


def remote(src, dst, send, recv, device):
    return pltpu.make_async_remote_copy(src_ref=src, dst_ref=dst, send_sem=send, recv_sem=recv, device_id=device, device_id_type=MESH)


def xor_bit(a, b):
    return a + b - 2 * a * b


def token_pieces(c, local):
    cut = local - LC
    low = cut - LC
    if c == 0:
        return [(0, local, 0, 0)]
    if c == 1:
        return [(0, cut, 0, local), (cut, local, 1, 0)]
    if c == 2:
        return [(0, local, 1, LC)]
    return [(0, low, 1, LC + local), (low, cut, 0, LP), (cut, local, 1, LP)]


class Gather:
    def __init__(self, weights, tokens, raw, w_send, w_recv, t_send, t_recv, here):
        g, r, c = lax.axis_index("grp"), lax.axis_index("row"), lax.axis_index("col")
        x, core = g // 2, g % 2
        self.g, self.r, self.c = g, r, c
        half = xor_bit(r, c % 2)
        self.firsts = ((g, r, 2 * half + c // 2), (g, 1 - r, 2 * (1 - half) + c // 2))
        self.alone = 2 * half + c // 2 == c
        self.ranks = (g, (1 - x) * 2 + core, x * 2 + 1 - core)
        self.x_dev, self.core_dev = (self.ranks[1], r, c), (self.ranks[2], r, c)
        self.y_dev, self.z_dev = (g, 1 - r, c), (g, r, c + 1 - 2 * (c % 2))
        self.weights, self.tokens, self.raw = weights, tokens, raw
        self.w_send, self.w_recv, self.t_send, self.t_recv, self.here = w_send, w_recv, t_send, t_recv, here

    def greet(self):
        barrier = pltpu.get_barrier_semaphore()
        for dr in range(2):
            for dc in range(4):
                if dr or dc:
                    device = (self.g, (self.r + dr) % 2, (self.c + dc) % 4)
                    pl.semaphore_signal(barrier, inc=1, device_id=device, device_id_type=MESH)
        for device in (self.x_dev, self.core_dev):
            pl.semaphore_signal(barrier, inc=1, device_id=device, device_id_type=MESH)
        pl.semaphore_wait(barrier, 9)

    def slot(self, n, k, d):
        if self.weights[n][2]:
            return (self.r if d == 0 else 1 - self.r) * 4 + self.ranks[k]
        return 2 * self.ranks[k] + d

    def first_hop(self, n, d):
        src, dst, by_row = self.weights[n]
        at = self.slot(n, 0, 0) if by_row else self.slot(n, 0, d)
        return remote(src, dst.at[at], self.w_send.at[n, d], self.w_recv.at[n, d], self.firsts[d])

    def at_home(self, n):
        src, dst, _ = self.weights[n]
        return pltpu.make_async_copy(src, dst.at[self.slot(n, 0, 0)], self.here.at[n])

    def hop(self, n, d, k, came):
        dst = self.weights[n][1]
        at = self.slot(n, k, d)
        i = (0, 2, 4, 6)[came] + d
        device = self.x_dev if came == 1 else self.core_dev
        return remote(dst.at[at], dst.at[at], self.w_send.at[n, i], self.w_recv.at[n, i], device)

    def begin(self, n):
        @pl.when(self.alone)
        def _():
            self.at_home(n).start()

        @pl.when(jnp.logical_not(self.alone))
        def _():
            self.first_hop(n, 0).start()

        self.first_hop(n, 1).start()

    def forward(self, n):
        for d in range(2):
            if d == 0:

                @pl.when(self.alone)
                def _():
                    self.at_home(n).wait()

                @pl.when(jnp.logical_not(self.alone))
                def _():
                    self.first_hop(n, 0).wait_recv()
            else:
                self.first_hop(n, 1).wait_recv()
            self.hop(n, d, 0, 1).start()
            self.hop(n, d, 0, 2).start()

    def forward_again(self, n):
        for d in range(2):
            self.hop(n, d, 0, 1).wait_recv()
            self.hop(n, d, 1, 3).start()

    def end(self, n):
        for d in range(2):
            self.hop(n, d, 0, 2).wait_recv()
            self.hop(n, d, 1, 3).wait_recv()
            self.hop(n, d, 0, 1).wait_send()
            self.hop(n, d, 0, 2).wait_send()
            self.hop(n, d, 1, 3).wait_send()

        @pl.when(jnp.logical_not(self.alone))
        def _():
            self.first_hop(n, 0).wait_send()

        self.first_hop(n, 1).wait_send()

    def ranges(self, k):
        local = self.tokens.shape[0]
        held = {0: (0, local), 1: (local, LP), 2: (LC, LC + local), 3: (LC + local, SEQ)}
        return held[k], held[k ^ 1], (LP, SEQ) if k < 2 else (0, LC)

    def part(self, d, rows):
        return self.raw.at[d, pl.ds(rows[0], rows[1] - rows[0])]

    def on_col(self, act):
        for k in range(4):

            @pl.when(self.c == k)
            def _(k=k):
                act(k)

    def sources(self, k, lo, hi):
        for a, b, s, at in token_pieces(k, self.tokens.shape[0]):
            first, end = max(lo, at), min(hi, at + b - a)
            if s == k // 2 and first < end:
                yield a + first - at, first, end

    def begin_half(self, h):
        def act(k):
            lo, hi = split(self.ranges(k)[0])[h]
            for src, first, end in self.sources(k, lo, hi):
                rows = self.tokens.at[pl.ds(src, end - first)]
                pltpu.make_async_copy(rows, self.part(0, (first, end)), self.here.at[2 + h]).start()
                remote(rows, self.part(1, (first, end)), self.t_send.at[h], self.t_recv.at[h], self.y_dev).start()
                remote(rows, self.part(0, (first, end)), self.t_send.at[2 + h], self.t_recv.at[2 + h], self.z_dev).start()

        self.on_col(act)

    def foreign_copies(self, k):
        copies = []
        for a, b, s, at in token_pieces(k, self.tokens.shape[0]):
            if s != k // 2:
                for dr in range(2):
                    for dc in range(2):
                        device = (self.g, self.r if dr == 0 else 1 - self.r, 2 * s + dc)
                        sems = self.t_send.at[6 + 2 * dr + dc], self.t_recv.at[6 + dr]
                        copies.append(remote(self.tokens.at[pl.ds(a, b - a)], self.part(dr, (at, at + b - a)), *sems, device))
        return copies

    def begin_foreign(self):
        def act(k):
            for copy in self.foreign_copies(k):
                copy.start()

        self.on_col(act)

    def relays(self, k):
        own, paired, _ = self.ranges(k)
        early, late = split(paired)[0], split(own)[1]
        return (
            remote(self.part(0, early), self.part(1, early), self.t_send.at[4], self.t_recv.at[4], self.y_dev),
            remote(self.part(1, late), self.part(1, late), self.t_send.at[5], self.t_recv.at[5], self.z_dev),
        )

    def settle(self, d, rows, sem):
        pltpu.make_async_copy(self.part(d, rows), self.part(d, rows), sem).wait()

    def relay(self):
        def act(k):
            own, paired, _ = self.ranges(k)
            by_y, by_z = self.relays(k)
            self.settle(0, split(paired)[0], self.t_recv.at[2])
            by_y.start()
            self.settle(1, split(own)[1], self.t_recv.at[1])
            by_z.start()

        self.on_col(act)

    def end_tokens(self):
        def act(k):
            own, paired, foreign = self.ranges(k)
            own, paired = split(own), split(paired)
            by_y, by_z = self.relays(k)
            self.settle(1, own[0], self.t_recv.at[0])
            self.settle(0, paired[1], self.t_recv.at[3])
            self.settle(1, paired[0], self.t_recv.at[4])
            self.settle(1, paired[1], self.t_recv.at[5])
            self.settle(0, foreign, self.t_recv.at[6])
            self.settle(1, foreign, self.t_recv.at[7])
            for h in range(2):
                self.settle(0, own[h], self.here.at[2 + h])
                self.settle(0, own[h], self.t_send.at[h])
                self.settle(0, own[h], self.t_send.at[2 + h])
            by_y.wait_send()
            by_z.wait_send()
            for copy in self.foreign_copies(k):
                copy.wait_send()

        self.on_col(act)


def split(rows):
    lo, hi = rows
    mid = lo + (hi - lo) // 2
    return (lo, mid), (mid, hi)


def gather_semaphores():
    return [pltpu.SemaphoreType.DMA(shape) for shape in ((2, 8), (2, 8), (10,), (8,), (4,))]


def gather_start(tokens, in_i, small, raw, wi, small_all, *sems):
    gather = Gather([(small, small_all, True), (in_i, wi, False)], tokens, raw, *sems)
    gather.greet()
    gather.begin(0)
    gather.begin(1)
    gather.begin_half(0)
    gather.begin_half(1)
    gather.begin_foreign()
    for n in range(2):
        gather.forward(n)
    gather.relay()
    for n in range(2):
        gather.forward_again(n)
    gather.end_tokens()
    for n in range(2):
        gather.end(n)


def run_gather_start(tokens, in_i, small):
    width = tokens.shape[1]
    return pl.pallas_call(
        gather_start,
        in_specs=[ANY] * 3,
        out_specs=[ANY] * 3,
        out_shape=(
            shaped(2, SEQ, width, dtype=bf16),
            shaped(8, *in_i.shape, dtype=bf16),
            shaped(8, *small.shape, dtype=bf16),
        ),
        scratch_shapes=gather_semaphores(),
        compiler_params=pltpu.CompilerParams(collective_id=0, has_side_effects=True, vmem_limit_bytes=VMEM_LIMIT),
    )(tokens, in_i, small)


LAG = 4
FIRST = BIG_STEPS
SECOND = FIRST + NCH
LAST = SECOND + NCH - 1
BEGIN = (0, SECOND)
FORWARD = (FIRST + 8, SECOND + 5)
FORWARD_AGAIN = (SECOND + 3, LAST)
HALVES = (FIRST + 6, SECOND + 1)
FOREIGN = SECOND + 2
RELAY = SECOND + 6


def pack_sum(ref, k, v):
    high = v[RANK:].astype(bf16)
    ref[k, :RANK] = v[:RANK].astype(bf16)
    ref[k, RANK:XW] = high
    ref[k, XW:] = (v[RANK:] - high.astype(f32)).astype(bf16)


def unpack_sum(ref, k):
    return jnp.concatenate([ref[k, :RANK].astype(f32), ref[k, RANK:XW].astype(f32) + ref[k, XW:].astype(f32)], axis=0)


def forward(raw_ref, gain_ref, wi_ref, mix_ref, conv_ref, xproj_ref, dtp_ref, vec_ref, rate_ref, in_g, out_w, cot_in,
            normed_ref, inv_ref, inner_ref, xconv_ref, yfull_ref, starts_ref, xdbl_ref, joined_ref, wg, wo, cot,
            inner_s, inv_s, buf, xc_s, part, ys, yr, zs, zr, tail_s, tail_r, state, last, last_r,
            dt_s, u_s, cb_s, h_s, y_s, y_send, y_recv, z_send, z_recv, e_send, e_recv, *sems):
    i = pl.program_id(0)
    gather = Gather([(in_g, wg, False), (out_w, wo, False)], cot_in, cot, *sems)
    g, r, c = gather.g, gather.r, gather.c
    y_dev, z_dev = gather.y_dev, gather.z_dev
    far_dev = (g, 1 - r, (c + 2) % 4)
    to_tail = remote(tail_s, tail_r, e_send.at[0], e_recv.at[0], far_dev)
    to_last = remote(last, last_r, e_send.at[1], e_recv.at[1], far_dev)

    def to_y(k):
        return remote(ys.at[k], yr.at[k], y_send.at[k], y_recv.at[k], y_dev)

    def to_z(k):
        return remote(zs.at[k], zr.at[k], z_send.at[k], z_recv.at[k], z_dev)

    @pl.when(i == 0)
    def _():
        gather.greet()

    @pl.when(i < FIRST)
    def _():
        rows = pl.ds(pl.multiple_of(i * BIG, BIG), BIG)
        project_first(raw_ref, gain_ref, wi_ref, normed_ref, inv_ref, inner_ref)
        inner_s[rows, :] = inner_ref[...]
        inv_s[rows, :] = inv_ref[...]

    @pl.when(i == FIRST)
    def _():
        tail_s[...] = inv_s[LP - 8 : LP] * inner_s[LP - 8 : LP]
        to_tail.start()
        buf[0:8] = jnp.zeros_like(buf[0:8])
        state[...] = jnp.zeros_like(state)

    mix = mix_ref[...]

    @pl.when(i == FIRST + PC)
    def _():
        to_tail.wait()
        joined = mix * tail_s[...] + (1.0 - mix) * tail_r[...]
        buf[0:8] = joined
        joined_ref[...] = joined

    @pl.when((i > FIRST) & (i < FIRST + PC))
    def _():
        buf[0:8] = buf[CH : CH + 8]

    @pl.when((i >= FIRST) & (i < SECOND))
    def _():
        k = i - FIRST
        rows = pl.ds(pl.multiple_of(k * CH, CH), CH)
        buf[8 : CH + 8] = inv_s[rows, :] * inner_s[rows, :]
        out = conv_ref[4:5]
        for tap in range(KCONV):
            out = out + conv_ref[tap : tap + 1] * buf[5 + tap : 5 + tap + CH]
        xconv = (out * jax.nn.sigmoid(out)).astype(bf16)
        xconv_ref[...] = xconv
        xc_s[k] = xconv
        part[k] = dot_nt(xproj_ref[...], xconv)
        pack_sum(ys, k, part[k])
        to_y(k).start()

    @pl.when((i >= FIRST + LAG) & (i < SECOND + LAG))
    def _():
        k = i - FIRST - LAG
        to_y(k).wait_recv()
        part[k] = part[k] + unpack_sum(yr, k)
        pack_sum(zs, k, part[k])
        to_z(k).start()

    @pl.when((i >= FIRST + 2 * LAG) & (i < SECOND + 2 * LAG))
    def _():
        k = i - FIRST - 2 * LAG
        to_z(k).wait_recv()
        xdbl_ref[k] = part[k] + unpack_sum(zr, k)

    for n in range(2):

        @pl.when(i == BEGIN[n])
        def _(n=n):
            gather.begin(n)

        @pl.when(i == FORWARD[n])
        def _(n=n):
            gather.forward(n)

        @pl.when(i == FORWARD_AGAIN[n])
        def _(n=n):
            gather.forward_again(n)

    for h in range(2):

        @pl.when(i == HALVES[h])
        def _(h=h):
            gather.begin_half(h)

    @pl.when(i == FOREIGN)
    def _():
        gather.begin_foreign()

    @pl.when(i == RELAY)
    def _():
        gather.relay()

    @pl.when(i == LAST)
    def _():
        to_last.wait()
        state[...] = mix_ref[0:1] * last[...] + (1.0 - mix_ref[0:1]) * last_r[...]

    @pl.when(i >= SECOND)
    def _():
        k = i - SECOND
        starts_ref[0] = state[...]
        h, yfull = scan_chunk(xdbl_ref.at[k], xc_s[k].astype(f32), dtp_ref, vec_ref, rate_ref, state[...], dt_s, u_s, cb_s, h_s, y_s)
        state[...] = h
        yfull_ref[...] = yfull.astype(bf16)

    @pl.when(i == LAST - 1)
    def _():
        last[...] = state[...]
        to_last.start()

    @pl.when(i == LAST)
    def _():
        gather.end_tokens()
        gather.end(0)
        gather.end(1)

        def sent(k, _):
            to_y(k).wait_send()
            to_z(k).wait_send()
            return 0

        lax.fori_loop(0, NCH, sent, 0)


def run_forward(raw, gain, wi, mix, conv, xproj, dtp, vec, rate, in_g, out_w, cot):
    w = SLOTS * wi.shape[2]
    width = raw.shape[2]
    zero = lambda i: jnp.minimum(i, FIRST - 1)
    first = lambda i: jnp.clip(i - FIRST, 0, NCH - 1)
    second = lambda i: jnp.maximum(i - SECOND, 0)
    dma = pltpu.SemaphoreType.DMA
    sums = pltpu.VMEM((NCH, XW + 2 * NSTATE, CH), bf16)
    return pl.pallas_call(
        forward,
        grid=(LAST + 1,),
        in_specs=[
            split_rows(width, zero, BIG),
            whole(2, width),
            whole(*wi.shape),
            whole(8, w),
            whole(8, w),
            whole(XW, w),
            whole(RANK, w),
            whole(8, w),
            whole(NSTATE, w),
            ANY,
            ANY,
            ANY,
        ],
        out_specs=(
            split_rows(width, zero, BIG),
            rows_of(1, zero, BIG),
            rows_of(w, zero, BIG),
            rows_of(w, first),
            rows_of(w, second),
            pl.BlockSpec((1, NSTATE, w), lambda i: (second(i), 0, 0)),
            whole(NCH, XW, CH),
            whole(8, w),
            ANY,
            ANY,
            ANY,
        ),
        out_shape=(
            shaped(2, SEQ, width, dtype=bf16),
            shaped(SEQ, 1),
            shaped(SEQ, w),
            shaped(SEQ, w, dtype=bf16),
            shaped(SEQ, w, dtype=bf16),
            shaped(NCH, NSTATE, w),
            shaped(NCH, XW, CH),
            shaped(8, w),
            shaped(8, *in_g.shape, dtype=bf16),
            shaped(8, *out_w.shape, dtype=bf16),
            shaped(2, SEQ, cot.shape[1], dtype=bf16),
        ),
        scratch_shapes=[
            pltpu.VMEM((SEQ, w), f32),
            pltpu.VMEM((SEQ, 1), f32),
            pltpu.VMEM((CH + 8, w), f32),
            pltpu.VMEM((NCH, CH, w), bf16),
            pltpu.VMEM((NCH, XW, CH), f32),
            sums,
            sums,
            sums,
            sums,
            pltpu.VMEM((8, w), f32),
            pltpu.VMEM((8, w), f32),
            pltpu.VMEM((NSTATE, w), f32),
            pltpu.VMEM((NSTATE, w), f32),
            pltpu.VMEM((NSTATE, w), f32),
            *scan_scratch(w),
            dma((NCH,)),
            dma((NCH,)),
            dma((NCH,)),
            dma((NCH,)),
            dma((2,)),
            dma((2,)),
            *gather_semaphores(),
        ],
        compiler_params=pltpu.CompilerParams(
            dimension_semantics=("arbitrary",), collective_id=2, has_side_effects=True, vmem_limit_bytes=VMEM_LIMIT
        ),
        cost_estimate=pl.CostEstimate(flops=60 * 1000000000, bytes_accessed=1000000, transcendentals=0),
    )(raw, gain, wi, mix, conv, xproj, dtp, vec, rate, in_g, out_w, cot)


def project_first(raw_ref, gain_ref, w_ref, normed_ref, inv_ref, out_ref):
    low = raw_ref[0].astype(f32)
    high = raw_ref[1].astype(f32)
    squares = jnp.sum(low * low + high * high, axis=1, keepdims=True)
    inv_ref[...] = lax.rsqrt(squares / D + eps)
    low = (low * gain_ref[0:1]).astype(bf16)
    high = (high * gain_ref[1:2]).astype(bf16)
    normed_ref[0] = low
    normed_ref[1] = high
    n = w_ref.shape[2]
    for k in range(SLOTS):
        out_ref[:, k * n : (k + 1) * n] = dot_nn(low, w_ref[2 * k]) + dot_nn(high, w_ref[2 * k + 1])


def split_rows(width, at, tall=CH):
    return pl.BlockSpec((2, tall, width), lambda i: (0, at(i), 0))


def run_project_first(raw, gain, w):
    width = raw.shape[2]
    at = lambda i: i
    n = SLOTS * w.shape[2]
    return call(
        project_first,
        BIG_STEPS,
        (raw, gain, w),
        [split_rows(width, at, BIG), whole(2, width), whole(*w.shape)],
        (shaped(2, SEQ, width, dtype=bf16), shaped(SEQ, 1), shaped(SEQ, n)),
        (split_rows(width, at, BIG), rows_of(1, at, BIG), rows_of(n, at, BIG)),
        [],
        9,
    )


def gate_backward(normed_ref, wg_ref, cot_ref, wo_ref, yfull_ref, inv_ref, gated_ref, dy_ref, dproj_ref, dscale_ref, own_ref, oth_ref, gate_s):
    n = wo_ref.shape[2]
    for k in range(SLOTS):
        gate_s[:, k * n : (k + 1) * n] = dot_nn(normed_ref[0], wg_ref[2 * k]) + dot_nn(normed_ref[1], wg_ref[2 * k + 1])
    d_gated = jnp.zeros(dy_ref.shape, f32)
    for k in range(SLOTS):
        for d in range(2):
            d_gated = d_gated + dot_nt(cot_ref[d, :, k * n : (k + 1) * n], wo_ref[2 * k + d])
    gate_in = gate_s[...]
    inv = inv_ref[...]
    yfull = yfull_ref[...].astype(f32)
    gate = inv * gate_in
    sig = jax.nn.sigmoid(gate)
    passed = gate * sig
    gated = (yfull * passed).astype(bf16)
    gated_ref[...] = gated
    for k in range(SLOTS):
        own_ref[:, k * n : (k + 1) * n] = dot_nn(gated, wo_ref[2 * k])
        oth_ref[:, k * n : (k + 1) * n] = dot_nn(gated, wo_ref[2 * k + 1]).astype(bf16)
    dy_ref[...] = d_gated * passed
    d_gate = d_gated * yfull * (sig * (1.0 + gate * (1.0 - sig)))
    dproj_ref[...] = (inv * d_gate).astype(bf16)
    dscale_ref[...] = jnp.sum(d_gate * gate_in, axis=1, keepdims=True)


def run_gate_backward(normed, wg, cot, wo, yfull, inv):
    width = cot.shape[2]
    w = yfull.shape[1]
    at = lambda i: i
    return call(
        gate_backward,
        BIG_STEPS,
        (normed, wg, cot, wo, yfull, inv),
        [split_rows(width, at, BIG), whole(*wg.shape), split_rows(width, at, BIG), whole(*wo.shape), rows_of(w, at, BIG), rows_of(1, at, BIG)],
        (shaped(SEQ, w, dtype=bf16), shaped(SEQ, w), shaped(SEQ, w, dtype=bf16), shaped(SEQ, 1), shaped(SEQ, width), shaped(SEQ, width, dtype=bf16)),
        (rows_of(w, at, BIG), rows_of(w, at, BIG), rows_of(w, at, BIG), rows_of(1, at, BIG), rows_of(width, at, BIG), rows_of(width, at, BIG)),
        [pltpu.VMEM((BIG, w), f32)],
        22,
    )


def normed_backward(inner_ref, gate_ref, wi_ref, wg_ref, own_ref, oth_ref):
    n = wi_ref.shape[2]
    for d, out_ref in ((1, oth_ref), (0, own_ref)):
        total = jnp.zeros(out_ref.shape, f32)
        for k in range(SLOTS):
            total = total + dot_nt(inner_ref[:, k * n : (k + 1) * n], wi_ref[2 * k + d])
            total = total + dot_nt(gate_ref[:, k * n : (k + 1) * n], wg_ref[2 * k + d])
        out_ref[...] = total.astype(out_ref.dtype)


def run_normed_backward(d_inner, d_gate, wi, wg):
    w = d_inner.shape[1]
    width = wi.shape[1]
    at = lambda i: i
    return call(
        normed_backward,
        BIG_STEPS,
        (d_inner, d_gate, wi, wg),
        [rows_of(w, at, BIG), rows_of(w, at, BIG), whole(*wi.shape), whole(*wg.shape)],
        (shaped(SEQ, width), shaped(SEQ, width, dtype=bf16)),
        (rows_of(width, at, BIG), rows_of(width, at, BIG)),
        [],
        12,
    )


def finish(inner_hbm, gate_hbm, normed_hbm, raw_hbm, wi_hbm, wg_hbm, gain_in_ref, pull_ref, conv_hbm, scan_hbm, alog_hbm, dtp_hbm, xproj_hbm,
           dn_ref, grad_ref, gain_ref, small_ref,
           inner, gate, normed, raw, wi, wg, cs, cr, pairs, xs, xr, fs, fr, ys, yr, zs, zr, own, fin, gs, gr, sv, sr,
           loc, c_send, c_recv, x_send, x_recv, f_send, f_recv, y_send, y_recv, z_send, z_recv, b_send, b_recv, g_send, g_recv, s_send, s_recv, s_load):
    g, r, c = lax.axis_index("grp"), lax.axis_index("row"), lax.axis_index("col")
    x, core, s, p = g // 2, g % 2, c // 2, c % 2
    tall, width = raw.shape
    part = tall // 2
    n = wi_hbm.shape[2]
    q = 2 * p + xor_bit(r, s)
    y_dev, z_dev = (g, 1 - r, c), (g, r, 2 * s + 1 - p)
    x_dev, core_dev = ((1 - x) * 2 + core, r, c), (2 * x + 1 - core, r, c)
    alone = q == c

    loads = [
        pltpu.make_async_copy(normed_hbm, normed, loc.at[0]),
        pltpu.make_async_copy(inner_hbm, inner, loc.at[1]),
        pltpu.make_async_copy(gate_hbm, gate, loc.at[2]),
        pltpu.make_async_copy(raw_hbm.at[0, pl.ds(pl.multiple_of(p * tall, 64), tall)], raw, loc.at[5]),
    ]
    for copy in loads[:3]:
        copy.start()
    for k in range(SLOTS):
        for d in range(2):
            cols = pl.ds(k * n, n)
            pltpu.make_async_copy(wi_hbm.at[2 * k + d], wi.at[d, :, cols], loc.at[3]).start()
            pltpu.make_async_copy(wg_hbm.at[2 * k + d], wg.at[d, :, cols], loc.at[4]).start()
    loads[3].start()

    barrier = pltpu.get_barrier_semaphore()
    for dg in range(4):
        for dr in range(2):
            for dc in range(4):
                if dg or dr or dc:
                    device = ((g + dg) % 4, (r + dr) % 2, (c + dc) % 4)
                    pl.semaphore_signal(barrier, inc=1, device_id=device, device_id_type=MESH)
    pl.semaphore_wait(barrier, 31)

    def small_loads():
        at = 0
        for ref in (conv_hbm, scan_hbm, alog_hbm, dtp_hbm, xproj_hbm):
            yield pltpu.make_async_copy(ref, sv.at[pl.ds(at, ref.shape[0])], s_load.at[0])
            at += ref.shape[0]

    def to_small(dg, dr):
        to_g, to_r = (g + dg) % 4, (r + dr) % 2
        cols = pl.ds(pl.multiple_of((to_r * 4 + to_g) * 128, 128), 128)
        src, dst = sv.at[:, cols], sr.at[g * 2 + s]
        return src, dst, remote(src, dst, s_send.at[2 * dg + dr], s_recv.at[0], (to_g, to_r, q))

    owners = [(dg, dr) for dg in range(4) for dr in range(2)]
    for copy in small_loads():
        copy.start()

    def weight_grad(at_x, d):
        cols = pl.ds(pl.multiple_of(at_x * 2 * n, 128), 2 * n)

        def tile(t, _):
            rows = pl.ds(pl.multiple_of(t * n, 128), n)
            pairs[d, rows, :] = dot_tn(normed[d, :, rows], inner[:, cols])
            return 0

        lax.fori_loop(0, width // n, tile, 0)

    def of_core(at_core):
        return pl.ds(pl.multiple_of(at_core * n, 128), n)

    def to_core(i, d):
        return remote(cs.at[i, d], cr.at[i, d], c_send.at[2 * i + d], c_recv.at[2 * i + d], core_dev)

    def to_x(d):
        return remote(xs.at[d], xr.at[d], x_send.at[d], x_recv.at[d], x_dev)

    def to_owner(d):
        return remote(fs.at[d], fr.at[d], f_send.at[d], f_recv.at[d], (g, r if d == 0 else 1 - r, q))

    def grad_to_core(i):
        for d in range(2):
            weight_grad(1 - x if i == 0 else x, d)
            cs[i, d] = pairs[d, :, of_core(1 - core)].astype(bf16)
            to_core(i, d).start()

    def start_of(mine, h):
        return pl.multiple_of((p if mine else 1 - p) * tall + h * part, 32)

    def normed_part(mine, h, d, store):
        rows = pl.ds(start_of(mine, h), part)

        def tile(t, _):
            cols = pl.ds(pl.multiple_of(t * n, 128), n)
            total = dot_nt(inner[rows, :], wi[d, cols, :]) + dot_nt(gate[rows, :], wg[d, cols, :])
            store(cols, total)
            return 0

        lax.fori_loop(0, width // n, tile, 0)

    def to_y(i):
        return remote(ys.at[i], yr.at[i], y_send.at[i], y_recv.at[i], y_dev)

    def to_z(i):
        return remote(zs.at[i], zr.at[i], z_send.at[i], z_recv.at[i], z_dev)

    def into(ref, i, added=None):
        def store(cols, v):
            if added is not None:
                v = v + added[0, :, cols].astype(f32)
            ref[i, :, cols] = v.astype(bf16)

        return store

    loads[0].wait()
    loads[1].wait()
    grad_to_core(0)
    loads[2].wait()
    pltpu.make_async_copy(wi, wi, loc.at[3]).wait()
    pltpu.make_async_copy(wg, wg, loc.at[4]).wait()
    for d in range(2):
        to_core(0, d).wait_recv()
        xs[d] = (pairs[d, :, of_core(core)] + cr[0, d].astype(f32)).astype(bf16)
        to_x(d).start()

    pltpu.make_async_copy(sv, sv, s_load.at[0]).wait()
    for dg, dr in owners:
        src, dst, copy = to_small(dg, dr)
        if dg or dr:
            copy.start()
        else:

            @pl.when(alone)
            def _(src=src, dst=dst):
                pltpu.make_async_copy(src, dst, s_load.at[1]).start()

            @pl.when(jnp.logical_not(alone))
            def _(copy=copy):
                copy.start()

    normed_part(False, 0, 1, into(ys, 0))
    to_y(0).start()
    normed_part(False, 1, 1, into(zs, 0))
    to_z(0).start()
    normed_part(False, 1, 0, into(zs, 2))
    to_z(2).start()
    normed_part(True, 0, 1, into(ys, 1))
    to_y(1).start()
    grad_to_core(1)
    to_y(0).wait_recv()
    normed_part(False, 0, 0, into(zs, 1, yr))
    to_z(1).start()
    to_z(0).wait_recv()
    normed_part(True, 1, 1, into(ys, 2, zr))
    to_y(2).start()

    for d in range(2):
        to_core(1, d).wait_recv()
        to_x(d).wait_recv()
        fs[d] = (pairs[d, :, of_core(core)] + cr[1, d].astype(f32) + xr[d].astype(f32)).astype(bf16)
        if d == 0:

            @pl.when(alone)
            def _():
                fr[0] = fs[0]

            @pl.when(jnp.logical_not(alone))
            def _():
                to_owner(0).start()
        else:
            to_owner(1).start()

    for h in range(2):

        def store(cols, v, h=h):
            own[h * part : (h + 1) * part, cols] = v

        normed_part(True, h, 0, store)

    loads[3].wait()
    for h in range(2):
        to_y(1 + h).wait_recv()
        to_z(1 + h).wait_recv()
        total = own[h * part : (h + 1) * part, :] + yr[1 + h].astype(f32) + zr[1 + h].astype(f32)
        tokens = raw[h * part : (h + 1) * part, :].astype(f32)
        pulled = total * gain_in_ref[0:1] - pull_ref[h * part : (h + 1) * part, :] * tokens
        fin[h * part : (h + 1) * part, :] = pulled.astype(bf16)
        product = total * tokens
        folded = jnp.sum(product.reshape(part // 8, 8, width), axis=0)
        for b in range(SLOTS):
            if h == 0:
                gs[b] = folded[:, b * n : (b + 1) * n]
            else:
                gs[b] = gs[b] + folded[:, b * n : (b + 1) * n]

    cut = tall - LC
    low = cut - LC
    moves = {
        0: ([(0, tall, 0)], None),
        1: ([(0, cut, 0)], (cut, 3, low)),
        2: ([(LC, tall, 0)], (0, 1, cut)),
        3: ([(LC, cut, 0), (cut, tall, cut)], (0, 2, cut)),
    }

    def border(k):
        stays, leaves = moves[k]
        mine = [pltpu.make_async_copy(fin.at[a:b], dn_ref.at[at : at + b - a], loc.at[i]) for i, (a, b, at) in enumerate(stays)]
        if leaves is None:
            return mine, None
        a, to, at = leaves
        return mine, remote(fin.at[a : a + LC], dn_ref.at[at : at + LC], b_send.at[0], b_recv.at[0], (g, r, to))

    for k in range(4):

        @pl.when(c == k)
        def _(k=k):
            mine, gone = border(k)
            if gone is not None:
                gone.start()
            for copy in mine:
                copy.start()

    def gain_copy(dg, dc):
        to = ((g + dg) % 4, r, (c + dc) % 4)
        i = 4 * dg + dc - 1
        return remote(gs.at[(g + dg) % 4], gr.at[i], g_send.at[i], g_recv.at[0], to)

    pairs = [(dg, dc) for dg in range(4) for dc in range(4) if dg or dc]
    for dg, dc in pairs:
        gain_copy(dg, dc).start()

    @pl.when(jnp.logical_not(alone))
    def _():
        to_owner(0).wait_recv()

    to_owner(1).wait_recv()
    grad_ref[...] = fr[0].astype(f32) + fr[1].astype(f32)

    pltpu.make_async_copy(gr, gr, g_recv.at[0]).wait()
    gain_ref[...] = jnp.sum(gr[...], axis=0) + gs[g]

    for k in range(4):

        @pl.when(c == k)
        def _(k=k):
            mine, gone = border(k)
            for copy in mine:
                copy.wait()
            if gone is not None:
                gone.wait()

    @pl.when(alone)
    def _():
        src, dst, _ = to_small(0, 0)
        pltpu.make_async_copy(src, dst, s_load.at[1]).wait()
        most = sr.at[pl.ds(0, 7)]
        pltpu.make_async_copy(most, most, s_recv.at[0]).wait()

    @pl.when(jnp.logical_not(alone))
    def _():
        pltpu.make_async_copy(sr, sr, s_recv.at[0]).wait()

    small_ref[...] = jnp.sum(sr[...], axis=0)
    for dg, dr in owners:
        if dg or dr:
            to_small(dg, dr)[2].wait_send()
        else:

            @pl.when(jnp.logical_not(alone))
            def _():
                to_small(0, 0)[2].wait_send()

    for dg, dc in pairs:
        gain_copy(dg, dc).wait_send()
    for i in range(3):
        to_y(i).wait_send()
        to_z(i).wait_send()
    for d in range(2):
        for i in range(2):
            to_core(i, d).wait_send()
        to_x(d).wait_send()

    @pl.when(jnp.logical_not(alone))
    def _():
        to_owner(0).wait_send()

    to_owner(1).wait_send()


def run_finish(d_inner, d_gate, normed, raw, wi, wg, gain, pull, small):
    w = d_inner.shape[1]
    width, n = wi.shape[1], wi.shape[2]
    tall = SEQ // 2
    part = tall // 2
    dma = pltpu.SemaphoreType.DMA
    low = lambda *shape: pltpu.VMEM(shape, bf16)
    vmem = pl.BlockSpec(memory_space=pltpu.VMEM)
    rows = sum(v.shape[0] for v in small)
    return pl.pallas_call(
        finish,
        in_specs=[ANY] * 6 + [vmem, vmem] + [ANY] * 5,
        out_specs=[ANY, vmem, vmem, vmem],
        out_shape=(shaped(tall, width, dtype=bf16), shaped(width, n), shaped(8, n), shaped(rows, 128)),
        scratch_shapes=[
            low(SEQ, w),
            low(SEQ, w),
            low(2, SEQ, width),
            low(tall, width),
            low(2, width, w),
            low(2, width, w),
            low(2, 2, width, n),
            low(2, 2, width, n),
            pltpu.VMEM((2, width, 2 * n), f32),
            low(2, width, n),
            low(2, width, n),
            low(2, width, n),
            low(2, width, n),
            low(3, part, width),
            low(3, part, width),
            low(3, part, width),
            low(3, part, width),
            pltpu.VMEM((tall, width), f32),
            low(tall, width),
            pltpu.VMEM((SLOTS, 8, n), f32),
            pltpu.VMEM((15, 8, n), f32),
            pltpu.VMEM((rows, w), f32),
            pltpu.VMEM((8, rows, 128), f32),
            dma((6,)),
            dma((4,)),
            dma((4,)),
            dma((2,)),
            dma((2,)),
            dma((2,)),
            dma((2,)),
            dma((3,)),
            dma((3,)),
            dma((3,)),
            dma((3,)),
            dma((1,)),
            dma((1,)),
            dma((15,)),
            dma((1,)),
            dma((8,)),
            dma((1,)),
            dma((2,)),
        ],
        compiler_params=pltpu.CompilerParams(collective_id=1, has_side_effects=True, vmem_limit_bytes=VMEM_LIMIT),
        cost_estimate=pl.CostEstimate(flops=60 * 1000000000, bytes_accessed=1000000, transcendentals=0),
    )(d_inner, d_gate, normed, raw, wi, wg, gain, pull, *small)


def late_parts(order_ref, normed_ref, gate_ref, gated_ref, cot_ref, gate_sent, out_sent, gate_kept, out_kept):
    t = pl.program_id(0)
    for d in range(2):
        low = dot_tn(normed_ref[d], gate_ref[...])
        high = dot_tn(gated_ref[...], cot_ref[d])

        @pl.when(t < 2)
        def _(d=d, low=low, high=high):
            gate_sent[0, d] = low.astype(bf16)
            out_sent[0, d] = high.astype(bf16)

        @pl.when(t >= 2)
        def _(d=d, low=low, high=high):
            gate_kept[0, d] = low
            out_kept[0, d] = high


def run_late_parts(order, normed, d_gate, gated, cot):
    width = normed.shape[2]
    w = gated.shape[1]
    n = w // SLOTS
    sent = pl.BlockSpec((1, 2, width, n), lambda t, o: (jnp.minimum(t, 1), 0, 0, 0))
    kept = pl.BlockSpec((1, 2, width, n), lambda t, o: (jnp.maximum(t - 2, 0), 0, 0, 0))
    return pl.pallas_call(
        late_parts,
        grid_spec=pltpu.PrefetchScalarGridSpec(
            num_scalar_prefetch=1,
            grid=(SLOTS,),
            in_specs=[
                pl.BlockSpec((2, SEQ, width), lambda t, o: (0, 0, 0)),
                pl.BlockSpec((SEQ, n), lambda t, o: (0, o[t])),
                pl.BlockSpec((SEQ, w), lambda t, o: (0, 0)),
                pl.BlockSpec((2, SEQ, n), lambda t, o: (0, 0, o[t])),
            ],
            out_specs=(sent, sent, kept, kept),
        ),
        out_shape=(shaped(2, 2, width, n, dtype=bf16), shaped(2, 2, width, n, dtype=bf16), shaped(2, 2, width, n), shaped(2, 2, width, n)),
        compiler_params=pltpu.CompilerParams(dimension_semantics=("arbitrary",), vmem_limit_bytes=VMEM_LIMIT),
        cost_estimate=pl.CostEstimate(flops=14 * 1000000000, bytes_accessed=1000000, transcendentals=0),
    )(order, normed, d_gate, gated, cot)


QUARTERS = 4
SUM_LAG = 3
PIECE = SEQ // 2 // QUARTERS
OTHER_STEP = (1, 2, 3, 4)
PAIR_STEP = (3, 4, 1, 2)
FINAL_STEP = (7, 7, 7, 7)
X_STEP = (0, 1)
OWNER_STEP = (2, 4)
DONE_STEP = (8, 8)
QUARTER_STEP = ((2, 3, 4, 5), (4, 5, 6, 7))


def border_moves(tall):
    cut = tall - LC
    low = cut - LC
    return {
        0: ([(0, tall, 0)], None),
        1: ([(0, cut, 0)], (cut, 3, low)),
        2: ([(LC, tall, 0)], (0, 1, cut)),
        3: ([(LC, cut, 0), (cut, tall, cut)], (0, 2, cut)),
    }


def backward(xdbl_ref, xconv_ref, dy_ref, dtp_ref, vec_ref, rate_ref, starts_ref, mix_ref, into_ref, sent_hbm, kept_hbm, own_hbm, oth_hbm,
             dxdbl_ref, dxc_ref, alog_ref, sums_ref, dtpg_ref, grad_ref, branch_ref,
             first, first_s, first_r, part, ys, yr, zs, zr, cr, kp, xs, xr, fs, fr, out, own, oth, by_s, by, bz_s, bz, fin,
             y_send, y_recv, z_send, z_recv, e_send, e_recv, c_send, c_recv, x_send, x_recv, f_send, f_recv,
             p_send, p_recv, q_send, q_recv, b_send, b_recv, load_k, load_o, stay, put, *scratch):
    i = pl.program_id(0)
    g, r, c = lax.axis_index("grp"), lax.axis_index("row"), lax.axis_index("col")
    x, core, s, p = g // 2, g % 2, c // 2, c % 2
    q = 2 * p + xor_bit(r, s)
    tall = SEQ // 2
    alone = q == c
    y_dev, z_dev, far_dev = (g, 1 - r, c), (g, r, 2 * s + 1 - p), (g, 1 - r, (c + 2) % 4)
    x_dev, core_dev = ((1 - x) * 2 + core, r, c), (2 * x + 1 - core, r, c)
    to_first = remote(first_s, first_r, e_send.at[0], e_recv.at[0], far_dev)

    def to_y(k):
        return remote(ys.at[k], yr.at[k], y_send.at[k], y_recv.at[k], y_dev)

    def to_z(k):
        return remote(zs.at[k], zr.at[k], z_send.at[k], z_recv.at[k], z_dev)

    def to_core(n, j):
        return remote(sent_hbm[n].at[j], cr.at[n, j], c_send.at[n, j], c_recv.at[n, j], core_dev)

    def load(n, j):
        return pltpu.make_async_copy(kept_hbm[n].at[j], kp.at[n], load_k.at[n])

    def to_x(n):
        return remote(xs.at[n], xr.at[n], x_send.at[n], x_recv.at[n], x_dev)

    def to_owner(n, d, at=None):
        device = (g, r if d == 0 else 1 - r, q)
        if at is None:
            return remote(fs.at[n, d], fr.at[n, d], f_send.at[n, d], f_recv.at[n, d], device)
        tall = fs.shape[2] // QUARTERS
        rows = pl.ds(at * tall, tall)
        return remote(fs.at[n, d, rows], fr.at[n, d, rows], f_send.at[n, d], f_recv.at[n, d], device)

    def rows_at(mine, j):
        return pl.ds(pl.multiple_of((p if mine else 1 - p) * tall + j * PIECE, 16), PIECE)

    def branch_y(m):
        if m >= QUARTERS:
            src = oth_hbm.at[rows_at(False, m - QUARTERS)]
        elif m < 2:
            src = oth_hbm.at[rows_at(True, m)]
        else:
            src = by_s.at[m - 2]
        return remote(src, by.at[m], p_send.at[m], p_recv.at[m], y_dev)

    def branch_z(m):
        src = bz_s.at[m] if m < QUARTERS else oth_hbm.at[rows_at(False, m - 2)]
        return remote(src, bz.at[m], q_send.at[m], q_recv.at[m], z_dev)

    load_own = pltpu.make_async_copy(own_hbm, own, load_o.at[0])
    load_oth = pltpu.make_async_copy(oth_hbm.at[pl.ds(pl.multiple_of(p * tall + 2 * PIECE, 16), 2 * PIECE)], oth, load_o.at[1])

    def border(k):
        stays, leaves = border_moves(tall)[k]
        mine = [pltpu.make_async_copy(fin.at[a:b], branch_ref.at[at : at + b - a], stay.at[n]) for n, (a, b, at) in enumerate(stays)]
        if leaves is None:
            return mine, None
        a, to, at = leaves
        return mine, remote(fin.at[a : a + LC], branch_ref.at[at : at + LC], b_send.at[0], b_recv.at[0], (g, r, to))

    def at_border(act):
        for k in range(4):

            @pl.when(c == k)
            def _(k=k):
                act(*border(k))

    def pass_on(k):
        to_y(k).wait_recv()
        part[k] = part[k] + yr[k].astype(f32)
        zs[k] = part[k].astype(bf16)
        to_z(k).start()

    def settle(k):
        to_z(k).wait_recv()
        dxdbl_ref[NCH - 1 - k] = part[k] + zr[k].astype(f32)

    @pl.when(i == 0)
    def _():
        barrier = pltpu.get_barrier_semaphore()
        for dr in range(2):
            for dc in range(4):
                if dr or dc:
                    pl.semaphore_signal(barrier, inc=1, device_id=(g, (r + dr) % 2, (c + dc) % 4), device_id_type=MESH)
        for device in (x_dev, core_dev):
            pl.semaphore_signal(barrier, inc=1, device_id=device, device_id_type=MESH)
        pl.semaphore_wait(barrier, 9)
        for j in range(2):
            for n in range(2):
                to_core(n, j).start()
        for n in range(2):
            load(n, 0).start()
        load_own.start()
        load_oth.start()
        for m in (QUARTERS, QUARTERS + 1):
            branch_y(m).start()
            branch_z(m).start()
        first[...] = jnp.zeros_like(first)
        alog_ref[...] = jnp.zeros_like(alog_ref)
        sums_ref[...] = jnp.zeros_like(sums_ref)
        dtpg_ref[...] = jnp.zeros_like(dtpg_ref)

    @pl.when(i == 1)
    def _():
        to_first.wait()
        first[...] = mix_ref[0:1] * first_s[...] + into_ref[0:1] * first_r[...]

    chunk_backward(xdbl_ref, xconv_ref, dy_ref, dtp_ref, vec_ref, rate_ref, starts_ref, part.at[i], dxc_ref, alog_ref, sums_ref, dtpg_ref, first, *scratch)

    @pl.when(i == 0)
    def _():
        first_s[...] = first[...]
        to_first.start()

    @pl.when(i == 1)
    def _():
        load_own.wait()
        load_oth.wait()

    for n in range(2):

        @pl.when(i == X_STEP[n])
        def _(n=n):
            to_core(n, 0).wait_recv()
            load(n, 0).wait()
            xs[n] = (kp[n] + cr[n, 0].astype(f32)).astype(bf16)
            to_x(n).start()
            load(n, 1).start()

        @pl.when(i == OWNER_STEP[n])
        def _(n=n):
            load(n, 1).wait()
            to_core(n, 1).wait_recv()
            to_x(n).wait_recv()
            fs[n] = (kp[n] + cr[n, 1].astype(f32) + xr[n].astype(f32)).astype(bf16)

            @pl.when(alone)
            def _():
                fr[n, 0] = fs[n, 0]

        for k in range(QUARTERS):

            @pl.when(i == QUARTER_STEP[n][k])
            def _(n=n, k=k):
                @pl.when(jnp.logical_not(alone))
                def _():
                    to_owner(n, 0, k).start()

                to_owner(n, 1, k).start()

        @pl.when(i == DONE_STEP[n])
        def _(n=n):
            @pl.when(jnp.logical_not(alone))
            def _():
                to_owner(n, 0).wait_recv()

            to_owner(n, 1).wait_recv()
            out[n] = fr[n, 0].astype(f32) + fr[n, 1].astype(f32)
            pltpu.make_async_copy(out.at[n], grad_ref.at[n], put.at[n]).start()

    for j in range(QUARTERS):

        @pl.when(i == OTHER_STEP[j])
        def _(j=j):
            if j >= 2:
                branch_z(QUARTERS + j - 2).wait_recv()
                mine = oth[(j - 2) * PIECE : (j - 1) * PIECE, :].astype(f32)
                by_s[j - 2] = (mine + bz[QUARTERS + j - 2].astype(f32)).astype(bf16)
            branch_y(j).start()

        @pl.when(i == PAIR_STEP[j])
        def _(j=j):
            total = own[rows_at(False, j), :]
            if j < 2:
                branch_y(QUARTERS + j).wait_recv()
                total = total + by[QUARTERS + j].astype(f32)
            bz_s[j] = total.astype(bf16)
            branch_z(j).start()

        @pl.when(i == FINAL_STEP[j])
        def _(j=j):
            branch_y(j).wait_recv()
            branch_z(j).wait_recv()
            fin[j * PIECE : (j + 1) * PIECE, :] = (own[rows_at(True, j), :] + by[j].astype(f32) + bz[j].astype(f32)).astype(bf16)

    @pl.when(i == 7)
    def _():
        def begin(mine, gone):
            if gone is not None:
                gone.start()
            for copy in mine:
                copy.start()

        at_border(begin)

    @pl.when(i >= SUM_LAG)
    def _():
        pass_on(i - SUM_LAG)

    ys[i] = part[i].astype(bf16)
    to_y(i).start()
    @pl.when(i == NCH - 1)
    def _():
        for k in range(NCH - SUM_LAG, NCH):
            pass_on(k)
        for k in range(NCH):
            settle(k)

        def finish_border(mine, gone):
            for copy in mine:
                copy.wait()
            if gone is not None:
                gone.wait()

        at_border(finish_border)

        def sent(k, _):
            to_y(k).wait_send()
            to_z(k).wait_send()
            return 0

        lax.fori_loop(0, NCH, sent, 0)
        for n in range(2):
            for j in range(2):
                to_core(n, j).wait_send()
            to_x(n).wait_send()

            @pl.when(jnp.logical_not(alone))
            def _(n=n):
                to_owner(n, 0).wait_send()

            to_owner(n, 1).wait_send()
            pltpu.make_async_copy(out.at[n], grad_ref.at[n], put.at[n]).wait()
        for m in range(QUARTERS + 2):
            branch_y(m).wait_send()
            branch_z(m).wait_send()


def backward_kernel(*refs):
    backward(*refs[:9], refs[9:11], refs[11:13], *refs[13:])


def run_backward(xdbl, xconv, dy, dtp, vec, rate, starts, mix, into, sent, kept, own, oth):
    w = xconv.shape[1]
    width = own.shape[1]
    _, _, tall, n = sent[0].shape
    at = lambda i: NCH - 1 - i
    dma = pltpu.SemaphoreType.DMA
    low = lambda *shape: pltpu.VMEM(shape, bf16)
    sums = low(NCH, XW, CH)
    state = pltpu.VMEM((NSTATE, w), f32)
    return pl.pallas_call(
        backward_kernel,
        grid=(NCH,),
        in_specs=[
            chunk_of(XW, at),
            rows_of(w, at),
            rows_of(w, at),
            whole(RANK, w),
            whole(8, w),
            whole(NSTATE, w),
            pl.BlockSpec((1, NSTATE, w), lambda i: (at(i), 0, 0)),
            whole(8, w),
            whole(8, w),
        ]
        + [ANY] * 6,
        out_specs=(whole(NCH, XW, CH), rows_of(w, at), whole(NSTATE, w), whole(8, w), whole(RANK, w), ANY, ANY),
        out_shape=(
            shaped(NCH, XW, CH),
            shaped(SEQ, w),
            shaped(NSTATE, w),
            shaped(8, w),
            shaped(RANK, w),
            shaped(2, tall, n),
            shaped(SEQ // 2, width, dtype=bf16),
        ),
        scratch_shapes=[
            state,
            state,
            state,
            pltpu.VMEM((NCH, XW, CH), f32),
            sums,
            sums,
            sums,
            sums,
            low(2, 2, 2, tall, n),
            pltpu.VMEM((2, 2, tall, n), f32),
            low(2, 2, tall, n),
            low(2, 2, tall, n),
            low(2, 2, tall, n),
            low(2, 2, tall, n),
            pltpu.VMEM((2, tall, n), f32),
            pltpu.VMEM((SEQ, width), f32),
            low(2 * PIECE, width),
            low(2, PIECE, width),
            low(QUARTERS + 2, PIECE, width),
            low(QUARTERS, PIECE, width),
            low(QUARTERS + 2, PIECE, width),
            low(SEQ // 2, width),
            dma((NCH,)),
            dma((NCH,)),
            dma((NCH,)),
            dma((NCH,)),
            dma((1,)),
            dma((1,)),
            dma((2, 2)),
            dma((2, 2)),
            dma((2,)),
            dma((2,)),
            dma((2, 2)),
            dma((2, 2)),
            dma((QUARTERS + 2,)),
            dma((QUARTERS + 2,)),
            dma((QUARTERS + 2,)),
            dma((QUARTERS + 2,)),
            dma((1,)),
            dma((1,)),
            dma((2,)),
            dma((2,)),
            dma((2,)),
            dma((2,)),
            *backward_scratch(w),
        ],
        compiler_params=pltpu.CompilerParams(
            dimension_semantics=("arbitrary",), collective_id=3, has_side_effects=True, vmem_limit_bytes=61 * 1024 * 1024
        ),
        cost_estimate=pl.CostEstimate(flops=120 * 1000000000, bytes_accessed=1000000, transcendentals=0),
    )(xdbl, xconv, dy, dtp, vec, rate, starts, mix, into, *sent, *kept, own, oth)


def conv_backward_far(inner_ref, halo_ref, inv_ref, halo_inv_ref, tail_ref, conv_ref, xproj_ref, dxc_ref, dxdbl_ref, mix_ref, into_ref,
                      dproj_ref, dscale_ref, sums_ref, xprojg_ref, head, sent, got, buf, dbuf, send_sem, recv_sem):
    i = pl.program_id(0)
    g, r, c = lax.axis_index("grp"), lax.axis_index("row"), lax.axis_index("col")
    far_dev = (g, 1 - r, (c + 2) % 4)
    to_far = remote(sent, got, send_sem.at[0], recv_sem.at[0], far_dev)

    @pl.when(i == 0)
    def _():
        barrier = pltpu.get_barrier_semaphore()
        pl.semaphore_signal(barrier, inc=1, device_id=far_dev, device_id_type=MESH)
        pl.semaphore_wait(barrier, 1)
        head[...] = jnp.zeros_like(head)
        sums_ref[...] = jnp.zeros_like(sums_ref)
        xprojg_ref[...] = jnp.zeros_like(xprojg_ref)

    @pl.when(i == 1)
    def _():
        to_far.wait()
        head[...] = mix_ref[...] * sent[...] + into_ref[...] * got[...]

    conv_chunk(NCH - 1 - i, inner_ref, halo_ref, inv_ref, halo_inv_ref, tail_ref, conv_ref, xproj_ref, dxc_ref, dxdbl_ref,
               dproj_ref, dscale_ref, sums_ref, xprojg_ref, head, buf, dbuf)

    @pl.when(i == 0)
    def _():
        sent[...] = head[...]
        to_far.start()


def run_conv_backward_far(inner, inv, tail, conv, xproj, dxc, dxdbl, mix, into):
    w = inner.shape[1]
    at = lambda i: NCH - 1 - i
    before = lambda i: (jnp.maximum(at(i) * (CH // 8) - 1, 0), 0)
    rows = pltpu.VMEM((8, w), f32)
    return pl.pallas_call(
        conv_backward_far,
        grid=(NCH,),
        in_specs=[
            rows_of(w, at),
            pl.BlockSpec((8, w), before),
            rows_of(1, at),
            pl.BlockSpec((8, 1), before),
            whole(8, w),
            whole(8, w),
            whole(XW, w),
            rows_of(w, at),
            chunk_of(XW, at),
            whole(8, w),
            whole(8, w),
        ],
        out_specs=(rows_of(w, at), rows_of(1, at), whole(8, w), whole(XW, w)),
        out_shape=(shaped(SEQ, w, dtype=bf16), shaped(SEQ, 1), shaped(8, w), shaped(XW, w)),
        scratch_shapes=[
            rows,
            rows,
            rows,
            pltpu.VMEM((CH + 8, w), f32),
            pltpu.VMEM((CH + 8, w), f32),
            pltpu.SemaphoreType.DMA((1,)),
            pltpu.SemaphoreType.DMA((1,)),
        ],
        compiler_params=pltpu.CompilerParams(
            dimension_semantics=("arbitrary",), collective_id=4, has_side_effects=True, vmem_limit_bytes=VMEM_LIMIT
        ),
        cost_estimate=pl.CostEstimate(flops=20 * 1000000000, bytes_accessed=1000000, transcendentals=0),
    )(inner, inner, inv, inv, tail, conv, xproj, dxc, dxdbl, mix, into)


def per_device(
    tokens,
    gain,
    in_proj,
    conv_weight,
    conv_bias,
    x_proj,
    dt_proj,
    dt_bias,
    a_log,
    d_skip,
    out_proj,
    table,
    cotangent,
):
    row = lax.axis_index("row")
    col = lax.axis_index("col")
    grp = lax.axis_index("grp")
    low_row = row == 0
    low_pair = col % 2 == 0
    half = col // 2
    places = [(r, c) for r in range(2) for c in range(4)]
    quick = lax.axis_size("grp") == 4

    def spot(r, c):
        return r * 4 + c

    def send(v, pairs):
        return lax.ppermute(v, ("row", "col"), [(spot(*a), spot(*b)) for a, b in pairs])

    def swap(v):
        return send(v, [((r, c), (1 - r, c)) for r, c in places])

    def pair(v):
        return send(v, [((r, c), (r, c ^ 1)) for r, c in places])

    def across(v):
        return send(v, [((r, c), (1 - r, c ^ 2)) for r, c in places])

    def quarter_spot(q, s):
        return ((q & 1) ^ s, 2 * s + (q >> 1))

    same = [((r, q), quarter_spot(q, r ^ (q & 1))) for r, q in places]
    other = [((r, q), quarter_spot(q, 1 ^ r ^ (q & 1))) for r, q in places]
    spread = [((r, q), quarter_spot(q, r)) for r, q in places]

    def back(pairs):
        return [(b, a) for a, b in pairs]

    def flip(v, bit):
        return lax.ppermute(v, "grp", [(g, g ^ bit) for g in range(4)])

    def scatter_grp(v, axis):
        return lax.psum_scatter(v, "grp", scatter_dimension=axis, tiled=True)

    def by_pair(own, paired):
        return jnp.where(low_pair, own, paired), jnp.where(low_pair, paired, own)

    local = tokens.shape[0]
    cut = local - LC
    tail_at = cut - LC

    def to_sequences(v):
        got = send(jnp.where(col == 3, v[tail_at:cut], v[cut:]), [((r, a), (r, b)) for r in range(2) for a, b in ((1, 2), (2, 3), (3, 1))])
        low = jnp.concatenate([v[:cut], jnp.where(col == 0, v[cut:], got)], axis=0)
        two = jnp.concatenate([got, v[:cut]], axis=0)
        three = jnp.concatenate([got, v[:tail_at], v[cut:]], axis=0)
        return jnp.where(col < 2, low, jnp.where(col == 2, two, three))

    def from_sequences(v):
        got = send(jnp.where(col == 1, v[cut:], v[:LC]), [((r, b), (r, a)) for r in range(2) for a, b in ((1, 2), (2, 3), (3, 1))])
        low = jnp.concatenate([v[:cut], jnp.where(col == 0, v[cut:], got)], axis=0)
        two = jnp.concatenate([v[LC:], got], axis=0)
        three = jnp.concatenate([v[LC:cut], got, v[cut:]], axis=0)
        return jnp.where(col < 2, low, jnp.where(col == 2, two, three))

    def gather_quad(v):
        swapped = swap(v)
        paired = pair(v)
        mid = v.shape[0] // 2
        diagonal = jnp.concatenate([pair(swapped[:mid]), swap(paired[mid:])], axis=0)
        first_own, second_own = by_pair(v, paired)
        first_oth, second_oth = by_pair(swapped, diagonal)
        return jnp.stack([jnp.concatenate([first_own, second_own], axis=0), jnp.concatenate([first_oth, second_oth], axis=0)])

    def scatter_quad(own, oth):
        v = own + swap(oth.astype(bf16)).astype(f32)
        first, second = v[:local], v[local:]
        kept, sent = jnp.where(low_pair, first, second), jnp.where(low_pair, second, first)
        return kept + pair(sent.astype(bf16)).astype(f32)

    own_table = jnp.where(half == 0, table[0], table[1])
    oth_table = jnp.where(half == 0, table[1], table[0])
    resumes_own = own_table == half
    resumed_by_other = oth_table == half

    small = jnp.concatenate([conv_weight, conv_bias[None], dt_bias[None], d_skip[None], a_log, dt_proj, x_proj.T], axis=0)
    lanes = small.shape[1]
    used = small.shape[0]
    gain_rows = gain.size // lanes
    width = tokens.shape[1]
    if quick:
        small = jnp.concatenate([small, gain.reshape(gain_rows, lanes)], axis=0)
        small = jnp.pad(small, ((0, -small.shape[0] % 16), (0, 0)))
        raw, wi, small = run_gather_start(tokens, in_proj[:, 0], small)
        gain_all = small[:, used : used + gain_rows].reshape(2, width).astype(f32)
        small = jnp.swapaxes(small, 0, 1).reshape(small.shape[1], 8 * lanes)
    else:
        raw = gather_quad(to_sequences(tokens))

        def weight(shard):
            v = lax.all_gather(jnp.stack([send(shard, same), send(shard, other)]), "grp", axis=2, tiled=True)
            v = v.reshape(2, v.shape[1], SLOTS, v.shape[2] // SLOTS)
            return jnp.transpose(v, (2, 0, 1, 3)).reshape(2 * SLOTS, v.shape[1], v.shape[3])

        wi = weight(in_proj[:, 0])
        small = send(lax.all_gather(small, ("row", "grp"), axis=1, tiled=True), spread)
        gain_all = lax.all_gather(gain, ("row", "grp"), axis=0, tiled=True).astype(f32).reshape(2, width)
    w = small.shape[1]
    zero_row = jnp.zeros((1, w), f32)
    conv = jnp.concatenate([small[0:5].astype(f32)] + [zero_row] * 3, axis=0)
    vec = jnp.concatenate([small[5:7].astype(f32)] + [zero_row] * 6, axis=0)
    rate = -jnp.exp(small[7 : 7 + NSTATE].astype(f32))
    dtp = small[7 + NSTATE : 7 + NSTATE + RANK]
    xproj = small[7 + NSTATE + RANK : 7 + NSTATE + RANK + XW]
    gain_own = jnp.where(low_row, gain_all[0], gain_all[1])
    gain_two = jnp.stack([gain_own, jnp.where(low_row, gain_all[1], gain_all[0])])

    zero_state = jnp.zeros((NSTATE, w), f32)
    if quick:
        mix = jnp.broadcast_to(resumes_own.astype(f32), (8, w))
        normed, inv, inner, xconv, yfull, starts, xdbl, tail, wg, wo, cot = run_forward(raw, gain_two, wi, mix, conv, xproj, dtp, vec, rate, in_proj[:, 1], out_proj, cotangent)
    else:
        normed, inv, inner = run_project_first(raw, gain_two, wi)
        tail_own = (inv * inner)[LP - 8 : LP]
        tail = jnp.where(resumes_own, tail_own, across(tail_own))
        xconv, xdbl = run_conv_forward(inner, inv, tail, conv, xproj)
        for move in (swap, pair):
            xdbl = xdbl + move(xdbl)
        xdbl = jnp.swapaxes(xdbl.reshape(XW, NCH, CH), 0, 1)
        *kept, final = run_scan_forward(0, PC, xdbl, xconv, dtp, vec, rate, zero_state)
        resumed = jnp.where(resumes_own, final, across(final))
        yfull, starts, _ = run_scan_forward(PC, NCH - PC, xdbl, xconv, dtp, vec, rate, resumed, kept)
        wg, wo = weight(in_proj[:, 1]), weight(out_proj)
        cot = gather_quad(to_sequences(cotangent))
    gated, d_yfull, d_gate_proj, gate_scale, branch_own, branch_oth = run_gate_backward(normed, wg, cot, wo, yfull, inv)

    def collect(v):
        return send(v[0].astype(bf16), back(same)).astype(f32) + send(v[1].astype(bf16), back(other)).astype(f32)

    def rows_product(a, b, out_dtype):
        return lax.dot_general(a, b, (((1,), (0,)), ((), ())), preferred_element_type=f32).astype(out_dtype)

    zero_head = jnp.zeros((8, w), f32)
    conv_back = functools.partial(run_conv_backward, inner=inner, inv=inv, tail=tail, conv=conv, xproj=xproj)
    if quick:
        x, core = grp // 2, grp % 2
        order = jnp.stack([2 * (1 - x) + 1 - core, 2 * x + 1 - core, 2 * (1 - x) + core, 2 * x + core]).astype(jnp.int32)
        gate_sent, out_sent, gate_kept, out_kept = run_late_parts(order, normed, d_gate_proj, gated, cot)
        sent, kept = (gate_sent, out_sent), (gate_kept, out_kept)
        into = jnp.broadcast_to(resumed_by_other.astype(f32), (8, w))
        dxdbl, dxc, alog_grad, scan_sums, dtp_grad, late_grads, branch = run_backward(
            xdbl, xconv, d_yfull, dtp, vec, rate, starts, mix, into, sent, kept, branch_own, branch_oth
        )
        gate_grad, out_grad = late_grads[0], late_grads[1]
    else:
        branch = from_sequences(scatter_quad(branch_own, branch_oth).astype(bf16))
        out_grad = collect([scatter_grp(dot_tn(gated, cot[d]), 1) for d in range(2)])
        gate_grad = collect([scatter_grp(dot_tn(normed[d], d_gate_proj), 1) for d in range(2)])
        sums = (zero_state, jnp.zeros((8, w), f32), jnp.zeros((RANK, w), f32))
        scan = functools.partial(run_scan_backward, xdbl=xdbl, xconv=xconv, dy=d_yfull, dtp=dtp, vec=vec, rate=rate, starts=starts)
        dx_c, dxc, *sums, g_first = scan(PC, NCH - PC, carry=zero_state, sums=sums)
        g_into = jnp.where(resumes_own, g_first, 0.0) + jnp.where(resumed_by_other, across(g_first), 0.0)
        dx_p, dxc, *sums, _ = scan(0, PC, carry=g_into, sums=sums, kept=(dxc,))
        alog_grad, scan_sums, dtp_grad = sums
        dxdbl = jnp.concatenate([dx_p, dx_c], axis=1)
        for move in (swap, pair):
            dxdbl = dxdbl + move(dxdbl)
        dxdbl = jnp.swapaxes(dxdbl.reshape(XW, NCH, CH), 0, 1)

    output = (tokens.astype(f32) + branch.astype(f32)).astype(bf16)
    if quick:
        d_inner_proj, inner_scale, conv_sums, xproj_grad = run_conv_backward_far(inner, inv, tail, conv, xproj, dxc, dxdbl, mix, into)
    else:
        sums = (jnp.zeros((8, w), f32), jnp.zeros((XW, w), f32))
        dp, ds, *sums, head = conv_back(PC, NCH - PC, dxc=dxc, dxdbl=dxdbl, follow=zero_head, sums=sums)
        follow = jnp.where(resumes_own, head, 0.0) + jnp.where(resumed_by_other, across(head), 0.0)
        d_inner_proj, inner_scale, conv_sums, xproj_grad, _ = conv_back(0, PC, dxc=dxc, dxdbl=dxdbl, follow=follow, sums=sums, kept=(dp, ds))

    scale = gate_scale + inner_scale

    def own_rows(v):
        return jnp.where(low_pair, v[:local], v[local:])

    def pair_rows(v):
        return jnp.where(low_pair, v[local:], v[:local])

    diagonal = send(pair_rows(scale), [((r, c), (1 - r, c ^ 1)) for r, c in places])
    scale = own_rows(scale) + swap(own_rows(scale)) + pair(pair_rows(scale)) + diagonal
    inv_own = own_rows(inv)
    pull = scale * inv_own * inv_own * inv_own / D
    small_parts = (conv_sums, scan_sums, alog_grad * rate, dtp_grad, xproj_grad)
    if quick:
        pulled, inner_grad, gain_sum, small_grad = run_finish(
            d_inner_proj, d_gate_proj, normed, raw, wi, wg, jnp.broadcast_to(gain_own[None], (8, width)), pull, small_parts
        )
        gain_grad = jnp.sum(gain_sum, axis=0)
    else:
        inner_grad = collect([scatter_grp(dot_tn(normed[d], d_inner_proj), 1) for d in range(2)])
        d_normed = scatter_quad(*run_normed_backward(d_inner_proj, d_gate_proj, wi, wg))
        fixed = own_rows(raw[0]).astype(f32)
        gain_grad = jnp.sum(d_normed * fixed, axis=0)
        gain_grad = lax.psum_scatter(lax.psum(gain_grad, "col"), "grp", scatter_dimension=0, tiled=True)
        pulled = from_sequences((d_normed * gain_own - pull * fixed).astype(bf16))
        small_grad = send(jnp.concatenate(small_parts, axis=0), back(spread))
        small_grad = lax.psum_scatter(small_grad, ("row", "grp"), scatter_dimension=1, tiled=True)
    input_grad = (cotangent.astype(f32) + pulled.astype(f32)).astype(bf16)
    in_grads = jnp.stack([inner_grad, gate_grad], axis=1)
    rank_at = 16 + NSTATE
    return (
        output,
        input_grad,
        gain_grad,
        in_grads,
        small_grad[0:4],
        small_grad[4],
        small_grad[rank_at + RANK :].T,
        small_grad[rank_at : rank_at + RANK],
        small_grad[8],
        small_grad[16 : 16 + NSTATE],
        small_grad[9],
        out_grad,
    )


def solution(mesh):
    placed = (
        P(("grp", "col"), "row"),
        P(("row", "grp")),
        P("row", None, ("col", "grp")),
        P(None, ("col", "row", "grp")),
        P(("col", "row", "grp")),
        P(("col", "row", "grp"), None),
        P(None, ("col", "row", "grp")),
        P(("col", "row", "grp")),
        P(None, ("col", "row", "grp")),
        P(("col", "row", "grp")),
        P("col", ("row", "grp")),
        P("grp"),
        P(("grp", "col"), "row"),
    )
    return jax.shard_map(
        per_device,
        mesh=mesh,
        in_specs=placed,
        out_specs=(
            P(("grp", "col"), "row"),
            P(("grp", "col"), "row"),
            P(("row", "grp")),
            P("row", None, ("col", "grp")),
            P(None, ("col", "row", "grp")),
            P(("col", "row", "grp")),
            P(("col", "row", "grp"), None),
            P(None, ("col", "row", "grp")),
            P(("col", "row", "grp")),
            P(None, ("col", "row", "grp")),
            P(("col", "row", "grp")),
            P("col", ("row", "grp")),
        ),
        check_vma=False,
    )
```

```python
import functools

import jax
import jax.numpy as jnp
from jax import lax
from jax.experimental import pallas as pl
from jax.experimental.pallas import tpu as pltpu
from jax.sharding import PartitionSpec as P

D = 2048
NSTATE = 16
KCONV = 4
RANK = 128
NPROMPT = 2
LP = 1024
LC = 128
NCONT = 2

eps = 1e-05
CH = 128
SUB = 16
PC = LP // CH
SEQ = LP + LC
NCH = SEQ // CH
XW = RANK + 2 * NSTATE
SPAN = SUB * NSTATE
LOG2E = 1.4426950408889634
VMEM_LIMIT = 58 * 1024 * 1024

f32 = jnp.float32
bf16 = jnp.bfloat16


def dot_nn(a, b):
    return lax.dot_general(a, b, (((1,), (0,)), ((), ())), preferred_element_type=f32)


def dot_nt(a, b):
    return lax.dot_general(a, b, (((1,), (1,)), ((), ())), preferred_element_type=f32)


def dot_tn(a, b):
    return lax.dot_general(a, b, (((0,), (0,)), ((), ())), preferred_element_type=f32)


def expand_tile():
    lane = lax.broadcasted_iota(jnp.int32, (NSTATE, SPAN), 1)
    row = lax.broadcasted_iota(jnp.int32, (NSTATE, SPAN), 0)
    return jnp.where(lane % NSTATE == row, 1.0, 0.0)


def own_token(rows):
    lane = lax.broadcasted_iota(jnp.int32, (rows, SPAN), 1)
    row = lax.broadcasted_iota(jnp.int32, (rows, SPAN), 0)
    return lane // NSTATE == row % SUB


def conv_forward(inner_ref, inv_ref, tail_ref, conv_ref, xproj_ref, xconv_ref, xdbl_ref, buf):
    i = pl.program_id(0)

    @pl.when(i == 0)
    def _():
        buf[0:8] = jnp.zeros_like(buf[0:8])

    @pl.when(i == PC)
    def _():
        buf[0:8] = tail_ref[...]

    @pl.when((i > 0) & (i < PC))
    def _():
        buf[0:8] = buf[CH : CH + 8]

    buf[8 : CH + 8] = inv_ref[...] * inner_ref[...]
    out = conv_ref[4:5]
    for k in range(KCONV):
        out = out + conv_ref[k : k + 1] * buf[5 + k : 5 + k + CH]
    xconv = (out * jax.nn.sigmoid(out)).astype(bf16)
    xconv_ref[...] = xconv
    xdbl_ref[...] = dot_nt(xproj_ref[...], xconv)


def softplus(v):
    return jnp.maximum(v, 0.0) + jnp.log1p(jnp.exp(-jnp.abs(v)))


def by_sub(v):
    return v.reshape(CH // SUB, SUB, v.shape[-1])


def scan_chunk(xdbl_ref, xconv, dtp_ref, vec_ref, rate_ref, state, dt_s, u_s, cb_s, h_s, y_s):
    step = softplus(dot_tn(xdbl_ref[:RANK].astype(bf16), dtp_ref[...]) + vec_ref[0:1])
    dt_s[...] = by_sub(step)
    u_s[...] = by_sub(step * xconv)
    reads = dot_tn(xdbl_ref[RANK + NSTATE :].astype(bf16), expand_tile().astype(bf16))
    cb_s[...] = jnp.where(own_token(CH), reads, 0.0).astype(bf16)
    rate = rate_ref[...] * LOG2E

    def block(j, carried):
        h, maps = carried
        for t in range(SUB):
            a = jnp.exp2(dt_s[j, t : t + 1, :] * rate)
            h = a * h + u_s[j, t : t + 1, :] * maps[:, t : t + 1]
            h_s[t * NSTATE : (t + 1) * NSTATE, :] = h.astype(bf16)
        rows = pl.ds(pl.multiple_of(j * SUB, SUB), SUB)
        y_s[rows, :] = dot_nn(cb_s[rows, :], h_s[...])
        return (h, pltpu.roll(maps, CH - SUB, 1))

    h, _ = lax.fori_loop(0, CH // SUB, block, (state, xdbl_ref[RANK : RANK + NSTATE]))
    return h, y_s[...] + vec_ref[1:2] * xconv


def scan_scratch(w):
    return [
        pltpu.VMEM((CH // SUB, SUB, w), f32),
        pltpu.VMEM((CH // SUB, SUB, w), f32),
        pltpu.VMEM((CH, SPAN), bf16),
        pltpu.VMEM((SPAN, w), bf16),
        pltpu.VMEM((CH, w), f32),
    ]


def scan_forward(kept, xdbl_ref, xconv_ref, dtp_ref, vec_ref, rate_ref, start_ref, *refs):
    yfull_ref, starts_ref, final_ref, *scratch = refs[kept:]

    @pl.when(pl.program_id(0) == 0)
    def _():
        final_ref[...] = start_ref[...]

    starts_ref[0] = final_ref[...]
    h, yfull = scan_chunk(xdbl_ref, xconv_ref[...].astype(f32), dtp_ref, vec_ref, rate_ref, final_ref[...], *scratch)
    final_ref[...] = h
    yfull_ref[...] = yfull.astype(bf16)


def chunk_backward(xdbl_ref, xconv_ref, dy_ref, dtp_ref, vec_ref, rate_ref, starts_ref, dxdbl_ref, dxc_ref, alog_ref, sums_ref, dtpg_ref, first_ref,
                   dt_s, u_s, x_s, dy_s, a_s, h_s, g_s, w_s, b_s, m1_s, m2_s, ds_s, dx_s, sig_s):
    low = xdbl_ref[:RANK].astype(bf16)
    step_inner = dot_tn(low, dtp_ref[...]) + vec_ref[0:1]
    step = softplus(step_inner)
    sig_s[...] = jax.nn.sigmoid(step_inner)
    xconv = xconv_ref[...].astype(f32)
    dy = dy_ref[...]
    dt_s[...] = by_sub(step)
    u_s[...] = by_sub(step * xconv)
    x_s[...] = by_sub(xconv)
    dy_s[...] = by_sub(dy)
    tile = expand_tile().astype(bf16)
    b_s[...] = jnp.where(own_token(CH), dot_tn(xdbl_ref[RANK : RANK + NSTATE].astype(bf16), tile), 0.0).astype(bf16)
    rate = rate_ref[...]
    rate2 = rate * LOG2E
    h_s[0:NSTATE] = starts_ref[0]

    def ahead(j, carried):
        h, maps = carried
        for t in range(SUB):
            a = jnp.exp2(dt_s[j, t : t + 1, :] * rate2)
            h = a * h + u_s[j, t : t + 1, :] * maps[:, t : t + 1]
            a_s[j, t * NSTATE : (t + 1) * NSTATE, :] = a
            at = pl.multiple_of(j * SPAN + (t + 1) * NSTATE, NSTATE)
            h_s[pl.ds(at, NSTATE), :] = h
        return (h, pltpu.roll(maps, CH - SUB, 1))

    lax.fori_loop(0, CH // SUB, ahead, (starts_ref[0], xdbl_ref[RANK : RANK + NSTATE]))
    ones = jnp.where(own_token(SUB), 1.0, 0.0).astype(bf16)
    mine_sub = own_token(SUB)

    def back(jj, carried):
        g, alog, maps = carried
        j = CH // SUB - 1 - jj
        maps = pltpu.roll(maps, SUB, 1)
        for t in reversed(range(SUB)):
            dt = dt_s[j, t : t + 1, :]
            gs = maps[:, t : t + 1] * dy_s[j, t : t + 1, :] + g
            g = a_s[j, t * NSTATE : (t + 1) * NSTATE, :] * gs
            prior = h_s[pl.ds(pl.multiple_of(j * SPAN + t * NSTATE, NSTATE), NSTATE), :]
            w = g * prior
            alog = alog + w * dt
            g_s[t * NSTATE : (t + 1) * NSTATE, :] = gs.astype(bf16)
            w_s[t * NSTATE : (t + 1) * NSTATE, :] = (w * rate).astype(bf16)
        rows = pl.ds(pl.multiple_of(j * SUB, SUB), SUB)
        gs_all = g_s[...]
        through = dot_nn(b_s[rows, :], gs_all)
        ds_s[rows, :] = dot_nn(ones, w_s[...]) + x_s[j] * through
        dx_s[rows, :] = dt_s[j] * through + vec_ref[1:2] * dy_s[j]
        hs = h_s[pl.ds(pl.multiple_of(j * SPAN + NSTATE, NSTATE), SPAN), :].astype(bf16)
        m1_s[rows, :] = jnp.where(mine_sub, dot_nt(u_s[j].astype(bf16), gs_all), 0.0).astype(bf16)
        m2_s[rows, :] = jnp.where(mine_sub, dot_nt(dy_s[j].astype(bf16), hs), 0.0).astype(bf16)
        return (g, alog, maps)

    g, alog, _ = lax.fori_loop(0, CH // SUB, back, (first_ref[...], alog_ref[...], xdbl_ref[RANK + NSTATE :]))
    first_ref[...] = g
    alog_ref[...] = alog
    d_inner = ds_s[...] * sig_s[...]
    d_low = d_inner.astype(bf16)
    sums_ref[0:1] = sums_ref[0:1] + jnp.sum(d_inner, axis=0, keepdims=True)
    sums_ref[1:2] = sums_ref[1:2] + jnp.sum(dy * xconv, axis=0, keepdims=True)
    dtpg_ref[...] = dtpg_ref[...] + dot_nn(low, d_low)
    dxdbl_ref[:RANK] = dot_nt(dtp_ref[...], d_low)
    dxdbl_ref[RANK : RANK + NSTATE] = dot_nt(tile, m1_s[...])
    dxdbl_ref[RANK + NSTATE :] = dot_nt(tile, m2_s[...])
    dxc_ref[...] = dx_s[...]


def scan_backward(kept, *refs):
    given, sums0, out = refs[:7], refs[7:11], refs[11 + kept :]
    dxdbl_ref, dxc_ref, alog_ref, sums_ref, dtpg_ref, first_ref = out[:6]

    @pl.when(pl.program_id(0) == 0)
    def _():
        first_ref[...] = sums0[0][...]
        alog_ref[...] = sums0[1][...]
        sums_ref[...] = sums0[2][...]
        dtpg_ref[...] = sums0[3][...]

    chunk_backward(*given, dxdbl_ref, dxc_ref, alog_ref, sums_ref, dtpg_ref, first_ref, *out[6:])


def backward_scratch(w):
    sub = pltpu.VMEM((CH // SUB, SUB, w), f32)
    return [
        sub,
        sub,
        sub,
        sub,
        pltpu.VMEM((CH // SUB, SPAN, w), f32),
        pltpu.VMEM(((CH + 1) * NSTATE, w), f32),
        pltpu.VMEM((SPAN, w), bf16),
        pltpu.VMEM((SPAN, w), bf16),
        pltpu.VMEM((CH, SPAN), bf16),
        pltpu.VMEM((CH, SPAN), bf16),
        pltpu.VMEM((CH, SPAN), bf16),
        pltpu.VMEM((CH, w), f32),
        pltpu.VMEM((CH, w), f32),
        pltpu.VMEM((CH, w), f32),
    ]


def conv_chunk(chunk, inner_ref, halo_ref, inv_ref, halo_inv_ref, tail_ref, conv_ref, xproj_ref, dxc_ref, dxdbl_ref, dproj_ref, dscale_ref, sums_ref, xprojg_ref, head_ref, buf, dbuf):
    projected = inner_ref[...]
    inv = inv_ref[...]
    before = halo_inv_ref[...] * halo_ref[...]
    before = jnp.where(chunk == 0, 0.0, jnp.where(chunk == PC, tail_ref[...], before))
    buf[0:8] = before
    buf[8 : CH + 8] = inv * projected
    out = conv_ref[4:5]
    for k in range(KCONV):
        out = out + conv_ref[k : k + 1] * buf[5 + k : 5 + k + CH]
    sig = jax.nn.sigmoid(out)
    xconv = (out * sig).astype(bf16)
    dxdbl = dxdbl_ref[...].astype(bf16)
    xprojg_ref[...] = xprojg_ref[...] + dot_nn(dxdbl, xconv)
    d_x = dxc_ref[...] + dot_tn(dxdbl, xproj_ref[...])
    d_conv = d_x * (sig * (1.0 + out * (1.0 - sig)))
    dbuf[CH : CH + 8] = head_ref[...]
    dbuf[0:CH] = d_conv
    d_inner = conv_ref[3:4] * d_conv
    for k in range(KCONV - 1):
        d_inner = d_inner + conv_ref[k : k + 1] * dbuf[3 - k : 3 - k + CH]
    for k in range(KCONV):
        sums_ref[k : k + 1] = sums_ref[k : k + 1] + jnp.sum(buf[5 + k : 5 + k + CH] * d_conv, axis=0, keepdims=True)
    sums_ref[4:5] = sums_ref[4:5] + jnp.sum(d_conv, axis=0, keepdims=True)
    dproj_ref[...] = (inv * d_inner).astype(bf16)
    dscale_ref[...] = jnp.sum(d_inner * projected, axis=1, keepdims=True)
    head_ref[...] = d_conv[0:8]


def conv_backward(kept, chunks, first, *refs):
    given, init, out = refs[:9], refs[9:12], refs[12 + kept :]
    dproj_ref, dscale_ref, sums_ref, xprojg_ref, head_ref, buf, dbuf = out
    i = pl.program_id(0)

    @pl.when(i == 0)
    def _():
        head_ref[...] = init[0][...]
        sums_ref[...] = init[1][...]
        xprojg_ref[...] = init[2][...]

    conv_chunk(first + chunks - 1 - i, *given, *out)


def call(body, chunks, args, in_specs, outs, out_specs, scratch, micros, aliases=None):
    return pl.pallas_call(
        body,
        grid=(chunks,),
        in_specs=in_specs,
        out_specs=out_specs,
        scratch_shapes=scratch,
        out_shape=outs,
        input_output_aliases=aliases or {},
        compiler_params=pltpu.CompilerParams(dimension_semantics=("arbitrary",), vmem_limit_bytes=VMEM_LIMIT),
        cost_estimate=pl.CostEstimate(flops=micros * 1000000000, bytes_accessed=1000000, transcendentals=0),
    )(*args)


def shaped(*shape, dtype=f32):
    return jax.ShapeDtypeStruct(shape, dtype)


def rows_of(width, place, tall=CH):
    return pl.BlockSpec((tall, width), lambda i: (place(i), 0))


def lanes_of(height, place):
    return pl.BlockSpec((height, CH), lambda i: (0, place(i)))


def whole(*shape):
    return pl.BlockSpec(shape, lambda i: (0,) * len(shape))


ANY = pl.BlockSpec(memory_space=pl.ANY)


def run_conv_forward(inner, inv, tail, conv, xproj):
    w = inner.shape[1]
    at = lambda i: i
    return call(
        conv_forward,
        NCH,
        (inner, inv, tail, conv, xproj),
        [rows_of(w, at), rows_of(1, at), whole(8, w), whole(8, w), whole(XW, w)],
        (shaped(SEQ, w, dtype=bf16), shaped(XW, SEQ)),
        (rows_of(w, at), lanes_of(XW, at)),
        [pltpu.VMEM((CH + 8, w), f32)],
        12,
    )


def chunk_of(height, place):
    return pl.BlockSpec((None, height, CH), lambda i: (place(i), 0, 0))


def run_scan_forward(first, chunks, xdbl, xconv, dtp, vec, rate, start, kept=()):
    w = xconv.shape[1]
    at = lambda i: first + i
    return call(
        functools.partial(scan_forward, len(kept)),
        chunks,
        (xdbl, xconv, dtp, vec, rate, start, *kept),
        [chunk_of(XW, at), rows_of(w, at), whole(RANK, w), whole(8, w), whole(NSTATE, w), whole(NSTATE, w)] + [ANY] * len(kept),
        (shaped(SEQ, w, dtype=bf16), shaped(NCH, NSTATE, w), shaped(NSTATE, w)),
        (rows_of(w, at), pl.BlockSpec((1, NSTATE, w), lambda i: (first + i, 0, 0)), whole(NSTATE, w)),
        scan_scratch(w),
        5 * chunks,
        {6 + k: k for k in range(len(kept))},
    )


def run_scan_backward(first, chunks, xdbl, xconv, dy, dtp, vec, rate, starts, carry, sums, kept=()):
    w = xconv.shape[1]
    at = lambda i: first + chunks - 1 - i
    local = lambda i: chunks - 1 - i
    return call(
        functools.partial(scan_backward, len(kept)),
        chunks,
        (xdbl, xconv, dy, dtp, vec, rate, starts, carry, *sums, *kept),
        [
            chunk_of(XW, at),
            rows_of(w, at),
            rows_of(w, at),
            whole(RANK, w),
            whole(8, w),
            whole(NSTATE, w),
            pl.BlockSpec((1, NSTATE, w), lambda i: (at(i), 0, 0)),
            whole(NSTATE, w),
            whole(NSTATE, w),
            whole(8, w),
            whole(RANK, w),
        ]
        + [ANY] * len(kept),
        (shaped(XW, chunks * CH), shaped(SEQ, w), shaped(NSTATE, w), shaped(8, w), shaped(RANK, w), shaped(NSTATE, w)),
        (lanes_of(XW, local), rows_of(w, at), whole(NSTATE, w), whole(8, w), whole(RANK, w), whole(NSTATE, w)),
        backward_scratch(w),
        11 * chunks,
        {11 + k: 1 + k for k in range(len(kept))},
    )


def run_conv_backward(first, chunks, inner, inv, tail, conv, xproj, dxc, dxdbl, follow, sums, kept=()):
    w = inner.shape[1]
    at = lambda i: first + chunks - 1 - i
    before = lambda i: (jnp.maximum(at(i) * (CH // 8) - 1, 0), 0)
    return call(
        functools.partial(conv_backward, len(kept), chunks, first),
        chunks,
        (inner, inner, inv, inv, tail, conv, xproj, dxc, dxdbl, follow, *sums, *kept),
        [
            rows_of(w, at),
            pl.BlockSpec((8, w), before),
            rows_of(1, at),
            pl.BlockSpec((8, 1), before),
            whole(8, w),
            whole(8, w),
            whole(XW, w),
            rows_of(w, at),
            chunk_of(XW, at),
            whole(8, w),
            whole(8, w),
            whole(XW, w),
        ]
        + [ANY] * len(kept),
        (shaped(SEQ, w, dtype=bf16), shaped(SEQ, 1), shaped(8, w), shaped(XW, w), shaped(8, w)),
        (rows_of(w, at), rows_of(1, at), whole(8, w), whole(XW, w), whole(8, w)),
        [pltpu.VMEM((CH + 8, w), f32), pltpu.VMEM((CH + 8, w), f32)],
        2 * chunks,
        {12 + k: k for k in range(len(kept))},
    )


MESH = pl.DeviceIdType.MESH
BIG = 384
BIG_STEPS = SEQ // BIG
SLOTS = 4


def remote(src, dst, send, recv, device):
    return pltpu.make_async_remote_copy(src_ref=src, dst_ref=dst, send_sem=send, recv_sem=recv, device_id=device, device_id_type=MESH)


def xor_bit(a, b):
    return a + b - 2 * a * b


def token_pieces(c, local):
    cut = local - LC
    low = cut - LC
    if c == 0:
        return [(0, local, 0, 0)]
    if c == 1:
        return [(0, cut, 0, local), (cut, local, 1, 0)]
    if c == 2:
        return [(0, local, 1, LC)]
    return [(0, low, 1, LC + local), (low, cut, 0, LP), (cut, local, 1, LP)]


class Gather:
    def __init__(self, weights, tokens, raw, w_send, w_recv, t_send, t_recv, here):
        g, r, c = lax.axis_index("grp"), lax.axis_index("row"), lax.axis_index("col")
        x, core = g // 2, g % 2
        self.g, self.r, self.c = g, r, c
        half = xor_bit(r, c % 2)
        self.firsts = ((g, r, 2 * half + c // 2), (g, 1 - r, 2 * (1 - half) + c // 2))
        self.alone = 2 * half + c // 2 == c
        self.ranks = (g, (1 - x) * 2 + core, x * 2 + 1 - core)
        self.x_dev, self.core_dev = (self.ranks[1], r, c), (self.ranks[2], r, c)
        self.y_dev, self.z_dev = (g, 1 - r, c), (g, r, c + 1 - 2 * (c % 2))
        self.weights, self.tokens, self.raw = weights, tokens, raw
        self.w_send, self.w_recv, self.t_send, self.t_recv, self.here = w_send, w_recv, t_send, t_recv, here

    def greet(self):
        barrier = pltpu.get_barrier_semaphore()
        for dr in range(2):
            for dc in range(4):
                if dr or dc:
                    device = (self.g, (self.r + dr) % 2, (self.c + dc) % 4)
                    pl.semaphore_signal(barrier, inc=1, device_id=device, device_id_type=MESH)
        for device in (self.x_dev, self.core_dev):
            pl.semaphore_signal(barrier, inc=1, device_id=device, device_id_type=MESH)
        pl.semaphore_wait(barrier, 9)

    def slot(self, n, k, d):
        if self.weights[n][2]:
            return (self.r if d == 0 else 1 - self.r) * 4 + self.ranks[k]
        return 2 * self.ranks[k] + d

    def first_hop(self, n, d):
        src, dst, by_row = self.weights[n]
        at = self.slot(n, 0, 0) if by_row else self.slot(n, 0, d)
        return remote(src, dst.at[at], self.w_send.at[n, d], self.w_recv.at[n, d], self.firsts[d])

    def at_home(self, n):
        src, dst, _ = self.weights[n]
        return pltpu.make_async_copy(src, dst.at[self.slot(n, 0, 0)], self.here.at[n])

    def hop(self, n, d, k, came):
        dst = self.weights[n][1]
        at = self.slot(n, k, d)
        i = (0, 2, 4, 6)[came] + d
        device = self.x_dev if came == 1 else self.core_dev
        return remote(dst.at[at], dst.at[at], self.w_send.at[n, i], self.w_recv.at[n, i], device)

    def begin(self, n):
        @pl.when(self.alone)
        def _():
            self.at_home(n).start()

        @pl.when(jnp.logical_not(self.alone))
        def _():
            self.first_hop(n, 0).start()

        self.first_hop(n, 1).start()

    def forward(self, n):
        for d in range(2):
            if d == 0:

                @pl.when(self.alone)
                def _():
                    self.at_home(n).wait()

                @pl.when(jnp.logical_not(self.alone))
                def _():
                    self.first_hop(n, 0).wait_recv()
            else:
                self.first_hop(n, 1).wait_recv()
            self.hop(n, d, 0, 1).start()
            self.hop(n, d, 0, 2).start()

    def forward_again(self, n):
        for d in range(2):
            self.hop(n, d, 0, 1).wait_recv()
            self.hop(n, d, 1, 3).start()

    def end(self, n):
        for d in range(2):
            self.hop(n, d, 0, 2).wait_recv()
            self.hop(n, d, 1, 3).wait_recv()
            self.hop(n, d, 0, 1).wait_send()
            self.hop(n, d, 0, 2).wait_send()
            self.hop(n, d, 1, 3).wait_send()

        @pl.when(jnp.logical_not(self.alone))
        def _():
            self.first_hop(n, 0).wait_send()

        self.first_hop(n, 1).wait_send()

    def ranges(self, k):
        local = self.tokens.shape[0]
        held = {0: (0, local), 1: (local, LP), 2: (LC, LC + local), 3: (LC + local, SEQ)}
        return held[k], held[k ^ 1], (LP, SEQ) if k < 2 else (0, LC)

    def part(self, d, rows):
        return self.raw.at[d, pl.ds(rows[0], rows[1] - rows[0])]

    def on_col(self, act):
        for k in range(4):

            @pl.when(self.c == k)
            def _(k=k):
                act(k)

    def sources(self, k, lo, hi):
        for a, b, s, at in token_pieces(k, self.tokens.shape[0]):
            first, end = max(lo, at), min(hi, at + b - a)
            if s == k // 2 and first < end:
                yield a + first - at, first, end

    def begin_half(self, h):
        def act(k):
            lo, hi = split(self.ranges(k)[0])[h]
            for src, first, end in self.sources(k, lo, hi):
                rows = self.tokens.at[pl.ds(src, end - first)]
                pltpu.make_async_copy(rows, self.part(0, (first, end)), self.here.at[2 + h]).start()
                remote(rows, self.part(1, (first, end)), self.t_send.at[h], self.t_recv.at[h], self.y_dev).start()
                remote(rows, self.part(0, (first, end)), self.t_send.at[2 + h], self.t_recv.at[2 + h], self.z_dev).start()

        self.on_col(act)

    def foreign_copies(self, k):
        copies = []
        for a, b, s, at in token_pieces(k, self.tokens.shape[0]):
            if s != k // 2:
                for dr in range(2):
                    for dc in range(2):
                        device = (self.g, self.r if dr == 0 else 1 - self.r, 2 * s + dc)
                        sems = self.t_send.at[6 + 2 * dr + dc], self.t_recv.at[6 + dr]
                        copies.append(remote(self.tokens.at[pl.ds(a, b - a)], self.part(dr, (at, at + b - a)), *sems, device))
        return copies

    def begin_foreign(self):
        def act(k):
            for copy in self.foreign_copies(k):
                copy.start()

        self.on_col(act)

    def relays(self, k):
        own, paired, _ = self.ranges(k)
        early, late = split(paired)[0], split(own)[1]
        return (
            remote(self.part(0, early), self.part(1, early), self.t_send.at[4], self.t_recv.at[4], self.y_dev),
            remote(self.part(1, late), self.part(1, late), self.t_send.at[5], self.t_recv.at[5], self.z_dev),
        )

    def settle(self, d, rows, sem):
        pltpu.make_async_copy(self.part(d, rows), self.part(d, rows), sem).wait()

    def relay(self):
        def act(k):
            own, paired, _ = self.ranges(k)
            by_y, by_z = self.relays(k)
            self.settle(0, split(paired)[0], self.t_recv.at[2])
            by_y.start()
            self.settle(1, split(own)[1], self.t_recv.at[1])
            by_z.start()

        self.on_col(act)

    def end_tokens(self):
        def act(k):
            own, paired, foreign = self.ranges(k)
            own, paired = split(own), split(paired)
            by_y, by_z = self.relays(k)
            self.settle(1, own[0], self.t_recv.at[0])
            self.settle(0, paired[1], self.t_recv.at[3])
            self.settle(1, paired[0], self.t_recv.at[4])
            self.settle(1, paired[1], self.t_recv.at[5])
            self.settle(0, foreign, self.t_recv.at[6])
            self.settle(1, foreign, self.t_recv.at[7])
            for h in range(2):
                self.settle(0, own[h], self.here.at[2 + h])
                self.settle(0, own[h], self.t_send.at[h])
                self.settle(0, own[h], self.t_send.at[2 + h])
            by_y.wait_send()
            by_z.wait_send()
            for copy in self.foreign_copies(k):
                copy.wait_send()

        self.on_col(act)


def split(rows):
    lo, hi = rows
    mid = lo + (hi - lo) // 2
    return (lo, mid), (mid, hi)


def gather_semaphores():
    return [pltpu.SemaphoreType.DMA(shape) for shape in ((2, 8), (2, 8), (10,), (8,), (4,))]


def gather_start(tokens, in_i, small, raw, wi, small_all, *sems):
    gather = Gather([(small, small_all, True), (in_i, wi, False)], tokens, raw, *sems)
    gather.greet()
    gather.begin(0)
    gather.begin(1)
    gather.begin_half(0)
    gather.begin_half(1)
    gather.begin_foreign()
    for n in range(2):
        gather.forward(n)
    gather.relay()
    for n in range(2):
        gather.forward_again(n)
    gather.end_tokens()
    for n in range(2):
        gather.end(n)


def run_gather_start(tokens, in_i, small):
    width = tokens.shape[1]
    return pl.pallas_call(
        gather_start,
        in_specs=[ANY] * 3,
        out_specs=[ANY] * 3,
        out_shape=(
            shaped(2, SEQ, width, dtype=bf16),
            shaped(8, *in_i.shape, dtype=bf16),
            shaped(8, *small.shape, dtype=bf16),
        ),
        scratch_shapes=gather_semaphores(),
        compiler_params=pltpu.CompilerParams(collective_id=0, has_side_effects=True, vmem_limit_bytes=VMEM_LIMIT),
    )(tokens, in_i, small)


LAG = 4
FIRST = BIG_STEPS
SECOND = FIRST + NCH
LAST = SECOND + NCH - 1
BEGIN = (0, SECOND)
FORWARD = (FIRST + 8, SECOND + 5)
FORWARD_AGAIN = (SECOND + 3, LAST)
HALVES = (FIRST + 6, SECOND + 1)
FOREIGN = SECOND + 2
RELAY = SECOND + 6


def pack_sum(ref, k, v):
    high = v[RANK:].astype(bf16)
    ref[k, :RANK] = v[:RANK].astype(bf16)
    ref[k, RANK:XW] = high
    ref[k, XW:] = (v[RANK:] - high.astype(f32)).astype(bf16)


def unpack_sum(ref, k):
    return jnp.concatenate([ref[k, :RANK].astype(f32), ref[k, RANK:XW].astype(f32) + ref[k, XW:].astype(f32)], axis=0)


def forward(raw_ref, gain_ref, wi_ref, mix_ref, conv_ref, xproj_ref, dtp_ref, vec_ref, rate_ref, in_g, out_w, cot_in,
            normed_ref, inv_ref, inner_ref, xconv_ref, yfull_ref, starts_ref, xdbl_ref, joined_ref, wg, wo, cot,
            inner_s, inv_s, buf, xc_s, part, ys, yr, zs, zr, tail_s, tail_r, state, last, last_r,
            dt_s, u_s, cb_s, h_s, y_s, y_send, y_recv, z_send, z_recv, e_send, e_recv, *sems):
    i = pl.program_id(0)
    gather = Gather([(in_g, wg, False), (out_w, wo, False)], cot_in, cot, *sems)
    g, r, c = gather.g, gather.r, gather.c
    y_dev, z_dev = gather.y_dev, gather.z_dev
    far_dev = (g, 1 - r, (c + 2) % 4)
    to_tail = remote(tail_s, tail_r, e_send.at[0], e_recv.at[0], far_dev)
    to_last = remote(last, last_r, e_send.at[1], e_recv.at[1], far_dev)

    def to_y(k):
        return remote(ys.at[k], yr.at[k], y_send.at[k], y_recv.at[k], y_dev)

    def to_z(k):
        return remote(zs.at[k], zr.at[k], z_send.at[k], z_recv.at[k], z_dev)

    @pl.when(i == 0)
    def _():
        gather.greet()

    @pl.when(i < FIRST)
    def _():
        rows = pl.ds(pl.multiple_of(i * BIG, BIG), BIG)
        project_first(raw_ref, gain_ref, wi_ref, normed_ref, inv_ref, inner_ref)
        inner_s[rows, :] = inner_ref[...]
        inv_s[rows, :] = inv_ref[...]

    @pl.when(i == FIRST)
    def _():
        tail_s[...] = inv_s[LP - 8 : LP] * inner_s[LP - 8 : LP]
        to_tail.start()
        buf[0:8] = jnp.zeros_like(buf[0:8])
        state[...] = jnp.zeros_like(state)

    mix = mix_ref[...]

    @pl.when(i == FIRST + PC)
    def _():
        to_tail.wait()
        joined = mix * tail_s[...] + (1.0 - mix) * tail_r[...]
        buf[0:8] = joined
        joined_ref[...] = joined

    @pl.when((i > FIRST) & (i < FIRST + PC))
    def _():
        buf[0:8] = buf[CH : CH + 8]

    @pl.when((i >= FIRST) & (i < SECOND))
    def _():
        k = i - FIRST
        rows = pl.ds(pl.multiple_of(k * CH, CH), CH)
        buf[8 : CH + 8] = inv_s[rows, :] * inner_s[rows, :]
        out = conv_ref[4:5]
        for tap in range(KCONV):
            out = out + conv_ref[tap : tap + 1] * buf[5 + tap : 5 + tap + CH]
        xconv = (out * jax.nn.sigmoid(out)).astype(bf16)
        xconv_ref[...] = xconv
        xc_s[k] = xconv
        part[k] = dot_nt(xproj_ref[...], xconv)
        pack_sum(ys, k, part[k])
        to_y(k).start()

    @pl.when((i >= FIRST + LAG) & (i < SECOND + LAG))
    def _():
        k = i - FIRST - LAG
        to_y(k).wait_recv()
        part[k] = part[k] + unpack_sum(yr, k)
        pack_sum(zs, k, part[k])
        to_z(k).start()

    @pl.when((i >= FIRST + 2 * LAG) & (i < SECOND + 2 * LAG))
    def _():
        k = i - FIRST - 2 * LAG
        to_z(k).wait_recv()
        xdbl_ref[k] = part[k] + unpack_sum(zr, k)

    for n in range(2):

        @pl.when(i == BEGIN[n])
        def _(n=n):
            gather.begin(n)

        @pl.when(i == FORWARD[n])
        def _(n=n):
            gather.forward(n)

        @pl.when(i == FORWARD_AGAIN[n])
        def _(n=n):
            gather.forward_again(n)

    for h in range(2):

        @pl.when(i == HALVES[h])
        def _(h=h):
            gather.begin_half(h)

    @pl.when(i == FOREIGN)
    def _():
        gather.begin_foreign()

    @pl.when(i == RELAY)
    def _():
        gather.relay()

    @pl.when(i == LAST)
    def _():
        to_last.wait()
        state[...] = mix_ref[0:1] * last[...] + (1.0 - mix_ref[0:1]) * last_r[...]

    @pl.when(i >= SECOND)
    def _():
        k = i - SECOND
        starts_ref[0] = state[...]
        h, yfull = scan_chunk(xdbl_ref.at[k], xc_s[k].astype(f32), dtp_ref, vec_ref, rate_ref, state[...], dt_s, u_s, cb_s, h_s, y_s)
        state[...] = h
        yfull_ref[...] = yfull.astype(bf16)

    @pl.when(i == LAST - 1)
    def _():
        last[...] = state[...]
        to_last.start()

    @pl.when(i == LAST)
    def _():
        gather.end_tokens()
        gather.end(0)
        gather.end(1)

        def sent(k, _):
            to_y(k).wait_send()
            to_z(k).wait_send()
            return 0

        lax.fori_loop(0, NCH, sent, 0)


def run_forward(raw, gain, wi, mix, conv, xproj, dtp, vec, rate, in_g, out_w, cot):
    w = SLOTS * wi.shape[2]
    width = raw.shape[2]
    zero = lambda i: jnp.minimum(i, FIRST - 1)
    first = lambda i: jnp.clip(i - FIRST, 0, NCH - 1)
    second = lambda i: jnp.maximum(i - SECOND, 0)
    dma = pltpu.SemaphoreType.DMA
    sums = pltpu.VMEM((NCH, XW + 2 * NSTATE, CH), bf16)
    return pl.pallas_call(
        forward,
        grid=(LAST + 1,),
        in_specs=[
            split_rows(width, zero, BIG),
            whole(2, width),
            whole(*wi.shape),
            whole(8, w),
            whole(8, w),
            whole(XW, w),
            whole(RANK, w),
            whole(8, w),
            whole(NSTATE, w),
            ANY,
            ANY,
            ANY,
        ],
        out_specs=(
            split_rows(width, zero, BIG),
            rows_of(1, zero, BIG),
            rows_of(w, zero, BIG),
            rows_of(w, first),
            rows_of(w, second),
            pl.BlockSpec((1, NSTATE, w), lambda i: (second(i), 0, 0)),
            whole(NCH, XW, CH),
            whole(8, w),
            ANY,
            ANY,
            ANY,
        ),
        out_shape=(
            shaped(2, SEQ, width, dtype=bf16),
            shaped(SEQ, 1),
            shaped(SEQ, w),
            shaped(SEQ, w, dtype=bf16),
            shaped(SEQ, w, dtype=bf16),
            shaped(NCH, NSTATE, w),
            shaped(NCH, XW, CH),
            shaped(8, w),
            shaped(8, *in_g.shape, dtype=bf16),
            shaped(8, *out_w.shape, dtype=bf16),
            shaped(2, SEQ, cot.shape[1], dtype=bf16),
        ),
        scratch_shapes=[
            pltpu.VMEM((SEQ, w), f32),
            pltpu.VMEM((SEQ, 1), f32),
            pltpu.VMEM((CH + 8, w), f32),
            pltpu.VMEM((NCH, CH, w), bf16),
            pltpu.VMEM((NCH, XW, CH), f32),
            sums,
            sums,
            sums,
            sums,
            pltpu.VMEM((8, w), f32),
            pltpu.VMEM((8, w), f32),
            pltpu.VMEM((NSTATE, w), f32),
            pltpu.VMEM((NSTATE, w), f32),
            pltpu.VMEM((NSTATE, w), f32),
            *scan_scratch(w),
            dma((NCH,)),
            dma((NCH,)),
            dma((NCH,)),
            dma((NCH,)),
            dma((2,)),
            dma((2,)),
            *gather_semaphores(),
        ],
        compiler_params=pltpu.CompilerParams(
            dimension_semantics=("arbitrary",), collective_id=2, has_side_effects=True, vmem_limit_bytes=VMEM_LIMIT
        ),
        cost_estimate=pl.CostEstimate(flops=60 * 1000000000, bytes_accessed=1000000, transcendentals=0),
    )(raw, gain, wi, mix, conv, xproj, dtp, vec, rate, in_g, out_w, cot)


def project_first(raw_ref, gain_ref, w_ref, normed_ref, inv_ref, out_ref):
    low = raw_ref[0].astype(f32)
    high = raw_ref[1].astype(f32)
    squares = jnp.sum(low * low + high * high, axis=1, keepdims=True)
    inv_ref[...] = lax.rsqrt(squares / D + eps)
    low = (low * gain_ref[0:1]).astype(bf16)
    high = (high * gain_ref[1:2]).astype(bf16)
    normed_ref[0] = low
    normed_ref[1] = high
    n = w_ref.shape[2]
    for k in range(SLOTS):
        out_ref[:, k * n : (k + 1) * n] = dot_nn(low, w_ref[2 * k]) + dot_nn(high, w_ref[2 * k + 1])


def split_rows(width, at, tall=CH):
    return pl.BlockSpec((2, tall, width), lambda i: (0, at(i), 0))


def run_project_first(raw, gain, w):
    width = raw.shape[2]
    at = lambda i: i
    n = SLOTS * w.shape[2]
    return call(
        project_first,
        BIG_STEPS,
        (raw, gain, w),
        [split_rows(width, at, BIG), whole(2, width), whole(*w.shape)],
        (shaped(2, SEQ, width, dtype=bf16), shaped(SEQ, 1), shaped(SEQ, n)),
        (split_rows(width, at, BIG), rows_of(1, at, BIG), rows_of(n, at, BIG)),
        [],
        9,
    )


def gate_backward(normed_ref, wg_ref, cot_ref, wo_ref, yfull_ref, inv_ref, gated_ref, dy_ref, dproj_ref, dscale_ref, own_ref, oth_ref, gate_s):
    n = wo_ref.shape[2]
    for k in range(SLOTS):
        gate_s[:, k * n : (k + 1) * n] = dot_nn(normed_ref[0], wg_ref[2 * k]) + dot_nn(normed_ref[1], wg_ref[2 * k + 1])
    d_gated = jnp.zeros(dy_ref.shape, f32)
    for k in range(SLOTS):
        for d in range(2):
            d_gated = d_gated + dot_nt(cot_ref[d, :, k * n : (k + 1) * n], wo_ref[2 * k + d])
    gate_in = gate_s[...]
    inv = inv_ref[...]
    yfull = yfull_ref[...].astype(f32)
    gate = inv * gate_in
    sig = jax.nn.sigmoid(gate)
    passed = gate * sig
    gated = (yfull * passed).astype(bf16)
    gated_ref[...] = gated
    for k in range(SLOTS):
        own_ref[:, k * n : (k + 1) * n] = dot_nn(gated, wo_ref[2 * k])
        oth_ref[:, k * n : (k + 1) * n] = dot_nn(gated, wo_ref[2 * k + 1]).astype(bf16)
    dy_ref[...] = d_gated * passed
    d_gate = d_gated * yfull * (sig * (1.0 + gate * (1.0 - sig)))
    dproj_ref[...] = (inv * d_gate).astype(bf16)
    dscale_ref[...] = jnp.sum(d_gate * gate_in, axis=1, keepdims=True)


def run_gate_backward(normed, wg, cot, wo, yfull, inv):
    width = cot.shape[2]
    w = yfull.shape[1]
    at = lambda i: i
    return call(
        gate_backward,
        BIG_STEPS,
        (normed, wg, cot, wo, yfull, inv),
        [split_rows(width, at, BIG), whole(*wg.shape), split_rows(width, at, BIG), whole(*wo.shape), rows_of(w, at, BIG), rows_of(1, at, BIG)],
        (shaped(SEQ, w, dtype=bf16), shaped(SEQ, w), shaped(SEQ, w, dtype=bf16), shaped(SEQ, 1), shaped(SEQ, width), shaped(SEQ, width, dtype=bf16)),
        (rows_of(w, at, BIG), rows_of(w, at, BIG), rows_of(w, at, BIG), rows_of(1, at, BIG), rows_of(width, at, BIG), rows_of(width, at, BIG)),
        [pltpu.VMEM((BIG, w), f32)],
        22,
    )


def normed_backward(inner_ref, gate_ref, wi_ref, wg_ref, own_ref, oth_ref):
    n = wi_ref.shape[2]
    for d, out_ref in ((1, oth_ref), (0, own_ref)):
        total = jnp.zeros(out_ref.shape, f32)
        for k in range(SLOTS):
            total = total + dot_nt(inner_ref[:, k * n : (k + 1) * n], wi_ref[2 * k + d])
            total = total + dot_nt(gate_ref[:, k * n : (k + 1) * n], wg_ref[2 * k + d])
        out_ref[...] = total.astype(out_ref.dtype)


def run_normed_backward(d_inner, d_gate, wi, wg):
    w = d_inner.shape[1]
    width = wi.shape[1]
    at = lambda i: i
    return call(
        normed_backward,
        BIG_STEPS,
        (d_inner, d_gate, wi, wg),
        [rows_of(w, at, BIG), rows_of(w, at, BIG), whole(*wi.shape), whole(*wg.shape)],
        (shaped(SEQ, width), shaped(SEQ, width, dtype=bf16)),
        (rows_of(width, at, BIG), rows_of(width, at, BIG)),
        [],
        12,
    )


def finish(inner_hbm, gate_hbm, normed_hbm, raw_hbm, wi_hbm, wg_hbm, gain_in_ref, pull_ref, conv_hbm, scan_hbm, alog_hbm, dtp_hbm, xproj_hbm,
           dn_ref, grad_ref, gain_ref, small_refs,
           inner, gate, normed, raw, wi, wg, cs, cr, pairs, xs, xr, fs, fr, ys, yr, zs, zr, own, fin, gs, gr, sv, kr, ks, kx, kf, kg,
           loc, c_send, c_recv, x_send, x_recv, f_send, f_recv, y_send, y_recv, z_send, z_recv, b_send, b_recv, g_send, g_recv, s_send, s_recv, s_load):
    g, r, c = lax.axis_index("grp"), lax.axis_index("row"), lax.axis_index("col")
    x, core, s, p = g // 2, g % 2, c // 2, c % 2
    tall, width = raw.shape
    part = tall // 2
    n = wi_hbm.shape[2]
    q = 2 * p + xor_bit(r, s)
    y_dev, z_dev = (g, 1 - r, c), (g, r, 2 * s + 1 - p)
    x_dev, core_dev = ((1 - x) * 2 + core, r, c), (2 * x + 1 - core, r, c)
    alone = q == c

    loads = [
        pltpu.make_async_copy(normed_hbm, normed, loc.at[0]),
        pltpu.make_async_copy(inner_hbm, inner, loc.at[1]),
        pltpu.make_async_copy(gate_hbm, gate, loc.at[2]),
        pltpu.make_async_copy(raw_hbm.at[0, pl.ds(pl.multiple_of(p * tall, 64), tall)], raw, loc.at[5]),
    ]
    for copy in loads[:3]:
        copy.start()
    for k in range(SLOTS):
        for d in range(2):
            cols = pl.ds(k * n, n)
            pltpu.make_async_copy(wi_hbm.at[2 * k + d], wi.at[d, :, cols], loc.at[3]).start()
            pltpu.make_async_copy(wg_hbm.at[2 * k + d], wg.at[d, :, cols], loc.at[4]).start()
    loads[3].start()

    barrier = pltpu.get_barrier_semaphore()
    for dg in range(4):
        for dc in range(4):
            if dg or dc:
                pl.semaphore_signal(barrier, inc=1, device_id=((g + dg) % 4, r, (c + dc) % 4), device_id_type=MESH)
    for dc in range(4):
        pl.semaphore_signal(barrier, inc=1, device_id=(g, 1 - r, (c + dc) % 4), device_id_type=MESH)
    pl.semaphore_wait(barrier, 19)

    def small_loads():
        at = 0
        for ref in (conv_hbm, scan_hbm, alog_hbm, dtp_hbm, xproj_hbm):
            yield pltpu.make_async_copy(ref, sv.at[pl.ds(at, ref.shape[0])], s_load.at[0])
            at += ref.shape[0]

    def channels(d, at_x, at_core):
        to_r = r if d == 0 else 1 - r
        return pl.ds(pl.multiple_of((to_r * 4 + 2 * at_x + at_core) * 128, 128), 128)

    def small_core(j, d):
        src = sv.at[:, channels(d, 1 - x if j == 0 else x, 1 - core)]
        return remote(src, kr.at[j, d], s_send.at[2 * j + d], s_recv.at[2 * j + d], core_dev)

    def small_x(d):
        return remote(ks.at[d], kx.at[d], s_send.at[4 + d], s_recv.at[4 + d], x_dev)

    def small_owner(d):
        return remote(kf.at[d], kg.at[d], s_send.at[6 + d], s_recv.at[6 + d], (g, r if d == 0 else 1 - r, q))

    for copy in small_loads():
        copy.start()

    def weight_grad(at_x, d):
        cols = pl.ds(pl.multiple_of(at_x * 2 * n, 128), 2 * n)

        def tile(t, _):
            rows = pl.ds(pl.multiple_of(t * n, 128), n)
            pairs[d, rows, :] = dot_tn(normed[d, :, rows], inner[:, cols])
            return 0

        lax.fori_loop(0, width // n, tile, 0)

    def of_core(at_core):
        return pl.ds(pl.multiple_of(at_core * n, 128), n)

    def to_core(i, d):
        return remote(cs.at[i, d], cr.at[i, d], c_send.at[2 * i + d], c_recv.at[2 * i + d], core_dev)

    def to_x(d):
        return remote(xs.at[d], xr.at[d], x_send.at[d], x_recv.at[d], x_dev)

    def to_owner(d):
        return remote(fs.at[d], fr.at[d], f_send.at[d], f_recv.at[d], (g, r if d == 0 else 1 - r, q))

    def grad_to_core(i):
        for d in range(2):
            weight_grad(1 - x if i == 0 else x, d)
            cs[i, d] = pairs[d, :, of_core(1 - core)].astype(bf16)
            to_core(i, d).start()

    def start_of(mine, h):
        return pl.multiple_of((p if mine else 1 - p) * tall + h * part, 32)

    def normed_part(mine, h, d, store):
        rows = pl.ds(start_of(mine, h), part)

        def tile(t, _):
            cols = pl.ds(pl.multiple_of(t * n, 128), n)
            total = dot_nt(inner[rows, :], wi[d, cols, :]) + dot_nt(gate[rows, :], wg[d, cols, :])
            store(cols, total)
            return 0

        lax.fori_loop(0, width // n, tile, 0)

    def to_y(i):
        return remote(ys.at[i], yr.at[i], y_send.at[i], y_recv.at[i], y_dev)

    def to_z(i):
        return remote(zs.at[i], zr.at[i], z_send.at[i], z_recv.at[i], z_dev)

    def into(ref, i, added=None):
        def store(cols, v):
            if added is not None:
                v = v + added[0, :, cols].astype(f32)
            ref[i, :, cols] = v.astype(bf16)

        return store

    pltpu.make_async_copy(sv, sv, s_load.at[0]).wait()
    for j in range(2):
        for d in range(2):
            small_core(j, d).start()
    loads[0].wait()
    loads[1].wait()
    grad_to_core(0)
    loads[2].wait()
    pltpu.make_async_copy(wi, wi, loc.at[3]).wait()
    pltpu.make_async_copy(wg, wg, loc.at[4]).wait()
    for d in range(2):
        to_core(0, d).wait_recv()
        xs[d] = (pairs[d, :, of_core(core)] + cr[0, d].astype(f32)).astype(bf16)
        to_x(d).start()

    for d in range(2):
        small_core(0, d).wait_recv()
        ks[d] = sv[:, channels(d, 1 - x, core)] + kr[0, d]
        small_x(d).start()

    normed_part(False, 0, 1, into(ys, 0))
    to_y(0).start()
    normed_part(False, 1, 1, into(zs, 0))
    to_z(0).start()
    normed_part(False, 1, 0, into(zs, 2))
    to_z(2).start()
    normed_part(True, 0, 1, into(ys, 1))
    to_y(1).start()
    grad_to_core(1)
    to_y(0).wait_recv()
    normed_part(False, 0, 0, into(zs, 1, yr))
    to_z(1).start()
    to_z(0).wait_recv()
    normed_part(True, 1, 1, into(ys, 2, zr))
    to_y(2).start()

    for d in range(2):
        to_core(1, d).wait_recv()
        to_x(d).wait_recv()
        fs[d] = (pairs[d, :, of_core(core)] + cr[1, d].astype(f32) + xr[d].astype(f32)).astype(bf16)
        if d == 0:

            @pl.when(alone)
            def _():
                fr[0] = fs[0]

            @pl.when(jnp.logical_not(alone))
            def _():
                to_owner(0).start()
        else:
            to_owner(1).start()
    for d in range(2):
        small_core(1, d).wait_recv()
        small_x(d).wait_recv()
        kf[d] = sv[:, channels(d, x, core)] + kr[1, d] + kx[d]

    @pl.when(alone)
    def _():
        kg[0] = kf[0]

    @pl.when(jnp.logical_not(alone))
    def _():
        small_owner(0).start()

    small_owner(1).start()

    for h in range(2):

        def store(cols, v, h=h):
            own[h * part : (h + 1) * part, cols] = v

        normed_part(True, h, 0, store)

    loads[3].wait()
    for h in range(2):
        to_y(1 + h).wait_recv()
        to_z(1 + h).wait_recv()
        total = own[h * part : (h + 1) * part, :] + yr[1 + h].astype(f32) + zr[1 + h].astype(f32)
        tokens = raw[h * part : (h + 1) * part, :].astype(f32)
        pulled = total * gain_in_ref[0:1] - pull_ref[h * part : (h + 1) * part, :] * tokens
        fin[h * part : (h + 1) * part, :] = pulled.astype(bf16)
        product = total * tokens
        folded = jnp.sum(product.reshape(part // 8, 8, width), axis=0)
        for b in range(SLOTS):
            if h == 0:
                gs[b] = folded[:, b * n : (b + 1) * n]
            else:
                gs[b] = gs[b] + folded[:, b * n : (b + 1) * n]

    cut = tall - LC
    low = cut - LC
    moves = {
        0: ([(0, tall, 0)], None),
        1: ([(0, cut, 0)], (cut, 3, low)),
        2: ([(LC, tall, 0)], (0, 1, cut)),
        3: ([(LC, cut, 0), (cut, tall, cut)], (0, 2, cut)),
    }

    def border(k):
        stays, leaves = moves[k]
        mine = [pltpu.make_async_copy(fin.at[a:b], dn_ref.at[at : at + b - a], loc.at[i]) for i, (a, b, at) in enumerate(stays)]
        if leaves is None:
            return mine, None
        a, to, at = leaves
        return mine, remote(fin.at[a : a + LC], dn_ref.at[at : at + LC], b_send.at[0], b_recv.at[0], (g, r, to))

    for k in range(4):

        @pl.when(c == k)
        def _(k=k):
            mine, gone = border(k)
            if gone is not None:
                gone.start()
            for copy in mine:
                copy.start()

    def gain_copy(dg, dc):
        to = ((g + dg) % 4, r, (c + dc) % 4)
        i = 4 * dg + dc - 1
        return remote(gs.at[(g + dg) % 4], gr.at[i], g_send.at[i], g_recv.at[0], to)

    pairs = [(dg, dc) for dg in range(4) for dc in range(4) if dg or dc]
    for dg, dc in pairs:
        gain_copy(dg, dc).start()

    @pl.when(jnp.logical_not(alone))
    def _():
        to_owner(0).wait_recv()

    to_owner(1).wait_recv()
    grad_ref[...] = fr[0].astype(f32) + fr[1].astype(f32)

    pltpu.make_async_copy(gr, gr, g_recv.at[0]).wait()
    gain_ref[...] = jnp.sum(gr[...], axis=0) + gs[g]

    for k in range(4):

        @pl.when(c == k)
        def _(k=k):
            mine, gone = border(k)
            for copy in mine:
                copy.wait()
            if gone is not None:
                gone.wait()

    @pl.when(jnp.logical_not(alone))
    def _():
        small_owner(0).wait()

    small_owner(1).wait()
    at = 0
    for ref in small_refs:
        ref[...] = kg[0, at : at + ref.shape[0], :] + kg[1, at : at + ref.shape[0], :]
        at += ref.shape[0]
    for d in range(2):
        for j in range(2):
            small_core(j, d).wait_send()
        small_x(d).wait_send()

    for dg, dc in pairs:
        gain_copy(dg, dc).wait_send()
    for i in range(3):
        to_y(i).wait_send()
        to_z(i).wait_send()
    for d in range(2):
        for i in range(2):
            to_core(i, d).wait_send()
        to_x(d).wait_send()

    @pl.when(jnp.logical_not(alone))
    def _():
        to_owner(0).wait_send()

    to_owner(1).wait_send()


SMALL_ROWS = (KCONV, 1, 3, 1, 1, 6, NSTATE, RANK, XW)


def finish_kernel(*refs):
    n = len(SMALL_ROWS)
    finish(*refs[:16], refs[16 : 16 + n], *refs[16 + n :])


def run_finish(d_inner, d_gate, normed, raw, wi, wg, gain, pull, small):
    w = d_inner.shape[1]
    width, n = wi.shape[1], wi.shape[2]
    tall = SEQ // 2
    part = tall // 2
    dma = pltpu.SemaphoreType.DMA
    low = lambda *shape: pltpu.VMEM(shape, bf16)
    vmem = pl.BlockSpec(memory_space=pltpu.VMEM)
    rows = sum(v.shape[0] for v in small)
    return pl.pallas_call(
        finish_kernel,
        in_specs=[ANY] * 6 + [vmem, vmem] + [ANY] * 5,
        out_specs=[ANY, vmem, vmem] + [vmem] * len(SMALL_ROWS),
        out_shape=(shaped(tall, width, dtype=bf16), shaped(width, n), shaped(8, n), *[shaped(v, 128) for v in SMALL_ROWS]),
        scratch_shapes=[
            low(SEQ, w),
            low(SEQ, w),
            low(2, SEQ, width),
            low(tall, width),
            low(2, width, w),
            low(2, width, w),
            low(2, 2, width, n),
            low(2, 2, width, n),
            pltpu.VMEM((2, width, 2 * n), f32),
            low(2, width, n),
            low(2, width, n),
            low(2, width, n),
            low(2, width, n),
            low(3, part, width),
            low(3, part, width),
            low(3, part, width),
            low(3, part, width),
            pltpu.VMEM((tall, width), f32),
            low(tall, width),
            pltpu.VMEM((SLOTS, 8, n), f32),
            pltpu.VMEM((15, 8, n), f32),
            pltpu.VMEM((rows, w), f32),
            pltpu.VMEM((2, 2, rows, 128), f32),
            pltpu.VMEM((2, rows, 128), f32),
            pltpu.VMEM((2, rows, 128), f32),
            pltpu.VMEM((2, rows, 128), f32),
            pltpu.VMEM((2, rows, 128), f32),
            dma((6,)),
            dma((4,)),
            dma((4,)),
            dma((2,)),
            dma((2,)),
            dma((2,)),
            dma((2,)),
            dma((3,)),
            dma((3,)),
            dma((3,)),
            dma((3,)),
            dma((1,)),
            dma((1,)),
            dma((15,)),
            dma((1,)),
            dma((8,)),
            dma((8,)),
            dma((1,)),
        ],
        compiler_params=pltpu.CompilerParams(collective_id=1, has_side_effects=True, vmem_limit_bytes=VMEM_LIMIT),
        cost_estimate=pl.CostEstimate(flops=60 * 1000000000, bytes_accessed=1000000, transcendentals=0),
    )(d_inner, d_gate, normed, raw, wi, wg, gain, pull, *small)


def late_parts(order_ref, normed_ref, gate_ref, gated_ref, cot_ref, gate_sent, out_sent, gate_kept, out_kept):
    t = pl.program_id(0)
    for d in range(2):
        low = dot_tn(normed_ref[d], gate_ref[...])
        high = dot_tn(gated_ref[...], cot_ref[d])

        @pl.when(t < 2)
        def _(d=d, low=low, high=high):
            gate_sent[0, d] = low.astype(bf16)
            out_sent[0, d] = high.astype(bf16)

        @pl.when(t >= 2)
        def _(d=d, low=low, high=high):
            gate_kept[0, d] = low
            out_kept[0, d] = high


def run_late_parts(order, normed, d_gate, gated, cot):
    width = normed.shape[2]
    w = gated.shape[1]
    n = w // SLOTS
    sent = pl.BlockSpec((1, 2, width, n), lambda t, o: (jnp.minimum(t, 1), 0, 0, 0))
    kept = pl.BlockSpec((1, 2, width, n), lambda t, o: (jnp.maximum(t - 2, 0), 0, 0, 0))
    return pl.pallas_call(
        late_parts,
        grid_spec=pltpu.PrefetchScalarGridSpec(
            num_scalar_prefetch=1,
            grid=(SLOTS,),
            in_specs=[
                pl.BlockSpec((2, SEQ, width), lambda t, o: (0, 0, 0)),
                pl.BlockSpec((SEQ, n), lambda t, o: (0, o[t])),
                pl.BlockSpec((SEQ, w), lambda t, o: (0, 0)),
                pl.BlockSpec((2, SEQ, n), lambda t, o: (0, 0, o[t])),
            ],
            out_specs=(sent, sent, kept, kept),
        ),
        out_shape=(shaped(2, 2, width, n, dtype=bf16), shaped(2, 2, width, n, dtype=bf16), shaped(2, 2, width, n), shaped(2, 2, width, n)),
        compiler_params=pltpu.CompilerParams(dimension_semantics=("arbitrary",), vmem_limit_bytes=VMEM_LIMIT),
        cost_estimate=pl.CostEstimate(flops=14 * 1000000000, bytes_accessed=1000000, transcendentals=0),
    )(order, normed, d_gate, gated, cot)


QUARTERS = 4
SUM_LAG = 3
PIECE = SEQ // 2 // QUARTERS
OTHER_STEP = (1, 2, 3, 4)
PAIR_STEP = (3, 4, 1, 2)
FINAL_STEP = (7, 7, 7, 7)
X_STEP = (0, 1)
OWNER_STEP = (2, 4)
DONE_STEP = (8, 8)
QUARTER_STEP = ((2, 3, 4, 5), (4, 5, 6, 7))


def border_moves(tall):
    cut = tall - LC
    low = cut - LC
    return {
        0: ([(0, tall, 0)], None),
        1: ([(0, cut, 0)], (cut, 3, low)),
        2: ([(LC, tall, 0)], (0, 1, cut)),
        3: ([(LC, cut, 0), (cut, tall, cut)], (0, 2, cut)),
    }


def backward(xdbl_ref, xconv_ref, dy_ref, dtp_ref, vec_ref, rate_ref, starts_ref, mix_ref, into_ref, sent_hbm, kept_hbm, own_hbm, oth_hbm,
             dxdbl_ref, dxc_ref, alog_ref, sums_ref, dtpg_ref, grad_ref, branch_ref,
             first, first_s, first_r, part, ys, yr, zs, zr, cr, kp, xs, xr, fs, fr, out, own, oth, by_s, by, bz_s, bz, fin,
             y_send, y_recv, z_send, z_recv, e_send, e_recv, c_send, c_recv, x_send, x_recv, f_send, f_recv,
             p_send, p_recv, q_send, q_recv, b_send, b_recv, load_k, load_o, stay, put, *scratch):
    i = pl.program_id(0)
    g, r, c = lax.axis_index("grp"), lax.axis_index("row"), lax.axis_index("col")
    x, core, s, p = g // 2, g % 2, c // 2, c % 2
    q = 2 * p + xor_bit(r, s)
    tall = SEQ // 2
    alone = q == c
    y_dev, z_dev, far_dev = (g, 1 - r, c), (g, r, 2 * s + 1 - p), (g, 1 - r, (c + 2) % 4)
    x_dev, core_dev = ((1 - x) * 2 + core, r, c), (2 * x + 1 - core, r, c)
    to_first = remote(first_s, first_r, e_send.at[0], e_recv.at[0], far_dev)

    def to_y(k):
        return remote(ys.at[k], yr.at[k], y_send.at[k], y_recv.at[k], y_dev)

    def to_z(k):
        return remote(zs.at[k], zr.at[k], z_send.at[k], z_recv.at[k], z_dev)

    def to_core(n, j):
        return remote(sent_hbm[n].at[j], cr.at[n, j], c_send.at[n, j], c_recv.at[n, j], core_dev)

    def load(n, j):
        return pltpu.make_async_copy(kept_hbm[n].at[j], kp.at[n], load_k.at[n])

    def to_x(n):
        return remote(xs.at[n], xr.at[n], x_send.at[n], x_recv.at[n], x_dev)

    def to_owner(n, d, at=None):
        device = (g, r if d == 0 else 1 - r, q)
        if at is None:
            return remote(fs.at[n, d], fr.at[n, d], f_send.at[n, d], f_recv.at[n, d], device)
        tall = fs.shape[2] // QUARTERS
        rows = pl.ds(at * tall, tall)
        return remote(fs.at[n, d, rows], fr.at[n, d, rows], f_send.at[n, d], f_recv.at[n, d], device)

    def rows_at(mine, j):
        return pl.ds(pl.multiple_of((p if mine else 1 - p) * tall + j * PIECE, 16), PIECE)

    def branch_y(m):
        if m >= QUARTERS:
            src = oth_hbm.at[rows_at(False, m - QUARTERS)]
        elif m < 2:
            src = oth_hbm.at[rows_at(True, m)]
        else:
            src = by_s.at[m - 2]
        return remote(src, by.at[m], p_send.at[m], p_recv.at[m], y_dev)

    def branch_z(m):
        src = bz_s.at[m] if m < QUARTERS else oth_hbm.at[rows_at(False, m - 2)]
        return remote(src, bz.at[m], q_send.at[m], q_recv.at[m], z_dev)

    load_own = pltpu.make_async_copy(own_hbm, own, load_o.at[0])
    load_oth = pltpu.make_async_copy(oth_hbm.at[pl.ds(pl.multiple_of(p * tall + 2 * PIECE, 16), 2 * PIECE)], oth, load_o.at[1])

    def border(k):
        stays, leaves = border_moves(tall)[k]
        mine = [pltpu.make_async_copy(fin.at[a:b], branch_ref.at[at : at + b - a], stay.at[n]) for n, (a, b, at) in enumerate(stays)]
        if leaves is None:
            return mine, None
        a, to, at = leaves
        return mine, remote(fin.at[a : a + LC], branch_ref.at[at : at + LC], b_send.at[0], b_recv.at[0], (g, r, to))

    def at_border(act):
        for k in range(4):

            @pl.when(c == k)
            def _(k=k):
                act(*border(k))

    def pass_on(k):
        to_y(k).wait_recv()
        part[k] = part[k] + yr[k].astype(f32)
        zs[k] = part[k].astype(bf16)
        to_z(k).start()

    def settle(k):
        to_z(k).wait_recv()
        dxdbl_ref[NCH - 1 - k] = part[k] + zr[k].astype(f32)

    @pl.when(i == 0)
    def _():
        barrier = pltpu.get_barrier_semaphore()
        for dr in range(2):
            for dc in range(4):
                if dr or dc:
                    pl.semaphore_signal(barrier, inc=1, device_id=(g, (r + dr) % 2, (c + dc) % 4), device_id_type=MESH)
        for device in (x_dev, core_dev):
            pl.semaphore_signal(barrier, inc=1, device_id=device, device_id_type=MESH)
        pl.semaphore_wait(barrier, 9)
        for j in range(2):
            for n in range(2):
                to_core(n, j).start()
        for n in range(2):
            load(n, 0).start()
        load_own.start()
        load_oth.start()
        for m in (QUARTERS, QUARTERS + 1):
            branch_y(m).start()
            branch_z(m).start()
        first[...] = jnp.zeros_like(first)
        alog_ref[...] = jnp.zeros_like(alog_ref)
        sums_ref[...] = jnp.zeros_like(sums_ref)
        dtpg_ref[...] = jnp.zeros_like(dtpg_ref)

    @pl.when(i == 1)
    def _():
        to_first.wait()
        first[...] = mix_ref[0:1] * first_s[...] + into_ref[0:1] * first_r[...]

    chunk_backward(xdbl_ref, xconv_ref, dy_ref, dtp_ref, vec_ref, rate_ref, starts_ref, part.at[i], dxc_ref, alog_ref, sums_ref, dtpg_ref, first, *scratch)

    @pl.when(i == 0)
    def _():
        first_s[...] = first[...]
        to_first.start()

    @pl.when(i == 1)
    def _():
        load_own.wait()
        load_oth.wait()

    for n in range(2):

        @pl.when(i == X_STEP[n])
        def _(n=n):
            to_core(n, 0).wait_recv()
            load(n, 0).wait()
            xs[n] = (kp[n] + cr[n, 0].astype(f32)).astype(bf16)
            to_x(n).start()
            load(n, 1).start()

        @pl.when(i == OWNER_STEP[n])
        def _(n=n):
            load(n, 1).wait()
            to_core(n, 1).wait_recv()
            to_x(n).wait_recv()
            fs[n] = (kp[n] + cr[n, 1].astype(f32) + xr[n].astype(f32)).astype(bf16)

            @pl.when(alone)
            def _():
                fr[n, 0] = fs[n, 0]

        for k in range(QUARTERS):

            @pl.when(i == QUARTER_STEP[n][k])
            def _(n=n, k=k):
                @pl.when(jnp.logical_not(alone))
                def _():
                    to_owner(n, 0, k).start()

                to_owner(n, 1, k).start()

        @pl.when(i == DONE_STEP[n])
        def _(n=n):
            @pl.when(jnp.logical_not(alone))
            def _():
                to_owner(n, 0).wait_recv()

            to_owner(n, 1).wait_recv()
            out[n] = fr[n, 0].astype(f32) + fr[n, 1].astype(f32)
            pltpu.make_async_copy(out.at[n], grad_ref.at[n], put.at[n]).start()

    for j in range(QUARTERS):

        @pl.when(i == OTHER_STEP[j])
        def _(j=j):
            if j >= 2:
                branch_z(QUARTERS + j - 2).wait_recv()
                mine = oth[(j - 2) * PIECE : (j - 1) * PIECE, :].astype(f32)
                by_s[j - 2] = (mine + bz[QUARTERS + j - 2].astype(f32)).astype(bf16)
            branch_y(j).start()

        @pl.when(i == PAIR_STEP[j])
        def _(j=j):
            total = own[rows_at(False, j), :]
            if j < 2:
                branch_y(QUARTERS + j).wait_recv()
                total = total + by[QUARTERS + j].astype(f32)
            bz_s[j] = total.astype(bf16)
            branch_z(j).start()

        @pl.when(i == FINAL_STEP[j])
        def _(j=j):
            branch_y(j).wait_recv()
            branch_z(j).wait_recv()
            fin[j * PIECE : (j + 1) * PIECE, :] = (own[rows_at(True, j), :] + by[j].astype(f32) + bz[j].astype(f32)).astype(bf16)

    @pl.when(i == 7)
    def _():
        def begin(mine, gone):
            if gone is not None:
                gone.start()
            for copy in mine:
                copy.start()

        at_border(begin)

    @pl.when(i >= SUM_LAG)
    def _():
        pass_on(i - SUM_LAG)

    ys[i] = part[i].astype(bf16)
    to_y(i).start()
    @pl.when(i == NCH - 1)
    def _():
        for k in range(NCH - SUM_LAG, NCH):
            pass_on(k)
        for k in range(NCH):
            settle(k)

        def finish_border(mine, gone):
            for copy in mine:
                copy.wait()
            if gone is not None:
                gone.wait()

        at_border(finish_border)

        def sent(k, _):
            to_y(k).wait_send()
            to_z(k).wait_send()
            return 0

        lax.fori_loop(0, NCH, sent, 0)
        for n in range(2):
            for j in range(2):
                to_core(n, j).wait_send()
            to_x(n).wait_send()

            @pl.when(jnp.logical_not(alone))
            def _(n=n):
                to_owner(n, 0).wait_send()

            to_owner(n, 1).wait_send()
            pltpu.make_async_copy(out.at[n], grad_ref.at[n], put.at[n]).wait()
        for m in range(QUARTERS + 2):
            branch_y(m).wait_send()
            branch_z(m).wait_send()


def backward_kernel(*refs):
    backward(*refs[:9], refs[9:11], refs[11:13], *refs[13:])


def run_backward(xdbl, xconv, dy, dtp, vec, rate, starts, mix, into, sent, kept, own, oth):
    w = xconv.shape[1]
    width = own.shape[1]
    _, _, tall, n = sent[0].shape
    at = lambda i: NCH - 1 - i
    dma = pltpu.SemaphoreType.DMA
    low = lambda *shape: pltpu.VMEM(shape, bf16)
    sums = low(NCH, XW, CH)
    state = pltpu.VMEM((NSTATE, w), f32)
    return pl.pallas_call(
        backward_kernel,
        grid=(NCH,),
        in_specs=[
            chunk_of(XW, at),
            rows_of(w, at),
            rows_of(w, at),
            whole(RANK, w),
            whole(8, w),
            whole(NSTATE, w),
            pl.BlockSpec((1, NSTATE, w), lambda i: (at(i), 0, 0)),
            whole(8, w),
            whole(8, w),
        ]
        + [ANY] * 6,
        out_specs=(whole(NCH, XW, CH), rows_of(w, at), whole(NSTATE, w), whole(8, w), whole(RANK, w), ANY, ANY),
        out_shape=(
            shaped(NCH, XW, CH),
            shaped(SEQ, w),
            shaped(NSTATE, w),
            shaped(8, w),
            shaped(RANK, w),
            shaped(2, tall, n),
            shaped(SEQ // 2, width, dtype=bf16),
        ),
        scratch_shapes=[
            state,
            state,
            state,
            pltpu.VMEM((NCH, XW, CH), f32),
            sums,
            sums,
            sums,
            sums,
            low(2, 2, 2, tall, n),
            pltpu.VMEM((2, 2, tall, n), f32),
            low(2, 2, tall, n),
            low(2, 2, tall, n),
            low(2, 2, tall, n),
            low(2, 2, tall, n),
            pltpu.VMEM((2, tall, n), f32),
            pltpu.VMEM((SEQ, width), f32),
            low(2 * PIECE, width),
            low(2, PIECE, width),
            low(QUARTERS + 2, PIECE, width),
            low(QUARTERS, PIECE, width),
            low(QUARTERS + 2, PIECE, width),
            low(SEQ // 2, width),
            dma((NCH,)),
            dma((NCH,)),
            dma((NCH,)),
            dma((NCH,)),
            dma((1,)),
            dma((1,)),
            dma((2, 2)),
            dma((2, 2)),
            dma((2,)),
            dma((2,)),
            dma((2, 2)),
            dma((2, 2)),
            dma((QUARTERS + 2,)),
            dma((QUARTERS + 2,)),
            dma((QUARTERS + 2,)),
            dma((QUARTERS + 2,)),
            dma((1,)),
            dma((1,)),
            dma((2,)),
            dma((2,)),
            dma((2,)),
            dma((2,)),
            *backward_scratch(w),
        ],
        compiler_params=pltpu.CompilerParams(
            dimension_semantics=("arbitrary",), collective_id=3, has_side_effects=True, vmem_limit_bytes=61 * 1024 * 1024
        ),
        cost_estimate=pl.CostEstimate(flops=120 * 1000000000, bytes_accessed=1000000, transcendentals=0),
    )(xdbl, xconv, dy, dtp, vec, rate, starts, mix, into, *sent, *kept, own, oth)


def conv_backward_far(inner_ref, halo_ref, inv_ref, halo_inv_ref, tail_ref, conv_ref, xproj_ref, dxc_ref, dxdbl_ref, mix_ref, into_ref,
                      dproj_ref, dscale_ref, sums_ref, xprojg_ref, head, sent, got, buf, dbuf, send_sem, recv_sem):
    i = pl.program_id(0)
    g, r, c = lax.axis_index("grp"), lax.axis_index("row"), lax.axis_index("col")
    far_dev = (g, 1 - r, (c + 2) % 4)
    to_far = remote(sent, got, send_sem.at[0], recv_sem.at[0], far_dev)

    @pl.when(i == 0)
    def _():
        barrier = pltpu.get_barrier_semaphore()
        pl.semaphore_signal(barrier, inc=1, device_id=far_dev, device_id_type=MESH)
        pl.semaphore_wait(barrier, 1)
        head[...] = jnp.zeros_like(head)
        sums_ref[...] = jnp.zeros_like(sums_ref)
        xprojg_ref[...] = jnp.zeros_like(xprojg_ref)

    @pl.when(i == 1)
    def _():
        to_far.wait()
        head[...] = mix_ref[...] * sent[...] + into_ref[...] * got[...]

    conv_chunk(NCH - 1 - i, inner_ref, halo_ref, inv_ref, halo_inv_ref, tail_ref, conv_ref, xproj_ref, dxc_ref, dxdbl_ref,
               dproj_ref, dscale_ref, sums_ref, xprojg_ref, head, buf, dbuf)

    @pl.when(i == 0)
    def _():
        sent[...] = head[...]
        to_far.start()


def run_conv_backward_far(inner, inv, tail, conv, xproj, dxc, dxdbl, mix, into):
    w = inner.shape[1]
    at = lambda i: NCH - 1 - i
    before = lambda i: (jnp.maximum(at(i) * (CH // 8) - 1, 0), 0)
    rows = pltpu.VMEM((8, w), f32)
    return pl.pallas_call(
        conv_backward_far,
        grid=(NCH,),
        in_specs=[
            rows_of(w, at),
            pl.BlockSpec((8, w), before),
            rows_of(1, at),
            pl.BlockSpec((8, 1), before),
            whole(8, w),
            whole(8, w),
            whole(XW, w),
            rows_of(w, at),
            chunk_of(XW, at),
            whole(8, w),
            whole(8, w),
        ],
        out_specs=(rows_of(w, at), rows_of(1, at), whole(8, w), whole(XW, w)),
        out_shape=(shaped(SEQ, w, dtype=bf16), shaped(SEQ, 1), shaped(8, w), shaped(XW, w)),
        scratch_shapes=[
            rows,
            rows,
            rows,
            pltpu.VMEM((CH + 8, w), f32),
            pltpu.VMEM((CH + 8, w), f32),
            pltpu.SemaphoreType.DMA((1,)),
            pltpu.SemaphoreType.DMA((1,)),
        ],
        compiler_params=pltpu.CompilerParams(
            dimension_semantics=("arbitrary",), collective_id=4, has_side_effects=True, vmem_limit_bytes=VMEM_LIMIT
        ),
        cost_estimate=pl.CostEstimate(flops=20 * 1000000000, bytes_accessed=1000000, transcendentals=0),
    )(inner, inner, inv, inv, tail, conv, xproj, dxc, dxdbl, mix, into)


def per_device(
    tokens,
    gain,
    in_proj,
    conv_weight,
    conv_bias,
    x_proj,
    dt_proj,
    dt_bias,
    a_log,
    d_skip,
    out_proj,
    table,
    cotangent,
):
    row = lax.axis_index("row")
    col = lax.axis_index("col")
    grp = lax.axis_index("grp")
    low_row = row == 0
    low_pair = col % 2 == 0
    half = col // 2
    places = [(r, c) for r in range(2) for c in range(4)]
    quick = lax.axis_size("grp") == 4

    def spot(r, c):
        return r * 4 + c

    def send(v, pairs):
        return lax.ppermute(v, ("row", "col"), [(spot(*a), spot(*b)) for a, b in pairs])

    def swap(v):
        return send(v, [((r, c), (1 - r, c)) for r, c in places])

    def pair(v):
        return send(v, [((r, c), (r, c ^ 1)) for r, c in places])

    def across(v):
        return send(v, [((r, c), (1 - r, c ^ 2)) for r, c in places])

    def quarter_spot(q, s):
        return ((q & 1) ^ s, 2 * s + (q >> 1))

    same = [((r, q), quarter_spot(q, r ^ (q & 1))) for r, q in places]
    other = [((r, q), quarter_spot(q, 1 ^ r ^ (q & 1))) for r, q in places]
    spread = [((r, q), quarter_spot(q, r)) for r, q in places]

    def back(pairs):
        return [(b, a) for a, b in pairs]

    def flip(v, bit):
        return lax.ppermute(v, "grp", [(g, g ^ bit) for g in range(4)])

    def scatter_grp(v, axis):
        return lax.psum_scatter(v, "grp", scatter_dimension=axis, tiled=True)

    def by_pair(own, paired):
        return jnp.where(low_pair, own, paired), jnp.where(low_pair, paired, own)

    local = tokens.shape[0]
    cut = local - LC
    tail_at = cut - LC

    def to_sequences(v):
        got = send(jnp.where(col == 3, v[tail_at:cut], v[cut:]), [((r, a), (r, b)) for r in range(2) for a, b in ((1, 2), (2, 3), (3, 1))])
        low = jnp.concatenate([v[:cut], jnp.where(col == 0, v[cut:], got)], axis=0)
        two = jnp.concatenate([got, v[:cut]], axis=0)
        three = jnp.concatenate([got, v[:tail_at], v[cut:]], axis=0)
        return jnp.where(col < 2, low, jnp.where(col == 2, two, three))

    def from_sequences(v):
        got = send(jnp.where(col == 1, v[cut:], v[:LC]), [((r, b), (r, a)) for r in range(2) for a, b in ((1, 2), (2, 3), (3, 1))])
        low = jnp.concatenate([v[:cut], jnp.where(col == 0, v[cut:], got)], axis=0)
        two = jnp.concatenate([v[LC:], got], axis=0)
        three = jnp.concatenate([v[LC:cut], got, v[cut:]], axis=0)
        return jnp.where(col < 2, low, jnp.where(col == 2, two, three))

    def gather_quad(v):
        swapped = swap(v)
        paired = pair(v)
        mid = v.shape[0] // 2
        diagonal = jnp.concatenate([pair(swapped[:mid]), swap(paired[mid:])], axis=0)
        first_own, second_own = by_pair(v, paired)
        first_oth, second_oth = by_pair(swapped, diagonal)
        return jnp.stack([jnp.concatenate([first_own, second_own], axis=0), jnp.concatenate([first_oth, second_oth], axis=0)])

    def scatter_quad(own, oth):
        v = own + swap(oth.astype(bf16)).astype(f32)
        first, second = v[:local], v[local:]
        kept, sent = jnp.where(low_pair, first, second), jnp.where(low_pair, second, first)
        return kept + pair(sent.astype(bf16)).astype(f32)

    own_table = jnp.where(half == 0, table[0], table[1])
    oth_table = jnp.where(half == 0, table[1], table[0])
    resumes_own = own_table == half
    resumed_by_other = oth_table == half

    small = jnp.concatenate([conv_weight, conv_bias[None], dt_bias[None], d_skip[None], a_log, dt_proj, x_proj.T], axis=0)
    lanes = small.shape[1]
    used = small.shape[0]
    gain_rows = gain.size // lanes
    width = tokens.shape[1]
    if quick:
        small = jnp.concatenate([small, gain.reshape(gain_rows, lanes)], axis=0)
        small = jnp.pad(small, ((0, -small.shape[0] % 16), (0, 0)))
        raw, wi, small = run_gather_start(tokens, in_proj[:, 0], small)
        gain_all = small[:, used : used + gain_rows].reshape(2, width).astype(f32)
        small = jnp.swapaxes(small, 0, 1).reshape(small.shape[1], 8 * lanes)
    else:
        raw = gather_quad(to_sequences(tokens))

        def weight(shard):
            v = lax.all_gather(jnp.stack([send(shard, same), send(shard, other)]), "grp", axis=2, tiled=True)
            v = v.reshape(2, v.shape[1], SLOTS, v.shape[2] // SLOTS)
            return jnp.transpose(v, (2, 0, 1, 3)).reshape(2 * SLOTS, v.shape[1], v.shape[3])

        wi = weight(in_proj[:, 0])
        small = send(lax.all_gather(small, ("row", "grp"), axis=1, tiled=True), spread)
        gain_all = lax.all_gather(gain, ("row", "grp"), axis=0, tiled=True).astype(f32).reshape(2, width)
    w = small.shape[1]
    zero_row = jnp.zeros((1, w), f32)
    conv = jnp.concatenate([small[0:5].astype(f32)] + [zero_row] * 3, axis=0)
    vec = jnp.concatenate([small[5:7].astype(f32)] + [zero_row] * 6, axis=0)
    rate = -jnp.exp(small[7 : 7 + NSTATE].astype(f32))
    dtp = small[7 + NSTATE : 7 + NSTATE + RANK]
    xproj = small[7 + NSTATE + RANK : 7 + NSTATE + RANK + XW]
    gain_own = jnp.where(low_row, gain_all[0], gain_all[1])
    gain_two = jnp.stack([gain_own, jnp.where(low_row, gain_all[1], gain_all[0])])

    zero_state = jnp.zeros((NSTATE, w), f32)
    if quick:
        mix = jnp.broadcast_to(resumes_own.astype(f32), (8, w))
        normed, inv, inner, xconv, yfull, starts, xdbl, tail, wg, wo, cot = run_forward(raw, gain_two, wi, mix, conv, xproj, dtp, vec, rate, in_proj[:, 1], out_proj, cotangent)
    else:
        normed, inv, inner = run_project_first(raw, gain_two, wi)
        tail_own = (inv * inner)[LP - 8 : LP]
        tail = jnp.where(resumes_own, tail_own, across(tail_own))
        xconv, xdbl = run_conv_forward(inner, inv, tail, conv, xproj)
        for move in (swap, pair):
            xdbl = xdbl + move(xdbl)
        xdbl = jnp.swapaxes(xdbl.reshape(XW, NCH, CH), 0, 1)
        *kept, final = run_scan_forward(0, PC, xdbl, xconv, dtp, vec, rate, zero_state)
        resumed = jnp.where(resumes_own, final, across(final))
        yfull, starts, _ = run_scan_forward(PC, NCH - PC, xdbl, xconv, dtp, vec, rate, resumed, kept)
        wg, wo = weight(in_proj[:, 1]), weight(out_proj)
        cot = gather_quad(to_sequences(cotangent))
    gated, d_yfull, d_gate_proj, gate_scale, branch_own, branch_oth = run_gate_backward(normed, wg, cot, wo, yfull, inv)

    def collect(v):
        return send(v[0].astype(bf16), back(same)).astype(f32) + send(v[1].astype(bf16), back(other)).astype(f32)

    def rows_product(a, b, out_dtype):
        return lax.dot_general(a, b, (((1,), (0,)), ((), ())), preferred_element_type=f32).astype(out_dtype)

    zero_head = jnp.zeros((8, w), f32)
    conv_back = functools.partial(run_conv_backward, inner=inner, inv=inv, tail=tail, conv=conv, xproj=xproj)
    if quick:
        x, core = grp // 2, grp % 2
        order = jnp.stack([2 * (1 - x) + 1 - core, 2 * x + 1 - core, 2 * (1 - x) + core, 2 * x + core]).astype(jnp.int32)
        gate_sent, out_sent, gate_kept, out_kept = run_late_parts(order, normed, d_gate_proj, gated, cot)
        sent, kept = (gate_sent, out_sent), (gate_kept, out_kept)
        into = jnp.broadcast_to(resumed_by_other.astype(f32), (8, w))
        dxdbl, dxc, alog_grad, scan_sums, dtp_grad, late_grads, branch = run_backward(
            xdbl, xconv, d_yfull, dtp, vec, rate, starts, mix, into, sent, kept, branch_own, branch_oth
        )
        gate_grad, out_grad = late_grads[0], late_grads[1]
    else:
        branch = from_sequences(scatter_quad(branch_own, branch_oth).astype(bf16))
        out_grad = collect([scatter_grp(dot_tn(gated, cot[d]), 1) for d in range(2)])
        gate_grad = collect([scatter_grp(dot_tn(normed[d], d_gate_proj), 1) for d in range(2)])
        sums = (zero_state, jnp.zeros((8, w), f32), jnp.zeros((RANK, w), f32))
        scan = functools.partial(run_scan_backward, xdbl=xdbl, xconv=xconv, dy=d_yfull, dtp=dtp, vec=vec, rate=rate, starts=starts)
        dx_c, dxc, *sums, g_first = scan(PC, NCH - PC, carry=zero_state, sums=sums)
        g_into = jnp.where(resumes_own, g_first, 0.0) + jnp.where(resumed_by_other, across(g_first), 0.0)
        dx_p, dxc, *sums, _ = scan(0, PC, carry=g_into, sums=sums, kept=(dxc,))
        alog_grad, scan_sums, dtp_grad = sums
        dxdbl = jnp.concatenate([dx_p, dx_c], axis=1)
        for move in (swap, pair):
            dxdbl = dxdbl + move(dxdbl)
        dxdbl = jnp.swapaxes(dxdbl.reshape(XW, NCH, CH), 0, 1)

    output = (tokens.astype(f32) + branch.astype(f32)).astype(bf16)
    if quick:
        d_inner_proj, inner_scale, conv_sums, xproj_grad = run_conv_backward_far(inner, inv, tail, conv, xproj, dxc, dxdbl, mix, into)
    else:
        sums = (jnp.zeros((8, w), f32), jnp.zeros((XW, w), f32))
        dp, ds, *sums, head = conv_back(PC, NCH - PC, dxc=dxc, dxdbl=dxdbl, follow=zero_head, sums=sums)
        follow = jnp.where(resumes_own, head, 0.0) + jnp.where(resumed_by_other, across(head), 0.0)
        d_inner_proj, inner_scale, conv_sums, xproj_grad, _ = conv_back(0, PC, dxc=dxc, dxdbl=dxdbl, follow=follow, sums=sums, kept=(dp, ds))

    scale = gate_scale + inner_scale

    def own_rows(v):
        return jnp.where(low_pair, v[:local], v[local:])

    def pair_rows(v):
        return jnp.where(low_pair, v[local:], v[:local])

    diagonal = send(pair_rows(scale), [((r, c), (1 - r, c ^ 1)) for r, c in places])
    scale = own_rows(scale) + swap(own_rows(scale)) + pair(pair_rows(scale)) + diagonal
    inv_own = own_rows(inv)
    pull = scale * inv_own * inv_own * inv_own / D
    small_parts = (conv_sums, scan_sums, alog_grad * rate, dtp_grad, xproj_grad)
    if quick:
        pulled, inner_grad, gain_sum, *small_grads = run_finish(
            d_inner_proj, d_gate_proj, normed, raw, wi, wg, jnp.broadcast_to(gain_own[None], (8, width)), pull, small_parts
        )
        gain_grad = jnp.sum(gain_sum, axis=0)
    else:
        inner_grad = collect([scatter_grp(dot_tn(normed[d], d_inner_proj), 1) for d in range(2)])
        d_normed = scatter_quad(*run_normed_backward(d_inner_proj, d_gate_proj, wi, wg))
        fixed = own_rows(raw[0]).astype(f32)
        gain_grad = jnp.sum(d_normed * fixed, axis=0)
        gain_grad = lax.psum_scatter(lax.psum(gain_grad, "col"), "grp", scatter_dimension=0, tiled=True)
        pulled = from_sequences((d_normed * gain_own - pull * fixed).astype(bf16))
        small_grad = send(jnp.concatenate(small_parts, axis=0), back(spread))
        small_grad = lax.psum_scatter(small_grad, ("row", "grp"), scatter_dimension=1, tiled=True)
        small_grads = jnp.split(small_grad, [sum(SMALL_ROWS[: k + 1]) for k in range(len(SMALL_ROWS) - 1)], axis=0)
    input_grad = (cotangent.astype(f32) + pulled.astype(f32)).astype(bf16)
    in_grads = jnp.stack([inner_grad, gate_grad], axis=1)
    return (
        output,
        input_grad,
        gain_grad,
        in_grads,
        small_grads[0],
        small_grads[1][0],
        small_grads[8].T,
        small_grads[7],
        small_grads[3][0],
        small_grads[6],
        small_grads[4][0],
        out_grad,
    )


def solution(mesh):
    placed = (
        P(("grp", "col"), "row"),
        P(("row", "grp")),
        P("row", None, ("col", "grp")),
        P(None, ("col", "row", "grp")),
        P(("col", "row", "grp")),
        P(("col", "row", "grp"), None),
        P(None, ("col", "row", "grp")),
        P(("col", "row", "grp")),
        P(None, ("col", "row", "grp")),
        P(("col", "row", "grp")),
        P("col", ("row", "grp")),
        P("grp"),
        P(("grp", "col"), "row"),
    )
    return jax.shard_map(
        per_device,
        mesh=mesh,
        in_specs=placed,
        out_specs=(
            P(("grp", "col"), "row"),
            P(("grp", "col"), "row"),
            P(("row", "grp")),
            P("row", None, ("col", "grp")),
            P(None, ("col", "row", "grp")),
            P(("col", "row", "grp")),
            P(("col", "row", "grp"), None),
            P(None, ("col", "row", "grp")),
            P(("col", "row", "grp")),
            P(None, ("col", "row", "grp")),
            P(("col", "row", "grp")),
            P("col", ("row", "grp")),
        ),
        check_vma=False,
    )
```

```python
import functools

import jax
import jax.numpy as jnp
from jax import lax
from jax.experimental import pallas as pl
from jax.experimental.pallas import tpu as pltpu
from jax.sharding import PartitionSpec as P

D = 2048
NSTATE = 16
KCONV = 4
RANK = 128
NPROMPT = 2
LP = 1024
LC = 128
NCONT = 2

eps = 1e-05
CH = 128
SUB = 16
PC = LP // CH
SEQ = LP + LC
NCH = SEQ // CH
XW = RANK + 2 * NSTATE
SPAN = SUB * NSTATE
LOG2E = 1.4426950408889634
VMEM_LIMIT = 58 * 1024 * 1024

f32 = jnp.float32
bf16 = jnp.bfloat16


def dot_nn(a, b):
    return lax.dot_general(a, b, (((1,), (0,)), ((), ())), preferred_element_type=f32)


def dot_nt(a, b):
    return lax.dot_general(a, b, (((1,), (1,)), ((), ())), preferred_element_type=f32)


def dot_tn(a, b):
    return lax.dot_general(a, b, (((0,), (0,)), ((), ())), preferred_element_type=f32)


def expand_tile():
    lane = lax.broadcasted_iota(jnp.int32, (NSTATE, SPAN), 1)
    row = lax.broadcasted_iota(jnp.int32, (NSTATE, SPAN), 0)
    return jnp.where(lane % NSTATE == row, 1.0, 0.0)


def own_token(rows):
    lane = lax.broadcasted_iota(jnp.int32, (rows, SPAN), 1)
    row = lax.broadcasted_iota(jnp.int32, (rows, SPAN), 0)
    return lane // NSTATE == row % SUB


def conv_forward(inner_ref, inv_ref, tail_ref, conv_ref, xproj_ref, xconv_ref, xdbl_ref, buf):
    i = pl.program_id(0)

    @pl.when(i == 0)
    def _():
        buf[0:8] = jnp.zeros_like(buf[0:8])

    @pl.when(i == PC)
    def _():
        buf[0:8] = tail_ref[...]

    @pl.when((i > 0) & (i < PC))
    def _():
        buf[0:8] = buf[CH : CH + 8]

    buf[8 : CH + 8] = inv_ref[...] * inner_ref[...]
    out = conv_ref[4:5]
    for k in range(KCONV):
        out = out + conv_ref[k : k + 1] * buf[5 + k : 5 + k + CH]
    xconv = (out * jax.nn.sigmoid(out)).astype(bf16)
    xconv_ref[...] = xconv
    xdbl_ref[...] = dot_nt(xproj_ref[...], xconv)


def softplus(v):
    return jnp.maximum(v, 0.0) + jnp.log1p(jnp.exp(-jnp.abs(v)))


def by_sub(v):
    return v.reshape(CH // SUB, SUB, v.shape[-1])


def scan_chunk(xdbl_ref, xconv, dtp_ref, vec_ref, rate_ref, state, dt_s, u_s, cb_s, h_s, y_s):
    step = softplus(dot_tn(xdbl_ref[:RANK].astype(bf16), dtp_ref[...]) + vec_ref[0:1])
    dt_s[...] = by_sub(step)
    u_s[...] = by_sub(step * xconv)
    reads = dot_tn(xdbl_ref[RANK + NSTATE :].astype(bf16), expand_tile().astype(bf16))
    cb_s[...] = jnp.where(own_token(CH), reads, 0.0).astype(bf16)
    rate = rate_ref[...] * LOG2E

    def block(j, carried):
        h, maps = carried
        for t in range(SUB):
            a = jnp.exp2(dt_s[j, t : t + 1, :] * rate)
            h = a * h + u_s[j, t : t + 1, :] * maps[:, t : t + 1]
            h_s[t * NSTATE : (t + 1) * NSTATE, :] = h.astype(bf16)
        rows = pl.ds(pl.multiple_of(j * SUB, SUB), SUB)
        y_s[rows, :] = dot_nn(cb_s[rows, :], h_s[...])
        return (h, pltpu.roll(maps, CH - SUB, 1))

    h, _ = lax.fori_loop(0, CH // SUB, block, (state, xdbl_ref[RANK : RANK + NSTATE]))
    return h, y_s[...] + vec_ref[1:2] * xconv


def scan_scratch(w):
    return [
        pltpu.VMEM((CH // SUB, SUB, w), f32),
        pltpu.VMEM((CH // SUB, SUB, w), f32),
        pltpu.VMEM((CH, SPAN), bf16),
        pltpu.VMEM((SPAN, w), bf16),
        pltpu.VMEM((CH, w), f32),
    ]


def scan_forward(kept, xdbl_ref, xconv_ref, dtp_ref, vec_ref, rate_ref, start_ref, *refs):
    yfull_ref, starts_ref, final_ref, *scratch = refs[kept:]

    @pl.when(pl.program_id(0) == 0)
    def _():
        final_ref[...] = start_ref[...]

    starts_ref[0] = final_ref[...]
    h, yfull = scan_chunk(xdbl_ref, xconv_ref[...].astype(f32), dtp_ref, vec_ref, rate_ref, final_ref[...], *scratch)
    final_ref[...] = h
    yfull_ref[...] = yfull.astype(bf16)


def chunk_backward(xdbl_ref, xconv_ref, dy_ref, dtp_ref, vec_ref, rate_ref, starts_ref, dxdbl_ref, dxc_ref, alog_ref, sums_ref, dtpg_ref, first_ref,
                   dt_s, u_s, x_s, dy_s, a_s, h_s, g_s, w_s, b_s, m1_s, m2_s, ds_s, dx_s, sig_s):
    low = xdbl_ref[:RANK].astype(bf16)
    step_inner = dot_tn(low, dtp_ref[...]) + vec_ref[0:1]
    step = softplus(step_inner)
    sig_s[...] = jax.nn.sigmoid(step_inner)
    xconv = xconv_ref[...].astype(f32)
    dy = dy_ref[...]
    dt_s[...] = by_sub(step)
    u_s[...] = by_sub(step * xconv)
    x_s[...] = by_sub(xconv)
    dy_s[...] = by_sub(dy)
    tile = expand_tile().astype(bf16)
    b_s[...] = jnp.where(own_token(CH), dot_tn(xdbl_ref[RANK : RANK + NSTATE].astype(bf16), tile), 0.0).astype(bf16)
    rate = rate_ref[...]
    rate2 = rate * LOG2E
    h_s[0:NSTATE] = starts_ref[0]

    def ahead(j, carried):
        h, maps = carried
        for t in range(SUB):
            a = jnp.exp2(dt_s[j, t : t + 1, :] * rate2)
            h = a * h + u_s[j, t : t + 1, :] * maps[:, t : t + 1]
            a_s[j, t * NSTATE : (t + 1) * NSTATE, :] = a
            at = pl.multiple_of(j * SPAN + (t + 1) * NSTATE, NSTATE)
            h_s[pl.ds(at, NSTATE), :] = h
        return (h, pltpu.roll(maps, CH - SUB, 1))

    lax.fori_loop(0, CH // SUB, ahead, (starts_ref[0], xdbl_ref[RANK : RANK + NSTATE]))
    ones = jnp.where(own_token(SUB), 1.0, 0.0).astype(bf16)
    mine_sub = own_token(SUB)

    def back(jj, carried):
        g, alog, maps = carried
        j = CH // SUB - 1 - jj
        maps = pltpu.roll(maps, SUB, 1)
        for t in reversed(range(SUB)):
            dt = dt_s[j, t : t + 1, :]
            gs = maps[:, t : t + 1] * dy_s[j, t : t + 1, :] + g
            g = a_s[j, t * NSTATE : (t + 1) * NSTATE, :] * gs
            prior = h_s[pl.ds(pl.multiple_of(j * SPAN + t * NSTATE, NSTATE), NSTATE), :]
            w = g * prior
            alog = alog + w * dt
            g_s[t * NSTATE : (t + 1) * NSTATE, :] = gs.astype(bf16)
            w_s[t * NSTATE : (t + 1) * NSTATE, :] = (w * rate).astype(bf16)
        rows = pl.ds(pl.multiple_of(j * SUB, SUB), SUB)
        gs_all = g_s[...]
        through = dot_nn(b_s[rows, :], gs_all)
        ds_s[rows, :] = dot_nn(ones, w_s[...]) + x_s[j] * through
        dx_s[rows, :] = dt_s[j] * through + vec_ref[1:2] * dy_s[j]
        hs = h_s[pl.ds(pl.multiple_of(j * SPAN + NSTATE, NSTATE), SPAN), :].astype(bf16)
        m1_s[rows, :] = jnp.where(mine_sub, dot_nt(u_s[j].astype(bf16), gs_all), 0.0).astype(bf16)
        m2_s[rows, :] = jnp.where(mine_sub, dot_nt(dy_s[j].astype(bf16), hs), 0.0).astype(bf16)
        return (g, alog, maps)

    g, alog, _ = lax.fori_loop(0, CH // SUB, back, (first_ref[...], alog_ref[...], xdbl_ref[RANK + NSTATE :]))
    first_ref[...] = g
    alog_ref[...] = alog
    d_inner = ds_s[...] * sig_s[...]
    d_low = d_inner.astype(bf16)
    sums_ref[0:1] = sums_ref[0:1] + jnp.sum(d_inner, axis=0, keepdims=True)
    sums_ref[1:2] = sums_ref[1:2] + jnp.sum(dy * xconv, axis=0, keepdims=True)
    dtpg_ref[...] = dtpg_ref[...] + dot_nn(low, d_low)
    dxdbl_ref[:RANK] = dot_nt(dtp_ref[...], d_low)
    dxdbl_ref[RANK : RANK + NSTATE] = dot_nt(tile, m1_s[...])
    dxdbl_ref[RANK + NSTATE :] = dot_nt(tile, m2_s[...])
    dxc_ref[...] = dx_s[...]


def scan_backward(kept, *refs):
    given, sums0, out = refs[:7], refs[7:11], refs[11 + kept :]
    dxdbl_ref, dxc_ref, alog_ref, sums_ref, dtpg_ref, first_ref = out[:6]

    @pl.when(pl.program_id(0) == 0)
    def _():
        first_ref[...] = sums0[0][...]
        alog_ref[...] = sums0[1][...]
        sums_ref[...] = sums0[2][...]
        dtpg_ref[...] = sums0[3][...]

    chunk_backward(*given, dxdbl_ref, dxc_ref, alog_ref, sums_ref, dtpg_ref, first_ref, *out[6:])


def backward_scratch(w):
    sub = pltpu.VMEM((CH // SUB, SUB, w), f32)
    return [
        sub,
        sub,
        sub,
        sub,
        pltpu.VMEM((CH // SUB, SPAN, w), f32),
        pltpu.VMEM(((CH + 1) * NSTATE, w), f32),
        pltpu.VMEM((SPAN, w), bf16),
        pltpu.VMEM((SPAN, w), bf16),
        pltpu.VMEM((CH, SPAN), bf16),
        pltpu.VMEM((CH, SPAN), bf16),
        pltpu.VMEM((CH, SPAN), bf16),
        pltpu.VMEM((CH, w), f32),
        pltpu.VMEM((CH, w), f32),
        pltpu.VMEM((CH, w), f32),
    ]


def conv_chunk(chunk, inner_ref, halo_ref, inv_ref, halo_inv_ref, tail_ref, conv_ref, xproj_ref, dxc_ref, dxdbl_ref, dproj_ref, dscale_ref, sums_ref, xprojg_ref, head_ref, buf, dbuf):
    projected = inner_ref[...]
    inv = inv_ref[...]
    before = halo_inv_ref[...] * halo_ref[...]
    before = jnp.where(chunk == 0, 0.0, jnp.where(chunk == PC, tail_ref[...], before))
    buf[0:8] = before
    buf[8 : CH + 8] = inv * projected
    out = conv_ref[4:5]
    for k in range(KCONV):
        out = out + conv_ref[k : k + 1] * buf[5 + k : 5 + k + CH]
    sig = jax.nn.sigmoid(out)
    xconv = (out * sig).astype(bf16)
    dxdbl = dxdbl_ref[...].astype(bf16)
    xprojg_ref[...] = xprojg_ref[...] + dot_nn(dxdbl, xconv)
    d_x = dxc_ref[...] + dot_tn(dxdbl, xproj_ref[...])
    d_conv = d_x * (sig * (1.0 + out * (1.0 - sig)))
    dbuf[CH : CH + 8] = head_ref[...]
    dbuf[0:CH] = d_conv
    d_inner = conv_ref[3:4] * d_conv
    for k in range(KCONV - 1):
        d_inner = d_inner + conv_ref[k : k + 1] * dbuf[3 - k : 3 - k + CH]
    for k in range(KCONV):
        sums_ref[k : k + 1] = sums_ref[k : k + 1] + jnp.sum(buf[5 + k : 5 + k + CH] * d_conv, axis=0, keepdims=True)
    sums_ref[4:5] = sums_ref[4:5] + jnp.sum(d_conv, axis=0, keepdims=True)
    dproj_ref[...] = (inv * d_inner).astype(bf16)
    dscale_ref[...] = jnp.sum(d_inner * projected, axis=1, keepdims=True)
    head_ref[...] = d_conv[0:8]


def conv_backward(kept, chunks, first, *refs):
    given, init, out = refs[:9], refs[9:12], refs[12 + kept :]
    dproj_ref, dscale_ref, sums_ref, xprojg_ref, head_ref, buf, dbuf = out
    i = pl.program_id(0)

    @pl.when(i == 0)
    def _():
        head_ref[...] = init[0][...]
        sums_ref[...] = init[1][...]
        xprojg_ref[...] = init[2][...]

    conv_chunk(first + chunks - 1 - i, *given, *out)


def call(body, chunks, args, in_specs, outs, out_specs, scratch, micros, aliases=None):
    return pl.pallas_call(
        body,
        grid=(chunks,),
        in_specs=in_specs,
        out_specs=out_specs,
        scratch_shapes=scratch,
        out_shape=outs,
        input_output_aliases=aliases or {},
        compiler_params=pltpu.CompilerParams(dimension_semantics=("arbitrary",), vmem_limit_bytes=VMEM_LIMIT),
        cost_estimate=pl.CostEstimate(flops=micros * 1000000000, bytes_accessed=1000000, transcendentals=0),
    )(*args)


def shaped(*shape, dtype=f32):
    return jax.ShapeDtypeStruct(shape, dtype)


def rows_of(width, place, tall=CH):
    return pl.BlockSpec((tall, width), lambda i: (place(i), 0))


def lanes_of(height, place):
    return pl.BlockSpec((height, CH), lambda i: (0, place(i)))


def whole(*shape):
    return pl.BlockSpec(shape, lambda i: (0,) * len(shape))


ANY = pl.BlockSpec(memory_space=pl.ANY)


def run_conv_forward(inner, inv, tail, conv, xproj):
    w = inner.shape[1]
    at = lambda i: i
    return call(
        conv_forward,
        NCH,
        (inner, inv, tail, conv, xproj),
        [rows_of(w, at), rows_of(1, at), whole(8, w), whole(8, w), whole(XW, w)],
        (shaped(SEQ, w, dtype=bf16), shaped(XW, SEQ)),
        (rows_of(w, at), lanes_of(XW, at)),
        [pltpu.VMEM((CH + 8, w), f32)],
        12,
    )


def chunk_of(height, place):
    return pl.BlockSpec((None, height, CH), lambda i: (place(i), 0, 0))


def run_scan_forward(first, chunks, xdbl, xconv, dtp, vec, rate, start, kept=()):
    w = xconv.shape[1]
    at = lambda i: first + i
    return call(
        functools.partial(scan_forward, len(kept)),
        chunks,
        (xdbl, xconv, dtp, vec, rate, start, *kept),
        [chunk_of(XW, at), rows_of(w, at), whole(RANK, w), whole(8, w), whole(NSTATE, w), whole(NSTATE, w)] + [ANY] * len(kept),
        (shaped(SEQ, w, dtype=bf16), shaped(NCH, NSTATE, w), shaped(NSTATE, w)),
        (rows_of(w, at), pl.BlockSpec((1, NSTATE, w), lambda i: (first + i, 0, 0)), whole(NSTATE, w)),
        scan_scratch(w),
        5 * chunks,
        {6 + k: k for k in range(len(kept))},
    )


def run_scan_backward(first, chunks, xdbl, xconv, dy, dtp, vec, rate, starts, carry, sums, kept=()):
    w = xconv.shape[1]
    at = lambda i: first + chunks - 1 - i
    local = lambda i: chunks - 1 - i
    return call(
        functools.partial(scan_backward, len(kept)),
        chunks,
        (xdbl, xconv, dy, dtp, vec, rate, starts, carry, *sums, *kept),
        [
            chunk_of(XW, at),
            rows_of(w, at),
            rows_of(w, at),
            whole(RANK, w),
            whole(8, w),
            whole(NSTATE, w),
            pl.BlockSpec((1, NSTATE, w), lambda i: (at(i), 0, 0)),
            whole(NSTATE, w),
            whole(NSTATE, w),
            whole(8, w),
            whole(RANK, w),
        ]
        + [ANY] * len(kept),
        (shaped(XW, chunks * CH), shaped(SEQ, w), shaped(NSTATE, w), shaped(8, w), shaped(RANK, w), shaped(NSTATE, w)),
        (lanes_of(XW, local), rows_of(w, at), whole(NSTATE, w), whole(8, w), whole(RANK, w), whole(NSTATE, w)),
        backward_scratch(w),
        11 * chunks,
        {11 + k: 1 + k for k in range(len(kept))},
    )


def run_conv_backward(first, chunks, inner, inv, tail, conv, xproj, dxc, dxdbl, follow, sums, kept=()):
    w = inner.shape[1]
    at = lambda i: first + chunks - 1 - i
    before = lambda i: (jnp.maximum(at(i) * (CH // 8) - 1, 0), 0)
    return call(
        functools.partial(conv_backward, len(kept), chunks, first),
        chunks,
        (inner, inner, inv, inv, tail, conv, xproj, dxc, dxdbl, follow, *sums, *kept),
        [
            rows_of(w, at),
            pl.BlockSpec((8, w), before),
            rows_of(1, at),
            pl.BlockSpec((8, 1), before),
            whole(8, w),
            whole(8, w),
            whole(XW, w),
            rows_of(w, at),
            chunk_of(XW, at),
            whole(8, w),
            whole(8, w),
            whole(XW, w),
        ]
        + [ANY] * len(kept),
        (shaped(SEQ, w, dtype=bf16), shaped(SEQ, 1), shaped(8, w), shaped(XW, w), shaped(8, w)),
        (rows_of(w, at), rows_of(1, at), whole(8, w), whole(XW, w), whole(8, w)),
        [pltpu.VMEM((CH + 8, w), f32), pltpu.VMEM((CH + 8, w), f32)],
        2 * chunks,
        {12 + k: k for k in range(len(kept))},
    )


MESH = pl.DeviceIdType.MESH
BIG = 384
BIG_STEPS = SEQ // BIG
SLOTS = 4


def remote(src, dst, send, recv, device):
    return pltpu.make_async_remote_copy(src_ref=src, dst_ref=dst, send_sem=send, recv_sem=recv, device_id=device, device_id_type=MESH)


def xor_bit(a, b):
    return a + b - 2 * a * b


def token_pieces(c, local):
    cut = local - LC
    low = cut - LC
    if c == 0:
        return [(0, local, 0, 0)]
    if c == 1:
        return [(0, cut, 0, local), (cut, local, 1, 0)]
    if c == 2:
        return [(0, local, 1, LC)]
    return [(0, low, 1, LC + local), (low, cut, 0, LP), (cut, local, 1, LP)]


class Gather:
    def __init__(self, weights, tokens, raw, w_send, w_recv, t_send, t_recv, here):
        g, r, c = lax.axis_index("grp"), lax.axis_index("row"), lax.axis_index("col")
        x, core = g // 2, g % 2
        self.g, self.r, self.c = g, r, c
        half = xor_bit(r, c % 2)
        self.firsts = ((g, r, 2 * half + c // 2), (g, 1 - r, 2 * (1 - half) + c // 2))
        self.alone = 2 * half + c // 2 == c
        self.ranks = (g, (1 - x) * 2 + core, x * 2 + 1 - core)
        self.x_dev, self.core_dev = (self.ranks[1], r, c), (self.ranks[2], r, c)
        self.y_dev, self.z_dev = (g, 1 - r, c), (g, r, c + 1 - 2 * (c % 2))
        self.weights, self.tokens, self.raw = weights, tokens, raw
        self.w_send, self.w_recv, self.t_send, self.t_recv, self.here = w_send, w_recv, t_send, t_recv, here

    def greet(self):
        barrier = pltpu.get_barrier_semaphore()
        for dr in range(2):
            for dc in range(4):
                if dr or dc:
                    device = (self.g, (self.r + dr) % 2, (self.c + dc) % 4)
                    pl.semaphore_signal(barrier, inc=1, device_id=device, device_id_type=MESH)
        for device in (self.x_dev, self.core_dev):
            pl.semaphore_signal(barrier, inc=1, device_id=device, device_id_type=MESH)
        pl.semaphore_wait(barrier, 9)

    def slot(self, n, k, d):
        if self.weights[n][2]:
            return (self.r if d == 0 else 1 - self.r) * 4 + self.ranks[k]
        return 2 * self.ranks[k] + d

    def first_hop(self, n, d):
        src, dst, by_row = self.weights[n]
        at = self.slot(n, 0, 0) if by_row else self.slot(n, 0, d)
        return remote(src, dst.at[at], self.w_send.at[n, d], self.w_recv.at[n, d], self.firsts[d])

    def at_home(self, n):
        src, dst, _ = self.weights[n]
        return pltpu.make_async_copy(src, dst.at[self.slot(n, 0, 0)], self.here.at[n])

    def hop(self, n, d, k, came):
        dst = self.weights[n][1]
        at = self.slot(n, k, d)
        i = (0, 2, 4, 6)[came] + d
        device = self.x_dev if came == 1 else self.core_dev
        return remote(dst.at[at], dst.at[at], self.w_send.at[n, i], self.w_recv.at[n, i], device)

    def begin(self, n):
        @pl.when(self.alone)
        def _():
            self.at_home(n).start()

        @pl.when(jnp.logical_not(self.alone))
        def _():
            self.first_hop(n, 0).start()

        self.first_hop(n, 1).start()

    def forward(self, n):
        for d in range(2):
            if d == 0:

                @pl.when(self.alone)
                def _():
                    self.at_home(n).wait()

                @pl.when(jnp.logical_not(self.alone))
                def _():
                    self.first_hop(n, 0).wait_recv()
            else:
                self.first_hop(n, 1).wait_recv()
            self.hop(n, d, 0, 1).start()
            self.hop(n, d, 0, 2).start()

    def forward_again(self, n):
        for d in range(2):
            self.hop(n, d, 0, 1).wait_recv()
            self.hop(n, d, 1, 3).start()

    def end(self, n):
        for d in range(2):
            self.hop(n, d, 0, 2).wait_recv()
            self.hop(n, d, 1, 3).wait_recv()
            self.hop(n, d, 0, 1).wait_send()
            self.hop(n, d, 0, 2).wait_send()
            self.hop(n, d, 1, 3).wait_send()

        @pl.when(jnp.logical_not(self.alone))
        def _():
            self.first_hop(n, 0).wait_send()

        self.first_hop(n, 1).wait_send()

    def ranges(self, k):
        local = self.tokens.shape[0]
        held = {0: (0, local), 1: (local, LP), 2: (LC, LC + local), 3: (LC + local, SEQ)}
        return held[k], held[k ^ 1], (LP, SEQ) if k < 2 else (0, LC)

    def part(self, d, rows):
        return self.raw.at[d, pl.ds(rows[0], rows[1] - rows[0])]

    def on_col(self, act):
        for k in range(4):

            @pl.when(self.c == k)
            def _(k=k):
                act(k)

    def sources(self, k, lo, hi):
        for a, b, s, at in token_pieces(k, self.tokens.shape[0]):
            first, end = max(lo, at), min(hi, at + b - a)
            if s == k // 2 and first < end:
                yield a + first - at, first, end

    def begin_half(self, h):
        def act(k):
            lo, hi = split(self.ranges(k)[0])[h]
            for src, first, end in self.sources(k, lo, hi):
                rows = self.tokens.at[pl.ds(src, end - first)]
                pltpu.make_async_copy(rows, self.part(0, (first, end)), self.here.at[2 + h]).start()
                remote(rows, self.part(1, (first, end)), self.t_send.at[h], self.t_recv.at[h], self.y_dev).start()
                remote(rows, self.part(0, (first, end)), self.t_send.at[2 + h], self.t_recv.at[2 + h], self.z_dev).start()

        self.on_col(act)

    def foreign_copies(self, k):
        copies = []
        for a, b, s, at in token_pieces(k, self.tokens.shape[0]):
            if s != k // 2:
                for dr in range(2):
                    for dc in range(2):
                        device = (self.g, self.r if dr == 0 else 1 - self.r, 2 * s + dc)
                        sems = self.t_send.at[6 + 2 * dr + dc], self.t_recv.at[6 + dr]
                        copies.append(remote(self.tokens.at[pl.ds(a, b - a)], self.part(dr, (at, at + b - a)), *sems, device))
        return copies

    def begin_foreign(self):
        def act(k):
            for copy in self.foreign_copies(k):
                copy.start()

        self.on_col(act)

    def relays(self, k):
        own, paired, _ = self.ranges(k)
        early, late = split(paired)[0], split(own)[1]
        return (
            remote(self.part(0, early), self.part(1, early), self.t_send.at[4], self.t_recv.at[4], self.y_dev),
            remote(self.part(1, late), self.part(1, late), self.t_send.at[5], self.t_recv.at[5], self.z_dev),
        )

    def settle(self, d, rows, sem):
        pltpu.make_async_copy(self.part(d, rows), self.part(d, rows), sem).wait()

    def relay(self):
        def act(k):
            own, paired, _ = self.ranges(k)
            by_y, by_z = self.relays(k)
            self.settle(0, split(paired)[0], self.t_recv.at[2])
            by_y.start()
            self.settle(1, split(own)[1], self.t_recv.at[1])
            by_z.start()

        self.on_col(act)

    def end_tokens(self):
        def act(k):
            own, paired, foreign = self.ranges(k)
            own, paired = split(own), split(paired)
            by_y, by_z = self.relays(k)
            self.settle(1, own[0], self.t_recv.at[0])
            self.settle(0, paired[1], self.t_recv.at[3])
            self.settle(1, paired[0], self.t_recv.at[4])
            self.settle(1, paired[1], self.t_recv.at[5])
            self.settle(0, foreign, self.t_recv.at[6])
            self.settle(1, foreign, self.t_recv.at[7])
            for h in range(2):
                self.settle(0, own[h], self.here.at[2 + h])
                self.settle(0, own[h], self.t_send.at[h])
                self.settle(0, own[h], self.t_send.at[2 + h])
            by_y.wait_send()
            by_z.wait_send()
            for copy in self.foreign_copies(k):
                copy.wait_send()

        self.on_col(act)


def split(rows):
    lo, hi = rows
    mid = lo + (hi - lo) // 2
    return (lo, mid), (mid, hi)


def gather_semaphores():
    return [pltpu.SemaphoreType.DMA(shape) for shape in ((2, 8), (2, 8), (10,), (8,), (4,))]


def gather_start(tokens, in_i, small, raw, wi, small_all, *sems):
    gather = Gather([(small, small_all, True), (in_i, wi, False)], tokens, raw, *sems)
    gather.greet()
    gather.begin(0)
    gather.begin(1)
    gather.begin_half(0)
    gather.begin_half(1)
    gather.begin_foreign()
    for n in range(2):
        gather.forward(n)
    gather.relay()
    for n in range(2):
        gather.forward_again(n)
    gather.end_tokens()
    for n in range(2):
        gather.end(n)


def run_gather_start(tokens, in_i, small):
    width = tokens.shape[1]
    return pl.pallas_call(
        gather_start,
        in_specs=[ANY] * 3,
        out_specs=[ANY] * 3,
        out_shape=(
            shaped(2, SEQ, width, dtype=bf16),
            shaped(8, *in_i.shape, dtype=bf16),
            shaped(8, *small.shape, dtype=bf16),
        ),
        scratch_shapes=gather_semaphores(),
        compiler_params=pltpu.CompilerParams(collective_id=0, has_side_effects=True, vmem_limit_bytes=VMEM_LIMIT),
    )(tokens, in_i, small)


LAG = 4
FIRST = BIG_STEPS
SECOND = FIRST + NCH
LAST = SECOND + NCH - 1
BEGIN = (0, SECOND)
FORWARD = (FIRST + 8, SECOND + 5)
FORWARD_AGAIN = (SECOND + 3, LAST)
HALVES = (FIRST + 6, SECOND + 1)
FOREIGN = SECOND + 2
RELAY = SECOND + 6


def pack_sum(ref, k, v):
    high = v[RANK:].astype(bf16)
    ref[k, :RANK] = v[:RANK].astype(bf16)
    ref[k, RANK:XW] = high
    ref[k, XW:] = (v[RANK:] - high.astype(f32)).astype(bf16)


def unpack_sum(ref, k):
    return jnp.concatenate([ref[k, :RANK].astype(f32), ref[k, RANK:XW].astype(f32) + ref[k, XW:].astype(f32)], axis=0)


def forward(raw_ref, gain_ref, wi_ref, mix_ref, conv_ref, xproj_ref, dtp_ref, vec_ref, rate_ref, in_g, out_w, cot_in,
            normed_ref, inv_ref, inner_ref, xconv_ref, yfull_ref, starts_ref, xdbl_ref, joined_ref, wg, wo, cot,
            inner_s, inv_s, buf, xc_s, part, ys, yr, zs, zr, tail_s, tail_r, state, last, last_r,
            dt_s, u_s, cb_s, h_s, y_s, y_send, y_recv, z_send, z_recv, e_send, e_recv, *sems):
    i = pl.program_id(0)
    gather = Gather([(in_g, wg, False), (out_w, wo, False)], cot_in, cot, *sems)
    g, r, c = gather.g, gather.r, gather.c
    y_dev, z_dev = gather.y_dev, gather.z_dev
    far_dev = (g, 1 - r, (c + 2) % 4)
    to_tail = remote(tail_s, tail_r, e_send.at[0], e_recv.at[0], far_dev)
    to_last = remote(last, last_r, e_send.at[1], e_recv.at[1], far_dev)

    def to_y(k):
        return remote(ys.at[k], yr.at[k], y_send.at[k], y_recv.at[k], y_dev)

    def to_z(k):
        return remote(zs.at[k], zr.at[k], z_send.at[k], z_recv.at[k], z_dev)

    @pl.when(i == 0)
    def _():
        gather.greet()

    @pl.when(i < FIRST)
    def _():
        rows = pl.ds(pl.multiple_of(i * BIG, BIG), BIG)
        project_first(raw_ref, gain_ref, wi_ref, normed_ref, inv_ref, inner_ref)
        inner_s[rows, :] = inner_ref[...]
        inv_s[rows, :] = inv_ref[...]

    @pl.when(i == FIRST)
    def _():
        tail_s[...] = inv_s[LP - 8 : LP] * inner_s[LP - 8 : LP]
        to_tail.start()
        buf[0:8] = jnp.zeros_like(buf[0:8])
        state[...] = jnp.zeros_like(state)

    mix = mix_ref[...]

    @pl.when(i == FIRST + PC)
    def _():
        to_tail.wait()
        joined = mix * tail_s[...] + (1.0 - mix) * tail_r[...]
        buf[0:8] = joined
        joined_ref[...] = joined

    @pl.when((i > FIRST) & (i < FIRST + PC))
    def _():
        buf[0:8] = buf[CH : CH + 8]

    @pl.when((i >= FIRST) & (i < SECOND))
    def _():
        k = i - FIRST
        rows = pl.ds(pl.multiple_of(k * CH, CH), CH)
        buf[8 : CH + 8] = inv_s[rows, :] * inner_s[rows, :]
        out = conv_ref[4:5]
        for tap in range(KCONV):
            out = out + conv_ref[tap : tap + 1] * buf[5 + tap : 5 + tap + CH]
        xconv = (out * jax.nn.sigmoid(out)).astype(bf16)
        xconv_ref[...] = xconv
        xc_s[k] = xconv
        part[k] = dot_nt(xproj_ref[...], xconv)
        pack_sum(ys, k, part[k])
        to_y(k).start()

    @pl.when((i >= FIRST + LAG) & (i < SECOND + LAG))
    def _():
        k = i - FIRST - LAG
        to_y(k).wait_recv()
        part[k] = part[k] + unpack_sum(yr, k)
        pack_sum(zs, k, part[k])
        to_z(k).start()

    @pl.when((i >= FIRST + 2 * LAG) & (i < SECOND + 2 * LAG))
    def _():
        k = i - FIRST - 2 * LAG
        to_z(k).wait_recv()
        xdbl_ref[k] = part[k] + unpack_sum(zr, k)

    for n in range(2):

        @pl.when(i == BEGIN[n])
        def _(n=n):
            gather.begin(n)

        @pl.when(i == FORWARD[n])
        def _(n=n):
            gather.forward(n)

        @pl.when(i == FORWARD_AGAIN[n])
        def _(n=n):
            gather.forward_again(n)

    for h in range(2):

        @pl.when(i == HALVES[h])
        def _(h=h):
            gather.begin_half(h)

    @pl.when(i == FOREIGN)
    def _():
        gather.begin_foreign()

    @pl.when(i == RELAY)
    def _():
        gather.relay()

    @pl.when(i == LAST)
    def _():
        to_last.wait()
        state[...] = mix_ref[0:1] * last[...] + (1.0 - mix_ref[0:1]) * last_r[...]

    @pl.when(i >= SECOND)
    def _():
        k = i - SECOND
        starts_ref[0] = state[...]
        h, yfull = scan_chunk(xdbl_ref.at[k], xc_s[k].astype(f32), dtp_ref, vec_ref, rate_ref, state[...], dt_s, u_s, cb_s, h_s, y_s)
        state[...] = h
        yfull_ref[...] = yfull.astype(bf16)

    @pl.when(i == LAST - 1)
    def _():
        last[...] = state[...]
        to_last.start()

    @pl.when(i == LAST)
    def _():
        gather.end_tokens()
        gather.end(0)
        gather.end(1)

        def sent(k, _):
            to_y(k).wait_send()
            to_z(k).wait_send()
            return 0

        lax.fori_loop(0, NCH, sent, 0)


def run_forward(raw, gain, wi, mix, conv, xproj, dtp, vec, rate, in_g, out_w, cot):
    w = SLOTS * wi.shape[2]
    width = raw.shape[2]
    zero = lambda i: jnp.minimum(i, FIRST - 1)
    first = lambda i: jnp.clip(i - FIRST, 0, NCH - 1)
    second = lambda i: jnp.maximum(i - SECOND, 0)
    dma = pltpu.SemaphoreType.DMA
    sums = pltpu.VMEM((NCH, XW + 2 * NSTATE, CH), bf16)
    return pl.pallas_call(
        forward,
        grid=(LAST + 1,),
        in_specs=[
            split_rows(width, zero, BIG),
            whole(2, width),
            whole(*wi.shape),
            whole(8, w),
            whole(8, w),
            whole(XW, w),
            whole(RANK, w),
            whole(8, w),
            whole(NSTATE, w),
            ANY,
            ANY,
            ANY,
        ],
        out_specs=(
            split_rows(width, zero, BIG),
            rows_of(1, zero, BIG),
            rows_of(w, zero, BIG),
            rows_of(w, first),
            rows_of(w, second),
            pl.BlockSpec((1, NSTATE, w), lambda i: (second(i), 0, 0)),
            whole(NCH, XW, CH),
            whole(8, w),
            ANY,
            ANY,
            ANY,
        ),
        out_shape=(
            shaped(2, SEQ, width, dtype=bf16),
            shaped(SEQ, 1),
            shaped(SEQ, w),
            shaped(SEQ, w, dtype=bf16),
            shaped(SEQ, w, dtype=bf16),
            shaped(NCH, NSTATE, w),
            shaped(NCH, XW, CH),
            shaped(8, w),
            shaped(8, *in_g.shape, dtype=bf16),
            shaped(8, *out_w.shape, dtype=bf16),
            shaped(2, SEQ, cot.shape[1], dtype=bf16),
        ),
        scratch_shapes=[
            pltpu.VMEM((SEQ, w), f32),
            pltpu.VMEM((SEQ, 1), f32),
            pltpu.VMEM((CH + 8, w), f32),
            pltpu.VMEM((NCH, CH, w), bf16),
            pltpu.VMEM((NCH, XW, CH), f32),
            sums,
            sums,
            sums,
            sums,
            pltpu.VMEM((8, w), f32),
            pltpu.VMEM((8, w), f32),
            pltpu.VMEM((NSTATE, w), f32),
            pltpu.VMEM((NSTATE, w), f32),
            pltpu.VMEM((NSTATE, w), f32),
            *scan_scratch(w),
            dma((NCH,)),
            dma((NCH,)),
            dma((NCH,)),
            dma((NCH,)),
            dma((2,)),
            dma((2,)),
            *gather_semaphores(),
        ],
        compiler_params=pltpu.CompilerParams(
            dimension_semantics=("arbitrary",), collective_id=2, has_side_effects=True, vmem_limit_bytes=VMEM_LIMIT
        ),
        cost_estimate=pl.CostEstimate(flops=60 * 1000000000, bytes_accessed=1000000, transcendentals=0),
    )(raw, gain, wi, mix, conv, xproj, dtp, vec, rate, in_g, out_w, cot)


def project_first(raw_ref, gain_ref, w_ref, normed_ref, inv_ref, out_ref):
    low = raw_ref[0].astype(f32)
    high = raw_ref[1].astype(f32)
    squares = jnp.sum(low * low + high * high, axis=1, keepdims=True)
    inv_ref[...] = lax.rsqrt(squares / D + eps)
    low = (low * gain_ref[0:1]).astype(bf16)
    high = (high * gain_ref[1:2]).astype(bf16)
    normed_ref[0] = low
    normed_ref[1] = high
    n = w_ref.shape[2]
    for k in range(SLOTS):
        out_ref[:, k * n : (k + 1) * n] = dot_nn(low, w_ref[2 * k]) + dot_nn(high, w_ref[2 * k + 1])


def split_rows(width, at, tall=CH):
    return pl.BlockSpec((2, tall, width), lambda i: (0, at(i), 0))


def run_project_first(raw, gain, w):
    width = raw.shape[2]
    at = lambda i: i
    n = SLOTS * w.shape[2]
    return call(
        project_first,
        BIG_STEPS,
        (raw, gain, w),
        [split_rows(width, at, BIG), whole(2, width), whole(*w.shape)],
        (shaped(2, SEQ, width, dtype=bf16), shaped(SEQ, 1), shaped(SEQ, n)),
        (split_rows(width, at, BIG), rows_of(1, at, BIG), rows_of(n, at, BIG)),
        [],
        9,
    )


def gate_backward(normed_ref, wg_ref, cot_ref, wo_ref, yfull_ref, inv_ref, gated_ref, dy_ref, dproj_ref, dscale_ref, own_ref, oth_ref, gate_s):
    n = wo_ref.shape[2]
    for k in range(SLOTS):
        gate_s[:, k * n : (k + 1) * n] = dot_nn(normed_ref[0], wg_ref[2 * k]) + dot_nn(normed_ref[1], wg_ref[2 * k + 1])
    d_gated = jnp.zeros(dy_ref.shape, f32)
    for k in range(SLOTS):
        for d in range(2):
            d_gated = d_gated + dot_nt(cot_ref[d, :, k * n : (k + 1) * n], wo_ref[2 * k + d])
    gate_in = gate_s[...]
    inv = inv_ref[...]
    yfull = yfull_ref[...].astype(f32)
    gate = inv * gate_in
    sig = jax.nn.sigmoid(gate)
    passed = gate * sig
    gated = (yfull * passed).astype(bf16)
    gated_ref[...] = gated
    for k in range(SLOTS):
        own_ref[:, k * n : (k + 1) * n] = dot_nn(gated, wo_ref[2 * k])
        oth_ref[:, k * n : (k + 1) * n] = dot_nn(gated, wo_ref[2 * k + 1]).astype(bf16)
    dy_ref[...] = d_gated * passed
    d_gate = d_gated * yfull * (sig * (1.0 + gate * (1.0 - sig)))
    dproj_ref[...] = (inv * d_gate).astype(bf16)
    dscale_ref[...] = jnp.sum(d_gate * gate_in, axis=1, keepdims=True)


def run_gate_backward(normed, wg, cot, wo, yfull, inv):
    width = cot.shape[2]
    w = yfull.shape[1]
    at = lambda i: i
    return call(
        gate_backward,
        BIG_STEPS,
        (normed, wg, cot, wo, yfull, inv),
        [split_rows(width, at, BIG), whole(*wg.shape), split_rows(width, at, BIG), whole(*wo.shape), rows_of(w, at, BIG), rows_of(1, at, BIG)],
        (shaped(SEQ, w, dtype=bf16), shaped(SEQ, w), shaped(SEQ, w, dtype=bf16), shaped(SEQ, 1), shaped(SEQ, width), shaped(SEQ, width, dtype=bf16)),
        (rows_of(w, at, BIG), rows_of(w, at, BIG), rows_of(w, at, BIG), rows_of(1, at, BIG), rows_of(width, at, BIG), rows_of(width, at, BIG)),
        [pltpu.VMEM((BIG, w), f32)],
        22,
    )


def normed_backward(inner_ref, gate_ref, wi_ref, wg_ref, own_ref, oth_ref):
    n = wi_ref.shape[2]
    for d, out_ref in ((1, oth_ref), (0, own_ref)):
        total = jnp.zeros(out_ref.shape, f32)
        for k in range(SLOTS):
            total = total + dot_nt(inner_ref[:, k * n : (k + 1) * n], wi_ref[2 * k + d])
            total = total + dot_nt(gate_ref[:, k * n : (k + 1) * n], wg_ref[2 * k + d])
        out_ref[...] = total.astype(out_ref.dtype)


def run_normed_backward(d_inner, d_gate, wi, wg):
    w = d_inner.shape[1]
    width = wi.shape[1]
    at = lambda i: i
    return call(
        normed_backward,
        BIG_STEPS,
        (d_inner, d_gate, wi, wg),
        [rows_of(w, at, BIG), rows_of(w, at, BIG), whole(*wi.shape), whole(*wg.shape)],
        (shaped(SEQ, width), shaped(SEQ, width, dtype=bf16)),
        (rows_of(width, at, BIG), rows_of(width, at, BIG)),
        [],
        12,
    )


def finish(inner_hbm, gate_hbm, normed_hbm, raw_hbm, wi_hbm, wg_hbm, gain_in_ref, pull_ref, conv_hbm, scan_hbm, alog_hbm, dtp_hbm, xproj_hbm,
           dn_ref, grad_ref, gain_ref, small_refs,
           inner, gate, normed, raw, wi, wg, cs, cr, pairs, xs, xr, fs, fr, fq, ys, yr, zs, zr, own, fin, gs, gr, sv, kr, ks, kx, kf, kg,
           loc, c_send, c_recv, x_send, x_recv, f_send, f_recv, r_send, r_recv, y_send, y_recv, z_send, z_recv, b_send, b_recv, g_send, g_recv, s_send, s_recv, s_load):
    g, r, c = lax.axis_index("grp"), lax.axis_index("row"), lax.axis_index("col")
    x, core, s, p = g // 2, g % 2, c // 2, c % 2
    tall, width = raw.shape
    part = tall // 2
    n = wi_hbm.shape[2]
    q = 2 * p + xor_bit(r, s)
    y_dev, z_dev = (g, 1 - r, c), (g, r, 2 * s + 1 - p)
    x_dev, core_dev = ((1 - x) * 2 + core, r, c), (2 * x + 1 - core, r, c)
    alone = q == c
    passed = 2 * p + xor_bit(1 - r, s)
    stays_here = passed == c

    loads = [
        pltpu.make_async_copy(normed_hbm, normed, loc.at[0]),
        pltpu.make_async_copy(inner_hbm, inner, loc.at[1]),
        pltpu.make_async_copy(gate_hbm, gate, loc.at[2]),
        pltpu.make_async_copy(raw_hbm.at[0, pl.ds(pl.multiple_of(p * tall, 64), tall)], raw, loc.at[5]),
    ]
    for copy in loads[:3]:
        copy.start()
    for k in range(SLOTS):
        for d in range(2):
            cols = pl.ds(k * n, n)
            pltpu.make_async_copy(wi_hbm.at[2 * k + d], wi.at[d, :, cols], loc.at[3]).start()
            pltpu.make_async_copy(wg_hbm.at[2 * k + d], wg.at[d, :, cols], loc.at[4]).start()
    loads[3].start()

    barrier = pltpu.get_barrier_semaphore()
    for dg in range(4):
        for dc in range(4):
            if dg or dc:
                pl.semaphore_signal(barrier, inc=1, device_id=((g + dg) % 4, r, (c + dc) % 4), device_id_type=MESH)
    for dc in range(4):
        pl.semaphore_signal(barrier, inc=1, device_id=(g, 1 - r, (c + dc) % 4), device_id_type=MESH)
    pl.semaphore_wait(barrier, 19)

    def small_loads():
        at = 0
        for ref in (conv_hbm, scan_hbm, alog_hbm, dtp_hbm, xproj_hbm):
            yield pltpu.make_async_copy(ref, sv.at[pl.ds(at, ref.shape[0])], s_load.at[0])
            at += ref.shape[0]

    def channels(d, at_x, at_core):
        to_r = r if d == 0 else 1 - r
        return pl.ds(pl.multiple_of((to_r * 4 + 2 * at_x + at_core) * 128, 128), 128)

    def small_core(j, d):
        src = sv.at[:, channels(d, 1 - x if j == 0 else x, 1 - core)]
        return remote(src, kr.at[j, d], s_send.at[2 * j + d], s_recv.at[2 * j + d], core_dev)

    def small_x(d):
        return remote(ks.at[d], kx.at[d], s_send.at[4 + d], s_recv.at[4 + d], x_dev)

    def small_owner(d):
        return remote(kf.at[d], kg.at[d], s_send.at[6 + d], s_recv.at[6 + d], (g, r if d == 0 else 1 - r, q))

    for copy in small_loads():
        copy.start()

    def weight_grad(at_x, d):
        cols = pl.ds(pl.multiple_of(at_x * 2 * n, 128), 2 * n)

        def tile(t, _):
            rows = pl.ds(pl.multiple_of(t * n, 128), n)
            pairs[d, rows, :] = dot_tn(normed[d, :, rows], inner[:, cols])
            return 0

        lax.fori_loop(0, width // n, tile, 0)

    def of_core(at_core):
        return pl.ds(pl.multiple_of(at_core * n, 128), n)

    def to_core(i, d):
        return remote(cs.at[i, d], cr.at[i, d], c_send.at[2 * i + d], c_recv.at[2 * i + d], core_dev)

    def to_x(d):
        return remote(xs.at[d], xr.at[d], x_send.at[d], x_recv.at[d], x_dev)

    def to_owner():
        return remote(fs.at[0], fr.at[0], f_send.at[0], f_recv.at[0], (g, r, q))

    def to_passer():
        return remote(fs.at[1], fq, r_send.at[0], r_recv.at[0], y_dev)

    def pass_owner():
        return remote(fq, fr.at[1], f_send.at[1], f_recv.at[1], (g, r, passed))

    def grad_to_core(i):
        for d in range(2):
            weight_grad(1 - x if i == 0 else x, d)
            cs[i, d] = pairs[d, :, of_core(1 - core)].astype(bf16)
            to_core(i, d).start()

    def start_of(mine, h):
        return pl.multiple_of((p if mine else 1 - p) * tall + h * part, 32)

    def normed_part(mine, h, d, store):
        rows = pl.ds(start_of(mine, h), part)

        def tile(t, _):
            cols = pl.ds(pl.multiple_of(t * n, 128), n)
            total = dot_nt(inner[rows, :], wi[d, cols, :]) + dot_nt(gate[rows, :], wg[d, cols, :])
            store(cols, total)
            return 0

        lax.fori_loop(0, width // n, tile, 0)

    def to_y(i):
        return remote(ys.at[i], yr.at[i], y_send.at[i], y_recv.at[i], y_dev)

    def to_z(i):
        return remote(zs.at[i], zr.at[i], z_send.at[i], z_recv.at[i], z_dev)

    def into(ref, i, added=None):
        def store(cols, v):
            if added is not None:
                v = v + added[0, :, cols].astype(f32)
            ref[i, :, cols] = v.astype(bf16)

        return store

    pltpu.make_async_copy(sv, sv, s_load.at[0]).wait()
    for j in range(2):
        for d in range(2):
            small_core(j, d).start()
    loads[0].wait()
    loads[1].wait()
    grad_to_core(0)
    loads[2].wait()
    pltpu.make_async_copy(wi, wi, loc.at[3]).wait()
    pltpu.make_async_copy(wg, wg, loc.at[4]).wait()
    for d in range(2):
        to_core(0, d).wait_recv()
        xs[d] = (pairs[d, :, of_core(core)] + cr[0, d].astype(f32)).astype(bf16)
        to_x(d).start()

    for d in range(2):
        small_core(0, d).wait_recv()
        ks[d] = sv[:, channels(d, 1 - x, core)] + kr[0, d]
        small_x(d).start()

    normed_part(False, 0, 1, into(ys, 0))
    to_y(0).start()
    normed_part(False, 1, 1, into(zs, 0))
    to_z(0).start()
    normed_part(False, 1, 0, into(zs, 2))
    to_z(2).start()
    normed_part(True, 0, 1, into(ys, 1))
    to_y(1).start()
    grad_to_core(1)
    to_y(0).wait_recv()
    normed_part(False, 0, 0, into(zs, 1, yr))
    to_z(1).start()
    to_z(0).wait_recv()
    normed_part(True, 1, 1, into(ys, 2, zr))
    to_y(2).start()

    for d in range(2):
        to_core(1, d).wait_recv()
        to_x(d).wait_recv()
        fs[d] = (pairs[d, :, of_core(core)] + cr[1, d].astype(f32) + xr[d].astype(f32)).astype(bf16)
        if d == 0:

            @pl.when(alone)
            def _():
                fr[0] = fs[0]

            @pl.when(jnp.logical_not(alone))
            def _():
                to_owner().start()
        else:
            to_passer().start()
    for d in range(2):
        small_core(1, d).wait_recv()
        small_x(d).wait_recv()
        kf[d] = sv[:, channels(d, x, core)] + kr[1, d] + kx[d]

    @pl.when(alone)
    def _():
        kg[0] = kf[0]

    @pl.when(jnp.logical_not(alone))
    def _():
        small_owner(0).start()

    small_owner(1).start()

    for h in range(2):

        def store(cols, v, h=h):
            own[h * part : (h + 1) * part, cols] = v

        normed_part(True, h, 0, store)

    to_passer().wait_recv()

    @pl.when(stays_here)
    def _():
        fr[1] = fq[...]

    @pl.when(jnp.logical_not(stays_here))
    def _():
        pass_owner().start()

    loads[3].wait()
    for h in range(2):
        to_y(1 + h).wait_recv()
        to_z(1 + h).wait_recv()
        total = own[h * part : (h + 1) * part, :] + yr[1 + h].astype(f32) + zr[1 + h].astype(f32)
        tokens = raw[h * part : (h + 1) * part, :].astype(f32)
        pulled = total * gain_in_ref[0:1] - pull_ref[h * part : (h + 1) * part, :] * tokens
        fin[h * part : (h + 1) * part, :] = pulled.astype(bf16)
        product = total * tokens
        folded = jnp.sum(product.reshape(part // 8, 8, width), axis=0)
        for b in range(SLOTS):
            if h == 0:
                gs[b] = folded[:, b * n : (b + 1) * n]
            else:
                gs[b] = gs[b] + folded[:, b * n : (b + 1) * n]

    cut = tall - LC
    low = cut - LC
    moves = {
        0: ([(0, tall, 0)], None),
        1: ([(0, cut, 0)], (cut, 3, low)),
        2: ([(LC, tall, 0)], (0, 1, cut)),
        3: ([(LC, cut, 0), (cut, tall, cut)], (0, 2, cut)),
    }

    def border(k):
        stays, leaves = moves[k]
        mine = [pltpu.make_async_copy(fin.at[a:b], dn_ref.at[at : at + b - a], loc.at[i]) for i, (a, b, at) in enumerate(stays)]
        if leaves is None:
            return mine, None
        a, to, at = leaves
        return mine, remote(fin.at[a : a + LC], dn_ref.at[at : at + LC], b_send.at[0], b_recv.at[0], (g, r, to))

    for k in range(4):

        @pl.when(c == k)
        def _(k=k):
            mine, gone = border(k)
            if gone is not None:
                gone.start()
            for copy in mine:
                copy.start()

    def gain_copy(dg, dc):
        to = ((g + dg) % 4, r, (c + dc) % 4)
        i = 4 * dg + dc - 1
        return remote(gs.at[(g + dg) % 4], gr.at[i], g_send.at[i], g_recv.at[0], to)

    pairs = [(dg, dc) for dg in range(4) for dc in range(4) if dg or dc]
    for dg, dc in pairs:
        gain_copy(dg, dc).start()

    @pl.when(jnp.logical_not(alone))
    def _():
        to_owner().wait_recv()

    @pl.when(jnp.logical_not(stays_here))
    def _():
        pass_owner().wait_recv()

    grad_ref[...] = fr[0].astype(f32) + fr[1].astype(f32)

    pltpu.make_async_copy(gr, gr, g_recv.at[0]).wait()
    gain_ref[...] = jnp.sum(gr[...], axis=0) + gs[g]

    for k in range(4):

        @pl.when(c == k)
        def _(k=k):
            mine, gone = border(k)
            for copy in mine:
                copy.wait()
            if gone is not None:
                gone.wait()

    @pl.when(jnp.logical_not(alone))
    def _():
        small_owner(0).wait()

    small_owner(1).wait()
    at = 0
    for ref in small_refs:
        ref[...] = kg[0, at : at + ref.shape[0], :] + kg[1, at : at + ref.shape[0], :]
        at += ref.shape[0]
    for d in range(2):
        for j in range(2):
            small_core(j, d).wait_send()
        small_x(d).wait_send()

    for dg, dc in pairs:
        gain_copy(dg, dc).wait_send()
    for i in range(3):
        to_y(i).wait_send()
        to_z(i).wait_send()
    for d in range(2):
        for i in range(2):
            to_core(i, d).wait_send()
        to_x(d).wait_send()

    @pl.when(jnp.logical_not(alone))
    def _():
        to_owner().wait_send()

    @pl.when(jnp.logical_not(stays_here))
    def _():
        pass_owner().wait_send()

    to_passer().wait_send()


SMALL_ROWS = (KCONV, 1, 3, 1, 1, 6, NSTATE, RANK, XW)


def finish_kernel(*refs):
    n = len(SMALL_ROWS)
    finish(*refs[:16], refs[16 : 16 + n], *refs[16 + n :])


def run_finish(d_inner, d_gate, normed, raw, wi, wg, gain, pull, small):
    w = d_inner.shape[1]
    width, n = wi.shape[1], wi.shape[2]
    tall = SEQ // 2
    part = tall // 2
    dma = pltpu.SemaphoreType.DMA
    low = lambda *shape: pltpu.VMEM(shape, bf16)
    vmem = pl.BlockSpec(memory_space=pltpu.VMEM)
    rows = sum(v.shape[0] for v in small)
    return pl.pallas_call(
        finish_kernel,
        in_specs=[ANY] * 6 + [vmem, vmem] + [ANY] * 5,
        out_specs=[ANY, vmem, vmem] + [vmem] * len(SMALL_ROWS),
        out_shape=(shaped(tall, width, dtype=bf16), shaped(width, n), shaped(8, n), *[shaped(v, 128) for v in SMALL_ROWS]),
        scratch_shapes=[
            low(SEQ, w),
            low(SEQ, w),
            low(2, SEQ, width),
            low(tall, width),
            low(2, width, w),
            low(2, width, w),
            low(2, 2, width, n),
            low(2, 2, width, n),
            pltpu.VMEM((2, width, 2 * n), f32),
            low(2, width, n),
            low(2, width, n),
            low(2, width, n),
            low(2, width, n),
            low(width, n),
            low(3, part, width),
            low(3, part, width),
            low(3, part, width),
            low(3, part, width),
            pltpu.VMEM((tall, width), f32),
            low(tall, width),
            pltpu.VMEM((SLOTS, 8, n), f32),
            pltpu.VMEM((15, 8, n), f32),
            pltpu.VMEM((rows, w), f32),
            pltpu.VMEM((2, 2, rows, 128), f32),
            pltpu.VMEM((2, rows, 128), f32),
            pltpu.VMEM((2, rows, 128), f32),
            pltpu.VMEM((2, rows, 128), f32),
            pltpu.VMEM((2, rows, 128), f32),
            dma((6,)),
            dma((4,)),
            dma((4,)),
            dma((2,)),
            dma((2,)),
            dma((2,)),
            dma((2,)),
            dma((1,)),
            dma((1,)),
            dma((3,)),
            dma((3,)),
            dma((3,)),
            dma((3,)),
            dma((1,)),
            dma((1,)),
            dma((15,)),
            dma((1,)),
            dma((8,)),
            dma((8,)),
            dma((1,)),
        ],
        compiler_params=pltpu.CompilerParams(collective_id=1, has_side_effects=True, vmem_limit_bytes=VMEM_LIMIT),
        cost_estimate=pl.CostEstimate(flops=60 * 1000000000, bytes_accessed=1000000, transcendentals=0),
    )(d_inner, d_gate, normed, raw, wi, wg, gain, pull, *small)


def late_parts(order_ref, normed_ref, gate_ref, gated_ref, cot_ref, gate_sent, out_sent, gate_kept, out_kept):
    t = pl.program_id(0)
    for d in range(2):
        low = dot_tn(normed_ref[d], gate_ref[...])
        high = dot_tn(gated_ref[...], cot_ref[d])

        @pl.when(t < 2)
        def _(d=d, low=low, high=high):
            gate_sent[0, d] = low.astype(bf16)
            out_sent[0, d] = high.astype(bf16)

        @pl.when(t >= 2)
        def _(d=d, low=low, high=high):
            gate_kept[0, d] = low
            out_kept[0, d] = high


def run_late_parts(order, normed, d_gate, gated, cot):
    width = normed.shape[2]
    w = gated.shape[1]
    n = w // SLOTS
    sent = pl.BlockSpec((1, 2, width, n), lambda t, o: (jnp.minimum(t, 1), 0, 0, 0))
    kept = pl.BlockSpec((1, 2, width, n), lambda t, o: (jnp.maximum(t - 2, 0), 0, 0, 0))
    return pl.pallas_call(
        late_parts,
        grid_spec=pltpu.PrefetchScalarGridSpec(
            num_scalar_prefetch=1,
            grid=(SLOTS,),
            in_specs=[
                pl.BlockSpec((2, SEQ, width), lambda t, o: (0, 0, 0)),
                pl.BlockSpec((SEQ, n), lambda t, o: (0, o[t])),
                pl.BlockSpec((SEQ, w), lambda t, o: (0, 0)),
                pl.BlockSpec((2, SEQ, n), lambda t, o: (0, 0, o[t])),
            ],
            out_specs=(sent, sent, kept, kept),
        ),
        out_shape=(shaped(2, 2, width, n, dtype=bf16), shaped(2, 2, width, n, dtype=bf16), shaped(2, 2, width, n), shaped(2, 2, width, n)),
        compiler_params=pltpu.CompilerParams(dimension_semantics=("arbitrary",), vmem_limit_bytes=VMEM_LIMIT),
        cost_estimate=pl.CostEstimate(flops=14 * 1000000000, bytes_accessed=1000000, transcendentals=0),
    )(order, normed, d_gate, gated, cot)


QUARTERS = 4
SUM_LAG = 3
PIECE = SEQ // 2 // QUARTERS
OTHER_STEP = (1, 2, 3, 4)
PAIR_STEP = (3, 4, 1, 2)
FINAL_STEP = (7, 7, 7, 7)
X_STEP = (0, 1)
OWNER_STEP = (2, 4)
DONE_STEP = (8, 8)
QUARTER_STEP = ((2, 2, 3, 3), (4, 4, 5, 5))
PASS_STEP = ((4, 4, 5, 5), (6, 6, 6, 6))


def border_moves(tall):
    cut = tall - LC
    low = cut - LC
    return {
        0: ([(0, tall, 0)], None),
        1: ([(0, cut, 0)], (cut, 3, low)),
        2: ([(LC, tall, 0)], (0, 1, cut)),
        3: ([(LC, cut, 0), (cut, tall, cut)], (0, 2, cut)),
    }


def backward(xdbl_ref, xconv_ref, dy_ref, dtp_ref, vec_ref, rate_ref, starts_ref, mix_ref, into_ref, sent_hbm, kept_hbm, own_hbm, oth_hbm,
             dxdbl_ref, dxc_ref, alog_ref, sums_ref, dtpg_ref, grad_ref, branch_ref,
             first, first_s, first_r, part, ys, yr, zs, zr, cr, kp, xs, xr, fs, fr, fq, out, own, oth, by_s, by, bz_s, bz, fin,
             y_send, y_recv, z_send, z_recv, e_send, e_recv, c_send, c_recv, x_send, x_recv, f_send, f_recv, r_send, r_recv,
             p_send, p_recv, q_send, q_recv, b_send, b_recv, load_k, load_o, stay, put, *scratch):
    i = pl.program_id(0)
    g, r, c = lax.axis_index("grp"), lax.axis_index("row"), lax.axis_index("col")
    x, core, s, p = g // 2, g % 2, c // 2, c % 2
    q = 2 * p + xor_bit(r, s)
    tall = SEQ // 2
    alone = q == c
    passed = 2 * p + xor_bit(1 - r, s)
    stays_here = passed == c
    y_dev, z_dev, far_dev = (g, 1 - r, c), (g, r, 2 * s + 1 - p), (g, 1 - r, (c + 2) % 4)
    x_dev, core_dev = ((1 - x) * 2 + core, r, c), (2 * x + 1 - core, r, c)
    to_first = remote(first_s, first_r, e_send.at[0], e_recv.at[0], far_dev)

    def to_y(k):
        return remote(ys.at[k], yr.at[k], y_send.at[k], y_recv.at[k], y_dev)

    def to_z(k):
        return remote(zs.at[k], zr.at[k], z_send.at[k], z_recv.at[k], z_dev)

    def to_core(n, j):
        return remote(sent_hbm[n].at[j], cr.at[n, j], c_send.at[n, j], c_recv.at[n, j], core_dev)

    def load(n, j):
        return pltpu.make_async_copy(kept_hbm[n].at[j], kp.at[n], load_k.at[n])

    def to_x(n):
        return remote(xs.at[n], xr.at[n], x_send.at[n], x_recv.at[n], x_dev)

    def quarter(ref, at):
        rows = ref.shape[0] // QUARTERS
        return ref if at is None else ref.at[pl.ds(at * rows, rows)]

    def to_owner(n, at=None):
        return remote(quarter(fs.at[n, 0], at), quarter(fr.at[n, 0], at), f_send.at[n, 0], f_recv.at[n, 0], (g, r, q))

    def to_passer(n):
        return remote(fs.at[n, 1], fq.at[n], r_send.at[n], r_recv.at[n], y_dev)

    def pass_owner(n, at=None):
        return remote(quarter(fq.at[n], at), quarter(fr.at[n, 1], at), f_send.at[n, 1], f_recv.at[n, 1], (g, r, passed))

    def rows_at(mine, j):
        return pl.ds(pl.multiple_of((p if mine else 1 - p) * tall + j * PIECE, 16), PIECE)

    def branch_y(m):
        if m >= QUARTERS:
            src = oth_hbm.at[rows_at(False, m - QUARTERS)]
        elif m < 2:
            src = oth_hbm.at[rows_at(True, m)]
        else:
            src = by_s.at[m - 2]
        return remote(src, by.at[m], p_send.at[m], p_recv.at[m], y_dev)

    def branch_z(m):
        src = bz_s.at[m] if m < QUARTERS else oth_hbm.at[rows_at(False, m - 2)]
        return remote(src, bz.at[m], q_send.at[m], q_recv.at[m], z_dev)

    load_own = pltpu.make_async_copy(own_hbm, own, load_o.at[0])
    load_oth = pltpu.make_async_copy(oth_hbm.at[pl.ds(pl.multiple_of(p * tall + 2 * PIECE, 16), 2 * PIECE)], oth, load_o.at[1])

    def border(k):
        stays, leaves = border_moves(tall)[k]
        mine = [pltpu.make_async_copy(fin.at[a:b], branch_ref.at[at : at + b - a], stay.at[n]) for n, (a, b, at) in enumerate(stays)]
        if leaves is None:
            return mine, None
        a, to, at = leaves
        return mine, remote(fin.at[a : a + LC], branch_ref.at[at : at + LC], b_send.at[0], b_recv.at[0], (g, r, to))

    def at_border(act):
        for k in range(4):

            @pl.when(c == k)
            def _(k=k):
                act(*border(k))

    def pass_on(k):
        to_y(k).wait_recv()
        part[k] = part[k] + yr[k].astype(f32)
        zs[k] = part[k].astype(bf16)
        to_z(k).start()

    def settle(k):
        to_z(k).wait_recv()
        dxdbl_ref[NCH - 1 - k] = part[k] + zr[k].astype(f32)

    @pl.when(i == 0)
    def _():
        barrier = pltpu.get_barrier_semaphore()
        for dr in range(2):
            for dc in range(4):
                if dr or dc:
                    pl.semaphore_signal(barrier, inc=1, device_id=(g, (r + dr) % 2, (c + dc) % 4), device_id_type=MESH)
        for device in (x_dev, core_dev):
            pl.semaphore_signal(barrier, inc=1, device_id=device, device_id_type=MESH)
        pl.semaphore_wait(barrier, 9)
        for j in range(2):
            for n in range(2):
                to_core(n, j).start()
        for n in range(2):
            load(n, 0).start()
        load_own.start()
        load_oth.start()
        for m in (QUARTERS, QUARTERS + 1):
            branch_y(m).start()
            branch_z(m).start()
        first[...] = jnp.zeros_like(first)
        alog_ref[...] = jnp.zeros_like(alog_ref)
        sums_ref[...] = jnp.zeros_like(sums_ref)
        dtpg_ref[...] = jnp.zeros_like(dtpg_ref)

    @pl.when(i == 1)
    def _():
        to_first.wait()
        first[...] = mix_ref[0:1] * first_s[...] + into_ref[0:1] * first_r[...]

    chunk_backward(xdbl_ref, xconv_ref, dy_ref, dtp_ref, vec_ref, rate_ref, starts_ref, part.at[i], dxc_ref, alog_ref, sums_ref, dtpg_ref, first, *scratch)

    @pl.when(i == 0)
    def _():
        first_s[...] = first[...]
        to_first.start()

    @pl.when(i == 1)
    def _():
        load_own.wait()
        load_oth.wait()

    for n in range(2):

        @pl.when(i == X_STEP[n])
        def _(n=n):
            to_core(n, 0).wait_recv()
            load(n, 0).wait()
            xs[n] = (kp[n] + cr[n, 0].astype(f32)).astype(bf16)
            to_x(n).start()
            load(n, 1).start()

        @pl.when(i == OWNER_STEP[n])
        def _(n=n):
            load(n, 1).wait()
            to_core(n, 1).wait_recv()
            to_x(n).wait_recv()
            fs[n] = (kp[n] + cr[n, 1].astype(f32) + xr[n].astype(f32)).astype(bf16)

            to_passer(n).start()

            @pl.when(alone)
            def _():
                fr[n, 0] = fs[n, 0]

        @pl.when(i == OWNER_STEP[n] + 2)
        def _(n=n):
            to_passer(n).wait_recv()

            @pl.when(stays_here)
            def _():
                fr[n, 1] = fq[n]

        for k in range(QUARTERS):

            @pl.when(jnp.logical_not(alone) & (i == QUARTER_STEP[n][k]))
            def _(n=n, k=k):
                to_owner(n, k).start()

            @pl.when(jnp.logical_not(stays_here) & (i == PASS_STEP[n][k]))
            def _(n=n, k=k):
                pass_owner(n, k).start()

        @pl.when(i == DONE_STEP[n])
        def _(n=n):
            @pl.when(jnp.logical_not(alone))
            def _():
                to_owner(n).wait_recv()

            @pl.when(jnp.logical_not(stays_here))
            def _():
                pass_owner(n).wait_recv()

            out[n] = fr[n, 0].astype(f32) + fr[n, 1].astype(f32)
            pltpu.make_async_copy(out.at[n], grad_ref.at[n], put.at[n]).start()

    for j in range(QUARTERS):

        @pl.when(i == OTHER_STEP[j])
        def _(j=j):
            if j >= 2:
                branch_z(QUARTERS + j - 2).wait_recv()
                mine = oth[(j - 2) * PIECE : (j - 1) * PIECE, :].astype(f32)
                by_s[j - 2] = (mine + bz[QUARTERS + j - 2].astype(f32)).astype(bf16)
            branch_y(j).start()

        @pl.when(i == PAIR_STEP[j])
        def _(j=j):
            total = own[rows_at(False, j), :]
            if j < 2:
                branch_y(QUARTERS + j).wait_recv()
                total = total + by[QUARTERS + j].astype(f32)
            bz_s[j] = total.astype(bf16)
            branch_z(j).start()

        @pl.when(i == FINAL_STEP[j])
        def _(j=j):
            branch_y(j).wait_recv()
            branch_z(j).wait_recv()
            fin[j * PIECE : (j + 1) * PIECE, :] = (own[rows_at(True, j), :] + by[j].astype(f32) + bz[j].astype(f32)).astype(bf16)

    @pl.when(i == 7)
    def _():
        def begin(mine, gone):
            if gone is not None:
                gone.start()
            for copy in mine:
                copy.start()

        at_border(begin)

    @pl.when(i >= SUM_LAG)
    def _():
        pass_on(i - SUM_LAG)

    ys[i] = part[i].astype(bf16)
    to_y(i).start()
    @pl.when(i == NCH - 1)
    def _():
        for k in range(NCH - SUM_LAG, NCH):
            pass_on(k)
        for k in range(NCH):
            settle(k)

        def finish_border(mine, gone):
            for copy in mine:
                copy.wait()
            if gone is not None:
                gone.wait()

        at_border(finish_border)

        def sent(k, _):
            to_y(k).wait_send()
            to_z(k).wait_send()
            return 0

        lax.fori_loop(0, NCH, sent, 0)
        for n in range(2):
            for j in range(2):
                to_core(n, j).wait_send()
            to_x(n).wait_send()

            to_passer(n).wait_send()

            @pl.when(jnp.logical_not(alone))
            def _(n=n):
                to_owner(n).wait_send()

            @pl.when(jnp.logical_not(stays_here))
            def _(n=n):
                pass_owner(n).wait_send()

            pltpu.make_async_copy(out.at[n], grad_ref.at[n], put.at[n]).wait()
        for m in range(QUARTERS + 2):
            branch_y(m).wait_send()
            branch_z(m).wait_send()


def backward_kernel(*refs):
    backward(*refs[:9], refs[9:11], refs[11:13], *refs[13:])


def run_backward(xdbl, xconv, dy, dtp, vec, rate, starts, mix, into, sent, kept, own, oth):
    w = xconv.shape[1]
    width = own.shape[1]
    _, _, tall, n = sent[0].shape
    at = lambda i: NCH - 1 - i
    dma = pltpu.SemaphoreType.DMA
    low = lambda *shape: pltpu.VMEM(shape, bf16)
    sums = low(NCH, XW, CH)
    state = pltpu.VMEM((NSTATE, w), f32)
    return pl.pallas_call(
        backward_kernel,
        grid=(NCH,),
        in_specs=[
            chunk_of(XW, at),
            rows_of(w, at),
            rows_of(w, at),
            whole(RANK, w),
            whole(8, w),
            whole(NSTATE, w),
            pl.BlockSpec((1, NSTATE, w), lambda i: (at(i), 0, 0)),
            whole(8, w),
            whole(8, w),
        ]
        + [ANY] * 6,
        out_specs=(whole(NCH, XW, CH), rows_of(w, at), whole(NSTATE, w), whole(8, w), whole(RANK, w), ANY, ANY),
        out_shape=(
            shaped(NCH, XW, CH),
            shaped(SEQ, w),
            shaped(NSTATE, w),
            shaped(8, w),
            shaped(RANK, w),
            shaped(2, tall, n),
            shaped(SEQ // 2, width, dtype=bf16),
        ),
        scratch_shapes=[
            state,
            state,
            state,
            pltpu.VMEM((NCH, XW, CH), f32),
            sums,
            sums,
            sums,
            sums,
            low(2, 2, 2, tall, n),
            pltpu.VMEM((2, 2, tall, n), f32),
            low(2, 2, tall, n),
            low(2, 2, tall, n),
            low(2, 2, tall, n),
            low(2, 2, tall, n),
            low(2, tall, n),
            pltpu.VMEM((2, tall, n), f32),
            pltpu.VMEM((SEQ, width), f32),
            low(2 * PIECE, width),
            low(2, PIECE, width),
            low(QUARTERS + 2, PIECE, width),
            low(QUARTERS, PIECE, width),
            low(QUARTERS + 2, PIECE, width),
            low(SEQ // 2, width),
            dma((NCH,)),
            dma((NCH,)),
            dma((NCH,)),
            dma((NCH,)),
            dma((1,)),
            dma((1,)),
            dma((2, 2)),
            dma((2, 2)),
            dma((2,)),
            dma((2,)),
            dma((2, 2)),
            dma((2, 2)),
            dma((2,)),
            dma((2,)),
            dma((QUARTERS + 2,)),
            dma((QUARTERS + 2,)),
            dma((QUARTERS + 2,)),
            dma((QUARTERS + 2,)),
            dma((1,)),
            dma((1,)),
            dma((2,)),
            dma((2,)),
            dma((2,)),
            dma((2,)),
            *backward_scratch(w),
        ],
        compiler_params=pltpu.CompilerParams(
            dimension_semantics=("arbitrary",), collective_id=3, has_side_effects=True, vmem_limit_bytes=61 * 1024 * 1024
        ),
        cost_estimate=pl.CostEstimate(flops=120 * 1000000000, bytes_accessed=1000000, transcendentals=0),
    )(xdbl, xconv, dy, dtp, vec, rate, starts, mix, into, *sent, *kept, own, oth)


def conv_backward_far(inner_ref, halo_ref, inv_ref, halo_inv_ref, tail_ref, conv_ref, xproj_ref, dxc_ref, dxdbl_ref, mix_ref, into_ref,
                      dproj_ref, dscale_ref, sums_ref, xprojg_ref, head, sent, got, buf, dbuf, send_sem, recv_sem):
    i = pl.program_id(0)
    g, r, c = lax.axis_index("grp"), lax.axis_index("row"), lax.axis_index("col")
    far_dev = (g, 1 - r, (c + 2) % 4)
    to_far = remote(sent, got, send_sem.at[0], recv_sem.at[0], far_dev)

    @pl.when(i == 0)
    def _():
        barrier = pltpu.get_barrier_semaphore()
        pl.semaphore_signal(barrier, inc=1, device_id=far_dev, device_id_type=MESH)
        pl.semaphore_wait(barrier, 1)
        head[...] = jnp.zeros_like(head)
        sums_ref[...] = jnp.zeros_like(sums_ref)
        xprojg_ref[...] = jnp.zeros_like(xprojg_ref)

    @pl.when(i == 1)
    def _():
        to_far.wait()
        head[...] = mix_ref[...] * sent[...] + into_ref[...] * got[...]

    conv_chunk(NCH - 1 - i, inner_ref, halo_ref, inv_ref, halo_inv_ref, tail_ref, conv_ref, xproj_ref, dxc_ref, dxdbl_ref,
               dproj_ref, dscale_ref, sums_ref, xprojg_ref, head, buf, dbuf)

    @pl.when(i == 0)
    def _():
        sent[...] = head[...]
        to_far.start()


def run_conv_backward_far(inner, inv, tail, conv, xproj, dxc, dxdbl, mix, into):
    w = inner.shape[1]
    at = lambda i: NCH - 1 - i
    before = lambda i: (jnp.maximum(at(i) * (CH // 8) - 1, 0), 0)
    rows = pltpu.VMEM((8, w), f32)
    return pl.pallas_call(
        conv_backward_far,
        grid=(NCH,),
        in_specs=[
            rows_of(w, at),
            pl.BlockSpec((8, w), before),
            rows_of(1, at),
            pl.BlockSpec((8, 1), before),
            whole(8, w),
            whole(8, w),
            whole(XW, w),
            rows_of(w, at),
            chunk_of(XW, at),
            whole(8, w),
            whole(8, w),
        ],
        out_specs=(rows_of(w, at), rows_of(1, at), whole(8, w), whole(XW, w)),
        out_shape=(shaped(SEQ, w, dtype=bf16), shaped(SEQ, 1), shaped(8, w), shaped(XW, w)),
        scratch_shapes=[
            rows,
            rows,
            rows,
            pltpu.VMEM((CH + 8, w), f32),
            pltpu.VMEM((CH + 8, w), f32),
            pltpu.SemaphoreType.DMA((1,)),
            pltpu.SemaphoreType.DMA((1,)),
        ],
        compiler_params=pltpu.CompilerParams(
            dimension_semantics=("arbitrary",), collective_id=4, has_side_effects=True, vmem_limit_bytes=VMEM_LIMIT
        ),
        cost_estimate=pl.CostEstimate(flops=20 * 1000000000, bytes_accessed=1000000, transcendentals=0),
    )(inner, inner, inv, inv, tail, conv, xproj, dxc, dxdbl, mix, into)


def per_device(
    tokens,
    gain,
    in_proj,
    conv_weight,
    conv_bias,
    x_proj,
    dt_proj,
    dt_bias,
    a_log,
    d_skip,
    out_proj,
    table,
    cotangent,
):
    row = lax.axis_index("row")
    col = lax.axis_index("col")
    grp = lax.axis_index("grp")
    low_row = row == 0
    low_pair = col % 2 == 0
    half = col // 2
    places = [(r, c) for r in range(2) for c in range(4)]
    quick = lax.axis_size("grp") == 4

    def spot(r, c):
        return r * 4 + c

    def send(v, pairs):
        return lax.ppermute(v, ("row", "col"), [(spot(*a), spot(*b)) for a, b in pairs])

    def swap(v):
        return send(v, [((r, c), (1 - r, c)) for r, c in places])

    def pair(v):
        return send(v, [((r, c), (r, c ^ 1)) for r, c in places])

    def across(v):
        return send(v, [((r, c), (1 - r, c ^ 2)) for r, c in places])

    def quarter_spot(q, s):
        return ((q & 1) ^ s, 2 * s + (q >> 1))

    same = [((r, q), quarter_spot(q, r ^ (q & 1))) for r, q in places]
    other = [((r, q), quarter_spot(q, 1 ^ r ^ (q & 1))) for r, q in places]
    spread = [((r, q), quarter_spot(q, r)) for r, q in places]

    def back(pairs):
        return [(b, a) for a, b in pairs]

    def flip(v, bit):
        return lax.ppermute(v, "grp", [(g, g ^ bit) for g in range(4)])

    def scatter_grp(v, axis):
        return lax.psum_scatter(v, "grp", scatter_dimension=axis, tiled=True)

    def by_pair(own, paired):
        return jnp.where(low_pair, own, paired), jnp.where(low_pair, paired, own)

    local = tokens.shape[0]
    cut = local - LC
    tail_at = cut - LC

    def to_sequences(v):
        got = send(jnp.where(col == 3, v[tail_at:cut], v[cut:]), [((r, a), (r, b)) for r in range(2) for a, b in ((1, 2), (2, 3), (3, 1))])
        low = jnp.concatenate([v[:cut], jnp.where(col == 0, v[cut:], got)], axis=0)
        two = jnp.concatenate([got, v[:cut]], axis=0)
        three = jnp.concatenate([got, v[:tail_at], v[cut:]], axis=0)
        return jnp.where(col < 2, low, jnp.where(col == 2, two, three))

    def from_sequences(v):
        got = send(jnp.where(col == 1, v[cut:], v[:LC]), [((r, b), (r, a)) for r in range(2) for a, b in ((1, 2), (2, 3), (3, 1))])
        low = jnp.concatenate([v[:cut], jnp.where(col == 0, v[cut:], got)], axis=0)
        two = jnp.concatenate([v[LC:], got], axis=0)
        three = jnp.concatenate([v[LC:cut], got, v[cut:]], axis=0)
        return jnp.where(col < 2, low, jnp.where(col == 2, two, three))

    def gather_quad(v):
        swapped = swap(v)
        paired = pair(v)
        mid = v.shape[0] // 2
        diagonal = jnp.concatenate([pair(swapped[:mid]), swap(paired[mid:])], axis=0)
        first_own, second_own = by_pair(v, paired)
        first_oth, second_oth = by_pair(swapped, diagonal)
        return jnp.stack([jnp.concatenate([first_own, second_own], axis=0), jnp.concatenate([first_oth, second_oth], axis=0)])

    def scatter_quad(own, oth):
        v = own + swap(oth.astype(bf16)).astype(f32)
        first, second = v[:local], v[local:]
        kept, sent = jnp.where(low_pair, first, second), jnp.where(low_pair, second, first)
        return kept + pair(sent.astype(bf16)).astype(f32)

    own_table = jnp.where(half == 0, table[0], table[1])
    oth_table = jnp.where(half == 0, table[1], table[0])
    resumes_own = own_table == half
    resumed_by_other = oth_table == half

    small = jnp.concatenate([conv_weight, conv_bias[None], dt_bias[None], d_skip[None], a_log, dt_proj, x_proj.T], axis=0)
    lanes = small.shape[1]
    used = small.shape[0]
    gain_rows = gain.size // lanes
    width = tokens.shape[1]
    if quick:
        small = jnp.concatenate([small, gain.reshape(gain_rows, lanes)], axis=0)
        small = jnp.pad(small, ((0, -small.shape[0] % 16), (0, 0)))
        raw, wi, small = run_gather_start(tokens, in_proj[:, 0], small)
        gain_all = small[:, used : used + gain_rows].reshape(2, width).astype(f32)
        small = jnp.swapaxes(small, 0, 1).reshape(small.shape[1], 8 * lanes)
    else:
        raw = gather_quad(to_sequences(tokens))

        def weight(shard):
            v = lax.all_gather(jnp.stack([send(shard, same), send(shard, other)]), "grp", axis=2, tiled=True)
            v = v.reshape(2, v.shape[1], SLOTS, v.shape[2] // SLOTS)
            return jnp.transpose(v, (2, 0, 1, 3)).reshape(2 * SLOTS, v.shape[1], v.shape[3])

        wi = weight(in_proj[:, 0])
        small = send(lax.all_gather(small, ("row", "grp"), axis=1, tiled=True), spread)
        gain_all = lax.all_gather(gain, ("row", "grp"), axis=0, tiled=True).astype(f32).reshape(2, width)
    w = small.shape[1]
    zero_row = jnp.zeros((1, w), f32)
    conv = jnp.concatenate([small[0:5].astype(f32)] + [zero_row] * 3, axis=0)
    vec = jnp.concatenate([small[5:7].astype(f32)] + [zero_row] * 6, axis=0)
    rate = -jnp.exp(small[7 : 7 + NSTATE].astype(f32))
    dtp = small[7 + NSTATE : 7 + NSTATE + RANK]
    xproj = small[7 + NSTATE + RANK : 7 + NSTATE + RANK + XW]
    gain_own = jnp.where(low_row, gain_all[0], gain_all[1])
    gain_two = jnp.stack([gain_own, jnp.where(low_row, gain_all[1], gain_all[0])])

    zero_state = jnp.zeros((NSTATE, w), f32)
    if quick:
        mix = jnp.broadcast_to(resumes_own.astype(f32), (8, w))
        normed, inv, inner, xconv, yfull, starts, xdbl, tail, wg, wo, cot = run_forward(raw, gain_two, wi, mix, conv, xproj, dtp, vec, rate, in_proj[:, 1], out_proj, cotangent)
    else:
        normed, inv, inner = run_project_first(raw, gain_two, wi)
        tail_own = (inv * inner)[LP - 8 : LP]
        tail = jnp.where(resumes_own, tail_own, across(tail_own))
        xconv, xdbl = run_conv_forward(inner, inv, tail, conv, xproj)
        for move in (swap, pair):
            xdbl = xdbl + move(xdbl)
        xdbl = jnp.swapaxes(xdbl.reshape(XW, NCH, CH), 0, 1)
        *kept, final = run_scan_forward(0, PC, xdbl, xconv, dtp, vec, rate, zero_state)
        resumed = jnp.where(resumes_own, final, across(final))
        yfull, starts, _ = run_scan_forward(PC, NCH - PC, xdbl, xconv, dtp, vec, rate, resumed, kept)
        wg, wo = weight(in_proj[:, 1]), weight(out_proj)
        cot = gather_quad(to_sequences(cotangent))
    gated, d_yfull, d_gate_proj, gate_scale, branch_own, branch_oth = run_gate_backward(normed, wg, cot, wo, yfull, inv)

    def collect(v):
        return send(v[0].astype(bf16), back(same)).astype(f32) + send(v[1].astype(bf16), back(other)).astype(f32)

    def rows_product(a, b, out_dtype):
        return lax.dot_general(a, b, (((1,), (0,)), ((), ())), preferred_element_type=f32).astype(out_dtype)

    zero_head = jnp.zeros((8, w), f32)
    conv_back = functools.partial(run_conv_backward, inner=inner, inv=inv, tail=tail, conv=conv, xproj=xproj)
    if quick:
        x, core = grp // 2, grp % 2
        order = jnp.stack([2 * (1 - x) + 1 - core, 2 * x + 1 - core, 2 * (1 - x) + core, 2 * x + core]).astype(jnp.int32)
        gate_sent, out_sent, gate_kept, out_kept = run_late_parts(order, normed, d_gate_proj, gated, cot)
        sent, kept = (gate_sent, out_sent), (gate_kept, out_kept)
        into = jnp.broadcast_to(resumed_by_other.astype(f32), (8, w))
        dxdbl, dxc, alog_grad, scan_sums, dtp_grad, late_grads, branch = run_backward(
            xdbl, xconv, d_yfull, dtp, vec, rate, starts, mix, into, sent, kept, branch_own, branch_oth
        )
        gate_grad, out_grad = late_grads[0], late_grads[1]
    else:
        branch = from_sequences(scatter_quad(branch_own, branch_oth).astype(bf16))
        out_grad = collect([scatter_grp(dot_tn(gated, cot[d]), 1) for d in range(2)])
        gate_grad = collect([scatter_grp(dot_tn(normed[d], d_gate_proj), 1) for d in range(2)])
        sums = (zero_state, jnp.zeros((8, w), f32), jnp.zeros((RANK, w), f32))
        scan = functools.partial(run_scan_backward, xdbl=xdbl, xconv=xconv, dy=d_yfull, dtp=dtp, vec=vec, rate=rate, starts=starts)
        dx_c, dxc, *sums, g_first = scan(PC, NCH - PC, carry=zero_state, sums=sums)
        g_into = jnp.where(resumes_own, g_first, 0.0) + jnp.where(resumed_by_other, across(g_first), 0.0)
        dx_p, dxc, *sums, _ = scan(0, PC, carry=g_into, sums=sums, kept=(dxc,))
        alog_grad, scan_sums, dtp_grad = sums
        dxdbl = jnp.concatenate([dx_p, dx_c], axis=1)
        for move in (swap, pair):
            dxdbl = dxdbl + move(dxdbl)
        dxdbl = jnp.swapaxes(dxdbl.reshape(XW, NCH, CH), 0, 1)

    output = (tokens.astype(f32) + branch.astype(f32)).astype(bf16)
    if quick:
        d_inner_proj, inner_scale, conv_sums, xproj_grad = run_conv_backward_far(inner, inv, tail, conv, xproj, dxc, dxdbl, mix, into)
    else:
        sums = (jnp.zeros((8, w), f32), jnp.zeros((XW, w), f32))
        dp, ds, *sums, head = conv_back(PC, NCH - PC, dxc=dxc, dxdbl=dxdbl, follow=zero_head, sums=sums)
        follow = jnp.where(resumes_own, head, 0.0) + jnp.where(resumed_by_other, across(head), 0.0)
        d_inner_proj, inner_scale, conv_sums, xproj_grad, _ = conv_back(0, PC, dxc=dxc, dxdbl=dxdbl, follow=follow, sums=sums, kept=(dp, ds))

    scale = gate_scale + inner_scale

    def own_rows(v):
        return jnp.where(low_pair, v[:local], v[local:])

    def pair_rows(v):
        return jnp.where(low_pair, v[local:], v[:local])

    diagonal = send(pair_rows(scale), [((r, c), (1 - r, c ^ 1)) for r, c in places])
    scale = own_rows(scale) + swap(own_rows(scale)) + pair(pair_rows(scale)) + diagonal
    inv_own = own_rows(inv)
    pull = scale * inv_own * inv_own * inv_own / D
    small_parts = (conv_sums, scan_sums, alog_grad * rate, dtp_grad, xproj_grad)
    if quick:
        pulled, inner_grad, gain_sum, *small_grads = run_finish(
            d_inner_proj, d_gate_proj, normed, raw, wi, wg, jnp.broadcast_to(gain_own[None], (8, width)), pull, small_parts
        )
        gain_grad = jnp.sum(gain_sum, axis=0)
    else:
        inner_grad = collect([scatter_grp(dot_tn(normed[d], d_inner_proj), 1) for d in range(2)])
        d_normed = scatter_quad(*run_normed_backward(d_inner_proj, d_gate_proj, wi, wg))
        fixed = own_rows(raw[0]).astype(f32)
        gain_grad = jnp.sum(d_normed * fixed, axis=0)
        gain_grad = lax.psum_scatter(lax.psum(gain_grad, "col"), "grp", scatter_dimension=0, tiled=True)
        pulled = from_sequences((d_normed * gain_own - pull * fixed).astype(bf16))
        small_grad = send(jnp.concatenate(small_parts, axis=0), back(spread))
        small_grad = lax.psum_scatter(small_grad, ("row", "grp"), scatter_dimension=1, tiled=True)
        small_grads = jnp.split(small_grad, [sum(SMALL_ROWS[: k + 1]) for k in range(len(SMALL_ROWS) - 1)], axis=0)
    input_grad = (cotangent.astype(f32) + pulled.astype(f32)).astype(bf16)
    in_grads = jnp.stack([inner_grad, gate_grad], axis=1)
    return (
        output,
        input_grad,
        gain_grad,
        in_grads,
        small_grads[0],
        small_grads[1][0],
        small_grads[8].T,
        small_grads[7],
        small_grads[3][0],
        small_grads[6],
        small_grads[4][0],
        out_grad,
    )


def solution(mesh):
    placed = (
        P(("grp", "col"), "row"),
        P(("row", "grp")),
        P("row", None, ("col", "grp")),
        P(None, ("col", "row", "grp")),
        P(("col", "row", "grp")),
        P(("col", "row", "grp"), None),
        P(None, ("col", "row", "grp")),
        P(("col", "row", "grp")),
        P(None, ("col", "row", "grp")),
        P(("col", "row", "grp")),
        P("col", ("row", "grp")),
        P("grp"),
        P(("grp", "col"), "row"),
    )
    return jax.shard_map(
        per_device,
        mesh=mesh,
        in_specs=placed,
        out_specs=(
            P(("grp", "col"), "row"),
            P(("grp", "col"), "row"),
            P(("row", "grp")),
            P("row", None, ("col", "grp")),
            P(None, ("col", "row", "grp")),
            P(("col", "row", "grp")),
            P(("col", "row", "grp"), None),
            P(None, ("col", "row", "grp")),
            P(("col", "row", "grp")),
            P(None, ("col", "row", "grp")),
            P(("col", "row", "grp")),
            P("col", ("row", "grp")),
        ),
        check_vma=False,
    )
```

```python
import functools

import jax
import jax.numpy as jnp
from jax import lax
from jax.experimental import pallas as pl
from jax.experimental.pallas import tpu as pltpu
from jax.sharding import PartitionSpec as P

D = 2048
NSTATE = 16
KCONV = 4
RANK = 128
NPROMPT = 2
LP = 1024
LC = 128
NCONT = 2

eps = 1e-05
CH = 128
SUB = 16
PC = LP // CH
SEQ = LP + LC
NCH = SEQ // CH
XW = RANK + 2 * NSTATE
SPAN = SUB * NSTATE
LOG2E = 1.4426950408889634
VMEM_LIMIT = 58 * 1024 * 1024

f32 = jnp.float32
bf16 = jnp.bfloat16


def dot_nn(a, b):
    return lax.dot_general(a, b, (((1,), (0,)), ((), ())), preferred_element_type=f32)


def dot_nt(a, b):
    return lax.dot_general(a, b, (((1,), (1,)), ((), ())), preferred_element_type=f32)


def dot_tn(a, b):
    return lax.dot_general(a, b, (((0,), (0,)), ((), ())), preferred_element_type=f32)


def expand_tile():
    lane = lax.broadcasted_iota(jnp.int32, (NSTATE, SPAN), 1)
    row = lax.broadcasted_iota(jnp.int32, (NSTATE, SPAN), 0)
    return jnp.where(lane % NSTATE == row, 1.0, 0.0)


def own_token(rows):
    lane = lax.broadcasted_iota(jnp.int32, (rows, SPAN), 1)
    row = lax.broadcasted_iota(jnp.int32, (rows, SPAN), 0)
    return lane // NSTATE == row % SUB


def conv_forward(inner_ref, inv_ref, tail_ref, conv_ref, xproj_ref, xconv_ref, xdbl_ref, buf):
    i = pl.program_id(0)

    @pl.when(i == 0)
    def _():
        buf[0:8] = jnp.zeros_like(buf[0:8])

    @pl.when(i == PC)
    def _():
        buf[0:8] = tail_ref[...]

    @pl.when((i > 0) & (i < PC))
    def _():
        buf[0:8] = buf[CH : CH + 8]

    buf[8 : CH + 8] = inv_ref[...] * inner_ref[...]
    out = conv_ref[4:5]
    for k in range(KCONV):
        out = out + conv_ref[k : k + 1] * buf[5 + k : 5 + k + CH]
    xconv = (out * jax.nn.sigmoid(out)).astype(bf16)
    xconv_ref[...] = xconv
    xdbl_ref[...] = dot_nt(xproj_ref[...], xconv)


def softplus(v):
    return jnp.maximum(v, 0.0) + jnp.log1p(jnp.exp(-jnp.abs(v)))


def by_sub(v):
    return v.reshape(CH // SUB, SUB, v.shape[-1])


def scan_chunk(xdbl_ref, xconv, dtp_ref, vec_ref, rate_ref, state, dt_s, u_s, cb_s, h_s, y_s):
    step = softplus(dot_tn(xdbl_ref[:RANK].astype(bf16), dtp_ref[...]) + vec_ref[0:1])
    dt_s[...] = by_sub(step)
    u_s[...] = by_sub(step * xconv)
    reads = dot_tn(xdbl_ref[RANK + NSTATE :].astype(bf16), expand_tile().astype(bf16))
    cb_s[...] = jnp.where(own_token(CH), reads, 0.0).astype(bf16)
    rate = rate_ref[...] * LOG2E

    def block(j, carried):
        h, maps = carried
        for t in range(SUB):
            a = jnp.exp2(dt_s[j, t : t + 1, :] * rate)
            h = a * h + u_s[j, t : t + 1, :] * maps[:, t : t + 1]
            h_s[t * NSTATE : (t + 1) * NSTATE, :] = h.astype(bf16)
        rows = pl.ds(pl.multiple_of(j * SUB, SUB), SUB)
        y_s[rows, :] = dot_nn(cb_s[rows, :], h_s[...])
        return (h, pltpu.roll(maps, CH - SUB, 1))

    h, _ = lax.fori_loop(0, CH // SUB, block, (state, xdbl_ref[RANK : RANK + NSTATE]))
    return h, y_s[...] + vec_ref[1:2] * xconv


def scan_scratch(w):
    return [
        pltpu.VMEM((CH // SUB, SUB, w), f32),
        pltpu.VMEM((CH // SUB, SUB, w), f32),
        pltpu.VMEM((CH, SPAN), bf16),
        pltpu.VMEM((SPAN, w), bf16),
        pltpu.VMEM((CH, w), f32),
    ]


def scan_forward(kept, xdbl_ref, xconv_ref, dtp_ref, vec_ref, rate_ref, start_ref, *refs):
    yfull_ref, starts_ref, final_ref, *scratch = refs[kept:]

    @pl.when(pl.program_id(0) == 0)
    def _():
        final_ref[...] = start_ref[...]

    starts_ref[0] = final_ref[...]
    h, yfull = scan_chunk(xdbl_ref, xconv_ref[...].astype(f32), dtp_ref, vec_ref, rate_ref, final_ref[...], *scratch)
    final_ref[...] = h
    yfull_ref[...] = yfull.astype(bf16)


def chunk_backward(xdbl_ref, xconv_ref, dy_ref, dtp_ref, vec_ref, rate_ref, starts_ref, dxdbl_ref, dxc_ref, alog_ref, sums_ref, dtpg_ref, first_ref,
                   dt_s, u_s, x_s, dy_s, a_s, h_s, g_s, w_s, b_s, m1_s, m2_s, ds_s, dx_s, sig_s):
    low = xdbl_ref[:RANK].astype(bf16)
    step_inner = dot_tn(low, dtp_ref[...]) + vec_ref[0:1]
    step = softplus(step_inner)
    sig_s[...] = jax.nn.sigmoid(step_inner)
    xconv = xconv_ref[...].astype(f32)
    dy = dy_ref[...]
    dt_s[...] = by_sub(step)
    u_s[...] = by_sub(step * xconv)
    x_s[...] = by_sub(xconv)
    dy_s[...] = by_sub(dy)
    tile = expand_tile().astype(bf16)
    b_s[...] = jnp.where(own_token(CH), dot_tn(xdbl_ref[RANK : RANK + NSTATE].astype(bf16), tile), 0.0).astype(bf16)
    rate = rate_ref[...]
    rate2 = rate * LOG2E
    h_s[0:NSTATE] = starts_ref[0]

    def ahead(j, carried):
        h, maps = carried
        for t in range(SUB):
            a = jnp.exp2(dt_s[j, t : t + 1, :] * rate2)
            h = a * h + u_s[j, t : t + 1, :] * maps[:, t : t + 1]
            a_s[j, t * NSTATE : (t + 1) * NSTATE, :] = a
            at = pl.multiple_of(j * SPAN + (t + 1) * NSTATE, NSTATE)
            h_s[pl.ds(at, NSTATE), :] = h
        return (h, pltpu.roll(maps, CH - SUB, 1))

    lax.fori_loop(0, CH // SUB, ahead, (starts_ref[0], xdbl_ref[RANK : RANK + NSTATE]))
    ones = jnp.where(own_token(SUB), 1.0, 0.0).astype(bf16)
    mine_sub = own_token(SUB)

    def back(jj, carried):
        g, alog, maps = carried
        j = CH // SUB - 1 - jj
        maps = pltpu.roll(maps, SUB, 1)
        for t in reversed(range(SUB)):
            dt = dt_s[j, t : t + 1, :]
            gs = maps[:, t : t + 1] * dy_s[j, t : t + 1, :] + g
            g = a_s[j, t * NSTATE : (t + 1) * NSTATE, :] * gs
            prior = h_s[pl.ds(pl.multiple_of(j * SPAN + t * NSTATE, NSTATE), NSTATE), :]
            w = g * prior
            alog = alog + w * dt
            g_s[t * NSTATE : (t + 1) * NSTATE, :] = gs.astype(bf16)
            w_s[t * NSTATE : (t + 1) * NSTATE, :] = (w * rate).astype(bf16)
        rows = pl.ds(pl.multiple_of(j * SUB, SUB), SUB)
        gs_all = g_s[...]
        through = dot_nn(b_s[rows, :], gs_all)
        ds_s[rows, :] = dot_nn(ones, w_s[...]) + x_s[j] * through
        dx_s[rows, :] = dt_s[j] * through + vec_ref[1:2] * dy_s[j]
        hs = h_s[pl.ds(pl.multiple_of(j * SPAN + NSTATE, NSTATE), SPAN), :].astype(bf16)
        m1_s[rows, :] = jnp.where(mine_sub, dot_nt(u_s[j].astype(bf16), gs_all), 0.0).astype(bf16)
        m2_s[rows, :] = jnp.where(mine_sub, dot_nt(dy_s[j].astype(bf16), hs), 0.0).astype(bf16)
        return (g, alog, maps)

    g, alog, _ = lax.fori_loop(0, CH // SUB, back, (first_ref[...], alog_ref[...], xdbl_ref[RANK + NSTATE :]))
    first_ref[...] = g
    alog_ref[...] = alog
    d_inner = ds_s[...] * sig_s[...]
    d_low = d_inner.astype(bf16)
    sums_ref[0:1] = sums_ref[0:1] + jnp.sum(d_inner, axis=0, keepdims=True)
    sums_ref[1:2] = sums_ref[1:2] + jnp.sum(dy * xconv, axis=0, keepdims=True)
    dtpg_ref[...] = dtpg_ref[...] + dot_nn(low, d_low)
    dxdbl_ref[:RANK] = dot_nt(dtp_ref[...], d_low)
    dxdbl_ref[RANK : RANK + NSTATE] = dot_nt(tile, m1_s[...])
    dxdbl_ref[RANK + NSTATE :] = dot_nt(tile, m2_s[...])
    dxc_ref[...] = dx_s[...]


def scan_backward(kept, *refs):
    given, sums0, out = refs[:7], refs[7:11], refs[11 + kept :]
    dxdbl_ref, dxc_ref, alog_ref, sums_ref, dtpg_ref, first_ref = out[:6]

    @pl.when(pl.program_id(0) == 0)
    def _():
        first_ref[...] = sums0[0][...]
        alog_ref[...] = sums0[1][...]
        sums_ref[...] = sums0[2][...]
        dtpg_ref[...] = sums0[3][...]

    chunk_backward(*given, dxdbl_ref, dxc_ref, alog_ref, sums_ref, dtpg_ref, first_ref, *out[6:])


def backward_scratch(w):
    sub = pltpu.VMEM((CH // SUB, SUB, w), f32)
    return [
        sub,
        sub,
        sub,
        sub,
        pltpu.VMEM((CH // SUB, SPAN, w), f32),
        pltpu.VMEM(((CH + 1) * NSTATE, w), f32),
        pltpu.VMEM((SPAN, w), bf16),
        pltpu.VMEM((SPAN, w), bf16),
        pltpu.VMEM((CH, SPAN), bf16),
        pltpu.VMEM((CH, SPAN), bf16),
        pltpu.VMEM((CH, SPAN), bf16),
        pltpu.VMEM((CH, w), f32),
        pltpu.VMEM((CH, w), f32),
        pltpu.VMEM((CH, w), f32),
    ]


def conv_chunk(chunk, inner_ref, halo_ref, inv_ref, halo_inv_ref, tail_ref, conv_ref, xproj_ref, dxc_ref, dxdbl_ref, dproj_ref, dscale_ref, sums_ref, xprojg_ref, head_ref, buf, dbuf):
    projected = inner_ref[...]
    inv = inv_ref[...]
    before = halo_inv_ref[...] * halo_ref[...]
    before = jnp.where(chunk == 0, 0.0, jnp.where(chunk == PC, tail_ref[...], before))
    buf[0:8] = before
    buf[8 : CH + 8] = inv * projected
    out = conv_ref[4:5]
    for k in range(KCONV):
        out = out + conv_ref[k : k + 1] * buf[5 + k : 5 + k + CH]
    sig = jax.nn.sigmoid(out)
    xconv = (out * sig).astype(bf16)
    dxdbl = dxdbl_ref[...].astype(bf16)
    xprojg_ref[...] = xprojg_ref[...] + dot_nn(dxdbl, xconv)
    d_x = dxc_ref[...] + dot_tn(dxdbl, xproj_ref[...])
    d_conv = d_x * (sig * (1.0 + out * (1.0 - sig)))
    dbuf[CH : CH + 8] = head_ref[...]
    dbuf[0:CH] = d_conv
    d_inner = conv_ref[3:4] * d_conv
    for k in range(KCONV - 1):
        d_inner = d_inner + conv_ref[k : k + 1] * dbuf[3 - k : 3 - k + CH]
    for k in range(KCONV):
        sums_ref[k : k + 1] = sums_ref[k : k + 1] + jnp.sum(buf[5 + k : 5 + k + CH] * d_conv, axis=0, keepdims=True)
    sums_ref[4:5] = sums_ref[4:5] + jnp.sum(d_conv, axis=0, keepdims=True)
    dproj_ref[...] = (inv * d_inner).astype(bf16)
    dscale_ref[...] = jnp.sum(d_inner * projected, axis=1, keepdims=True)
    head_ref[...] = d_conv[0:8]


def conv_backward(kept, chunks, first, *refs):
    given, init, out = refs[:9], refs[9:12], refs[12 + kept :]
    dproj_ref, dscale_ref, sums_ref, xprojg_ref, head_ref, buf, dbuf = out
    i = pl.program_id(0)

    @pl.when(i == 0)
    def _():
        head_ref[...] = init[0][...]
        sums_ref[...] = init[1][...]
        xprojg_ref[...] = init[2][...]

    conv_chunk(first + chunks - 1 - i, *given, *out)


def call(body, chunks, args, in_specs, outs, out_specs, scratch, micros, aliases=None):
    return pl.pallas_call(
        body,
        grid=(chunks,),
        in_specs=in_specs,
        out_specs=out_specs,
        scratch_shapes=scratch,
        out_shape=outs,
        input_output_aliases=aliases or {},
        compiler_params=pltpu.CompilerParams(dimension_semantics=("arbitrary",), vmem_limit_bytes=VMEM_LIMIT),
        cost_estimate=pl.CostEstimate(flops=micros * 1000000000, bytes_accessed=1000000, transcendentals=0),
    )(*args)


def shaped(*shape, dtype=f32):
    return jax.ShapeDtypeStruct(shape, dtype)


def rows_of(width, place, tall=CH):
    return pl.BlockSpec((tall, width), lambda i: (place(i), 0))


def lanes_of(height, place):
    return pl.BlockSpec((height, CH), lambda i: (0, place(i)))


def whole(*shape):
    return pl.BlockSpec(shape, lambda i: (0,) * len(shape))


ANY = pl.BlockSpec(memory_space=pl.ANY)


def run_conv_forward(inner, inv, tail, conv, xproj):
    w = inner.shape[1]
    at = lambda i: i
    return call(
        conv_forward,
        NCH,
        (inner, inv, tail, conv, xproj),
        [rows_of(w, at), rows_of(1, at), whole(8, w), whole(8, w), whole(XW, w)],
        (shaped(SEQ, w, dtype=bf16), shaped(XW, SEQ)),
        (rows_of(w, at), lanes_of(XW, at)),
        [pltpu.VMEM((CH + 8, w), f32)],
        12,
    )


def chunk_of(height, place):
    return pl.BlockSpec((None, height, CH), lambda i: (place(i), 0, 0))


def run_scan_forward(first, chunks, xdbl, xconv, dtp, vec, rate, start, kept=()):
    w = xconv.shape[1]
    at = lambda i: first + i
    return call(
        functools.partial(scan_forward, len(kept)),
        chunks,
        (xdbl, xconv, dtp, vec, rate, start, *kept),
        [chunk_of(XW, at), rows_of(w, at), whole(RANK, w), whole(8, w), whole(NSTATE, w), whole(NSTATE, w)] + [ANY] * len(kept),
        (shaped(SEQ, w, dtype=bf16), shaped(NCH, NSTATE, w), shaped(NSTATE, w)),
        (rows_of(w, at), pl.BlockSpec((1, NSTATE, w), lambda i: (first + i, 0, 0)), whole(NSTATE, w)),
        scan_scratch(w),
        5 * chunks,
        {6 + k: k for k in range(len(kept))},
    )


def run_scan_backward(first, chunks, xdbl, xconv, dy, dtp, vec, rate, starts, carry, sums, kept=()):
    w = xconv.shape[1]
    at = lambda i: first + chunks - 1 - i
    local = lambda i: chunks - 1 - i
    return call(
        functools.partial(scan_backward, len(kept)),
        chunks,
        (xdbl, xconv, dy, dtp, vec, rate, starts, carry, *sums, *kept),
        [
            chunk_of(XW, at),
            rows_of(w, at),
            rows_of(w, at),
            whole(RANK, w),
            whole(8, w),
            whole(NSTATE, w),
            pl.BlockSpec((1, NSTATE, w), lambda i: (at(i), 0, 0)),
            whole(NSTATE, w),
            whole(NSTATE, w),
            whole(8, w),
            whole(RANK, w),
        ]
        + [ANY] * len(kept),
        (shaped(XW, chunks * CH), shaped(SEQ, w), shaped(NSTATE, w), shaped(8, w), shaped(RANK, w), shaped(NSTATE, w)),
        (lanes_of(XW, local), rows_of(w, at), whole(NSTATE, w), whole(8, w), whole(RANK, w), whole(NSTATE, w)),
        backward_scratch(w),
        11 * chunks,
        {11 + k: 1 + k for k in range(len(kept))},
    )


def run_conv_backward(first, chunks, inner, inv, tail, conv, xproj, dxc, dxdbl, follow, sums, kept=()):
    w = inner.shape[1]
    at = lambda i: first + chunks - 1 - i
    before = lambda i: (jnp.maximum(at(i) * (CH // 8) - 1, 0), 0)
    return call(
        functools.partial(conv_backward, len(kept), chunks, first),
        chunks,
        (inner, inner, inv, inv, tail, conv, xproj, dxc, dxdbl, follow, *sums, *kept),
        [
            rows_of(w, at),
            pl.BlockSpec((8, w), before),
            rows_of(1, at),
            pl.BlockSpec((8, 1), before),
            whole(8, w),
            whole(8, w),
            whole(XW, w),
            rows_of(w, at),
            chunk_of(XW, at),
            whole(8, w),
            whole(8, w),
            whole(XW, w),
        ]
        + [ANY] * len(kept),
        (shaped(SEQ, w, dtype=bf16), shaped(SEQ, 1), shaped(8, w), shaped(XW, w), shaped(8, w)),
        (rows_of(w, at), rows_of(1, at), whole(8, w), whole(XW, w), whole(8, w)),
        [pltpu.VMEM((CH + 8, w), f32), pltpu.VMEM((CH + 8, w), f32)],
        2 * chunks,
        {12 + k: k for k in range(len(kept))},
    )


MESH = pl.DeviceIdType.MESH
BIG = 384
BIG_STEPS = SEQ // BIG
SLOTS = 4


def remote(src, dst, send, recv, device):
    return pltpu.make_async_remote_copy(src_ref=src, dst_ref=dst, send_sem=send, recv_sem=recv, device_id=device, device_id_type=MESH)


def xor_bit(a, b):
    return a + b - 2 * a * b


def token_pieces(c, local):
    cut = local - LC
    low = cut - LC
    if c == 0:
        return [(0, local, 0, 0)]
    if c == 1:
        return [(0, cut, 0, local), (cut, local, 1, 0)]
    if c == 2:
        return [(0, local, 1, LC)]
    return [(0, low, 1, LC + local), (low, cut, 0, LP), (cut, local, 1, LP)]


class Gather:
    def __init__(self, weights, tokens, raw, w_send, w_recv, t_send, t_recv, here):
        g, r, c = lax.axis_index("grp"), lax.axis_index("row"), lax.axis_index("col")
        x, core = g // 2, g % 2
        self.g, self.r, self.c = g, r, c
        half = xor_bit(r, c % 2)
        self.firsts = ((g, r, 2 * half + c // 2), (g, 1 - r, 2 * (1 - half) + c // 2))
        self.alone = 2 * half + c // 2 == c
        self.ranks = (g, (1 - x) * 2 + core, x * 2 + 1 - core)
        self.x_dev, self.core_dev = (self.ranks[1], r, c), (self.ranks[2], r, c)
        self.y_dev, self.z_dev = (g, 1 - r, c), (g, r, c + 1 - 2 * (c % 2))
        self.weights, self.tokens, self.raw = weights, tokens, raw
        self.w_send, self.w_recv, self.t_send, self.t_recv, self.here = w_send, w_recv, t_send, t_recv, here

    def greet(self):
        barrier = pltpu.get_barrier_semaphore()
        for dr in range(2):
            for dc in range(4):
                if dr or dc:
                    device = (self.g, (self.r + dr) % 2, (self.c + dc) % 4)
                    pl.semaphore_signal(barrier, inc=1, device_id=device, device_id_type=MESH)
        for device in (self.x_dev, self.core_dev):
            pl.semaphore_signal(barrier, inc=1, device_id=device, device_id_type=MESH)
        pl.semaphore_wait(barrier, 9)

    def slot(self, n, k, d):
        if self.weights[n][2]:
            return (self.r if d == 0 else 1 - self.r) * 4 + self.ranks[k]
        return 2 * self.ranks[k] + d

    def first_hop(self, n, d):
        src, dst, by_row = self.weights[n]
        at = self.slot(n, 0, 0) if by_row else self.slot(n, 0, d)
        return remote(src, dst.at[at], self.w_send.at[n, d], self.w_recv.at[n, d], self.firsts[d])

    def at_home(self, n):
        src, dst, _ = self.weights[n]
        return pltpu.make_async_copy(src, dst.at[self.slot(n, 0, 0)], self.here.at[n])

    def hop(self, n, d, k, came):
        dst = self.weights[n][1]
        at = self.slot(n, k, d)
        i = (0, 2, 4, 6)[came] + d
        device = self.x_dev if came == 1 else self.core_dev
        return remote(dst.at[at], dst.at[at], self.w_send.at[n, i], self.w_recv.at[n, i], device)

    def begin(self, n):
        @pl.when(self.alone)
        def _():
            self.at_home(n).start()

        @pl.when(jnp.logical_not(self.alone))
        def _():
            self.first_hop(n, 0).start()

        self.first_hop(n, 1).start()

    def forward(self, n):
        for d in range(2):
            if d == 0:

                @pl.when(self.alone)
                def _():
                    self.at_home(n).wait()

                @pl.when(jnp.logical_not(self.alone))
                def _():
                    self.first_hop(n, 0).wait_recv()
            else:
                self.first_hop(n, 1).wait_recv()
            self.hop(n, d, 0, 1).start()
            self.hop(n, d, 0, 2).start()

    def forward_again(self, n):
        for d in range(2):
            self.hop(n, d, 0, 1).wait_recv()
            self.hop(n, d, 1, 3).start()

    def end(self, n):
        for d in range(2):
            self.hop(n, d, 0, 2).wait_recv()
            self.hop(n, d, 1, 3).wait_recv()
            self.hop(n, d, 0, 1).wait_send()
            self.hop(n, d, 0, 2).wait_send()
            self.hop(n, d, 1, 3).wait_send()

        @pl.when(jnp.logical_not(self.alone))
        def _():
            self.first_hop(n, 0).wait_send()

        self.first_hop(n, 1).wait_send()

    def ranges(self, k):
        local = self.tokens.shape[0]
        held = {0: (0, local), 1: (local, LP), 2: (LC, LC + local), 3: (LC + local, SEQ)}
        return held[k], held[k ^ 1], (LP, SEQ) if k < 2 else (0, LC)

    def part(self, d, rows):
        return self.raw.at[d, pl.ds(rows[0], rows[1] - rows[0])]

    def on_col(self, act):
        for k in range(4):

            @pl.when(self.c == k)
            def _(k=k):
                act(k)

    def sources(self, k, lo, hi):
        for a, b, s, at in token_pieces(k, self.tokens.shape[0]):
            first, end = max(lo, at), min(hi, at + b - a)
            if s == k // 2 and first < end:
                yield a + first - at, first, end

    def begin_half(self, h):
        def act(k):
            lo, hi = split(self.ranges(k)[0])[h]
            for src, first, end in self.sources(k, lo, hi):
                rows = self.tokens.at[pl.ds(src, end - first)]
                pltpu.make_async_copy(rows, self.part(0, (first, end)), self.here.at[2 + h]).start()
                remote(rows, self.part(1, (first, end)), self.t_send.at[h], self.t_recv.at[h], self.y_dev).start()
                remote(rows, self.part(0, (first, end)), self.t_send.at[2 + h], self.t_recv.at[2 + h], self.z_dev).start()

        self.on_col(act)

    def foreign_copies(self, k):
        copies = []
        for a, b, s, at in token_pieces(k, self.tokens.shape[0]):
            if s != k // 2:
                for dr in range(2):
                    for dc in range(2):
                        device = (self.g, self.r if dr == 0 else 1 - self.r, 2 * s + dc)
                        sems = self.t_send.at[6 + 2 * dr + dc], self.t_recv.at[6 + dr]
                        copies.append(remote(self.tokens.at[pl.ds(a, b - a)], self.part(dr, (at, at + b - a)), *sems, device))
        return copies

    def begin_foreign(self):
        def act(k):
            for copy in self.foreign_copies(k):
                copy.start()

        self.on_col(act)

    def relays(self, k):
        own, paired, _ = self.ranges(k)
        early, late = split(paired)[0], split(own)[1]
        return (
            remote(self.part(0, early), self.part(1, early), self.t_send.at[4], self.t_recv.at[4], self.y_dev),
            remote(self.part(1, late), self.part(1, late), self.t_send.at[5], self.t_recv.at[5], self.z_dev),
        )

    def settle(self, d, rows, sem):
        pltpu.make_async_copy(self.part(d, rows), self.part(d, rows), sem).wait()

    def relay(self):
        def act(k):
            own, paired, _ = self.ranges(k)
            by_y, by_z = self.relays(k)
            self.settle(0, split(paired)[0], self.t_recv.at[2])
            by_y.start()
            self.settle(1, split(own)[1], self.t_recv.at[1])
            by_z.start()

        self.on_col(act)

    def end_tokens(self):
        def act(k):
            own, paired, foreign = self.ranges(k)
            own, paired = split(own), split(paired)
            by_y, by_z = self.relays(k)
            self.settle(1, own[0], self.t_recv.at[0])
            self.settle(0, paired[1], self.t_recv.at[3])
            self.settle(1, paired[0], self.t_recv.at[4])
            self.settle(1, paired[1], self.t_recv.at[5])
            self.settle(0, foreign, self.t_recv.at[6])
            self.settle(1, foreign, self.t_recv.at[7])
            for h in range(2):
                self.settle(0, own[h], self.here.at[2 + h])
                self.settle(0, own[h], self.t_send.at[h])
                self.settle(0, own[h], self.t_send.at[2 + h])
            by_y.wait_send()
            by_z.wait_send()
            for copy in self.foreign_copies(k):
                copy.wait_send()

        self.on_col(act)


def split(rows):
    lo, hi = rows
    mid = lo + (hi - lo) // 2
    return (lo, mid), (mid, hi)


def gather_semaphores():
    return [pltpu.SemaphoreType.DMA(shape) for shape in ((2, 8), (2, 8), (10,), (8,), (4,))]


def gather_start(tokens, in_i, small, raw, wi, small_all, *sems):
    gather = Gather([(small, small_all, True), (in_i, wi, False)], tokens, raw, *sems)
    gather.greet()
    gather.begin(0)
    gather.begin(1)
    gather.begin_half(0)
    gather.begin_half(1)
    gather.begin_foreign()
    for n in range(2):
        gather.forward(n)
    gather.relay()
    for n in range(2):
        gather.forward_again(n)
    gather.end_tokens()
    for n in range(2):
        gather.end(n)


def run_gather_start(tokens, in_i, small):
    width = tokens.shape[1]
    return pl.pallas_call(
        gather_start,
        in_specs=[ANY] * 3,
        out_specs=[ANY] * 3,
        out_shape=(
            shaped(2, SEQ, width, dtype=bf16),
            shaped(8, *in_i.shape, dtype=bf16),
            shaped(8, *small.shape, dtype=bf16),
        ),
        scratch_shapes=gather_semaphores(),
        compiler_params=pltpu.CompilerParams(collective_id=0, has_side_effects=True, vmem_limit_bytes=VMEM_LIMIT),
    )(tokens, in_i, small)


LAG = 4
FIRST = BIG_STEPS
SECOND = FIRST + NCH
LAST = SECOND + NCH - 1
BEGIN = (0, SECOND)
FORWARD = (FIRST + 8, SECOND + 5)
FORWARD_AGAIN = (SECOND + 3, LAST)
HALVES = (FIRST + 6, SECOND + 1)
FOREIGN = SECOND + 2
RELAY = SECOND + 6


def pack_sum(ref, k, v):
    high = v[RANK:].astype(bf16)
    ref[k, :RANK] = v[:RANK].astype(bf16)
    ref[k, RANK:XW] = high
    ref[k, XW:] = (v[RANK:] - high.astype(f32)).astype(bf16)


def unpack_sum(ref, k):
    return jnp.concatenate([ref[k, :RANK].astype(f32), ref[k, RANK:XW].astype(f32) + ref[k, XW:].astype(f32)], axis=0)


def forward(raw_ref, gain_ref, wi_ref, mix_ref, conv_ref, xproj_ref, dtp_ref, vec_ref, rate_ref, in_g, out_w, cot_in,
            normed_ref, inv_ref, inner_ref, xconv_ref, yfull_ref, starts_ref, xdbl_ref, joined_ref, wg, wo, cot,
            inner_s, inv_s, buf, xc_s, part, ys, yr, zs, zr, tail_s, tail_r, state, last, last_r,
            dt_s, u_s, cb_s, h_s, y_s, y_send, y_recv, z_send, z_recv, e_send, e_recv, *sems):
    i = pl.program_id(0)
    gather = Gather([(in_g, wg, False), (out_w, wo, False)], cot_in, cot, *sems)
    g, r, c = gather.g, gather.r, gather.c
    y_dev, z_dev = gather.y_dev, gather.z_dev
    far_dev = (g, 1 - r, (c + 2) % 4)
    to_tail = remote(tail_s, tail_r, e_send.at[0], e_recv.at[0], far_dev)
    to_last = remote(last, last_r, e_send.at[1], e_recv.at[1], far_dev)

    def to_y(k):
        return remote(ys.at[k], yr.at[k], y_send.at[k], y_recv.at[k], y_dev)

    def to_z(k):
        return remote(zs.at[k], zr.at[k], z_send.at[k], z_recv.at[k], z_dev)

    @pl.when(i == 0)
    def _():
        gather.greet()

    @pl.when(i < FIRST)
    def _():
        rows = pl.ds(pl.multiple_of(i * BIG, BIG), BIG)
        project_first(raw_ref, gain_ref, wi_ref, normed_ref, inv_ref, inner_ref)
        inner_s[rows, :] = inner_ref[...]
        inv_s[rows, :] = inv_ref[...]

    @pl.when(i == FIRST)
    def _():
        tail_s[...] = inv_s[LP - 8 : LP] * inner_s[LP - 8 : LP]
        to_tail.start()
        buf[0:8] = jnp.zeros_like(buf[0:8])
        state[...] = jnp.zeros_like(state)

    mix = mix_ref[...]

    @pl.when(i == FIRST + PC)
    def _():
        to_tail.wait()
        joined = mix * tail_s[...] + (1.0 - mix) * tail_r[...]
        buf[0:8] = joined
        joined_ref[...] = joined

    @pl.when((i > FIRST) & (i < FIRST + PC))
    def _():
        buf[0:8] = buf[CH : CH + 8]

    @pl.when((i >= FIRST) & (i < SECOND))
    def _():
        k = i - FIRST
        rows = pl.ds(pl.multiple_of(k * CH, CH), CH)
        buf[8 : CH + 8] = inv_s[rows, :] * inner_s[rows, :]
        out = conv_ref[4:5]
        for tap in range(KCONV):
            out = out + conv_ref[tap : tap + 1] * buf[5 + tap : 5 + tap + CH]
        xconv = (out * jax.nn.sigmoid(out)).astype(bf16)
        xconv_ref[...] = xconv
        xc_s[k] = xconv
        part[k] = dot_nt(xproj_ref[...], xconv)
        pack_sum(ys, k, part[k])
        to_y(k).start()

    @pl.when((i >= FIRST + LAG) & (i < SECOND + LAG))
    def _():
        k = i - FIRST - LAG
        to_y(k).wait_recv()
        part[k] = part[k] + unpack_sum(yr, k)
        pack_sum(zs, k, part[k])
        to_z(k).start()

    @pl.when((i >= FIRST + 2 * LAG) & (i < SECOND + 2 * LAG))
    def _():
        k = i - FIRST - 2 * LAG
        to_z(k).wait_recv()
        xdbl_ref[k] = part[k] + unpack_sum(zr, k)

    for n in range(2):

        @pl.when(i == BEGIN[n])
        def _(n=n):
            gather.begin(n)

        @pl.when(i == FORWARD[n])
        def _(n=n):
            gather.forward(n)

        @pl.when(i == FORWARD_AGAIN[n])
        def _(n=n):
            gather.forward_again(n)

    for h in range(2):

        @pl.when(i == HALVES[h])
        def _(h=h):
            gather.begin_half(h)

    @pl.when(i == FOREIGN)
    def _():
        gather.begin_foreign()

    @pl.when(i == RELAY)
    def _():
        gather.relay()

    @pl.when(i == LAST)
    def _():
        to_last.wait()
        state[...] = mix_ref[0:1] * last[...] + (1.0 - mix_ref[0:1]) * last_r[...]

    @pl.when(i >= SECOND)
    def _():
        k = i - SECOND
        starts_ref[0] = state[...]
        h, yfull = scan_chunk(xdbl_ref.at[k], xc_s[k].astype(f32), dtp_ref, vec_ref, rate_ref, state[...], dt_s, u_s, cb_s, h_s, y_s)
        state[...] = h
        yfull_ref[...] = yfull.astype(bf16)

    @pl.when(i == LAST - 1)
    def _():
        last[...] = state[...]
        to_last.start()

    @pl.when(i == LAST)
    def _():
        gather.end_tokens()
        gather.end(0)
        gather.end(1)

        def sent(k, _):
            to_y(k).wait_send()
            to_z(k).wait_send()
            return 0

        lax.fori_loop(0, NCH, sent, 0)


def run_forward(raw, gain, wi, mix, conv, xproj, dtp, vec, rate, in_g, out_w, cot):
    w = SLOTS * wi.shape[2]
    width = raw.shape[2]
    zero = lambda i: jnp.minimum(i, FIRST - 1)
    first = lambda i: jnp.clip(i - FIRST, 0, NCH - 1)
    second = lambda i: jnp.maximum(i - SECOND, 0)
    dma = pltpu.SemaphoreType.DMA
    sums = pltpu.VMEM((NCH, XW + 2 * NSTATE, CH), bf16)
    return pl.pallas_call(
        forward,
        grid=(LAST + 1,),
        in_specs=[
            split_rows(width, zero, BIG),
            whole(2, width),
            whole(*wi.shape),
            whole(8, w),
            whole(8, w),
            whole(XW, w),
            whole(RANK, w),
            whole(8, w),
            whole(NSTATE, w),
            ANY,
            ANY,
            ANY,
        ],
        out_specs=(
            split_rows(width, zero, BIG),
            rows_of(1, zero, BIG),
            rows_of(w, zero, BIG),
            rows_of(w, first),
            rows_of(w, second),
            pl.BlockSpec((1, NSTATE, w), lambda i: (second(i), 0, 0)),
            whole(NCH, XW, CH),
            whole(8, w),
            ANY,
            ANY,
            ANY,
        ),
        out_shape=(
            shaped(2, SEQ, width, dtype=bf16),
            shaped(SEQ, 1),
            shaped(SEQ, w),
            shaped(SEQ, w, dtype=bf16),
            shaped(SEQ, w, dtype=bf16),
            shaped(NCH, NSTATE, w),
            shaped(NCH, XW, CH),
            shaped(8, w),
            shaped(8, *in_g.shape, dtype=bf16),
            shaped(8, *out_w.shape, dtype=bf16),
            shaped(2, SEQ, cot.shape[1], dtype=bf16),
        ),
        scratch_shapes=[
            pltpu.VMEM((SEQ, w), f32),
            pltpu.VMEM((SEQ, 1), f32),
            pltpu.VMEM((CH + 8, w), f32),
            pltpu.VMEM((NCH, CH, w), bf16),
            pltpu.VMEM((NCH, XW, CH), f32),
            sums,
            sums,
            sums,
            sums,
            pltpu.VMEM((8, w), f32),
            pltpu.VMEM((8, w), f32),
            pltpu.VMEM((NSTATE, w), f32),
            pltpu.VMEM((NSTATE, w), f32),
            pltpu.VMEM((NSTATE, w), f32),
            *scan_scratch(w),
            dma((NCH,)),
            dma((NCH,)),
            dma((NCH,)),
            dma((NCH,)),
            dma((2,)),
            dma((2,)),
            *gather_semaphores(),
        ],
        compiler_params=pltpu.CompilerParams(
            dimension_semantics=("arbitrary",), collective_id=2, has_side_effects=True, vmem_limit_bytes=VMEM_LIMIT
        ),
        cost_estimate=pl.CostEstimate(flops=60 * 1000000000, bytes_accessed=1000000, transcendentals=0),
    )(raw, gain, wi, mix, conv, xproj, dtp, vec, rate, in_g, out_w, cot)


def project_first(raw_ref, gain_ref, w_ref, normed_ref, inv_ref, out_ref):
    low = raw_ref[0].astype(f32)
    high = raw_ref[1].astype(f32)
    squares = jnp.sum(low * low + high * high, axis=1, keepdims=True)
    inv_ref[...] = lax.rsqrt(squares / D + eps)
    low = (low * gain_ref[0:1]).astype(bf16)
    high = (high * gain_ref[1:2]).astype(bf16)
    normed_ref[0] = low
    normed_ref[1] = high
    n = w_ref.shape[2]
    for k in range(SLOTS):
        out_ref[:, k * n : (k + 1) * n] = dot_nn(low, w_ref[2 * k]) + dot_nn(high, w_ref[2 * k + 1])


def split_rows(width, at, tall=CH):
    return pl.BlockSpec((2, tall, width), lambda i: (0, at(i), 0))


def run_project_first(raw, gain, w):
    width = raw.shape[2]
    at = lambda i: i
    n = SLOTS * w.shape[2]
    return call(
        project_first,
        BIG_STEPS,
        (raw, gain, w),
        [split_rows(width, at, BIG), whole(2, width), whole(*w.shape)],
        (shaped(2, SEQ, width, dtype=bf16), shaped(SEQ, 1), shaped(SEQ, n)),
        (split_rows(width, at, BIG), rows_of(1, at, BIG), rows_of(n, at, BIG)),
        [],
        9,
    )


def gate_backward(normed_ref, wg_ref, cot_ref, wo_ref, yfull_ref, inv_ref, gated_ref, dy_ref, dproj_ref, dscale_ref, own_ref, oth_ref, gate_s):
    n = wo_ref.shape[2]
    for k in range(SLOTS):
        gate_s[:, k * n : (k + 1) * n] = dot_nn(normed_ref[0], wg_ref[2 * k]) + dot_nn(normed_ref[1], wg_ref[2 * k + 1])
    d_gated = jnp.zeros(dy_ref.shape, f32)
    for k in range(SLOTS):
        for d in range(2):
            d_gated = d_gated + dot_nt(cot_ref[d, :, k * n : (k + 1) * n], wo_ref[2 * k + d])
    gate_in = gate_s[...]
    inv = inv_ref[...]
    yfull = yfull_ref[...].astype(f32)
    gate = inv * gate_in
    sig = jax.nn.sigmoid(gate)
    passed = gate * sig
    gated = (yfull * passed).astype(bf16)
    gated_ref[...] = gated
    for k in range(SLOTS):
        own_ref[:, k * n : (k + 1) * n] = dot_nn(gated, wo_ref[2 * k])
        oth_ref[:, k * n : (k + 1) * n] = dot_nn(gated, wo_ref[2 * k + 1]).astype(bf16)
    dy_ref[...] = d_gated * passed
    d_gate = d_gated * yfull * (sig * (1.0 + gate * (1.0 - sig)))
    dproj_ref[...] = (inv * d_gate).astype(bf16)
    dscale_ref[...] = jnp.sum(d_gate * gate_in, axis=1, keepdims=True)


def run_gate_backward(normed, wg, cot, wo, yfull, inv):
    width = cot.shape[2]
    w = yfull.shape[1]
    at = lambda i: i
    return call(
        gate_backward,
        BIG_STEPS,
        (normed, wg, cot, wo, yfull, inv),
        [split_rows(width, at, BIG), whole(*wg.shape), split_rows(width, at, BIG), whole(*wo.shape), rows_of(w, at, BIG), rows_of(1, at, BIG)],
        (shaped(SEQ, w, dtype=bf16), shaped(SEQ, w), shaped(SEQ, w, dtype=bf16), shaped(SEQ, 1), shaped(SEQ, width), shaped(SEQ, width, dtype=bf16)),
        (rows_of(w, at, BIG), rows_of(w, at, BIG), rows_of(w, at, BIG), rows_of(1, at, BIG), rows_of(width, at, BIG), rows_of(width, at, BIG)),
        [pltpu.VMEM((BIG, w), f32)],
        22,
    )


def normed_backward(inner_ref, gate_ref, wi_ref, wg_ref, own_ref, oth_ref):
    n = wi_ref.shape[2]
    for d, out_ref in ((1, oth_ref), (0, own_ref)):
        total = jnp.zeros(out_ref.shape, f32)
        for k in range(SLOTS):
            total = total + dot_nt(inner_ref[:, k * n : (k + 1) * n], wi_ref[2 * k + d])
            total = total + dot_nt(gate_ref[:, k * n : (k + 1) * n], wg_ref[2 * k + d])
        out_ref[...] = total.astype(out_ref.dtype)


def run_normed_backward(d_inner, d_gate, wi, wg):
    w = d_inner.shape[1]
    width = wi.shape[1]
    at = lambda i: i
    return call(
        normed_backward,
        BIG_STEPS,
        (d_inner, d_gate, wi, wg),
        [rows_of(w, at, BIG), rows_of(w, at, BIG), whole(*wi.shape), whole(*wg.shape)],
        (shaped(SEQ, width), shaped(SEQ, width, dtype=bf16)),
        (rows_of(width, at, BIG), rows_of(width, at, BIG)),
        [],
        12,
    )


def finish(inner_hbm, gate_hbm, normed_hbm, raw_hbm, wi_hbm, wg_hbm, gain_in_ref, pull_ref, conv_hbm, scan_hbm, alog_hbm, dtp_hbm, xproj_hbm,
           dn_ref, grad_ref, gain_ref, small_refs,
           inner, gate, normed, raw, wi, wg, cs, cr, pairs, xs, xr, fs, fr, fq, ys, yr, zs, zr, own, fin, gs, gr, sv, kr, ks, kx, kf, kg,
           loc, c_send, c_recv, x_send, x_recv, f_send, f_recv, r_send, r_recv, y_send, y_recv, z_send, z_recv, b_send, b_recv, g_send, g_recv, s_send, s_recv, s_load):
    g, r, c = lax.axis_index("grp"), lax.axis_index("row"), lax.axis_index("col")
    x, core, s, p = g // 2, g % 2, c // 2, c % 2
    tall, width = raw.shape
    part = tall // 2
    n = wi_hbm.shape[2]
    q = 2 * p + xor_bit(r, s)
    y_dev, z_dev = (g, 1 - r, c), (g, r, 2 * s + 1 - p)
    x_dev, core_dev = ((1 - x) * 2 + core, r, c), (2 * x + 1 - core, r, c)
    alone = q == c
    passed = 2 * p + xor_bit(1 - r, s)
    stays_here = passed == c

    loads = [
        pltpu.make_async_copy(normed_hbm, normed, loc.at[0]),
        pltpu.make_async_copy(inner_hbm, inner, loc.at[1]),
        pltpu.make_async_copy(gate_hbm, gate, loc.at[2]),
        pltpu.make_async_copy(raw_hbm.at[0, pl.ds(pl.multiple_of(p * tall, 64), tall)], raw, loc.at[5]),
    ]
    for copy in loads[:3]:
        copy.start()
    for k in range(SLOTS):
        for d in range(2):
            cols = pl.ds(k * n, n)
            pltpu.make_async_copy(wi_hbm.at[2 * k + d], wi.at[d, :, cols], loc.at[3]).start()
            pltpu.make_async_copy(wg_hbm.at[2 * k + d], wg.at[d, :, cols], loc.at[4]).start()
    loads[3].start()

    barrier = pltpu.get_barrier_semaphore()
    for dg in range(4):
        for dc in range(4):
            if dg or dc:
                pl.semaphore_signal(barrier, inc=1, device_id=((g + dg) % 4, r, (c + dc) % 4), device_id_type=MESH)
    for dc in range(4):
        pl.semaphore_signal(barrier, inc=1, device_id=(g, 1 - r, (c + dc) % 4), device_id_type=MESH)
    pl.semaphore_wait(barrier, 19)

    def small_loads():
        at = 0
        for ref in (conv_hbm, scan_hbm, alog_hbm, dtp_hbm, xproj_hbm):
            yield pltpu.make_async_copy(ref, sv.at[pl.ds(at, ref.shape[0])], s_load.at[0])
            at += ref.shape[0]

    def channels(d, at_x, at_core):
        to_r = r if d == 0 else 1 - r
        return pl.ds(pl.multiple_of((to_r * 4 + 2 * at_x + at_core) * 128, 128), 128)

    def small_core(j, d):
        src = sv.at[:, channels(d, 1 - x if j == 0 else x, 1 - core)]
        return remote(src, kr.at[j, d], s_send.at[2 * j + d], s_recv.at[2 * j + d], core_dev)

    def small_x(d):
        return remote(ks.at[d], kx.at[d], s_send.at[4 + d], s_recv.at[4 + d], x_dev)

    def small_owner(d):
        return remote(kf.at[d], kg.at[d], s_send.at[6 + d], s_recv.at[6 + d], (g, r if d == 0 else 1 - r, q))

    for copy in small_loads():
        copy.start()

    def weight_grad(at_x, d):
        cols = pl.ds(pl.multiple_of(at_x * 2 * n, 128), 2 * n)

        def tile(t, _):
            rows = pl.ds(pl.multiple_of(t * n, 128), n)
            pairs[d, rows, :] = dot_tn(normed[d, :, rows], inner[:, cols])
            return 0

        lax.fori_loop(0, width // n, tile, 0)

    def of_core(at_core):
        return pl.ds(pl.multiple_of(at_core * n, 128), n)

    def to_core(i, d):
        return remote(cs.at[i, d], cr.at[i, d], c_send.at[2 * i + d], c_recv.at[2 * i + d], core_dev)

    def to_x(d):
        return remote(xs.at[d], xr.at[d], x_send.at[d], x_recv.at[d], x_dev)

    def to_owner():
        return remote(fs.at[0], fr.at[0], f_send.at[0], f_recv.at[0], (g, r, q))

    def to_passer():
        return remote(fs.at[1], fq, r_send.at[0], r_recv.at[0], y_dev)

    def pass_owner():
        return remote(fq, fr.at[1], f_send.at[1], f_recv.at[1], (g, r, passed))

    def grad_to_core(i):
        for d in range(2):
            weight_grad(1 - x if i == 0 else x, d)
            cs[i, d] = pairs[d, :, of_core(1 - core)].astype(bf16)
            to_core(i, d).start()

    def start_of(mine, h):
        return pl.multiple_of((p if mine else 1 - p) * tall + h * part, 32)

    def normed_part(mine, h, d, store):
        rows = pl.ds(start_of(mine, h), part)

        def tile(t, _):
            cols = pl.ds(pl.multiple_of(t * n, 128), n)
            total = dot_nt(inner[rows, :], wi[d, cols, :]) + dot_nt(gate[rows, :], wg[d, cols, :])
            store(cols, total)
            return 0

        lax.fori_loop(0, width // n, tile, 0)

    def to_y(i):
        return remote(ys.at[i], yr.at[i], y_send.at[i], y_recv.at[i], y_dev)

    def to_z(i):
        return remote(zs.at[i], zr.at[i], z_send.at[i], z_recv.at[i], z_dev)

    def into(ref, i, added=None):
        def store(cols, v):
            if added is not None:
                v = v + added[0, :, cols].astype(f32)
            ref[i, :, cols] = v.astype(bf16)

        return store

    pltpu.make_async_copy(sv, sv, s_load.at[0]).wait()
    for j in range(2):
        for d in range(2):
            small_core(j, d).start()
    loads[0].wait()
    loads[1].wait()
    grad_to_core(0)
    loads[2].wait()
    pltpu.make_async_copy(wi, wi, loc.at[3]).wait()
    pltpu.make_async_copy(wg, wg, loc.at[4]).wait()
    for d in range(2):
        to_core(0, d).wait_recv()
        xs[d] = (pairs[d, :, of_core(core)] + cr[0, d].astype(f32)).astype(bf16)
        to_x(d).start()

    for d in range(2):
        small_core(0, d).wait_recv()
        ks[d] = sv[:, channels(d, 1 - x, core)] + kr[0, d]
        small_x(d).start()

    normed_part(False, 0, 1, into(ys, 0))
    to_y(0).start()
    normed_part(False, 1, 1, into(zs, 0))
    to_z(0).start()
    normed_part(False, 1, 0, into(zs, 2))
    to_z(2).start()
    normed_part(True, 0, 1, into(ys, 1))
    to_y(1).start()
    grad_to_core(1)
    to_y(0).wait_recv()
    normed_part(False, 0, 0, into(zs, 1, yr))
    to_z(1).start()
    to_z(0).wait_recv()
    normed_part(True, 1, 1, into(ys, 2, zr))
    to_y(2).start()

    for d in range(2):
        to_core(1, d).wait_recv()
        to_x(d).wait_recv()
        fs[d] = (pairs[d, :, of_core(core)] + cr[1, d].astype(f32) + xr[d].astype(f32)).astype(bf16)
        if d == 0:

            @pl.when(alone)
            def _():
                fr[0] = fs[0]

            @pl.when(jnp.logical_not(alone))
            def _():
                to_owner().start()
        else:
            to_passer().start()
    for d in range(2):
        small_core(1, d).wait_recv()
        small_x(d).wait_recv()
        kf[d] = sv[:, channels(d, x, core)] + kr[1, d] + kx[d]

    @pl.when(alone)
    def _():
        kg[0] = kf[0]

    @pl.when(jnp.logical_not(alone))
    def _():
        small_owner(0).start()

    small_owner(1).start()

    for h in range(2):

        def store(cols, v, h=h):
            own[h * part : (h + 1) * part, cols] = v

        normed_part(True, h, 0, store)

    to_passer().wait_recv()

    @pl.when(stays_here)
    def _():
        fr[1] = fq[...]

    @pl.when(jnp.logical_not(stays_here))
    def _():
        pass_owner().start()

    loads[3].wait()
    for h in range(2):
        to_y(1 + h).wait_recv()
        to_z(1 + h).wait_recv()
        total = own[h * part : (h + 1) * part, :] + yr[1 + h].astype(f32) + zr[1 + h].astype(f32)
        tokens = raw[h * part : (h + 1) * part, :].astype(f32)
        pulled = total * gain_in_ref[0:1] - pull_ref[h * part : (h + 1) * part, :] * tokens
        fin[h * part : (h + 1) * part, :] = pulled.astype(bf16)
        product = total * tokens
        folded = jnp.sum(product.reshape(part // 8, 8, width), axis=0)
        for b in range(SLOTS):
            if h == 0:
                gs[b] = folded[:, b * n : (b + 1) * n]
            else:
                gs[b] = gs[b] + folded[:, b * n : (b + 1) * n]

    cut = tall - LC
    low = cut - LC
    moves = {
        0: ([(0, tall, 0)], None),
        1: ([(0, cut, 0)], (cut, 3, low)),
        2: ([(LC, tall, 0)], (0, 1, cut)),
        3: ([(LC, cut, 0), (cut, tall, cut)], (0, 2, cut)),
    }

    def border(k):
        stays, leaves = moves[k]
        mine = [pltpu.make_async_copy(fin.at[a:b], dn_ref.at[at : at + b - a], loc.at[i]) for i, (a, b, at) in enumerate(stays)]
        if leaves is None:
            return mine, None
        a, to, at = leaves
        return mine, remote(fin.at[a : a + LC], dn_ref.at[at : at + LC], b_send.at[0], b_recv.at[0], (g, r, to))

    for k in range(4):

        @pl.when(c == k)
        def _(k=k):
            mine, gone = border(k)
            if gone is not None:
                gone.start()
            for copy in mine:
                copy.start()

    def gain_copy(dg, dc):
        to = ((g + dg) % 4, r, (c + dc) % 4)
        i = 4 * dg + dc - 1
        return remote(gs.at[(g + dg) % 4], gr.at[i], g_send.at[i], g_recv.at[0], to)

    pairs = [(dg, dc) for dg in range(4) for dc in range(4) if dg or dc]
    for dg, dc in pairs:
        gain_copy(dg, dc).start()

    @pl.when(jnp.logical_not(alone))
    def _():
        to_owner().wait_recv()

    @pl.when(jnp.logical_not(stays_here))
    def _():
        pass_owner().wait_recv()

    grad_ref[...] = fr[0].astype(f32) + fr[1].astype(f32)

    pltpu.make_async_copy(gr, gr, g_recv.at[0]).wait()
    gain_ref[...] = jnp.sum(gr[...], axis=0) + gs[g]

    for k in range(4):

        @pl.when(c == k)
        def _(k=k):
            mine, gone = border(k)
            for copy in mine:
                copy.wait()
            if gone is not None:
                gone.wait()

    @pl.when(jnp.logical_not(alone))
    def _():
        small_owner(0).wait()

    small_owner(1).wait()
    at = 0
    for ref in small_refs:
        ref[...] = kg[0, at : at + ref.shape[0], :] + kg[1, at : at + ref.shape[0], :]
        at += ref.shape[0]
    for d in range(2):
        for j in range(2):
            small_core(j, d).wait_send()
        small_x(d).wait_send()

    for dg, dc in pairs:
        gain_copy(dg, dc).wait_send()
    for i in range(3):
        to_y(i).wait_send()
        to_z(i).wait_send()
    for d in range(2):
        for i in range(2):
            to_core(i, d).wait_send()
        to_x(d).wait_send()

    @pl.when(jnp.logical_not(alone))
    def _():
        to_owner().wait_send()

    @pl.when(jnp.logical_not(stays_here))
    def _():
        pass_owner().wait_send()

    to_passer().wait_send()


SMALL_ROWS = (KCONV, 1, 3, 1, 1, 6, NSTATE, RANK, XW)


def finish_kernel(*refs):
    n = len(SMALL_ROWS)
    finish(*refs[:16], refs[16 : 16 + n], *refs[16 + n :])


def run_finish(d_inner, d_gate, normed, raw, wi, wg, gain, pull, small):
    w = d_inner.shape[1]
    width, n = wi.shape[1], wi.shape[2]
    tall = SEQ // 2
    part = tall // 2
    dma = pltpu.SemaphoreType.DMA
    low = lambda *shape: pltpu.VMEM(shape, bf16)
    vmem = pl.BlockSpec(memory_space=pltpu.VMEM)
    rows = sum(v.shape[0] for v in small)
    return pl.pallas_call(
        finish_kernel,
        in_specs=[ANY] * 6 + [vmem, vmem] + [ANY] * 5,
        out_specs=[ANY, vmem, vmem] + [vmem] * len(SMALL_ROWS),
        out_shape=(shaped(tall, width, dtype=bf16), shaped(width, n), shaped(8, n), *[shaped(v, 128) for v in SMALL_ROWS]),
        scratch_shapes=[
            low(SEQ, w),
            low(SEQ, w),
            low(2, SEQ, width),
            low(tall, width),
            low(2, width, w),
            low(2, width, w),
            low(2, 2, width, n),
            low(2, 2, width, n),
            pltpu.VMEM((2, width, 2 * n), f32),
            low(2, width, n),
            low(2, width, n),
            low(2, width, n),
            low(2, width, n),
            low(width, n),
            low(3, part, width),
            low(3, part, width),
            low(3, part, width),
            low(3, part, width),
            pltpu.VMEM((tall, width), f32),
            low(tall, width),
            pltpu.VMEM((SLOTS, 8, n), f32),
            pltpu.VMEM((15, 8, n), f32),
            pltpu.VMEM((rows, w), f32),
            pltpu.VMEM((2, 2, rows, 128), f32),
            pltpu.VMEM((2, rows, 128), f32),
            pltpu.VMEM((2, rows, 128), f32),
            pltpu.VMEM((2, rows, 128), f32),
            pltpu.VMEM((2, rows, 128), f32),
            dma((6,)),
            dma((4,)),
            dma((4,)),
            dma((2,)),
            dma((2,)),
            dma((2,)),
            dma((2,)),
            dma((1,)),
            dma((1,)),
            dma((3,)),
            dma((3,)),
            dma((3,)),
            dma((3,)),
            dma((1,)),
            dma((1,)),
            dma((15,)),
            dma((1,)),
            dma((8,)),
            dma((8,)),
            dma((1,)),
        ],
        compiler_params=pltpu.CompilerParams(collective_id=1, has_side_effects=True, vmem_limit_bytes=VMEM_LIMIT),
        cost_estimate=pl.CostEstimate(flops=60 * 1000000000, bytes_accessed=1000000, transcendentals=0),
    )(d_inner, d_gate, normed, raw, wi, wg, gain, pull, *small)


def late_parts(order_ref, normed_ref, gate_ref, gated_ref, cot_ref, gate_sent, out_sent, gate_kept, out_kept):
    t = pl.program_id(0)
    for d in range(2):
        low = dot_tn(normed_ref[d], gate_ref[...])
        high = dot_tn(gated_ref[...], cot_ref[d])

        @pl.when(t < 2)
        def _(d=d, low=low, high=high):
            gate_sent[0, d] = low.astype(bf16)
            out_sent[0, d] = high.astype(bf16)

        @pl.when(t >= 2)
        def _(d=d, low=low, high=high):
            gate_kept[0, d] = low
            out_kept[0, d] = high


def run_late_parts(order, normed, d_gate, gated, cot):
    width = normed.shape[2]
    w = gated.shape[1]
    n = w // SLOTS
    sent = pl.BlockSpec((1, 2, width, n), lambda t, o: (jnp.minimum(t, 1), 0, 0, 0))
    kept = pl.BlockSpec((1, 2, width, n), lambda t, o: (jnp.maximum(t - 2, 0), 0, 0, 0))
    return pl.pallas_call(
        late_parts,
        grid_spec=pltpu.PrefetchScalarGridSpec(
            num_scalar_prefetch=1,
            grid=(SLOTS,),
            in_specs=[
                pl.BlockSpec((2, SEQ, width), lambda t, o: (0, 0, 0)),
                pl.BlockSpec((SEQ, n), lambda t, o: (0, o[t])),
                pl.BlockSpec((SEQ, w), lambda t, o: (0, 0)),
                pl.BlockSpec((2, SEQ, n), lambda t, o: (0, 0, o[t])),
            ],
            out_specs=(sent, sent, kept, kept),
        ),
        out_shape=(shaped(2, 2, width, n, dtype=bf16), shaped(2, 2, width, n, dtype=bf16), shaped(2, 2, width, n), shaped(2, 2, width, n)),
        compiler_params=pltpu.CompilerParams(dimension_semantics=("arbitrary",), vmem_limit_bytes=VMEM_LIMIT),
        cost_estimate=pl.CostEstimate(flops=14 * 1000000000, bytes_accessed=1000000, transcendentals=0),
    )(order, normed, d_gate, gated, cot)


QUARTERS = 4
SUM_LAG = 3
PIECE = SEQ // 2 // QUARTERS
OTHER_STEP = (1, 2, 3, 4)
PAIR_STEP = (3, 4, 1, 2)
FINAL_STEP = (7, 7, 7, 7)
X_STEP = (0, 1)
OWNER_STEP = (2, 4)
DONE_STEP = (8, 8)
QUARTER_STEP = ((2, 2, 3, 3), (4, 4, 5, 5))
PASS_STEP = ((4, 4, 5, 5), (6, 6, 6, 6))


def border_moves(tall):
    cut = tall - LC
    low = cut - LC
    return {
        0: ([(0, tall, 0)], None),
        1: ([(0, cut, 0)], (cut, 3, low)),
        2: ([(LC, tall, 0)], (0, 1, cut)),
        3: ([(LC, cut, 0), (cut, tall, cut)], (0, 2, cut)),
    }


def backward(xdbl_ref, xconv_ref, dy_ref, dtp_ref, vec_ref, rate_ref, starts_ref, mix_ref, into_ref, sent_hbm, kept_hbm, own_hbm, oth_hbm,
             dxdbl_ref, dxc_ref, alog_ref, sums_ref, dtpg_ref, grad_refs, branch_ref,
             first, first_s, first_r, part, ys, yr, zs, zr, cr, kp, xs, xr, fs, fr, fq, out, own, oth, by_s, by, bz_s, bz, fin,
             y_send, y_recv, z_send, z_recv, e_send, e_recv, c_send, c_recv, x_send, x_recv, f_send, f_recv, r_send, r_recv,
             p_send, p_recv, q_send, q_recv, b_send, b_recv, load_k, load_o, stay, put, *scratch):
    i = pl.program_id(0)
    g, r, c = lax.axis_index("grp"), lax.axis_index("row"), lax.axis_index("col")
    x, core, s, p = g // 2, g % 2, c // 2, c % 2
    q = 2 * p + xor_bit(r, s)
    tall = SEQ // 2
    alone = q == c
    passed = 2 * p + xor_bit(1 - r, s)
    stays_here = passed == c
    y_dev, z_dev, far_dev = (g, 1 - r, c), (g, r, 2 * s + 1 - p), (g, 1 - r, (c + 2) % 4)
    x_dev, core_dev = ((1 - x) * 2 + core, r, c), (2 * x + 1 - core, r, c)
    to_first = remote(first_s, first_r, e_send.at[0], e_recv.at[0], far_dev)

    def to_y(k):
        return remote(ys.at[k], yr.at[k], y_send.at[k], y_recv.at[k], y_dev)

    def to_z(k):
        return remote(zs.at[k], zr.at[k], z_send.at[k], z_recv.at[k], z_dev)

    def to_core(n, j):
        return remote(sent_hbm[n].at[j], cr.at[n, j], c_send.at[n, j], c_recv.at[n, j], core_dev)

    def load(n, j):
        return pltpu.make_async_copy(kept_hbm[n].at[j], kp.at[n], load_k.at[n])

    def to_x(n):
        return remote(xs.at[n], xr.at[n], x_send.at[n], x_recv.at[n], x_dev)

    def quarter(ref, at):
        rows = ref.shape[0] // QUARTERS
        return ref if at is None else ref.at[pl.ds(at * rows, rows)]

    def to_owner(n, at=None):
        return remote(quarter(fs.at[n, 0], at), quarter(fr.at[n, 0], at), f_send.at[n, 0], f_recv.at[n, 0], (g, r, q))

    def to_passer(n):
        return remote(fs.at[n, 1], fq.at[n], r_send.at[n], r_recv.at[n], y_dev)

    def pass_owner(n, at=None):
        return remote(quarter(fq.at[n], at), quarter(fr.at[n, 1], at), f_send.at[n, 1], f_recv.at[n, 1], (g, r, passed))

    def rows_at(mine, j):
        return pl.ds(pl.multiple_of((p if mine else 1 - p) * tall + j * PIECE, 16), PIECE)

    def branch_y(m):
        if m >= QUARTERS:
            src = oth_hbm.at[rows_at(False, m - QUARTERS)]
        elif m < 2:
            src = oth_hbm.at[rows_at(True, m)]
        else:
            src = by_s.at[m - 2]
        return remote(src, by.at[m], p_send.at[m], p_recv.at[m], y_dev)

    def branch_z(m):
        src = bz_s.at[m] if m < QUARTERS else oth_hbm.at[rows_at(False, m - 2)]
        return remote(src, bz.at[m], q_send.at[m], q_recv.at[m], z_dev)

    load_own = pltpu.make_async_copy(own_hbm, own, load_o.at[0])
    load_oth = pltpu.make_async_copy(oth_hbm.at[pl.ds(pl.multiple_of(p * tall + 2 * PIECE, 16), 2 * PIECE)], oth, load_o.at[1])

    def border(k):
        stays, leaves = border_moves(tall)[k]
        mine = [pltpu.make_async_copy(fin.at[a:b], branch_ref.at[at : at + b - a], stay.at[n]) for n, (a, b, at) in enumerate(stays)]
        if leaves is None:
            return mine, None
        a, to, at = leaves
        return mine, remote(fin.at[a : a + LC], branch_ref.at[at : at + LC], b_send.at[0], b_recv.at[0], (g, r, to))

    def at_border(act):
        for k in range(4):

            @pl.when(c == k)
            def _(k=k):
                act(*border(k))

    def pass_on(k):
        to_y(k).wait_recv()
        part[k] = part[k] + yr[k].astype(f32)
        zs[k] = part[k].astype(bf16)
        to_z(k).start()

    def settle(k):
        to_z(k).wait_recv()
        dxdbl_ref[NCH - 1 - k] = part[k] + zr[k].astype(f32)

    @pl.when(i == 0)
    def _():
        barrier = pltpu.get_barrier_semaphore()
        for dr in range(2):
            for dc in range(4):
                if dr or dc:
                    pl.semaphore_signal(barrier, inc=1, device_id=(g, (r + dr) % 2, (c + dc) % 4), device_id_type=MESH)
        for device in (x_dev, core_dev):
            pl.semaphore_signal(barrier, inc=1, device_id=device, device_id_type=MESH)
        pl.semaphore_wait(barrier, 9)
        for j in range(2):
            for n in range(2):
                to_core(n, j).start()
        for n in range(2):
            load(n, 0).start()
        load_own.start()
        load_oth.start()
        for m in (QUARTERS, QUARTERS + 1):
            branch_y(m).start()
            branch_z(m).start()
        first[...] = jnp.zeros_like(first)
        alog_ref[...] = jnp.zeros_like(alog_ref)
        sums_ref[...] = jnp.zeros_like(sums_ref)
        dtpg_ref[...] = jnp.zeros_like(dtpg_ref)

    @pl.when(i == 1)
    def _():
        to_first.wait()
        first[...] = mix_ref[0:1] * first_s[...] + into_ref[0:1] * first_r[...]

    chunk_backward(xdbl_ref, xconv_ref, dy_ref, dtp_ref, vec_ref, rate_ref, starts_ref, part.at[i], dxc_ref, alog_ref, sums_ref, dtpg_ref, first, *scratch)

    @pl.when(i == 0)
    def _():
        first_s[...] = first[...]
        to_first.start()

    @pl.when(i == 1)
    def _():
        load_own.wait()
        load_oth.wait()

    for n in range(2):

        @pl.when(i == X_STEP[n])
        def _(n=n):
            to_core(n, 0).wait_recv()
            load(n, 0).wait()
            xs[n] = (kp[n] + cr[n, 0].astype(f32)).astype(bf16)
            to_x(n).start()
            load(n, 1).start()

        @pl.when(i == OWNER_STEP[n])
        def _(n=n):
            load(n, 1).wait()
            to_core(n, 1).wait_recv()
            to_x(n).wait_recv()
            fs[n] = (kp[n] + cr[n, 1].astype(f32) + xr[n].astype(f32)).astype(bf16)

            to_passer(n).start()

            @pl.when(alone)
            def _():
                fr[n, 0] = fs[n, 0]

        @pl.when(i == OWNER_STEP[n] + 2)
        def _(n=n):
            to_passer(n).wait_recv()

            @pl.when(stays_here)
            def _():
                fr[n, 1] = fq[n]

        for k in range(QUARTERS):

            @pl.when(jnp.logical_not(alone) & (i == QUARTER_STEP[n][k]))
            def _(n=n, k=k):
                to_owner(n, k).start()

            @pl.when(jnp.logical_not(stays_here) & (i == PASS_STEP[n][k]))
            def _(n=n, k=k):
                pass_owner(n, k).start()

        @pl.when(i == DONE_STEP[n])
        def _(n=n):
            @pl.when(jnp.logical_not(alone))
            def _():
                to_owner(n).wait_recv()

            @pl.when(jnp.logical_not(stays_here))
            def _():
                pass_owner(n).wait_recv()

            out[n] = fr[n, 0].astype(f32) + fr[n, 1].astype(f32)
            pltpu.make_async_copy(out.at[n], grad_refs[n], put.at[n]).start()

    for j in range(QUARTERS):

        @pl.when(i == OTHER_STEP[j])
        def _(j=j):
            if j >= 2:
                branch_z(QUARTERS + j - 2).wait_recv()
                mine = oth[(j - 2) * PIECE : (j - 1) * PIECE, :].astype(f32)
                by_s[j - 2] = (mine + bz[QUARTERS + j - 2].astype(f32)).astype(bf16)
            branch_y(j).start()

        @pl.when(i == PAIR_STEP[j])
        def _(j=j):
            total = own[rows_at(False, j), :]
            if j < 2:
                branch_y(QUARTERS + j).wait_recv()
                total = total + by[QUARTERS + j].astype(f32)
            bz_s[j] = total.astype(bf16)
            branch_z(j).start()

        @pl.when(i == FINAL_STEP[j])
        def _(j=j):
            branch_y(j).wait_recv()
            branch_z(j).wait_recv()
            fin[j * PIECE : (j + 1) * PIECE, :] = (own[rows_at(True, j), :] + by[j].astype(f32) + bz[j].astype(f32)).astype(bf16)

    @pl.when(i == 7)
    def _():
        def begin(mine, gone):
            if gone is not None:
                gone.start()
            for copy in mine:
                copy.start()

        at_border(begin)

    @pl.when(i >= SUM_LAG)
    def _():
        pass_on(i - SUM_LAG)

    ys[i] = part[i].astype(bf16)
    to_y(i).start()
    @pl.when(i == NCH - 1)
    def _():
        alog_ref[...] = alog_ref[...] * rate_ref[...]
        for k in range(NCH - SUM_LAG, NCH):
            pass_on(k)
        for k in range(NCH):
            settle(k)

        def finish_border(mine, gone):
            for copy in mine:
                copy.wait()
            if gone is not None:
                gone.wait()

        at_border(finish_border)

        def sent(k, _):
            to_y(k).wait_send()
            to_z(k).wait_send()
            return 0

        lax.fori_loop(0, NCH, sent, 0)
        for n in range(2):
            for j in range(2):
                to_core(n, j).wait_send()
            to_x(n).wait_send()

            to_passer(n).wait_send()

            @pl.when(jnp.logical_not(alone))
            def _(n=n):
                to_owner(n).wait_send()

            @pl.when(jnp.logical_not(stays_here))
            def _(n=n):
                pass_owner(n).wait_send()

            pltpu.make_async_copy(out.at[n], grad_refs[n], put.at[n]).wait()
        for m in range(QUARTERS + 2):
            branch_y(m).wait_send()
            branch_z(m).wait_send()


def backward_kernel(*refs):
    backward(*refs[:9], refs[9:11], refs[11:13], *refs[13:20], refs[20:22], *refs[22:])


def run_backward(xdbl, xconv, dy, dtp, vec, rate, starts, mix, into, sent, kept, own, oth):
    w = xconv.shape[1]
    width = own.shape[1]
    _, _, tall, n = sent[0].shape
    at = lambda i: NCH - 1 - i
    dma = pltpu.SemaphoreType.DMA
    low = lambda *shape: pltpu.VMEM(shape, bf16)
    sums = low(NCH, XW, CH)
    state = pltpu.VMEM((NSTATE, w), f32)
    return pl.pallas_call(
        backward_kernel,
        grid=(NCH,),
        in_specs=[
            chunk_of(XW, at),
            rows_of(w, at),
            rows_of(w, at),
            whole(RANK, w),
            whole(8, w),
            whole(NSTATE, w),
            pl.BlockSpec((1, NSTATE, w), lambda i: (at(i), 0, 0)),
            whole(8, w),
            whole(8, w),
        ]
        + [ANY] * 6,
        out_specs=(whole(NCH, XW, CH), rows_of(w, at), whole(NSTATE, w), whole(8, w), whole(RANK, w), ANY, ANY, ANY),
        out_shape=(
            shaped(NCH, XW, CH),
            shaped(SEQ, w),
            shaped(NSTATE, w),
            shaped(8, w),
            shaped(RANK, w),
            shaped(tall, n),
            shaped(tall, n),
            shaped(SEQ // 2, width, dtype=bf16),
        ),
        scratch_shapes=[
            state,
            state,
            state,
            pltpu.VMEM((NCH, XW, CH), f32),
            sums,
            sums,
            sums,
            sums,
            low(2, 2, 2, tall, n),
            pltpu.VMEM((2, 2, tall, n), f32),
            low(2, 2, tall, n),
            low(2, 2, tall, n),
            low(2, 2, tall, n),
            low(2, 2, tall, n),
            low(2, tall, n),
            pltpu.VMEM((2, tall, n), f32),
            pltpu.VMEM((SEQ, width), f32),
            low(2 * PIECE, width),
            low(2, PIECE, width),
            low(QUARTERS + 2, PIECE, width),
            low(QUARTERS, PIECE, width),
            low(QUARTERS + 2, PIECE, width),
            low(SEQ // 2, width),
            dma((NCH,)),
            dma((NCH,)),
            dma((NCH,)),
            dma((NCH,)),
            dma((1,)),
            dma((1,)),
            dma((2, 2)),
            dma((2, 2)),
            dma((2,)),
            dma((2,)),
            dma((2, 2)),
            dma((2, 2)),
            dma((2,)),
            dma((2,)),
            dma((QUARTERS + 2,)),
            dma((QUARTERS + 2,)),
            dma((QUARTERS + 2,)),
            dma((QUARTERS + 2,)),
            dma((1,)),
            dma((1,)),
            dma((2,)),
            dma((2,)),
            dma((2,)),
            dma((2,)),
            *backward_scratch(w),
        ],
        compiler_params=pltpu.CompilerParams(
            dimension_semantics=("arbitrary",), collective_id=3, has_side_effects=True, vmem_limit_bytes=61 * 1024 * 1024
        ),
        cost_estimate=pl.CostEstimate(flops=120 * 1000000000, bytes_accessed=1000000, transcendentals=0),
    )(xdbl, xconv, dy, dtp, vec, rate, starts, mix, into, *sent, *kept, own, oth)


def conv_backward_far(inner_ref, halo_ref, inv_ref, halo_inv_ref, tail_ref, conv_ref, xproj_ref, dxc_ref, dxdbl_ref, mix_ref, into_ref,
                      dproj_ref, dscale_ref, sums_ref, xprojg_ref, head, sent, got, buf, dbuf, send_sem, recv_sem):
    i = pl.program_id(0)
    g, r, c = lax.axis_index("grp"), lax.axis_index("row"), lax.axis_index("col")
    far_dev = (g, 1 - r, (c + 2) % 4)
    to_far = remote(sent, got, send_sem.at[0], recv_sem.at[0], far_dev)

    @pl.when(i == 0)
    def _():
        barrier = pltpu.get_barrier_semaphore()
        pl.semaphore_signal(barrier, inc=1, device_id=far_dev, device_id_type=MESH)
        pl.semaphore_wait(barrier, 1)
        head[...] = jnp.zeros_like(head)
        sums_ref[...] = jnp.zeros_like(sums_ref)
        xprojg_ref[...] = jnp.zeros_like(xprojg_ref)

    @pl.when(i == 1)
    def _():
        to_far.wait()
        head[...] = mix_ref[...] * sent[...] + into_ref[...] * got[...]

    conv_chunk(NCH - 1 - i, inner_ref, halo_ref, inv_ref, halo_inv_ref, tail_ref, conv_ref, xproj_ref, dxc_ref, dxdbl_ref,
               dproj_ref, dscale_ref, sums_ref, xprojg_ref, head, buf, dbuf)

    @pl.when(i == 0)
    def _():
        sent[...] = head[...]
        to_far.start()


def run_conv_backward_far(inner, inv, tail, conv, xproj, dxc, dxdbl, mix, into):
    w = inner.shape[1]
    at = lambda i: NCH - 1 - i
    before = lambda i: (jnp.maximum(at(i) * (CH // 8) - 1, 0), 0)
    rows = pltpu.VMEM((8, w), f32)
    return pl.pallas_call(
        conv_backward_far,
        grid=(NCH,),
        in_specs=[
            rows_of(w, at),
            pl.BlockSpec((8, w), before),
            rows_of(1, at),
            pl.BlockSpec((8, 1), before),
            whole(8, w),
            whole(8, w),
            whole(XW, w),
            rows_of(w, at),
            chunk_of(XW, at),
            whole(8, w),
            whole(8, w),
        ],
        out_specs=(rows_of(w, at), rows_of(1, at), whole(8, w), whole(XW, w)),
        out_shape=(shaped(SEQ, w, dtype=bf16), shaped(SEQ, 1), shaped(8, w), shaped(XW, w)),
        scratch_shapes=[
            rows,
            rows,
            rows,
            pltpu.VMEM((CH + 8, w), f32),
            pltpu.VMEM((CH + 8, w), f32),
            pltpu.SemaphoreType.DMA((1,)),
            pltpu.SemaphoreType.DMA((1,)),
        ],
        compiler_params=pltpu.CompilerParams(
            dimension_semantics=("arbitrary",), collective_id=4, has_side_effects=True, vmem_limit_bytes=VMEM_LIMIT
        ),
        cost_estimate=pl.CostEstimate(flops=20 * 1000000000, bytes_accessed=1000000, transcendentals=0),
    )(inner, inner, inv, inv, tail, conv, xproj, dxc, dxdbl, mix, into)


def per_device(
    tokens,
    gain,
    in_proj,
    conv_weight,
    conv_bias,
    x_proj,
    dt_proj,
    dt_bias,
    a_log,
    d_skip,
    out_proj,
    table,
    cotangent,
):
    row = lax.axis_index("row")
    col = lax.axis_index("col")
    grp = lax.axis_index("grp")
    low_row = row == 0
    low_pair = col % 2 == 0
    half = col // 2
    places = [(r, c) for r in range(2) for c in range(4)]
    quick = lax.axis_size("grp") == 4

    def spot(r, c):
        return r * 4 + c

    def send(v, pairs):
        return lax.ppermute(v, ("row", "col"), [(spot(*a), spot(*b)) for a, b in pairs])

    def swap(v):
        return send(v, [((r, c), (1 - r, c)) for r, c in places])

    def pair(v):
        return send(v, [((r, c), (r, c ^ 1)) for r, c in places])

    def across(v):
        return send(v, [((r, c), (1 - r, c ^ 2)) for r, c in places])

    def quarter_spot(q, s):
        return ((q & 1) ^ s, 2 * s + (q >> 1))

    same = [((r, q), quarter_spot(q, r ^ (q & 1))) for r, q in places]
    other = [((r, q), quarter_spot(q, 1 ^ r ^ (q & 1))) for r, q in places]
    spread = [((r, q), quarter_spot(q, r)) for r, q in places]

    def back(pairs):
        return [(b, a) for a, b in pairs]

    def flip(v, bit):
        return lax.ppermute(v, "grp", [(g, g ^ bit) for g in range(4)])

    def scatter_grp(v, axis):
        return lax.psum_scatter(v, "grp", scatter_dimension=axis, tiled=True)

    def by_pair(own, paired):
        return jnp.where(low_pair, own, paired), jnp.where(low_pair, paired, own)

    local = tokens.shape[0]
    cut = local - LC
    tail_at = cut - LC

    def to_sequences(v):
        got = send(jnp.where(col == 3, v[tail_at:cut], v[cut:]), [((r, a), (r, b)) for r in range(2) for a, b in ((1, 2), (2, 3), (3, 1))])
        low = jnp.concatenate([v[:cut], jnp.where(col == 0, v[cut:], got)], axis=0)
        two = jnp.concatenate([got, v[:cut]], axis=0)
        three = jnp.concatenate([got, v[:tail_at], v[cut:]], axis=0)
        return jnp.where(col < 2, low, jnp.where(col == 2, two, three))

    def from_sequences(v):
        got = send(jnp.where(col == 1, v[cut:], v[:LC]), [((r, b), (r, a)) for r in range(2) for a, b in ((1, 2), (2, 3), (3, 1))])
        low = jnp.concatenate([v[:cut], jnp.where(col == 0, v[cut:], got)], axis=0)
        two = jnp.concatenate([v[LC:], got], axis=0)
        three = jnp.concatenate([v[LC:cut], got, v[cut:]], axis=0)
        return jnp.where(col < 2, low, jnp.where(col == 2, two, three))

    def gather_quad(v):
        swapped = swap(v)
        paired = pair(v)
        mid = v.shape[0] // 2
        diagonal = jnp.concatenate([pair(swapped[:mid]), swap(paired[mid:])], axis=0)
        first_own, second_own = by_pair(v, paired)
        first_oth, second_oth = by_pair(swapped, diagonal)
        return jnp.stack([jnp.concatenate([first_own, second_own], axis=0), jnp.concatenate([first_oth, second_oth], axis=0)])

    def scatter_quad(own, oth):
        v = own + swap(oth.astype(bf16)).astype(f32)
        first, second = v[:local], v[local:]
        kept, sent = jnp.where(low_pair, first, second), jnp.where(low_pair, second, first)
        return kept + pair(sent.astype(bf16)).astype(f32)

    own_table = jnp.where(half == 0, table[0], table[1])
    oth_table = jnp.where(half == 0, table[1], table[0])
    resumes_own = own_table == half
    resumed_by_other = oth_table == half

    small = jnp.concatenate([conv_weight, conv_bias[None], dt_bias[None], d_skip[None], a_log, dt_proj, x_proj.T], axis=0)
    lanes = small.shape[1]
    used = small.shape[0]
    gain_rows = gain.size // lanes
    width = tokens.shape[1]
    if quick:
        small = jnp.concatenate([small, gain.reshape(gain_rows, lanes)], axis=0)
        small = jnp.pad(small, ((0, -small.shape[0] % 16), (0, 0)))
        raw, wi, small = run_gather_start(tokens, in_proj[:, 0], small)
        gain_all = small[:, used : used + gain_rows].reshape(2, width).astype(f32)
        small = jnp.swapaxes(small, 0, 1).reshape(small.shape[1], 8 * lanes)
    else:
        raw = gather_quad(to_sequences(tokens))

        def weight(shard):
            v = lax.all_gather(jnp.stack([send(shard, same), send(shard, other)]), "grp", axis=2, tiled=True)
            v = v.reshape(2, v.shape[1], SLOTS, v.shape[2] // SLOTS)
            return jnp.transpose(v, (2, 0, 1, 3)).reshape(2 * SLOTS, v.shape[1], v.shape[3])

        wi = weight(in_proj[:, 0])
        small = send(lax.all_gather(small, ("row", "grp"), axis=1, tiled=True), spread)
        gain_all = lax.all_gather(gain, ("row", "grp"), axis=0, tiled=True).astype(f32).reshape(2, width)
    w = small.shape[1]
    zero_row = jnp.zeros((1, w), f32)
    conv = jnp.concatenate([small[0:5].astype(f32)] + [zero_row] * 3, axis=0)
    vec = jnp.concatenate([small[5:7].astype(f32)] + [zero_row] * 6, axis=0)
    rate = -jnp.exp(small[7 : 7 + NSTATE].astype(f32))
    dtp = small[7 + NSTATE : 7 + NSTATE + RANK]
    xproj = small[7 + NSTATE + RANK : 7 + NSTATE + RANK + XW]
    gain_own = jnp.where(low_row, gain_all[0], gain_all[1])
    gain_two = jnp.stack([gain_own, jnp.where(low_row, gain_all[1], gain_all[0])])

    zero_state = jnp.zeros((NSTATE, w), f32)
    if quick:
        mix = jnp.broadcast_to(resumes_own.astype(f32), (8, w))
        normed, inv, inner, xconv, yfull, starts, xdbl, tail, wg, wo, cot = run_forward(raw, gain_two, wi, mix, conv, xproj, dtp, vec, rate, in_proj[:, 1], out_proj, cotangent)
    else:
        normed, inv, inner = run_project_first(raw, gain_two, wi)
        tail_own = (inv * inner)[LP - 8 : LP]
        tail = jnp.where(resumes_own, tail_own, across(tail_own))
        xconv, xdbl = run_conv_forward(inner, inv, tail, conv, xproj)
        for move in (swap, pair):
            xdbl = xdbl + move(xdbl)
        xdbl = jnp.swapaxes(xdbl.reshape(XW, NCH, CH), 0, 1)
        *kept, final = run_scan_forward(0, PC, xdbl, xconv, dtp, vec, rate, zero_state)
        resumed = jnp.where(resumes_own, final, across(final))
        yfull, starts, _ = run_scan_forward(PC, NCH - PC, xdbl, xconv, dtp, vec, rate, resumed, kept)
        wg, wo = weight(in_proj[:, 1]), weight(out_proj)
        cot = gather_quad(to_sequences(cotangent))
    gated, d_yfull, d_gate_proj, gate_scale, branch_own, branch_oth = run_gate_backward(normed, wg, cot, wo, yfull, inv)

    def collect(v):
        return send(v[0].astype(bf16), back(same)).astype(f32) + send(v[1].astype(bf16), back(other)).astype(f32)

    def rows_product(a, b, out_dtype):
        return lax.dot_general(a, b, (((1,), (0,)), ((), ())), preferred_element_type=f32).astype(out_dtype)

    zero_head = jnp.zeros((8, w), f32)
    conv_back = functools.partial(run_conv_backward, inner=inner, inv=inv, tail=tail, conv=conv, xproj=xproj)
    if quick:
        x, core = grp // 2, grp % 2
        order = jnp.stack([2 * (1 - x) + 1 - core, 2 * x + 1 - core, 2 * (1 - x) + core, 2 * x + core]).astype(jnp.int32)
        gate_sent, out_sent, gate_kept, out_kept = run_late_parts(order, normed, d_gate_proj, gated, cot)
        sent, kept = (gate_sent, out_sent), (gate_kept, out_kept)
        into = jnp.broadcast_to(resumed_by_other.astype(f32), (8, w))
        dxdbl, dxc, alog_grad, scan_sums, dtp_grad, gate_grad, out_grad, branch = run_backward(
            xdbl, xconv, d_yfull, dtp, vec, rate, starts, mix, into, sent, kept, branch_own, branch_oth
        )
    else:
        branch = from_sequences(scatter_quad(branch_own, branch_oth).astype(bf16))
        out_grad = collect([scatter_grp(dot_tn(gated, cot[d]), 1) for d in range(2)])
        gate_grad = collect([scatter_grp(dot_tn(normed[d], d_gate_proj), 1) for d in range(2)])
        sums = (zero_state, jnp.zeros((8, w), f32), jnp.zeros((RANK, w), f32))
        scan = functools.partial(run_scan_backward, xdbl=xdbl, xconv=xconv, dy=d_yfull, dtp=dtp, vec=vec, rate=rate, starts=starts)
        dx_c, dxc, *sums, g_first = scan(PC, NCH - PC, carry=zero_state, sums=sums)
        g_into = jnp.where(resumes_own, g_first, 0.0) + jnp.where(resumed_by_other, across(g_first), 0.0)
        dx_p, dxc, *sums, _ = scan(0, PC, carry=g_into, sums=sums, kept=(dxc,))
        alog_grad, scan_sums, dtp_grad = sums
        alog_grad = alog_grad * rate
        dxdbl = jnp.concatenate([dx_p, dx_c], axis=1)
        for move in (swap, pair):
            dxdbl = dxdbl + move(dxdbl)
        dxdbl = jnp.swapaxes(dxdbl.reshape(XW, NCH, CH), 0, 1)

    output = (tokens.astype(f32) + branch.astype(f32)).astype(bf16)
    if quick:
        d_inner_proj, inner_scale, conv_sums, xproj_grad = run_conv_backward_far(inner, inv, tail, conv, xproj, dxc, dxdbl, mix, into)
    else:
        sums = (jnp.zeros((8, w), f32), jnp.zeros((XW, w), f32))
        dp, ds, *sums, head = conv_back(PC, NCH - PC, dxc=dxc, dxdbl=dxdbl, follow=zero_head, sums=sums)
        follow = jnp.where(resumes_own, head, 0.0) + jnp.where(resumed_by_other, across(head), 0.0)
        d_inner_proj, inner_scale, conv_sums, xproj_grad, _ = conv_back(0, PC, dxc=dxc, dxdbl=dxdbl, follow=follow, sums=sums, kept=(dp, ds))

    scale = gate_scale + inner_scale

    def own_rows(v):
        return jnp.where(low_pair, v[:local], v[local:])

    def pair_rows(v):
        return jnp.where(low_pair, v[local:], v[:local])

    diagonal = send(pair_rows(scale), [((r, c), (1 - r, c ^ 1)) for r, c in places])
    scale = own_rows(scale) + swap(own_rows(scale)) + pair(pair_rows(scale)) + diagonal
    inv_own = own_rows(inv)
    pull = scale * inv_own * inv_own * inv_own / D
    small_parts = (conv_sums, scan_sums, alog_grad, dtp_grad, xproj_grad)
    if quick:
        pulled, inner_grad, gain_sum, *small_grads = run_finish(
            d_inner_proj, d_gate_proj, normed, raw, wi, wg, gain_two, pull, small_parts
        )
        gain_grad = jnp.sum(gain_sum, axis=0)
    else:
        inner_grad = collect([scatter_grp(dot_tn(normed[d], d_inner_proj), 1) for d in range(2)])
        d_normed = scatter_quad(*run_normed_backward(d_inner_proj, d_gate_proj, wi, wg))
        fixed = own_rows(raw[0]).astype(f32)
        gain_grad = jnp.sum(d_normed * fixed, axis=0)
        gain_grad = lax.psum_scatter(lax.psum(gain_grad, "col"), "grp", scatter_dimension=0, tiled=True)
        pulled = from_sequences((d_normed * gain_own - pull * fixed).astype(bf16))
        small_grad = send(jnp.concatenate(small_parts, axis=0), back(spread))
        small_grad = lax.psum_scatter(small_grad, ("row", "grp"), scatter_dimension=1, tiled=True)
        small_grads = jnp.split(small_grad, [sum(SMALL_ROWS[: k + 1]) for k in range(len(SMALL_ROWS) - 1)], axis=0)
    input_grad = (cotangent.astype(f32) + pulled.astype(f32)).astype(bf16)
    in_grads = jnp.stack([inner_grad, gate_grad], axis=1)
    return (
        output,
        input_grad,
        gain_grad,
        in_grads,
        small_grads[0],
        small_grads[1][0],
        small_grads[8].T,
        small_grads[7],
        small_grads[3][0],
        small_grads[6],
        small_grads[4][0],
        out_grad,
    )


def solution(mesh):
    placed = (
        P(("grp", "col"), "row"),
        P(("row", "grp")),
        P("row", None, ("col", "grp")),
        P(None, ("col", "row", "grp")),
        P(("col", "row", "grp")),
        P(("col", "row", "grp"), None),
        P(None, ("col", "row", "grp")),
        P(("col", "row", "grp")),
        P(None, ("col", "row", "grp")),
        P(("col", "row", "grp")),
        P("col", ("row", "grp")),
        P("grp"),
        P(("grp", "col"), "row"),
    )
    return jax.shard_map(
        per_device,
        mesh=mesh,
        in_specs=placed,
        out_specs=(
            P(("grp", "col"), "row"),
            P(("grp", "col"), "row"),
            P(("row", "grp")),
            P("row", None, ("col", "grp")),
            P(None, ("col", "row", "grp")),
            P(("col", "row", "grp")),
            P(("col", "row", "grp"), None),
            P(None, ("col", "row", "grp")),
            P(("col", "row", "grp")),
            P(None, ("col", "row", "grp")),
            P(("col", "row", "grp")),
            P("col", ("row", "grp")),
        ),
        check_vma=False,
    )
```
